32 devices in a mesh: expert: 8 (over y, x, core), hidden: 4 (over z).
Axes of the slice: x: 2, y: 2, z: 4, core: 2. Of those that a mesh axis runs over, the one named last changes fastest.
Arguments:
- tokens: bfloat16 [6144, 1024], P(('expert', 'hidden')), may hold values from -6 to 6
- cotangent: bfloat16 [6144, 1024], P(('expert', 'hidden')), may hold values from -6 to 6
- routes: int32 [6144, 1], P(('expert', 'hidden')), may hold values from 0 to 7; in each aligned block of 192 rows (0 to 191, 192 to 383, ...) at most 48 rows name the same one
- attn_weight: float32 [4, 1024, 1024], P(None, ('expert', 'hidden')), may hold values from -0.75 to 0.75
- attn_first: float32 [4, 1024, 1024], P(None, ('expert', 'hidden')), may hold values from -7.6293945e-05 to 7.6293945e-05
- attn_second: float32 [4, 1024, 1024], P(None, ('expert', 'hidden')), may hold values from 7.0096936e-12 to 1.121551e-10
- norm_param: float32 [2, 1024], P(None, ('expert', 'hidden')), may hold values from -1.2 to 3.2
- norm_first: float32 [2, 1024], P(None, ('expert', 'hidden')), may hold values from -0.00030517578 to 0.00030517578
- norm_second: float32 [2, 1024], P(None, ('expert', 'hidden')), may hold values from 1.121551e-10 to 1.7944816e-09
- up_weight: bfloat16 [8, 1024, 4096], P('expert', None, 'hidden'), may hold values from -0.4375 to 0.4375
- up_first: float32 [8, 1024, 4096], P('expert', None, 'hidden'), may hold values from -7.6293945e-05 to 7.6293945e-05
- up_second: float32 [8, 1024, 4096], P('expert', None, 'hidden'), may hold values from 7.0096936e-12 to 1.121551e-10
- down_weight: bfloat16 [8, 4096, 1024], P('expert', 'hidden'), may hold values from -0.4375 to 0.4375
- down_first: float32 [8, 4096, 1024], P('expert', 'hidden'), may hold values from -7.6293945e-05 to 7.6293945e-05
- down_second: float32 [8, 4096, 1024], P('expert', 'hidden'), may hold values from 7.0096936e-12 to 1.121551e-10
- expert_vector: float32 [8, 3, 1024], P('expert'), may hold values from -1.2 to 1.4
- vector_first: float32 [8, 3, 1024], P('expert'), may hold values from -0.00030517578 to 0.00030517578
- vector_second: float32 [8, 3, 1024], P('expert'), may hold values from 1.121551e-10 to 1.7944816e-09
Outputs:
- block_out: bfloat16 [6144, 1024], P(('expert', 'hidden'))
- token_grad: bfloat16 [6144, 1024], P(('expert', 'hidden'))
- grad_norm: float32 [], replicated
- attn_update: float32 [4, 1024, 1024], P(None, ('expert', 'hidden'))
- attn_moment: float32 [4, 1024, 1024], P(None, ('expert', 'hidden'))
- attn_square: float32 [4, 1024, 1024], P(None, ('expert', 'hidden'))
- norm_update: float32 [2, 1024], P(None, ('expert', 'hidden'))
- norm_moment: float32 [2, 1024], P(None, ('expert', 'hidden'))
- norm_square: float32 [2, 1024], P(None, ('expert', 'hidden'))
- up_update: float32 [8, 1024, 4096], P('expert', None, 'hidden')
- up_moment: float32 [8, 1024, 4096], P('expert', None, 'hidden')
- up_square: float32 [8, 1024, 4096], P('expert', None, 'hidden')
- down_update: float32 [8, 4096, 1024], P('expert', 'hidden')
- down_moment: float32 [8, 4096, 1024], P('expert', 'hidden')
- down_square: float32 [8, 4096, 1024], P('expert', 'hidden')
- vector_update: float32 [8, 3, 1024], P('expert')
- vector_moment: float32 [8, 3, 1024], P('expert')
- vector_square: float32 [8, 3, 1024], P('expert')
- expert_stats: float32 [2, 8], P(None, 'expert')
The draws below stay inside these ranges and needn't reach their ends.
Inputs may be any that keep to these rules, and one draw needn't show every extreme that they name: `routes`: one expert per token; the tokens of one device name one expert at most 48 times; every expert is named.
All inputs are finite; a program needn't handle non-finite values.
Results may differ from the reference program's by a relative error of at most 0.018.
Values may be sent and summed in bfloat16 or wider, within the bound.
A program may use at most 256 MiB of HBM per device.

```python
import math
import jax
import jax.numpy as jnp
import numpy as np
from jax import lax

D = 1024
HEADS = 16
HEAD_DIM = 64
FF = 4096
TOK_DEV = 192
STEP = 10
EXPERTS = 8
CAP = 48
TOKENS = 6144
N_EXPERT = 8
N_HIDDEN = 4


def rise_factor(positions, ratio):
    return jnp.exp(math.log(ratio) * (positions - 0.5))


def draw_attn_weight(key, part):
    key = jax.random.fold_in(key, 11)
    base = jnp.clip(jax.random.normal(key, (4, D, D), jnp.float32), -6.0, 6.0)
    slab_scale = jnp.array([1.0, 1.0, 1.0, 4.0], jnp.float32)
    return base * slab_scale[:, None, None] * D ** (-0.5)


def draw_norm_param(key, part):
    key = jax.random.fold_in(key, 12)
    first_key, second_key = jax.random.split(key)
    positions = jnp.arange(D, dtype=jnp.float32) / (D - 1)
    rising = rise_factor(positions, 3.0)
    noise = jnp.clip(jax.random.normal(first_key, (D,), jnp.float32), -4.0, 4.0)
    gains = rising * (1.0 + 0.1 * noise)
    biases = 0.3 * jnp.clip(jax.random.normal(second_key, (D,), jnp.float32), -4.0, 4.0)
    return jnp.stack([gains, biases])


def expert_factor(ratio, width):
    by_expert = jnp.arange(EXPERTS, dtype=jnp.float32) / (EXPERTS - 1)
    by_unit = jnp.arange(width, dtype=jnp.float32) / (width - 1)
    return jnp.exp(math.log(ratio) * (0.5 * by_expert[:, None] + 0.5 * by_unit[None, :] - 0.5))


def draw_up_weight(key, part):
    key = jax.random.fold_in(key, 13)
    base = jnp.clip(jax.random.normal(key, (EXPERTS, D, FF), jnp.float32), -6.0, 6.0)
    factor = expert_factor(3.0, FF)
    return (base * factor[:, None, :] * D ** (-0.5)).astype(jnp.bfloat16)


def draw_down_weight(key, part):
    key = jax.random.fold_in(key, 14)
    base = jnp.clip(jax.random.normal(key, (EXPERTS, FF, D), jnp.float32), -6.0, 6.0)
    factor = expert_factor(3.0, FF)
    return (base * factor[:, :, None] * (2.0 * FF ** (-0.5))).astype(jnp.bfloat16)


def draw_expert_vector(key, part):
    key = jax.random.fold_in(key, 15)
    first_key, second_key, third_key = jax.random.split(key, 3)
    centroid = jnp.clip(jax.random.normal(first_key, (EXPERTS, D), jnp.float32), -6.0, 6.0)
    centroid = 0.4 * centroid * D ** (-0.5)
    gains = 1.0 + 0.1 * jnp.clip(jax.random.normal(second_key, (EXPERTS, D), jnp.float32), -4.0, 4.0)
    biases = 0.3 * jnp.clip(jax.random.normal(third_key, (EXPERTS, D), jnp.float32), -4.0, 4.0)
    return jnp.stack([centroid, gains, biases], axis=1)


def block_scale(own_key, dims, shards, smallest, largest):
    def one(dim, blocks):
        heights = jax.random.uniform(jax.random.fold_in(jax.random.fold_in(own_key, 6), dim), (blocks,), jnp.float32, smallest / len(shards), largest / len(shards))
        return jnp.repeat(jnp.exp(heights), dims[dim] // blocks).reshape((-1,) + (1,) * (len(dims) - dim - 1))

    gain = one(*shards[0])
    for cut in shards[1:]:
        gain = gain * one(*cut)
    return gain


def routed_block(key, own, number, rows, count, top, reach, slope):
    order = jax.random.permutation(key, count)
    crowded, common = shares(count, rows * top, reach, slope, True), shares(count, rows * top, reach, slope, False)
    places = jnp.arange(count)

    def named(lengths, offset_by):
        used = int((lengths > 0).sum())
        fixed = max(1, used // 4)
        passed = fixed + (places - fixed + offset_by * (used - fixed)) % max(1, count - fixed)
        return jnp.zeros((count,), jnp.int32).at[order[jnp.where(places < fixed, places, passed)]].set(jnp.asarray(lengths, jnp.int32))

    lengths = jnp.where(number % 4 == 0, named(crowded, number // 4), named(common, number - number // 4 - 1))
    mixed = jax.random.permutation(jax.random.fold_in(own, 3), count)
    giver, receiver = mixed[0:count // 2 * 2:2], mixed[1:count // 2 * 2:2]
    margin = jnp.minimum(lengths[giver] - 1, reach - lengths[receiver]) // 2
    margin = jnp.where((giver == order[0]) | (receiver == order[0]) | (lengths[receiver] == 0), 0, jnp.maximum(margin, 0))
    passed = jax.random.randint(jax.random.fold_in(own, 4), (count // 2,), 0, 1 << 20) % (margin + 1)
    lengths = lengths.at[giver].add(-passed).at[receiver].add(passed)
    members = jnp.searchsorted(jnp.cumsum(lengths), jnp.arange(rows * top), side="right").astype(jnp.int32)
    table = members.reshape(top, rows).T
    table = table[jax.random.permutation(jax.random.fold_in(own, 1), rows)]
    offset_by = jax.random.randint(jax.random.fold_in(own, 2), (rows, 1), 0, top)
    return jnp.take_along_axis(table, (jnp.arange(top)[None, :] + offset_by) % top, axis=1)


def shares(count, total, limit, skew, full):
    weights = [(1 << 20) // math.isqrt(grade ** skew) + 1 for grade in range(1, count + 1)]
    largest = limit if full else min(limit, max(-(-total // count), total * weights[0] // sum(weights)))
    least = 1 if total - largest >= count - 1 else 0
    given, surplus = [largest] + [least] * (count - 1), total - largest - least * (count - 1)
    while surplus > 0:
        free = [i for i in range(1, count) if given[i] < largest] or [i for i in range(1, count) if given[i] < limit]
        pool, remaining = sum([weights[i] for i in free]), surplus
        for i in free:
            addition = min(limit - given[i], max(1, remaining * weights[i] // pool), surplus)
            given[i] = given[i] + addition
            surplus = surplus - addition
    return np.array(given)


def bell_draw(own_key, dims, scale, bound, cuts=(), kind=jnp.bfloat16):
    values = jax.random.normal(own_key, dims, jnp.float32) * scale
    if len(cuts) > 0:
        values = block_scale(own_key, dims, cuts, -0.22, 0.18) * values
    return jnp.clip(values, min=-bound, max=bound).astype(kind)


def setup_inputs(seed: int = 0) -> dict:
    key_of = jax.random.split(jax.random.key(seed), 19)
    tokens = bell_draw(key_of[0], (TOKENS, D), 1.0, 6.0, ((0, 32),))
    cotangent = bell_draw(key_of[1], (TOKENS, D), 1.0, 6.0, ((0, 32),))
    routes_keys = jax.random.split(jax.random.fold_in(key_of[2], 1), TOKENS // TOK_DEV)
    routes_turns = jax.random.permutation(jax.random.fold_in(key_of[2], 3), TOKENS // TOK_DEV)
    routes = jax.vmap(lambda own, number: routed_block(jax.random.fold_in(key_of[2], 2), own, number, TOK_DEV, EXPERTS, 1, CAP, 2))(routes_keys, routes_turns).reshape((TOKENS, 1))
    attn_weight = draw_attn_weight(jax.random.fold_in(key_of[18], 71), 0)
    attn_first = bell_draw(key_of[4], (4, D, D), (0.111 * (4 * D * D + 2 * D + EXPERTS * (2 * D * FF + 3 * D)) ** -0.5), 7.62939453125e-05, ((1, 32),), jnp.float32)
    attn_second = jnp.clip(jnp.exp(math.log(1.1215509770901022e-10) - 2.7725887 * jax.random.uniform(key_of[5], (4, D, D), jnp.float32) ** block_scale(key_of[5], (4, D, D), ((1, 32),), -0.2, 0.2)), 7.009693606813139e-12, 1.1215509770901022e-10)
    norm_param = draw_norm_param(jax.random.fold_in(key_of[18], 71), 0)
    norm_first = bell_draw(key_of[7], (2, D), (0.444 * (4 * D * D + 2 * D + EXPERTS * (2 * D * FF + 3 * D)) ** -0.5), 0.00030517578, ((1, 32),), jnp.float32)
    norm_second = jnp.clip(jnp.exp(math.log(1.7944815633441635e-09) - 2.7725887 * jax.random.uniform(key_of[8], (2, D), jnp.float32) ** block_scale(key_of[8], (2, D), ((1, 32),), -0.2, 0.2)), 1.1215509770901022e-10, 1.7944815633441635e-09)
    up_weight = draw_up_weight(jax.random.fold_in(key_of[18], 71), 0)
    up_first = bell_draw(key_of[10], (EXPERTS, D, FF), (0.111 * (4 * D * D + 2 * D + EXPERTS * (2 * D * FF + 3 * D)) ** -0.5), 7.62939453125e-05, ((0, 8), (2, 4)), jnp.float32)
    up_second = jnp.clip(jnp.exp(math.log(1.1215509770901022e-10) - 2.7725887 * jax.random.uniform(key_of[11], (EXPERTS, D, FF), jnp.float32) ** block_scale(key_of[11], (EXPERTS, D, FF), ((0, 8), (2, 4)), -0.2, 0.2)), 7.009693606813139e-12, 1.1215509770901022e-10)
    down_weight = draw_down_weight(jax.random.fold_in(key_of[18], 71), 0)
    down_first = bell_draw(key_of[13], (EXPERTS, FF, D), (0.111 * (4 * D * D + 2 * D + EXPERTS * (2 * D * FF + 3 * D)) ** -0.5), 7.62939453125e-05, ((0, 8), (1, 4)), jnp.float32)
    down_second = jnp.clip(jnp.exp(math.log(1.1215509770901022e-10) - 2.7725887 * jax.random.uniform(key_of[14], (EXPERTS, FF, D), jnp.float32) ** block_scale(key_of[14], (EXPERTS, FF, D), ((0, 8), (1, 4)), -0.2, 0.2)), 7.009693606813139e-12, 1.1215509770901022e-10)
    expert_vector = draw_expert_vector(jax.random.fold_in(key_of[18], 71), 0)
    vector_first = bell_draw(key_of[16], (EXPERTS, 3, D), (0.444 * (4 * D * D + 2 * D + EXPERTS * (2 * D * FF + 3 * D)) ** -0.5), 0.00030517578, ((0, 8),), jnp.float32)
    vector_second = jnp.clip(jnp.exp(math.log(1.7944815633441635e-09) - 2.7725887 * jax.random.uniform(key_of[17], (EXPERTS, 3, D), jnp.float32) ** block_scale(key_of[17], (EXPERTS, 3, D), ((0, 8),), -0.2, 0.2)), 1.1215509770901022e-10, 1.7944815633441635e-09)
    return {"tokens": tokens, "cotangent": cotangent, "routes": routes, "attn_weight": attn_weight, "attn_first": attn_first, "attn_second": attn_second, "norm_param": norm_param, "norm_first": norm_first, "norm_second": norm_second, "up_weight": up_weight, "up_first": up_first, "up_second": up_second, "down_weight": down_weight, "down_first": down_first, "down_second": down_second, "expert_vector": expert_vector, "vector_first": vector_first, "vector_second": vector_second}


@jax.custom_vjp
def low(v):
    return lax.optimization_barrier(v.astype(jnp.bfloat16)).astype(jnp.float32)

@jax.custom_vjp
def low_back(v):
    return v

def low_keep(v):
    return (low(v), None)

def low_pass(kept, grad):
    return (grad,)

def back_keep(v):
    return (v, None)

def back_low(kept, grad):
    return (low(grad),)
low.defvjp(low_keep, low_pass)
low_back.defvjp(back_keep, back_low)
highest = lax.Precision.HIGHEST
norm_eps = 1e-05
clip_level = 1.0
beta_one = 0.9
beta_two = 0.999
adam_eps = 1e-08
decay_rate = 0.1
rate_matrix = 0.05
rate_vector = 0.5
masked_fill = -1e+30

def both_ways(values):
    return low_back(low(values))

def layer_norm(inputs, gain_row, bias_row):
    average = lax.optimization_barrier(jnp.mean(inputs, axis=-1, keepdims=True))
    centred = inputs - average
    variance = lax.optimization_barrier(jnp.mean(centred * centred, axis=-1, keepdims=True))
    return centred * lax.rsqrt(variance + norm_eps) * gain_row + bias_row

def gelu_exact(values):
    return jax.nn.gelu(values, approximate=False)

def attend(block, attn_work, norm_work):
    groups = block.shape[0]
    length = block.shape[1]
    normed = low(layer_norm(block, norm_work[0], norm_work[1]))
    projected = jnp.einsum('gtd,sde->sgte', normed, attn_work[:3], precision=highest, preferred_element_type=jnp.float32)
    query = both_ways(projected[0]).reshape(groups, length, HEADS, HEAD_DIM)
    keys_all = both_ways(projected[1]).reshape(groups, length, HEADS, HEAD_DIM)
    values_all = both_ways(projected[2]).reshape(groups, length, HEADS, HEAD_DIM)
    scores = jnp.einsum('gqhe,gkhe->ghqk', query, keys_all, precision=highest, preferred_element_type=jnp.float32) * HEAD_DIM ** (-0.5)
    causal = jnp.arange(length)[:, None] >= jnp.arange(length)[None, :]
    scores = low_back(jnp.where(causal[None, None], scores, masked_fill))
    row_max = lax.optimization_barrier(jnp.max(scores, axis=-1, keepdims=True))
    expo = jnp.exp(scores - row_max)
    attn_probs = expo / lax.optimization_barrier(jnp.sum(expo, axis=-1, keepdims=True))
    context = jnp.einsum('ghqk,gkhe->gqhe', low(attn_probs), values_all, precision=highest, preferred_element_type=jnp.float32)
    context = both_ways(context.reshape(groups, length, D))
    output_proj = low_back(jnp.einsum('gtd,de->gte', context, attn_work[3], precision=highest, preferred_element_type=jnp.float32))
    return block + output_proj

def run_expert(packed):
    rows, up_mat, down_mat, vector_row = packed
    gating = jax.nn.sigmoid(lax.optimization_barrier(jnp.sum(rows * vector_row[0], axis=-1)))
    normed = low(layer_norm(rows, vector_row[1], vector_row[2]))
    before = low_back(jnp.dot(normed, up_mat, precision=highest, preferred_element_type=jnp.float32))
    after = low(gelu_exact(before))
    result = low_back(jnp.dot(after, down_mat, precision=highest, preferred_element_type=jnp.float32))
    return (gating, result)

def adam_step(weight, first, second, grad, clip_factor, rate, decay):
    clipped = grad * clip_factor
    moment = beta_one * first + (1.0 - beta_one) * clipped
    square = beta_two * second + (1.0 - beta_two) * clipped * clipped
    corr_one = 1.0 - beta_one ** STEP
    corr_two = 1.0 - beta_two ** STEP
    update = moment / corr_one / (jnp.sqrt(square / corr_two) + adam_eps) + decay * weight
    return (weight - rate * update, moment, square)

def reference(tokens, cotangent, routes, attn_weight, attn_first, attn_second, norm_param, norm_first, norm_second, up_weight, up_first, up_second, down_weight, down_first, down_second, expert_vector, vector_first, vector_second):
    device_count = N_EXPERT * N_HIDDEN
    group = math.gcd(device_count, max(1, 4096 // TOK_DEV))
    route = routes[:, 0].astype(jnp.int32)
    chosen = (route[:, None] == jnp.arange(EXPERTS, dtype=jnp.int32)[None, :]).astype(jnp.int32)
    running = jnp.cumsum(chosen.reshape(device_count, TOK_DEV, EXPERTS), axis=1).reshape(TOKENS, EXPERTS)
    ranked = lax.optimization_barrier(jnp.sum((running - 1) * chosen, axis=1)).astype(jnp.int32)
    placed = (jnp.arange(TOKENS, dtype=jnp.int32) // TOK_DEV * CAP + ranked).astype(jnp.int32)

    def forward(token_in, attn_in, norm_in, up_in, down_in, vector_in):
        attn_work = low(attn_in)
        norm_work = low(norm_in)
        blocks = token_in.reshape(device_count // group, group, TOK_DEV, D)

        def run_block(block_in):
            return attend(block_in, attn_work, norm_work)
        resid = lax.map(jax.checkpoint(run_block), blocks).reshape(TOKENS, D)
        dispatched = both_ways(resid)
        buffers = jnp.zeros((EXPERTS, device_count * CAP, D), jnp.float32).at[route, placed].set(dispatched)
        gatings, results = lax.map(jax.checkpoint(run_expert), (buffers, up_in, down_in, vector_in))
        token_gate = gatings[route, placed]
        delta = both_ways(token_gate[:, None] * results[route, placed])
        return (resid + delta, token_gate)
    (block_value, token_gate), pullback = jax.vjp(forward, tokens.astype(jnp.float32), attn_weight, norm_param, up_weight.astype(jnp.float32), down_weight.astype(jnp.float32), expert_vector)
    grad_tok, grad_attn, grad_normp, grad_up, grad_down, grad_vec = pullback((cotangent.astype(jnp.float32), jnp.zeros_like(token_gate)))
    total = jnp.sum(grad_attn * grad_attn) + jnp.sum(grad_normp * grad_normp) + jnp.sum(grad_up * grad_up) + jnp.sum(grad_down * grad_down) + jnp.sum(grad_vec * grad_vec)
    grad_norm = jnp.sqrt(total)
    clip_factor = clip_level / jnp.maximum(grad_norm, clip_level)
    attn_new = adam_step(attn_weight, attn_first, attn_second, grad_attn, clip_factor, rate_matrix, decay_rate)
    norm_new = adam_step(norm_param, norm_first, norm_second, grad_normp, clip_factor, rate_vector, 0.0)
    up_new = adam_step(up_weight.astype(jnp.float32), up_first, up_second, grad_up, clip_factor, rate_matrix, decay_rate)
    down_new = adam_step(down_weight.astype(jnp.float32), down_first, down_second, grad_down, clip_factor, rate_matrix, decay_rate)
    vector_new = adam_step(expert_vector, vector_first, vector_second, grad_vec, clip_factor, rate_vector, 0.0)
    chosen_float = chosen.astype(jnp.float32)
    counts = lax.optimization_barrier(jnp.sum(chosen_float, axis=0))
    gate_sums = lax.optimization_barrier(jnp.sum(chosen_float * token_gate[:, None], axis=0))
    expert_stats = jnp.stack([counts / (TOKENS // EXPERTS), gate_sums / counts])
    return (block_value.astype(jnp.bfloat16), grad_tok.astype(jnp.bfloat16), grad_norm, attn_new[0], attn_new[1], attn_new[2], norm_new[0], norm_new[1], norm_new[2], up_new[0], up_new[1], up_new[2], down_new[0], down_new[1], down_new[2], vector_new[0], vector_new[1], vector_new[2], expert_stats)
```

```python
import functools
import math

import jax
import jax.numpy as jnp
from jax import lax
from jax.experimental import pallas as pl
from jax.experimental.pallas import tpu as pltpu
from jax.sharding import PartitionSpec as P

HEADS = 16
STEP = 10


norm_eps = 1e-05
clip_level = 1.0
beta_one = 0.9
beta_two = 0.999
adam_eps = 1e-08
decay_rate = 0.1
rate_matrix = 0.05
rate_vector = 0.5
masked_fill = -1e30
EX, HI = "expert", "hidden"
BOTH = (EX, HI)


def layer_norm(inputs, gain_row, bias_row):
    average = jnp.mean(inputs, axis=-1, keepdims=True)
    centred = inputs - average
    variance = jnp.mean(centred * centred, axis=-1, keepdims=True)
    return centred * lax.rsqrt(variance + norm_eps) * gain_row + bias_row


def gelu_exact(values):
    return jax.nn.gelu(values, approximate=False)


def adam_step(weight, first, second, grad, clip_factor, rate, decay):
    clipped = grad * clip_factor
    moment = beta_one * first + (1.0 - beta_one) * clipped
    square = beta_two * second + (1.0 - beta_two) * clipped * clipped
    corr_one = 1.0 - beta_one**STEP
    corr_two = 1.0 - beta_two**STEP
    update = moment / corr_one / (jnp.sqrt(square / corr_two) + adam_eps) + decay * weight
    return (weight - rate * update, moment, square)


MESH = pl.DeviceIdType.MESH
VMEM_SPEC = pl.BlockSpec(memory_space=pltpu.VMEM)
ANY_SPEC = pl.BlockSpec(memory_space=pl.ANY)

class Place:
    def __init__(self, depth):
        self.e = lax.axis_index(EX)
        self.z = lax.axis_index(HI)
        self.depth = depth
        self.core = lax.rem(self.e, 2)
        self.x = lax.rem(lax.div(self.e, 2), 2)
        self.y = lax.div(self.e, 4)
        self.ex = self.e + 2 - 4 * self.x
        self.ey = self.e + 4 - 8 * self.y
        self.exy = self.ex + 4 - 8 * self.y

    def across(self, k):
        c = lax.rem(self.core + k % 2, 2)
        x = lax.rem(self.x + (k // 2) % 2, 2)
        y = lax.rem(self.y + k // 4, 2)
        return 4 * y + 2 * x + c

    def up(self, d):
        return lax.rem(self.z + d, self.depth)

    def down(self, d):
        return lax.rem(self.z + self.depth - d, self.depth)

    def twin(self, e=None):
        e = self.e if e is None else e
        return e + 1 - 2 * self.core


class Wire:
    def __init__(self, send_sem, recv_sem):
        self.send_sem, self.recv_sem = send_sem, recv_sem
        self.count = 0
        self.sent = []

    def send(self, src, dst, device):
        i = self.count
        self.count += 1
        copy = pltpu.make_async_remote_copy(
            src_ref=src,
            dst_ref=dst,
            send_sem=self.send_sem.at[i],
            recv_sem=self.recv_sem.at[i],
            device_id=device,
            device_id_type=MESH,
        )
        copy.start()
        self.sent.append(copy)
        return copy

    def left(self, copy):
        copy.wait_send()
        self.sent = [one for one in self.sent if one is not copy]

    def drain(self):
        for copy in self.sent:
            copy.wait_send()


def meet(devices):
    barrier = pltpu.get_barrier_semaphore()
    for device in devices:
        pl.semaphore_signal(barrier, inc=1, device_id=device, device_id_type=MESH)
    pl.semaphore_wait(barrier, len(devices))


def dot(a, b, ca=1, cb=0):
    return lax.dot_general(a, b, (((ca,), (cb,)), ((), ())), preferred_element_type=jnp.float32)


def attend_kernel(
    depth,
    cap,
    tok,
    w_own,
    norm_own,
    route,
    cot,
    w_out,
    qkv,
    normed,
    ctx,
    resid,
    sent,
    placed,
    gains,
    cot_raw,
    wfull,
    norm_in,
    norm_sum,
    send_sem,
    recv_sem,
    local_sem,
):
    at = Place(depth)
    e, z = at.e, at.z
    count, width = tok.shape
    shard = w_own.shape[1]
    meet(
        [(e, at.up(d)) for d in range(1, depth)]
        + [(at.ex, z), (at.ey, z), (at.twin(), z)]
    )
    wire = Wire(send_sem, recv_sem)
    groups = [(0, 3), (3, 1)]

    def block(g, who, zz):
        first, mats = groups[g]
        start = pl.multiple_of((who * depth + zz) * shard, shard)
        return wfull.at[pl.ds(first, mats), pl.ds(start, shard)]

    norm_z = [wire.send(norm_own, norm_in.at[d - 1], (e, at.up(d))) for d in range(1, depth)]
    own = []
    for g, (first, mats) in enumerate(groups):
        copy = pltpu.make_async_copy(
            w_own.at[pl.ds(first, mats)], block(g, e, z), local_sem.at[g]
        )
        copy.start()
        own.append(copy)
    unit_z = {}
    for g, (first, mats) in enumerate(groups):
        for d in range(1, depth):
            unit_z[g, d] = wire.send(
                w_own.at[pl.ds(first, mats)], block(g, e, z), (e, at.up(d))
            )

    cot_z = [wire.send(cot, cot_raw.at[d], (e, at.up(d))) for d in range(1, depth)]
    cot_raw[0] = cot[...]

    to_x, to_y, to_far, to_twin = {}, {}, {}, {}

    def plane(g, d):
        zz = at.down(d)
        if d == 0:
            own[g].wait()
        else:
            unit_z[g, d].wait_recv()
        here = block(g, e, zz)
        to_x[g, d] = wire.send(here, here, (at.ex, z))
        to_y[g, d] = wire.send(here, here, (at.ey, z))
        to_twin[g, d, 0] = wire.send(here, here, (at.twin(), z))

    def forward(g, d):
        zz = at.down(d)
        from_x, from_y = block(g, at.ex, zz), block(g, at.ey, zz)
        to_x[g, d].wait_recv()
        if 2 * d < depth:
            to_far[g, d] = wire.send(from_x, from_x, (at.ey, z))
        to_twin[g, d, 1] = wire.send(from_x, from_x, (at.twin(), z))
        to_y[g, d].wait_recv()
        if 2 * d >= depth:
            to_far[g, d] = wire.send(from_y, from_y, (at.ex, z))
        to_twin[g, d, 2] = wire.send(from_y, from_y, (at.twin(), z))

    def far(g, d):
        zz = at.down(d)
        to_far[g, d].wait_recv()
        there = block(g, at.exy, zz)
        to_twin[g, d, 3] = wire.send(there, there, (at.twin(), z))

    def finish(g):
        for d in range(depth):
            for k in range(4):
                to_twin[g, d, k].wait_recv()

    def norm_step(k, device):
        copy = wire.send(norm_sum.at[k], norm_in.at[depth - 1 + k], device)
        return copy

    plane(0, 0)
    lanes = lax.broadcasted_iota(jnp.int32, (count, 128), 1)
    chosen = jnp.where(route[...] == lanes, 1.0, 0.0)
    rows_i = lax.broadcasted_iota(jnp.int32, (count, count), 0)
    cols_i = lax.broadcasted_iota(jnp.int32, (count, count), 1)
    lower = jnp.where(rows_i >= cols_i, 1.0, 0.0)
    running = dot(lower.astype(jnp.bfloat16), chosen.astype(jnp.bfloat16))
    rank = jnp.sum((running - 1.0) * chosen, axis=1, keepdims=True)
    column = route[...].astype(jnp.float32) * float(cap) + rank
    wide_r = lax.broadcasted_iota(jnp.int32, (count, 256), 0)
    wide_c = lax.broadcasted_iota(jnp.int32, (count, 256), 1)
    row = jnp.sum(jnp.where(wide_r == wide_c, column + 1.0, 0.0), axis=0, keepdims=True) - 1.0
    placed[0] = jnp.broadcast_to(row, (8, 256)).astype(jnp.int32)
    placed_z = [
        wire.send(placed.at[0], placed.at[d], (e, at.up(d))) for d in range(1, depth)
    ]
    for copy in norm_z:
        copy.wait_recv()
    total = norm_own[...]
    for d in range(1, depth):
        total = total + norm_in[d - 1]
    norm_sum[0] = total
    norm_x = norm_step(0, (at.ex, z))
    plane(0, 1)
    norm_x.wait_recv()
    norm_sum[1] = norm_sum[0] + norm_in[depth - 1]
    norm_y = norm_step(1, (at.ey, z))
    forward(0, 0)
    plane(0, 2)
    norm_y.wait_recv()
    norm_sum[2] = norm_sum[1] + norm_in[depth]
    norm_twin = norm_step(2, (at.twin(), z))
    for d in range(3, depth):
        plane(0, d)
    norm_twin.wait_recv()
    gain_rows = norm_sum[2] + norm_in[depth + 1]
    tally = jnp.concatenate(
        [
            jnp.broadcast_to(jnp.sum(chosen, axis=0, keepdims=True), (16, 128)),
            jnp.zeros((16, width - 128), jnp.float32),
        ],
        axis=1,
    )
    third_row = lax.broadcasted_iota(jnp.int32, (16, width), 0) == 2
    gains[...] = jnp.where(third_row, tally, gain_rows.astype(jnp.float32)).astype(jnp.bfloat16)
    gain = gains[0:1, :].astype(jnp.float32)
    bias = gains[1:2, :].astype(jnp.float32)
    for i in range(0, count, 64):
        piece = tok[i : i + 64, :].astype(jnp.float32)
        average = jnp.mean(piece, axis=-1, keepdims=True)
        centred = piece - average
        variance = jnp.mean(centred * centred, axis=-1, keepdims=True)
        normed[i : i + 64, :] = (
            centred * lax.rsqrt(variance + norm_eps) * gain + bias
        ).astype(jnp.bfloat16)
    for d in range(1, depth):
        far(0, d - 1)
        forward(0, d)
    for d in range(depth):
        plane(1, d)
    far(0, depth - 1)
    finish(0)
    keep = pltpu.make_async_copy(
        wfull.at[pl.ds(0, 3)], w_out.at[pl.ds(0, 3)], local_sem.at[2]
    )
    keep.start()
    tiles = width // 256

    @pl.loop(0, 3 * tiles)
    def _(i):
        m = lax.div(i, tiles)
        cols = pl.ds(pl.multiple_of(lax.rem(i, tiles) * 256, 256), 256)
        qkv[m, :, cols] = dot(normed[...], wfull[m, :, cols]).astype(jnp.bfloat16)

    forward(1, 0)
    forward(1, 1)
    causal = rows_i >= cols_i
    left = lax.broadcasted_iota(jnp.int32, (count, 128), 1) < 64
    scaling = jnp.asarray(64 ** (-0.5), jnp.bfloat16)

    def pair(i):
        cols = pl.ds(pl.multiple_of(i * 128, 128), 128)
        query = qkv[0, :, cols] * scaling
        keys = qkv[1, :, cols]
        values = qkv[2, :, cols]
        halves = []
        for side in range(2):
            mask = left if side == 0 else jnp.logical_not(left)
            scores = dot(jnp.where(mask, query, jnp.zeros_like(query)), keys, 1, 1)
            scores = jnp.where(causal, scores, masked_fill)
            top = jnp.max(scores, axis=-1, keepdims=True)
            expo = jnp.exp(scores - top)
            probs = expo / jnp.sum(expo, axis=-1, keepdims=True)
            halves.append(dot(probs.astype(jnp.bfloat16), values))
        ctx[:, cols] = jnp.where(left, halves[0], halves[1]).astype(jnp.bfloat16)

    pl.loop(0, width // 256)(pair)
    far(1, 0)
    far(1, 1)
    for d in range(2, depth):
        forward(1, d)
    pl.loop(width // 256, width // 128)(pair)
    for d in range(2, depth):
        far(1, d)
    finish(1)
    keep_out = pltpu.make_async_copy(
        wfull.at[pl.ds(3, 1)], w_out.at[pl.ds(3, 1)], local_sem.at[3]
    )
    keep_out.start()

    @pl.loop(0, tiles)
    def _(i):
        cols = pl.ds(pl.multiple_of(i * 256, 256), 256)
        value = tok[:, cols].astype(jnp.float32) + dot(ctx[...], wfull[3, :, cols])
        resid[:, cols] = value
        sent[:, cols] = value.astype(jnp.bfloat16)

    for copy in placed_z + cot_z:
        copy.wait_recv()
    wire.drain()
    keep.wait()
    keep_out.wait()


def attend(depth, cap, tokens, w_own, norm_own, routes, cotangent):
    count, width = tokens.shape
    bf = jnp.bfloat16
    copies = 128
    return pl.pallas_call(
        functools.partial(attend_kernel, depth, cap),
        out_shape=(
            jax.ShapeDtypeStruct((4, width, width), bf),
            jax.ShapeDtypeStruct((3, count, width), bf),
            jax.ShapeDtypeStruct((count, width), bf),
            jax.ShapeDtypeStruct((count, width), bf),
            jax.ShapeDtypeStruct((count, width), jnp.float32),
            jax.ShapeDtypeStruct((count, width), bf),
            jax.ShapeDtypeStruct((depth, 8, 256), jnp.int32),
            jax.ShapeDtypeStruct((16, width), bf),
            jax.ShapeDtypeStruct((depth, count, width), bf),
        ),
        in_specs=[VMEM_SPEC] * 5,
        out_specs=(ANY_SPEC,) + (VMEM_SPEC,) * 8,
        scratch_shapes=[
            pltpu.VMEM((4, width, width), bf),
            pltpu.VMEM((depth + 2, 16, width), bf),
            pltpu.VMEM((3, 16, width), bf),
            pltpu.SemaphoreType.DMA((copies,)),
            pltpu.SemaphoreType.DMA((copies,)),
            pltpu.SemaphoreType.DMA((4,)),
        ],
        compiler_params=pltpu.CompilerParams(
            collective_id=0, has_side_effects=True, vmem_limit_bytes=40 << 20
        ),
    )(tokens, w_own, norm_own, routes, cotangent)


def pick(placed_row, slots):
    which = lax.broadcasted_iota(jnp.int32, (slots, placed_row.shape[1]), 0)
    return jnp.where(which == placed_row, 1.0, 0.0).astype(jnp.bfloat16)


def gelu_pair(v):
    cdf = 0.5 + 0.5 * lax.erf(v * (0.5**0.5))
    pdf = jnp.exp(-0.5 * v * v) * ((2.0 * math.pi) ** -0.5)
    return v * cdf, cdf + v * pdf


def fold(v):
    total = v[0:8]
    for i in range(8, v.shape[0], 8):
        total = total + v[i : i + 8]
    return total


def spread(column, lanes):
    return jnp.concatenate([column] * (lanes // 128), axis=1)


def expert_kernel(
    depth,
    cap,
    sent,
    placed,
    cot_raw,
    up,
    down,
    vec,
    d_sum,
    g_up,
    g_down,
    delta,
    vec_part,
    scal,
    raw,
    stage,
    rows,
    cots,
    xn,
    act,
    slope,
    d_slots,
    back,
    part,
    z_in,
    d_xn,
    gate,
    d_logit,
    g_stage,
    send_sem,
    recv_sem,
    local_sem,
):
    at = Place(depth)
    e, z = at.e, at.z
    count, width = sent.shape
    planes = 8
    slots = planes * cap
    units = up.shape[1]
    meet(
        [(e, at.up(d)) for d in range(1, depth)]
        + [(at.across(k), z) for k in range(1, planes)]
    )
    wire = Wire(send_sem, recv_sem)
    vec_part[...] = jnp.zeros_like(vec_part)
    scal[...] = jnp.zeros_like(scal)
    centroid = lambda: vec[0:1, :]
    raw_z = {d: wire.send(sent, raw.at[d - 1], (e, at.up(d))) for d in range(1, depth)}

    def build(b, source):
        onehot = pick(placed[b, 0:1, :count], slots)

        @pl.loop(0, width // 512)
        def _(i):
            cols = pl.ds(pl.multiple_of(i * 512, 512), 512)
            value = dot(onehot, source[:, cols]).astype(jnp.bfloat16)
            for k in range(planes):
                stage[b, k, :, cols] = value[k * cap : (k + 1) * cap]

    def exchange(b, dst):
        copies = [
            wire.send(stage.at[b, at.across(k)], dst.at[b, k], (at.across(k), z))
            for k in range(1, planes)
        ]
        dst[b, 0] = stage[b, e]
        return copies

    row_copies, cot_copies, ret_copies, part_copies = {}, {}, {}, {}

    def rows_out(b):
        if b:
            raw_z[b].wait_recv()
        build(b, sent if b == 0 else raw.at[b - 1])
        row_copies[b] = exchange(b, rows)

    def cots_out(b):
        for copy in row_copies[b]:
            wire.left(copy)
        build(b, cot_raw.at[b])
        cot_copies[b] = exchange(b, cots)

    def forward(b):
        for copy in row_copies[b]:
            copy.wait_recv()
        gain, bias = vec[1:2, :], vec[2:3, :]

        @pl.loop(0, planes)
        def _(i):
            r = rows[b, i].astype(jnp.float32)
            logit = jnp.sum(r * centroid(), axis=-1, keepdims=True)
            g = jax.nn.sigmoid(logit)
            wide = jnp.broadcast_to(g, (cap, 128))
            gate[b, i] = wide
            scal[0:8] += fold(wide)
            average = jnp.mean(r, axis=-1, keepdims=True)
            centred = r - average
            variance = jnp.mean(centred * centred, axis=-1, keepdims=True)
            xn[b, pl.ds(pl.multiple_of(i * cap, 16), cap), :] = (
                centred * lax.rsqrt(variance + norm_eps) * gain + bias
            ).astype(jnp.bfloat16)

        @pl.loop(0, units // 256)
        def _(j):
            cols = pl.ds(pl.multiple_of(j * 256, 256), 256)
            value, rate = gelu_pair(dot(xn[b], up[:, cols]))
            act[b, :, cols] = value.astype(jnp.bfloat16)
            slope[b, :, cols] = rate.astype(jnp.bfloat16)

        @pl.loop(0, width // 256)
        def _(j):
            cols = pl.ds(pl.multiple_of(j * 256, 256), 256)
            branch = dot(act[b], down[:, cols])
            wide = spread(gate[b].reshape(slots, 128), 256)
            value = (wide * branch).astype(jnp.bfloat16)
            for k in range(planes):
                delta[b, k, :, cols] = value[k * cap : (k + 1) * cap]

    def backward(b):
        for copy in cot_copies[b]:
            copy.wait_recv()

        @pl.loop(0, planes)
        def _(i):
            c = cots[b, i].astype(jnp.float32)
            g = gate[b, i]
            inner = jnp.sum(c * delta[b, i].astype(jnp.float32), axis=-1, keepdims=True)
            dl = (1.0 - g) * inner
            d_logit[b, i] = dl
            cots[b, i] = (c * spread(g, width)).astype(jnp.bfloat16)
            vec_part[0] += fold(rows[b, i].astype(jnp.float32) * spread(dl, width))

        @pl.loop(0, units // 256)
        def _(j):
            cols = pl.ds(pl.multiple_of(j * 256, 256), 256)
            d_act = dot(cots[b].reshape(slots, width), down[cols, :], 1, 1)
            slope[b, :, cols] = (d_act * slope[b, :, cols].astype(jnp.float32)).astype(
                jnp.bfloat16
            )

        @pl.loop(0, width // 256)
        def _(j):
            cols = pl.ds(pl.multiple_of(j * 256, 256), 256)
            value = dot(slope[b], up[cols, :], 1, 1)
            for k in range(planes):
                d_xn[k, :, cols] = value[k * cap : (k + 1) * cap]

        @pl.loop(0, planes)
        def _(i):
            r = rows[b, i].astype(jnp.float32)
            average = jnp.mean(r, axis=-1, keepdims=True)
            centred = r - average
            variance = jnp.mean(centred * centred, axis=-1, keepdims=True)
            scale = lax.rsqrt(variance + norm_eps)
            hat = centred * scale
            dx = d_xn[i]
            vec_part[1] += fold(dx * hat)
            vec_part[2] += fold(dx)
            dh = dx * vec[1:2, :]
            first = jnp.mean(dh, axis=-1, keepdims=True)
            second = jnp.mean(dh * hat, axis=-1, keepdims=True)
            d_in = scale * (dh - first - hat * second)
            d_slots[b, i] = (d_in + spread(d_logit[b, i], width) * centroid()).astype(jnp.bfloat16)

        ret_copies[b] = [
            wire.send(d_slots.at[b, k], back.at[b, e], (at.across(k), z))
            for k in range(1, planes)
        ]
        back[b, e] = d_slots[b, 0]

    def collect(b):
        for copy in ret_copies[b]:
            copy.wait_recv()
        onehot = pick(placed[b, 0:1, :count], slots)

        @pl.loop(0, width // 256)
        def _(j):
            cols = pl.ds(pl.multiple_of(j * 256, 256), 256)
            value = back[b, :, :, cols].reshape(slots, 256)
            part[b, :, cols] = dot(onehot, value, 0, 0).astype(jnp.bfloat16)

        if b:
            part_copies[b] = wire.send(part.at[b], z_in.at[b - 1], (e, at.down(b)))

    def weight_grad(lhs, rhs, index, out):
        @pl.loop(0, lhs.shape[-1] // 256)
        def _(j):
            cols = pl.ds(pl.multiple_of(j * 256, 256), 256)
            left = lhs[:, :, cols].reshape(depth * slots, 256)
            value = dot(left, rhs[...].reshape(depth * slots, rhs.shape[-1]), 0, 0)
            scal[8:16] += fold(square_lanes(value))
            g_stage[index, cols, :] = value.astype(jnp.bfloat16)

        copy = pltpu.make_async_copy(g_stage.at[index], out, local_sem.at[index])
        copy.start()
        return copy

    rows_out(0)
    for b in range(1, depth):
        rows_out(b)
        forward(b - 1)
    order = list(range(1, depth)) + [0]
    cots_out(order[0])
    cots_out(order[1])
    forward(depth - 1)
    for b in order[2:]:
        cots_out(b)
    backward(order[0])
    for i in range(1, depth):
        backward(order[i])
        collect(order[i - 1])
    keep_down = weight_grad(act, cots, 0, g_down)
    collect(order[-1])
    keep_up = weight_grad(xn, slope, 1, g_up)
    for b in range(1, depth):
        part_copies[b].wait_recv()

    @pl.loop(0, width // 256)
    def _(j):
        cols = pl.ds(pl.multiple_of(j * 256, 256), 256)
        total = part[0, :, cols].astype(jnp.float32)
        for b in range(1, depth):
            total = total + z_in[b - 1, :, cols].astype(jnp.float32)
        d_sum[:, cols] = total

    wire.drain()
    keep_down.wait()
    keep_up.wait()


def square_lanes(v):
    total = v[:, 0:128] * v[:, 0:128]
    for i in range(128, v.shape[1], 128):
        total = total + v[:, i : i + 128] * v[:, i : i + 128]
    return total


def expert_layer(depth, cap, sent, placed, cot_raw, up, down, vec):
    count, width = sent.shape
    units = up.shape[1]
    bf, full = jnp.bfloat16, jnp.float32
    slots = 8 * cap
    copies = 3 * 7 * depth + 2 * depth
    return pl.pallas_call(
        functools.partial(expert_kernel, depth, cap),
        out_shape=(
            jax.ShapeDtypeStruct((count, width), full),
            jax.ShapeDtypeStruct((width, units), bf),
            jax.ShapeDtypeStruct((units, width), bf),
            jax.ShapeDtypeStruct((depth, 8, cap, width), bf),
            jax.ShapeDtypeStruct((3, 8, width), full),
            jax.ShapeDtypeStruct((16, 128), full),
        ),
        in_specs=[VMEM_SPEC] * 6,
        out_specs=(VMEM_SPEC, ANY_SPEC, ANY_SPEC) + (VMEM_SPEC,) * 3,
        scratch_shapes=[
            pltpu.VMEM((depth - 1, count, width), bf),
            pltpu.VMEM((depth, 8, cap, width), bf),
            pltpu.VMEM((depth, 8, cap, width), bf),
            pltpu.VMEM((depth, 8, cap, width), bf),
            pltpu.VMEM((depth, slots, width), bf),
            pltpu.VMEM((depth, slots, units), bf),
            pltpu.VMEM((depth, slots, units), bf),
            pltpu.VMEM((depth, 8, cap, width), bf),
            pltpu.VMEM((depth, 8, cap, width), bf),
            pltpu.VMEM((depth, count, width), bf),
            pltpu.VMEM((depth - 1, count, width), bf),
            pltpu.VMEM((8, cap, width), full),
            pltpu.VMEM((depth, 8, cap, 128), full),
            pltpu.VMEM((depth, 8, cap, 128), full),
            pltpu.VMEM((2, max(width, units), max(width, units)), bf),
            pltpu.SemaphoreType.DMA((copies,)),
            pltpu.SemaphoreType.DMA((copies,)),
            pltpu.SemaphoreType.DMA((2,)),
        ],
        compiler_params=pltpu.CompilerParams(
            collective_id=1, has_side_effects=True, vmem_limit_bytes=62 << 20
        ),
    )(sent, placed, cot_raw, up, down, vec)


def reduce_kernel(
    depth,
    cap,
    d_sum,
    cot,
    w_in,
    qkv,
    normed,
    ctx,
    tok,
    gains,
    placed,
    delta,
    resid,
    vec_part,
    scal,
    block_out,
    token_grad,
    shard_out,
    norm_out,
    vec_out,
    square_out,
    wfull,
    d_resid,
    d_proj,
    d_ctx,
    d_qkv,
    d_norm,
    stage,
    twin_in,
    x_in,
    y_in,
    x_last,
    y_last,
    done,
    z_last,
    back,
    part,
    z_in,
    small,
    small_in,
    small_z,
    square,
    square_z,
    send_sem,
    recv_sem,
    local_sem,
):
    at = Place(depth)
    e, z = at.e, at.z
    count, width = tok.shape
    planes = 8
    slots = planes * cap
    shard = shard_out.shape[1]
    column = depth * shard
    half = column // 2
    meet(
        [(e, at.up(d)) for d in range(1, depth)]
        + [(at.across(k), z) for k in range(1, planes)]
    )
    wire = Wire(send_sem, recv_sem)
    loads = []
    for m in (3, 2, 1, 0):
        copy = pltpu.make_async_copy(w_in.at[m], wfull.at[m], local_sem.at[m])
        copy.start()
        loads.append(copy)
    ret, order = {}, list(range(1, depth)) + [0]
    for b in order:
        ret[b] = [
            wire.send(delta.at[b, k], back.at[b, e], (at.across(k), z)) for k in range(1, planes)
        ]
        back[b, e] = delta[b, 0]
    part_copies = {}

    def collect(b):
        for copy in ret[b]:
            copy.wait_recv()
        onehot = pick(placed[b, 0:1, :count], slots)

        @pl.loop(0, width // 256)
        def _(j):
            cols = pl.ds(pl.multiple_of(j * 256, 256), 256)
            value = back[b, :, :, cols].reshape(slots, 256)
            part[b, :, cols] = dot(onehot, value, 0, 0).astype(jnp.bfloat16)

        if b:
            part_copies[b] = wire.send(part.at[b], z_in.at[b - 1], (e, at.down(b)))

    def weight_grad(m, left_ref, right):
        @pl.loop(0, planes)
        def _(i):
            cols = pl.ds(pl.multiple_of(i * column, column), column)
            value = dot(left_ref[:, cols], right[...], 0, 0).astype(jnp.bfloat16)
            stage[m, lax.div(i, 4), lax.rem(lax.div(i, 2), 2), lax.rem(i, 2)] = value

    other = 1 - at.core
    first, second, third, fourth = {}, {}, {}, {}

    def to_core(m):
        first[m] = wire.send(stage.at[m, :, :, other], twin_in.at[m], (at.twin(), z))

    def to_plane(m):
        first[m].wait_recv()
        for j in range(2):
            for i in range(2):
                twin_in[m, j, i] = twin_in[m, j, i] + stage[m, j, i, at.core]
        second[m] = (
            wire.send(twin_in.at[m, :, 1 - at.x, pl.ds(0, half)], x_in.at[m], (at.ex, z)),
            wire.send(twin_in.at[m, 1 - at.y, :, pl.ds(half, half)], y_in.at[m], (at.ey, z)),
        )

    def to_last(m):
        second[m][0].wait_recv()
        for j in range(2):
            x_in[m, j] = x_in[m, j] + twin_in[m, j, at.x, 0:half]
        one = wire.send(x_in.at[m, 1 - at.y], x_last.at[m], (at.ey, z))
        second[m][1].wait_recv()
        for i in range(2):
            y_in[m, i] = y_in[m, i] + twin_in[m, at.y, i, half:]
        two = wire.send(y_in.at[m, 1 - at.x], y_last.at[m], (at.ex, z))
        third[m] = (one, two)

    def to_owner(m):
        third[m][0].wait_recv()
        done[m, 0:half] = x_in[m, at.y] + x_last[m]
        third[m][1].wait_recv()
        done[m, half:] = y_in[m, at.x] + y_last[m]
        fourth[m] = [
            wire.send(
                done.at[m, pl.ds(pl.multiple_of(at.up(d) * shard, shard), shard)],
                z_last.at[m, d - 1],
                (e, at.up(d)),
            )
            for d in range(1, depth)
        ]

    def own(m):
        total = done[m, pl.ds(pl.multiple_of(z * shard, shard), shard), :].astype(jnp.float32)
        for d in range(1, depth):
            fourth[m][d - 1].wait_recv()
            total = total + z_last[m, d - 1].astype(jnp.float32)
        shard_out[m] = total

    value = cot[...].astype(jnp.float32) + d_sum[...]
    d_resid[...] = value
    d_proj[...] = value.astype(jnp.bfloat16)
    weight_grad(3, ctx, d_proj)
    to_core(3)
    loads[0].wait()

    @pl.loop(0, width // 256)
    def _(j):
        cols = pl.ds(pl.multiple_of(j * 256, 256), 256)
        d_ctx[:, cols] = dot(d_proj[...], wfull[3, cols, :], 1, 1).astype(jnp.bfloat16)

    to_plane(3)
    causal = lax.broadcasted_iota(jnp.int32, (count, count), 0) >= lax.broadcasted_iota(
        jnp.int32, (count, count), 1
    )
    left = lax.broadcasted_iota(jnp.int32, (count, 128), 1) < 64
    scaling = 64 ** (-0.5)

    @pl.loop(0, width // 128)
    def _(i):
        cols = pl.ds(pl.multiple_of(i * 128, 128), 128)
        query = qkv[0, :, cols]
        keys = qkv[1, :, cols]
        values = qkv[2, :, cols]
        d_out = d_ctx[:, cols]
        zero = jnp.zeros_like(query)
        got = []
        for side in range(2):
            mask = left if side == 0 else jnp.logical_not(left)
            q_side = jnp.where(mask, query, zero)
            k_side = jnp.where(mask, keys, zero)
            o_side = jnp.where(mask, d_out, zero)
            scores = dot(q_side, keys, 1, 1) * scaling
            scores = jnp.where(causal, scores, masked_fill)
            top = jnp.max(scores, axis=-1, keepdims=True)
            expo = jnp.exp(scores - top)
            probs = expo / jnp.sum(expo, axis=-1, keepdims=True)
            d_probs = dot(o_side, values, 1, 1)
            inner = jnp.sum(d_probs * probs, axis=-1, keepdims=True)
            d_scores = (probs * (d_probs - inner)).astype(jnp.bfloat16)
            got.append(
                (
                    dot(d_scores, k_side),
                    dot(d_scores, q_side, 0, 0),
                    dot(probs.astype(jnp.bfloat16), o_side, 0, 0),
                )
            )
        d_qkv[0, :, cols] = ((got[0][0] + got[1][0]) * scaling).astype(jnp.bfloat16)
        d_qkv[1, :, cols] = ((got[0][1] + got[1][1]) * scaling).astype(jnp.bfloat16)
        d_qkv[2, :, cols] = (got[0][2] + got[1][2]).astype(jnp.bfloat16)

    for m in (2, 1, 0):
        weight_grad(m, normed, d_qkv.at[m])
        to_core(m)
        if m < 2:
            to_plane(m + 1)
    to_last(3)
    to_plane(0)
    for copy in loads[1:]:
        copy.wait()

    @pl.loop(0, width // 256)
    def _(j):
        cols = pl.ds(pl.multiple_of(j * 256, 256), 256)
        d_norm[:, cols] = (
            dot(d_qkv[0], wfull[0, cols, :], 1, 1)
            + dot(d_qkv[1], wfull[1, cols, :], 1, 1)
            + dot(d_qkv[2], wfull[2, cols, :], 1, 1)
        )

    gain = gains[0:1, :].astype(jnp.float32)
    d_gain = jnp.zeros((8, width), jnp.float32)
    d_bias = jnp.zeros((8, width), jnp.float32)
    for i in range(0, count, 64):
        piece = tok[i : i + 64, :].astype(jnp.float32)
        average = jnp.mean(piece, axis=-1, keepdims=True)
        centred = piece - average
        variance = jnp.mean(centred * centred, axis=-1, keepdims=True)
        scale = lax.rsqrt(variance + norm_eps)
        hat = centred * scale
        dx = d_norm[i : i + 64, :]
        d_gain = d_gain + fold(dx * hat)
        d_bias = d_bias + fold(dx)
        dh = dx * gain
        mean_one = jnp.mean(dh, axis=-1, keepdims=True)
        mean_two = jnp.mean(dh * hat, axis=-1, keepdims=True)
        d_in = scale * (dh - mean_one - hat * mean_two)
        token_grad[i : i + 64, :] = (d_resid[i : i + 64, :] + d_in).astype(jnp.bfloat16)
    mine = small_z.at[z]
    mine[...] = jnp.zeros((16, width), jnp.float32)
    mine[2:3, :] = gains[2:3, :].astype(jnp.float32)
    mine[0:1, :] = jnp.sum(d_gain, axis=0, keepdims=True)
    mine[1:2, :] = jnp.sum(d_bias, axis=0, keepdims=True)
    for k in range(3):
        mine[8 + k : 9 + k, :] = jnp.sum(vec_part[k], axis=0, keepdims=True)
    small_copies = [wire.send(mine, mine, (e, at.up(d))) for d in range(1, depth)]
    to_owner(3)
    for b in order[:2]:
        collect(b)
    to_last(2)
    for copy in small_copies:
        copy.wait_recv()
    total = small_z[0]
    for d in range(1, depth):
        total = total + small_z[d]
    small[0] = total[0:8]
    vec_out[...] = total[8:16]
    x_copy = wire.send(small.at[0], small_in.at[0], (at.ex, z))
    own(3)
    to_last(1)
    to_owner(2)
    x_copy.wait_recv()
    small[1] = small[0] + small_in[0]
    y_copy = wire.send(small.at[1], small_in.at[1], (at.ey, z))
    for b in order[2:]:
        collect(b)
    own(2)
    y_copy.wait_recv()
    small[2] = small[1] + small_in[1]
    core_copy = wire.send(small.at[2], small_in.at[2], (at.twin(), z))
    to_last(0)
    to_owner(1)
    core_copy.wait_recv()
    norm_out[...] = small[2] + small_in[2]
    to_owner(0)
    own(1)
    for b in range(1, depth):
        part_copies[b].wait_recv()

    @pl.loop(0, width // 256)
    def _(j):
        cols = pl.ds(pl.multiple_of(j * 256, 256), 256)
        total = part[0, :, cols].astype(jnp.float32)
        for b in range(1, depth):
            total = total + z_in[b - 1, :, cols].astype(jnp.float32)
        block_out[:, cols] = (resid[:, cols] + total).astype(jnp.bfloat16)

    norm_rows = norm_out[0:2, :]
    vec_rows = vec_out[0:3, :]
    squares = jnp.sum(norm_rows * norm_rows, axis=0, keepdims=True) / (planes * depth) + jnp.sum(
        vec_rows * vec_rows, axis=0, keepdims=True
    ) / depth
    own(0)
    local = scal[8:16, :]
    for m in range(4):
        local = local + fold(square_lanes(shard_out[m]))
    lane_squares = squares[:, 0:128]
    for i in range(128, width, 128):
        lane_squares = lane_squares + squares[:, i : i + 128]
    head = lax.broadcasted_iota(jnp.int32, (8, 128), 0) == 0
    local = local + jnp.where(head, jnp.broadcast_to(lane_squares, (8, 128)), 0.0)
    square[e] = local
    spot = square.at[e]
    copies = [wire.send(spot, spot, (at.across(k), z)) for k in range(1, planes)]
    for copy in copies:
        copy.wait_recv()
    total = square[0]
    for k in range(1, planes):
        total = total + square[k]
    square_z[z] = total
    spot = square_z.at[z]
    copies = [wire.send(spot, spot, (e, at.up(d))) for d in range(1, depth)]
    for copy in copies:
        copy.wait_recv()
    total = square_z[0]
    for d in range(1, depth):
        total = total + square_z[d]
    square_out[...] = total
    wire.drain()


def attend_back(depth, cap, shard, *args):
    tokens = args[6]
    count, width = tokens.shape
    bf, full = jnp.bfloat16, jnp.float32
    column = depth * shard
    half = column // 2
    copies = 7 * depth + depth + 32 + 16 + 16
    return pl.pallas_call(
        functools.partial(reduce_kernel, depth, cap),
        out_shape=(
            jax.ShapeDtypeStruct((count, width), bf),
            jax.ShapeDtypeStruct((count, width), bf),
            jax.ShapeDtypeStruct((4, shard, width), full),
            jax.ShapeDtypeStruct((8, width), full),
            jax.ShapeDtypeStruct((8, width), full),
            jax.ShapeDtypeStruct((8, 128), full),
        ),
        in_specs=[VMEM_SPEC] * 2 + [ANY_SPEC] + [VMEM_SPEC] * 10,
        out_specs=(VMEM_SPEC,) * 6,
        scratch_shapes=[
            pltpu.VMEM((4, width, width), bf),
            pltpu.VMEM((count, width), full),
            pltpu.VMEM((count, width), bf),
            pltpu.VMEM((count, width), bf),
            pltpu.VMEM((3, count, width), bf),
            pltpu.VMEM((count, width), full),
            pltpu.VMEM((4, 2, 2, 2, column, width), bf),
            pltpu.VMEM((4, 2, 2, column, width), bf),
            pltpu.VMEM((4, 2, half, width), bf),
            pltpu.VMEM((4, 2, half, width), bf),
            pltpu.VMEM((4, half, width), bf),
            pltpu.VMEM((4, half, width), bf),
            pltpu.VMEM((4, column, width), bf),
            pltpu.VMEM((4, depth - 1, shard, width), bf),
            pltpu.VMEM((depth, 8, cap, width), bf),
            pltpu.VMEM((depth, count, width), bf),
            pltpu.VMEM((depth - 1, count, width), bf),
            pltpu.VMEM((3, 8, width), full),
            pltpu.VMEM((3, 8, width), full),
            pltpu.VMEM((depth, 16, width), full),
            pltpu.VMEM((8, 8, 128), full),
            pltpu.VMEM((depth, 8, 128), full),
            pltpu.SemaphoreType.DMA((copies,)),
            pltpu.SemaphoreType.DMA((copies,)),
            pltpu.SemaphoreType.DMA((4,)),
        ],
        compiler_params=pltpu.CompilerParams(
            collective_id=2, has_side_effects=True, vmem_limit_bytes=62 << 20
        ),
    )(*args)


def shards(
    tokens,
    cotangent,
    routes,
    attn_weight,
    attn_first,
    attn_second,
    norm_param,
    norm_first,
    norm_second,
    up_weight,
    up_first,
    up_second,
    down_weight,
    down_first,
    down_second,
    expert_vector,
    vector_first,
    vector_second,
):
    experts_here = lax.axis_size(EX)
    hidden_size = lax.axis_size(HI)
    token_count = tokens.shape[0]
    features = tokens.shape[1]
    capacity = 2 * token_count // experts_here
    slot_rows = experts_here * capacity
    head_dim = features // HEADS
    scaling = head_dim ** (-0.5)
    attn_low = attn_weight.astype(jnp.bfloat16)
    norm_low = norm_param.astype(jnp.bfloat16)
    attn_full, norm_full = (
        lax.all_gather(attn_low, BOTH, axis=1, tiled=True),
        lax.all_gather(norm_low, BOTH, axis=1, tiled=True),
    )
    inputs = tokens.astype(jnp.float32)
    normed, norm_pull = jax.vjp(
        layer_norm, inputs, norm_full[0].astype(jnp.float32), norm_full[1].astype(jnp.float32)
    )
    normed_low = normed.astype(jnp.bfloat16)
    projected = jnp.einsum(
        "td,sde->ste", normed_low, attn_full[:3], preferred_element_type=jnp.float32
    ).astype(jnp.bfloat16)
    query = projected[0].reshape(token_count, HEADS, head_dim)
    keys_all = projected[1].reshape(token_count, HEADS, head_dim)
    values_all = projected[2].reshape(token_count, HEADS, head_dim)
    causal = jnp.arange(token_count)[:, None] >= jnp.arange(token_count)[None, :]

    def score_rows():
        raw = (
            jnp.einsum("qhe,khe->hqk", query, keys_all, preferred_element_type=jnp.float32)
            * scaling
        )
        return jnp.where(causal[None], raw, masked_fill)

    scores = score_rows()
    row_max = jnp.max(scores, axis=-1, keepdims=True)
    expo = jnp.exp(scores - row_max)
    row_total = jnp.sum(expo, axis=-1, keepdims=True)
    log_total = row_max + jnp.log(row_total)
    probs_low = (expo / row_total).astype(jnp.bfloat16)
    context = jnp.einsum("hqk,khe->qhe", probs_low, values_all, preferred_element_type=jnp.float32)
    context = context.reshape(token_count, features).astype(jnp.bfloat16)
    resid = inputs + jnp.dot(context, attn_full[3], preferred_element_type=jnp.float32)
    route = routes[:, 0]
    chosen = (route[:, None] == jnp.arange(experts_here, dtype=jnp.int32)[None, :]).astype(
        jnp.int32
    )
    ranked = jnp.sum((jnp.cumsum(chosen, axis=0) - 1) * chosen, axis=1)
    placed = route * capacity + ranked
    placing = (jnp.arange(slot_rows, dtype=jnp.int32)[:, None] == placed[None, :]).astype(
        jnp.bfloat16
    )
    outgoing = jnp.dot(
        placing, resid.astype(jnp.bfloat16), preferred_element_type=jnp.float32
    ).astype(jnp.bfloat16)
    occupied = jnp.sum(placing.astype(jnp.float32), axis=1).astype(jnp.bfloat16)
    arrived, arrived_mask = (
        lax.all_to_all(
            outgoing.reshape(experts_here, capacity, features),
            EX,
            split_axis=0,
            concat_axis=0,
            tiled=True,
        ),
        lax.all_to_all(
            occupied.reshape(experts_here, capacity),
            EX,
            split_axis=0,
            concat_axis=0,
            tiled=True,
        ),
    )
    gathered, gathered_mask = (
        lax.all_gather(arrived, HI, axis=0, tiled=True),
        lax.all_gather(arrived_mask, HI, axis=0, tiled=True),
    )
    rows_all = gathered.reshape(-1, features)
    mask_all = gathered_mask.reshape(-1).astype(jnp.float32)
    rows_float = rows_all.astype(jnp.float32)
    centroid = expert_vector[0, 0]
    gating = jax.nn.sigmoid(jnp.sum(rows_float * centroid, axis=-1))
    expert_normed, expert_pull = jax.vjp(
        layer_norm, rows_float, expert_vector[0, 1], expert_vector[0, 2]
    )
    expert_low = expert_normed.astype(jnp.bfloat16)
    before = jnp.dot(expert_low, up_weight[0], preferred_element_type=jnp.float32)
    after, gelu_pull = jax.vjp(gelu_exact, before)
    after_low = after.astype(jnp.bfloat16)
    branch_own = lax.psum_scatter(
        jnp.dot(after_low, down_weight[0], preferred_element_type=jnp.float32).astype(jnp.bfloat16),
        HI,
        scatter_dimension=0,
        tiled=True,
    ).astype(jnp.float32)
    own_start = lax.axis_index(HI) * slot_rows
    gating_own = lax.dynamic_slice_in_dim(gating, own_start, slot_rows, 0)
    delta = (gating_own[:, None] * branch_own).astype(jnp.bfloat16)
    returned = lax.all_to_all(
        delta.reshape(experts_here, capacity, features),
        EX,
        split_axis=0,
        concat_axis=0,
        tiled=True,
    )
    delta_tokens = jnp.einsum(
        "st,sd->td",
        placing,
        returned.reshape(slot_rows, features),
        preferred_element_type=jnp.float32,
    )
    block_out = (resid + delta_tokens).astype(jnp.bfloat16)
    routed_count = jnp.sum(mask_all)
    gate_total = jnp.sum(mask_all * gating)
    expert_stats = jnp.stack(
        [routed_count / (token_count * hidden_size), gate_total / routed_count]
    )[:, None]
    cot_slots = jnp.dot(placing, cotangent, preferred_element_type=jnp.float32).astype(jnp.bfloat16)
    cot_arrived = lax.all_to_all(
        cot_slots.reshape(experts_here, capacity, features),
        EX,
        split_axis=0,
        concat_axis=0,
        tiled=True,
    )
    cot_rows = lax.all_gather(cot_arrived, HI, axis=0, tiled=True).reshape(-1, features)
    d_branch = (gating[:, None] * cot_rows.astype(jnp.float32)).astype(jnp.bfloat16)
    grad_down = jnp.einsum("gf,gd->fd", after_low, d_branch, preferred_element_type=jnp.float32)
    d_after = jnp.einsum("gd,fd->gf", d_branch, down_weight[0], preferred_element_type=jnp.float32)
    d_before = gelu_pull(d_after)[0].astype(jnp.bfloat16)
    grad_up = jnp.einsum("gd,gf->df", expert_low, d_before, preferred_element_type=jnp.float32)
    d_expert_normed = jnp.einsum(
        "gf,df->gd", d_before, up_weight[0], preferred_element_type=jnp.float32
    )
    d_rows, d_expert_gain, d_expert_bias = expert_pull(d_expert_normed)
    d_rows_own = lax.psum_scatter(
        d_rows.astype(jnp.bfloat16), HI, scatter_dimension=0, tiled=True
    ).astype(jnp.float32)
    cot_own = lax.dynamic_slice_in_dim(cot_rows, own_start, slot_rows, 0).astype(jnp.float32)
    rows_own = lax.dynamic_slice_in_dim(rows_float, own_start, slot_rows, 0)
    d_gating = jnp.sum(cot_own * branch_own, axis=-1)
    d_logit = d_gating * gating_own * (1.0 - gating_own)
    d_centroid = jnp.sum(d_logit[:, None] * rows_own, axis=0)
    d_sent = (d_rows_own + d_logit[:, None] * centroid).astype(jnp.bfloat16)
    back_slots = lax.all_to_all(
        d_sent.reshape(experts_here, capacity, features),
        EX,
        split_axis=0,
        concat_axis=0,
        tiled=True,
    )
    d_resid = cotangent.astype(jnp.float32) + jnp.einsum(
        "st,sd->td",
        placing,
        back_slots.reshape(slot_rows, features),
        preferred_element_type=jnp.float32,
    )
    vector_grad = lax.psum(jnp.stack([d_centroid, d_expert_gain, d_expert_bias])[None], HI)
    d_project = d_resid.astype(jnp.bfloat16)
    grad_out_proj = jnp.einsum("td,te->de", context, d_project, preferred_element_type=jnp.float32)
    d_context = jnp.einsum(
        "te,de->td", d_project, attn_full[3], preferred_element_type=jnp.float32
    ).astype(jnp.bfloat16)
    d_context = d_context.reshape(token_count, HEADS, head_dim)
    attn_probs = jnp.exp(score_rows() - log_total)
    probs_again = attn_probs.astype(jnp.bfloat16)
    d_probs = jnp.einsum("qhe,khe->hqk", d_context, values_all, preferred_element_type=jnp.float32)
    d_values = jnp.einsum(
        "hqk,qhe->khe", probs_again, d_context, preferred_element_type=jnp.float32
    ).astype(jnp.bfloat16)
    d_scores = (
        attn_probs * (d_probs - jnp.sum(d_probs * attn_probs, axis=-1, keepdims=True))
    ).astype(jnp.bfloat16)
    d_query = (
        jnp.einsum("hqk,khe->qhe", d_scores, keys_all, preferred_element_type=jnp.float32) * scaling
    ).astype(jnp.bfloat16)
    d_keys = (
        jnp.einsum("hqk,qhe->khe", d_scores, query, preferred_element_type=jnp.float32) * scaling
    ).astype(jnp.bfloat16)
    d_projected = jnp.stack(
        [
            d_query.reshape(token_count, features),
            d_keys.reshape(token_count, features),
            d_values.reshape(token_count, features),
        ]
    )
    grad_qkv = jnp.einsum(
        "td,ste->sde", normed_low, d_projected, preferred_element_type=jnp.float32
    )
    d_normed = jnp.einsum(
        "ste,sde->td", d_projected, attn_full[:3], preferred_element_type=jnp.float32
    )
    d_inputs, d_norm_gain, d_norm_bias = norm_pull(d_normed)
    token_grad = (d_resid + d_inputs).astype(jnp.bfloat16)
    grad_attn = jnp.concatenate([grad_qkv, grad_out_proj[None]], axis=0)
    grad_norm_param = jnp.stack([d_norm_gain, d_norm_bias])
    attn_shard, norm_shard = (
        lax.psum_scatter(grad_attn, BOTH, scatter_dimension=1, tiled=True),
        lax.psum_scatter(grad_norm_param, BOTH, scatter_dimension=1, tiled=True),
    )
    local_square = (
        jnp.sum(attn_shard * attn_shard)
        + jnp.sum(norm_shard * norm_shard)
        + jnp.sum(grad_up * grad_up)
        + jnp.sum(grad_down * grad_down)
        + jnp.sum(vector_grad * vector_grad) / hidden_size
    )
    grad_norm = jnp.sqrt(lax.psum(local_square, BOTH))
    clip_factor = clip_level / jnp.maximum(grad_norm, clip_level)
    attn_new = adam_step(
        attn_weight, attn_first, attn_second, attn_shard, clip_factor, rate_matrix, decay_rate
    )
    norm_new = adam_step(
        norm_param, norm_first, norm_second, norm_shard, clip_factor, rate_vector, 0.0
    )
    up_new = adam_step(
        up_weight.astype(jnp.float32),
        up_first,
        up_second,
        grad_up[None],
        clip_factor,
        rate_matrix,
        decay_rate,
    )
    down_new = adam_step(
        down_weight.astype(jnp.float32),
        down_first,
        down_second,
        grad_down[None],
        clip_factor,
        rate_matrix,
        decay_rate,
    )
    vector_new = adam_step(
        expert_vector, vector_first, vector_second, vector_grad, clip_factor, rate_vector, 0.0
    )
    return (
        block_out,
        token_grad,
        grad_norm,
        attn_new[0],
        attn_new[1],
        attn_new[2],
        norm_new[0],
        norm_new[1],
        norm_new[2],
        up_new[0],
        up_new[1],
        up_new[2],
        down_new[0],
        down_new[1],
        down_new[2],
        vector_new[0],
        vector_new[1],
        vector_new[2],
        expert_stats,
    )


def fast_shards(
    tokens,
    cotangent,
    routes,
    attn_weight,
    attn_first,
    attn_second,
    norm_param,
    norm_first,
    norm_second,
    up_weight,
    up_first,
    up_second,
    down_weight,
    down_first,
    down_second,
    expert_vector,
    vector_first,
    vector_second,
):
    experts = lax.axis_size(EX)
    depth = lax.axis_size(HI)
    count, width = tokens.shape
    cap = 2 * count // experts
    shard = attn_weight.shape[1]
    lanes = norm_param.shape[1]
    place = lax.axis_index(EX) * depth + lax.axis_index(HI)
    owner = jnp.arange(width, dtype=jnp.int32) // lanes
    norm_own = jnp.where(owner[None] == place, jnp.tile(norm_param, (8, width // lanes)), 0.0)
    w_full, qkv, normed, ctx, resid, sent, placed, gains, cot_raw = attend(
        depth,
        cap,
        tokens,
        attn_weight.astype(jnp.bfloat16),
        norm_own.astype(jnp.bfloat16),
        routes,
        cotangent,
    )
    vec = jnp.pad(expert_vector[0], ((0, 5), (0, 0)))
    d_sum, grad_up, grad_down, delta, vec_part, scal = expert_layer(
        depth, cap, sent, placed, cot_raw, up_weight[0], down_weight[0], vec
    )
    block_out, token_grad, attn_shard, norm_grads, vec_grads, squares = attend_back(
        depth,
        cap,
        shard,
        d_sum,
        cotangent,
        w_full,
        qkv,
        normed,
        ctx,
        tokens,
        gains,
        placed,
        delta,
        resid,
        vec_part,
        scal,
    )
    here = lax.axis_index(EX)
    routed = lax.dynamic_slice(norm_grads, (2, here), (1, 1))[0, 0]
    empty = depth * experts * cap - routed
    gate_total = jnp.sum(scal[0:8, 0]) - 0.5 * empty
    expert_stats = jnp.stack([routed / (count * depth), gate_total / routed])[:, None]
    norm_shard = lax.dynamic_slice(norm_grads, (0, place * lanes), (2, lanes))
    vector_grad = vec_grads[None, 0:3]
    grad_norm = jnp.sqrt(jnp.sum(squares))
    clip_factor = clip_level / jnp.maximum(grad_norm, clip_level)
    attn_new = adam_step(
        attn_weight, attn_first, attn_second, attn_shard, clip_factor, rate_matrix, decay_rate
    )
    norm_new = adam_step(
        norm_param, norm_first, norm_second, norm_shard, clip_factor, rate_vector, 0.0
    )
    up_new = adam_step(
        up_weight.astype(jnp.float32),
        up_first,
        up_second,
        grad_up[None].astype(jnp.float32),
        clip_factor,
        rate_matrix,
        decay_rate,
    )
    down_new = adam_step(
        down_weight.astype(jnp.float32),
        down_first,
        down_second,
        grad_down[None].astype(jnp.float32),
        clip_factor,
        rate_matrix,
        decay_rate,
    )
    vector_new = adam_step(
        expert_vector, vector_first, vector_second, vector_grad, clip_factor, rate_vector, 0.0
    )
    return (
        block_out,
        token_grad,
        grad_norm,
        *attn_new,
        *norm_new,
        *up_new,
        *down_new,
        *vector_new,
        expert_stats,
    )


def solution(mesh):
    small = mesh.shape[EX] == 8 and mesh.shape[HI] == 4
    return jax.shard_map(
        fast_shards if small else shards,
        mesh=mesh,
        in_specs=(
            P(BOTH, None),
            P(BOTH, None),
            P(BOTH, None),
            P(None, BOTH, None),
            P(None, BOTH, None),
            P(None, BOTH, None),
            P(None, BOTH),
            P(None, BOTH),
            P(None, BOTH),
            P(EX, None, HI),
            P(EX, None, HI),
            P(EX, None, HI),
            P(EX, HI, None),
            P(EX, HI, None),
            P(EX, HI, None),
            P(EX, None, None),
            P(EX, None, None),
            P(EX, None, None),
        ),
        out_specs=(
            P(BOTH, None),
            P(BOTH, None),
            P(),
            P(None, BOTH, None),
            P(None, BOTH, None),
            P(None, BOTH, None),
            P(None, BOTH),
            P(None, BOTH),
            P(None, BOTH),
            P(EX, None, HI),
            P(EX, None, HI),
            P(EX, None, HI),
            P(EX, HI, None),
            P(EX, HI, None),
            P(EX, HI, None),
            P(EX, None, None),
            P(EX, None, None),
            P(EX, None, None),
            P(None, EX),
        ),
        check_vma=False,
    )
```

```python
import functools
import math

import jax
import jax.numpy as jnp
from jax import lax
from jax.experimental import pallas as pl
from jax.experimental.pallas import tpu as pltpu
from jax.sharding import PartitionSpec as P

HEADS = 16
STEP = 10


norm_eps = 1e-05
clip_level = 1.0
beta_one = 0.9
beta_two = 0.999
adam_eps = 1e-08
decay_rate = 0.1
rate_matrix = 0.05
rate_vector = 0.5
masked_fill = -1e30
EX, HI = "expert", "hidden"
BOTH = (EX, HI)


def layer_norm(inputs, gain_row, bias_row):
    average = jnp.mean(inputs, axis=-1, keepdims=True)
    centred = inputs - average
    variance = jnp.mean(centred * centred, axis=-1, keepdims=True)
    return centred * lax.rsqrt(variance + norm_eps) * gain_row + bias_row


def gelu_exact(values):
    return jax.nn.gelu(values, approximate=False)


def adam_step(weight, first, second, grad, clip_factor, rate, decay):
    clipped = grad * clip_factor
    moment = beta_one * first + (1.0 - beta_one) * clipped
    square = beta_two * second + (1.0 - beta_two) * clipped * clipped
    corr_one = 1.0 - beta_one**STEP
    corr_two = 1.0 - beta_two**STEP
    update = moment / corr_one / (jnp.sqrt(square / corr_two) + adam_eps) + decay * weight
    return (weight - rate * update, moment, square)


MESH = pl.DeviceIdType.MESH
VMEM_SPEC = pl.BlockSpec(memory_space=pltpu.VMEM)
ANY_SPEC = pl.BlockSpec(memory_space=pl.ANY)


class Place:
    def __init__(self):
        self.e = lax.axis_index(EX)
        self.z = lax.axis_index(HI)
        high, low = lax.div(self.z, 2), lax.rem(self.z, 2)
        self.middle = high + low == 1
        self.ends = jnp.logical_not(self.middle)
        self.line = [self.z, self.z + 1 - 2 * low, 2 - high, 3 - 3 * high]
        self.core = lax.rem(self.e, 2)
        self.x = lax.rem(lax.div(self.e, 2), 2)
        self.y = lax.div(self.e, 4)
        self.ex = self.e + 2 - 4 * self.x
        self.ey = self.e + 4 - 8 * self.y
        self.exy = self.ex + 4 - 8 * self.y
        self.twin = (self.e + 1 - 2 * self.core, self.z)
        self.over_x = (self.ex, self.z)
        self.over_y = (self.ey, self.z)
        self.partner = (self.e, self.line[1])
        self.mirror = (self.e, 3 - self.z)
        self.mates = [None, self.partner, (self.e, self.z + 2 - 4 * high), self.mirror]

    def across(self, k):
        c = lax.rem(self.core + k % 2, 2)
        x = lax.rem(self.x + (k // 2) % 2, 2)
        y = lax.rem(self.y + k // 4, 2)
        return 4 * y + 2 * x + c

    def everyone(self):
        plane = [(self.across(k), self.z) for k in range(1, 8)]
        return plane + self.mates[1:]

    def meet(self):
        barrier = pltpu.get_barrier_semaphore()
        for device in self.everyone():
            pl.semaphore_signal(barrier, inc=1, device_id=device, device_id_type=MESH)
        pl.semaphore_wait(barrier, len(self.everyone()))


class Wire:
    def __init__(self, send_sem, recv_sem):
        self.send_sem, self.recv_sem = send_sem, recv_sem
        self.count = 0
        self.tags = {}
        self.sent = []

    def next(self):
        self.count += 1
        return self.count - 1

    def send(self, src, dst, device, tag=None, when=None):
        i = self.next()
        if tag is not None:
            if tag not in self.tags:
                self.tags[tag] = self.next()
            j = self.tags[tag]
        else:
            j = i
        copy = pltpu.make_async_remote_copy(
            src_ref=src,
            dst_ref=dst,
            send_sem=self.send_sem.at[i],
            recv_sem=self.recv_sem.at[j],
            device_id=device,
            device_id_type=MESH,
        )
        if when is None:
            copy.start()
        else:
            pl.when(when)(copy.start)
        self.sent.append((copy, when))
        return copy

    def arrived(self, tag, dst, device):
        if tag not in self.tags:
            self.tags[tag] = self.next()
        j = self.tags[tag]
        pltpu.make_async_remote_copy(
            src_ref=dst,
            dst_ref=dst,
            send_sem=self.send_sem.at[j],
            recv_sem=self.recv_sem.at[j],
            device_id=device,
            device_id_type=MESH,
        ).wait_recv()

    def left(self, copy):
        copy.wait_send()
        self.sent = [one for one in self.sent if one[0] is not copy]

    def drain(self):
        for copy, when in self.sent:
            if when is None:
                copy.wait_send()
            else:
                pl.when(when)(copy.wait_send)
        self.sent = []


class Line:
    def __init__(self, wire, at, name, slot):
        self.wire, self.at, self.name, self.slot = wire, at, name, slot

    def begin(self, own=None):
        at = self.at
        here = self.slot(at.z)
        own = here if own is None else own
        self.wire.send(own, here, at.partner, (self.name, 1))
        self.wire.send(own, here, at.mirror, (self.name, 2), at.middle)

    def take(self, i, when=None):
        at = self.at
        block = self.slot(at.line[i])
        if when is None:
            self.wire.arrived((self.name, i), block, at.partner)
        else:
            pl.when(when)(lambda: self.wire.arrived((self.name, i), block, at.partner))
        if when is not at.ends:
            to, tag = (at.mirror, 3) if i == 1 else (at.partner, i)
            self.wire.send(block, block, to, (self.name, tag), at.middle)
        return block


class Fetch:
    def __init__(self, sem):
        self.sem = sem
        self.count = 0
        self.open = []

    def start(self, src, dst):
        copy = pltpu.make_async_copy(src, dst, self.sem.at[self.count])
        self.count += 1
        copy.start()
        self.open.append(copy)
        return copy

    def done(self, copy):
        copy.wait()
        self.open = [one for one in self.open if one is not copy]

    def drain(self):
        for copy in self.open:
            copy.wait()
        self.open = []


def dot(a, b, ca=1, cb=0):
    return lax.dot_general(a, b, (((ca,), (cb,)), ((), ())), preferred_element_type=jnp.float32)


def tile(i, size=256):
    return pl.ds(pl.multiple_of(i * size, size), size)


def pick(placed_row, slots):
    which = lax.broadcasted_iota(jnp.int32, (slots, placed_row.shape[1]), 0)
    return jnp.where(which == placed_row, 1.0, 0.0).astype(jnp.bfloat16)


def build(stage, source, placed_row):
    planes, cap, width = stage.shape
    onehot = pick(placed_row, planes * cap)

    @pl.loop(0, width // 512)
    def _(i):
        cols = tile(i, 512)
        value = dot(onehot, source[:, cols]).astype(jnp.bfloat16)
        for k in range(planes):
            stage[k, :, cols] = value[k * cap : (k + 1) * cap]


def attend_kernel(
    cap,
    tok,
    w_own,
    norm_in,
    route,
    cot,
    w_out,
    qkv_out,
    normed_out,
    ctx_out,
    resid_out,
    sent_out,
    placed_out,
    gains_out,
    cot_raw,
    cot_zero,
    w_low,
    wfull,
    norm_sum,
    norm_got,
    qkv,
    normed,
    ctx,
    resid,
    sent,
    placed,
    gains,
    stage,
    send_sem,
    recv_sem,
    local_sem,
):
    at = Place()
    e, z = at.e, at.z
    depth = 4
    count, width = tok.shape
    shard = w_own.shape[1]
    wire = Wire(send_sem, recv_sem)
    fetch = Fetch(local_sem)
    groups = [(0, 3), (3, 1)]
    fetch.start(cot, cot_raw.at[z])
    w_low[...] = w_own[...].astype(jnp.bfloat16)
    lanes = norm_in.shape[1]
    columns = lax.broadcasted_iota(jnp.int32, (lanes, width), 1)
    offset = columns - (e * depth + z) * lanes
    ours = lax.broadcasted_iota(jnp.int32, (lanes, width), 0) == offset
    low = norm_in[...].astype(jnp.bfloat16)
    norm_sum[0] = jnp.zeros((16, width), jnp.bfloat16)
    norm_sum[0, 0:2, :] = dot(low, jnp.where(ours, 1.0, 0.0).astype(jnp.bfloat16)).astype(
        jnp.bfloat16
    )
    at.meet()

    def block(g, who, zz):
        first, mats = groups[g]
        start = pl.multiple_of((who * depth + zz) * shard, shard)
        return wfull.at[pl.ds(first, mats), pl.ds(start, shard)]

    def mine(g):
        first, mats = groups[g]
        return w_low.at[pl.ds(first, mats)]

    lines = [Line(wire, at, g, lambda zz, g=g: block(g, e, zz)) for g in range(2)]
    lines[0].begin(mine(0))
    norm_to = [at.partner, at.mirror, at.over_x, at.over_y, at.twin]
    norm_copy = wire.send(norm_sum.at[0], norm_got.at[0], norm_to[0])
    own = [fetch.start(mine(g), block(g, e, z)) for g in range(2)]
    to_x, to_y, to_far, to_twin = {}, {}, {}, {}

    def norm_next(k):
        norm_copy.wait_recv()
        norm_sum[k] = norm_sum[k - 1] + norm_got[k - 1]
        return wire.send(norm_sum.at[k], norm_got.at[k], norm_to[k])

    def plane(g, i):
        here = block(g, e, at.line[i])
        if i == 0:
            fetch.done(own[g])
        else:
            lines[g].take(i)
        to_x[g, i] = wire.send(here, here, at.over_x)
        to_y[g, i] = wire.send(here, here, at.over_y)
        to_twin[g, i, 0] = wire.send(here, here, at.twin)

    def forward(g, i):
        zz = at.line[i]
        from_x, from_y = block(g, at.ex, zz), block(g, at.ey, zz)
        to_x[g, i].wait_recv()
        if i in (0, 3):
            to_far[g, i] = wire.send(from_x, from_x, at.over_y)
        to_twin[g, i, 1] = wire.send(from_x, from_x, at.twin)
        to_y[g, i].wait_recv()
        if i in (1, 2):
            to_far[g, i] = wire.send(from_y, from_y, at.over_x)
        to_twin[g, i, 2] = wire.send(from_y, from_y, at.twin)

    def far(g, i):
        to_far[g, i].wait_recv()
        there = block(g, at.exy, at.line[i])
        to_twin[g, i, 3] = wire.send(there, there, at.twin)

    def finish(g):
        for i in range(depth):
            for k in range(4):
                to_twin[g, i, k].wait_recv()

    plane(0, 0)
    lane = lax.broadcasted_iota(jnp.int32, (count, 128), 1)
    chosen = jnp.where(route[...] == lane, 1.0, 0.0)
    rows_i = lax.broadcasted_iota(jnp.int32, (count, count), 0)
    cols_i = lax.broadcasted_iota(jnp.int32, (count, count), 1)
    lower = jnp.where(rows_i >= cols_i, 1.0, 0.0)
    running = dot(lower.astype(jnp.bfloat16), chosen.astype(jnp.bfloat16))
    rank = jnp.sum((running - 1.0) * chosen, axis=1, keepdims=True)
    column = route[...].astype(jnp.float32) * float(cap) + rank
    wide_r = lax.broadcasted_iota(jnp.int32, (count, 256), 0)
    wide_c = lax.broadcasted_iota(jnp.int32, (count, 256), 1)
    row = jnp.sum(jnp.where(wide_r == wide_c, column + 1.0, 0.0), axis=0, keepdims=True) - 1.0
    placed[z] = jnp.broadcast_to(row, (8, 256)).astype(jnp.int32)
    plane(0, 1)
    norm_copy = norm_next(1)
    forward(0, 0)
    plane(0, 2)
    norm_copy = norm_next(2)
    forward(0, 1)
    far(0, 0)
    plane(0, 3)
    lines[1].begin(mine(1))
    build(stage, cot, placed[z, 0:1, :count])
    norm_copy = norm_next(3)
    far(0, 1)
    forward(0, 2)
    plane(1, 0)
    plane(1, 1)
    norm_copy = norm_next(4)
    norm_copy.wait_recv()
    gain_rows = norm_sum[4] + norm_got[4]
    tally = jnp.concatenate(
        [
            jnp.broadcast_to(jnp.sum(chosen, axis=0, keepdims=True), (16, 128)),
            jnp.zeros((16, width - 128), jnp.float32),
        ],
        axis=1,
    )
    third_row = lax.broadcasted_iota(jnp.int32, (16, width), 0) == 2
    gains[...] = jnp.where(third_row, tally, gain_rows.astype(jnp.float32)).astype(jnp.bfloat16)
    fetch.start(gains, gains_out)
    gain = gains[0:1, :].astype(jnp.float32)
    bias = gains[1:2, :].astype(jnp.float32)

    @pl.loop(0, count // 64)
    def _(i):
        rows = tile(i, 64)
        piece = tok[rows, :].astype(jnp.float32)
        average = jnp.mean(piece, axis=-1, keepdims=True)
        centred = piece - average
        variance = jnp.mean(centred * centred, axis=-1, keepdims=True)
        normed[rows, :] = (centred * lax.rsqrt(variance + norm_eps) * gain + bias).astype(
            jnp.bfloat16
        )

    fetch.start(normed, normed_out)
    far(0, 2)
    forward(0, 3)
    plane(1, 2)
    plane(1, 3)
    cots = Line(wire, at, "cot", lambda zz: cot_raw.at[zz])
    places = Line(wire, at, "place", lambda zz: placed.at[zz])
    cots.begin(cot)
    places.begin()
    far(0, 3)
    finish(0)
    fetch.start(wfull.at[pl.ds(0, 3)], w_out.at[pl.ds(0, 3)])
    tiles = width // 256

    @pl.loop(0, 3 * tiles)
    def _(i):
        m = lax.div(i, tiles)
        cols = tile(lax.rem(i, tiles))
        qkv[m, :, cols] = dot(normed[...], wfull[m, :, cols]).astype(jnp.bfloat16)

    fetch.start(qkv, qkv_out)
    for i in range(depth):
        forward(1, i)
    places.take(1)
    cots.take(1)
    places.take(2, at.middle)
    cots.take(2, at.middle)
    slots_out = [
        wire.send(stage.at[at.across(k)], cot_zero.at[k], (at.across(k), z)) for k in range(1, 8)
    ]
    fetch.start(stage.at[e], cot_zero.at[0])
    causal = rows_i >= cols_i
    left = lax.broadcasted_iota(jnp.int32, (count, 128), 1) < 64
    scaling = jnp.asarray(64 ** (-0.5), jnp.bfloat16)

    def pair(i):
        cols = tile(i, 128)
        query = qkv[0, :, cols] * scaling
        keys = qkv[1, :, cols]
        values = qkv[2, :, cols]
        halves = []
        for side in range(2):
            mask = left if side == 0 else jnp.logical_not(left)
            scores = dot(jnp.where(mask, query, jnp.zeros_like(query)), keys, 1, 1)
            scores = jnp.where(causal, scores, masked_fill)
            top = jnp.max(scores, axis=-1, keepdims=True)
            expo = jnp.exp(scores - top)
            probs = expo / jnp.sum(expo, axis=-1, keepdims=True)
            halves.append(dot(probs.astype(jnp.bfloat16), values))
        ctx[:, cols] = jnp.where(left, halves[0], halves[1]).astype(jnp.bfloat16)

    pl.loop(0, width // 256)(pair)
    for i in range(depth):
        far(1, i)
    places.take(2, at.ends)
    cots.take(2, at.ends)
    places.take(3, at.middle)
    cots.take(3, at.middle)
    pl.loop(width // 256, width // 128)(pair)
    fetch.start(ctx, ctx_out)
    finish(1)
    fetch.start(wfull.at[pl.ds(3, 1)], w_out.at[pl.ds(3, 1)])

    @pl.loop(0, tiles)
    def _(i):
        cols = tile(i)
        value = tok[:, cols].astype(jnp.float32) + dot(ctx[...], wfull[3, :, cols])
        resid[:, cols] = value
        sent[:, cols] = value.astype(jnp.bfloat16)

    fetch.start(sent, sent_out)
    fetch.start(resid, resid_out)
    places.take(3, at.ends)
    cots.take(3, at.ends)
    fetch.start(placed, placed_out)
    for copy in slots_out:
        copy.wait_recv()
    wire.drain()
    fetch.drain()


def attend(cap, tokens, w_own, norm_own, routes, cotangent):
    count, width = tokens.shape
    bf, full = jnp.bfloat16, jnp.float32
    copies = 128
    shapes = [
        ((4, width, width), bf),
        ((3, count, width), bf),
        ((count, width), bf),
        ((count, width), bf),
        ((count, width), full),
        ((count, width), bf),
        ((4, 8, 256), jnp.int32),
        ((16, width), bf),
        ((4, count, width), bf),
        ((8, cap, width), bf),
    ]
    return pl.pallas_call(
        functools.partial(attend_kernel, cap),
        out_shape=[jax.ShapeDtypeStruct(*one) for one in shapes],
        in_specs=[VMEM_SPEC] * 5,
        out_specs=[ANY_SPEC] * len(shapes),
        scratch_shapes=[
            pltpu.VMEM((4, w_own.shape[1], width), bf),
            pltpu.VMEM((4, width, width), bf),
            pltpu.VMEM((5, 16, width), bf),
            pltpu.VMEM((5, 16, width), bf),
            pltpu.VMEM((3, count, width), bf),
            pltpu.VMEM((count, width), bf),
            pltpu.VMEM((count, width), bf),
            pltpu.VMEM((count, width), full),
            pltpu.VMEM((count, width), bf),
            pltpu.VMEM((4, 8, 256), jnp.int32),
            pltpu.VMEM((16, width), bf),
            pltpu.VMEM((8, cap, width), bf),
            pltpu.SemaphoreType.DMA((copies,)),
            pltpu.SemaphoreType.DMA((copies,)),
            pltpu.SemaphoreType.DMA((16,)),
        ],
        compiler_params=pltpu.CompilerParams(
            collective_id=0, has_side_effects=True, vmem_limit_bytes=62 << 20
        ),
    )(tokens, w_own, norm_own, routes, cotangent)


def gelu_pair(v):
    cdf = 0.5 + 0.5 * lax.erf(v * (0.5**0.5))
    pdf = jnp.exp(-0.5 * v * v) * ((2.0 * math.pi) ** -0.5)
    return v * cdf, cdf + v * pdf


def fold(v):
    total = v[0:8]
    for i in range(8, v.shape[0], 8):
        total = total + v[i : i + 8]
    return total


def spread(column, lanes):
    return jnp.concatenate([column] * (lanes // 128), axis=1)


def square_lanes(v):
    total = v[:, 0:128] * v[:, 0:128]
    for i in range(128, v.shape[1], 128):
        total = total + v[:, i : i + 128] * v[:, i : i + 128]
    return total


def unslot(placed_row, slots, out):
    planes, cap, width = slots.shape
    onehot = pick(placed_row, planes * cap)

    @pl.loop(0, width // 256)
    def _(j):
        cols = tile(j)
        value = slots[:, :, cols].reshape(planes * cap, 256)
        out[:, cols] = dot(onehot, value, 0, 0).astype(jnp.bfloat16)


class Home:
    def __init__(self, wire, at, name, part, got):
        self.wire, self.at, self.name = wire, at, name
        self.part, self.got = part, got

    def add(self, i, k):
        part = self.part(i)
        part[...] = (part[...].astype(jnp.float32) + self.got[k].astype(jnp.float32)).astype(
            jnp.bfloat16
        )

    def push(self, i):
        here = self.part(i)
        at = self.at
        self.wire.send(here, self.got.at[i - 1], at.partner, (self.name, i), at.ends)

    def pass_on(self, i):
        at, wire, name = self.at, self.wire, self.name

        @pl.when(at.middle)
        def _():
            wire.arrived((name, i), self.got.at[i - 1], at.partner)
            self.add(i, i - 1)

        k = {3: 3, 2: 4}[i]
        wire.send(self.part(i), self.got.at[k], at.mirror, (name, k + 1), at.middle)

    def near(self):
        at, wire, name = self.at, self.wire, self.name

        @pl.when(at.middle)
        def _():
            wire.arrived((name, 4), self.got.at[3], at.mirror)
            self.add(1, 3)

        wire.send(self.part(1), self.got.at[0], at.partner, (name, 1))

    def last(self):
        self.wire.arrived((self.name, 1), self.got.at[0], self.at.partner)

        @pl.when(self.at.middle)
        def _():
            self.wire.arrived((self.name, 5), self.got.at[4], self.at.mirror)
            self.add(0, 4)

    def total(self, cols):
        return self.part(0)[:, cols].astype(jnp.float32) + self.got[0, :, cols].astype(jnp.float32)


def expert_kernel(
    cap,
    sent_in,
    placed_in,
    cot_raw,
    cot_zero,
    up_in,
    down_in,
    vec,
    d_sum,
    g_up,
    g_down,
    delta_out,
    vec_part,
    scal,
    sent,
    placed,
    cot_line,
    up,
    down,
    raw,
    stage,
    rows,
    cots,
    xn,
    act,
    slope,
    delta,
    d_slots,
    back,
    part,
    z_in,
    d_xn,
    gate,
    d_logit,
    g_stage,
    send_sem,
    recv_sem,
    local_sem,
):
    at = Place()
    e, z = at.e, at.z
    depth, planes = 4, 8
    count, width = sent.shape
    slots = planes * cap
    units = up.shape[1]
    wire = Wire(send_sem, recv_sem)
    fetch = Fetch(local_sem)
    in_sent = fetch.start(sent_in, sent)
    in_placed = fetch.start(placed_in, placed)
    in_up = fetch.start(up_in, up)
    in_down = fetch.start(down_in, down)
    in_cot = fetch.start(cot_raw, cot_line)
    in_zero = fetch.start(cot_zero, cots.at[0])
    at.meet()
    fetch.done(in_sent)
    line = Line(wire, at, "row", lambda zz: raw.at[zz])
    line.begin(sent)
    vec_part[...] = jnp.zeros_like(vec_part)
    scal[...] = jnp.zeros_like(scal)
    fetch.done(in_placed)
    centroid = lambda: vec[0:1, :]
    row_copies, cot_copies, ret_copies = {}, {}, {}

    def exchange(i, dst):
        copies = [
            wire.send(stage.at[i, at.across(k)], dst.at[i, k], (at.across(k), z))
            for k in range(1, planes)
        ]
        dst[i, 0] = stage[i, e]
        return copies

    def slot_row(i):
        return placed[at.line[i], 0:1, :count]

    def rows_out(i):
        source = sent if i == 0 else raw.at[at.line[i]]
        build(stage.at[i], source, slot_row(i))
        row_copies[i] = exchange(i, rows)

    def cots_out(i):
        for copy in row_copies[i]:
            wire.left(copy)
        build(stage.at[i], cot_line.at[at.line[i]], slot_row(i))
        cot_copies[i] = exchange(i, cots)

    def forward(i):
        for copy in row_copies[i]:
            copy.wait_recv()
        gain, bias = vec[1:2, :], vec[2:3, :]

        @pl.loop(0, planes)
        def _(k):
            r = rows[i, k].astype(jnp.float32)
            logit = jnp.sum(r * centroid(), axis=-1, keepdims=True)
            g = jax.nn.sigmoid(logit)
            wide = jnp.broadcast_to(g, (cap, 128))
            gate[i, k] = wide
            scal[0:8] += fold(wide)
            average = jnp.mean(r, axis=-1, keepdims=True)
            centred = r - average
            variance = jnp.mean(centred * centred, axis=-1, keepdims=True)
            xn[i, pl.ds(pl.multiple_of(k * cap, 16), cap), :] = (
                centred * lax.rsqrt(variance + norm_eps) * gain + bias
            ).astype(jnp.bfloat16)

        if i == 0:
            fetch.done(in_up)

        @pl.loop(0, units // 256)
        def _(j):
            cols = tile(j)
            value, rate = gelu_pair(dot(xn[i], up[:, cols]))
            act[i, :, cols] = value.astype(jnp.bfloat16)
            slope[i, :, cols] = rate.astype(jnp.bfloat16)

        if i == 0:
            fetch.done(in_down)

        @pl.loop(0, width // 256)
        def _(j):
            cols = tile(j)
            branch = dot(act[i], down[:, cols])
            wide = spread(gate[i].reshape(slots, 128), 256)
            value = (wide * branch).astype(jnp.bfloat16)
            for k in range(planes):
                delta[i, k, :, cols] = value[k * cap : (k + 1) * cap]

        fetch.start(delta.at[i], delta_out.at[i])

    def backward(i):
        for copy in cot_copies[i]:
            copy.wait_recv()
        if i == 0:
            wire.left(cot_copies[1][0])

        @pl.loop(0, planes)
        def _(k):
            c = cots[i, k].astype(jnp.float32)
            g = gate[i, k]
            inner = jnp.sum(c * delta[i, k].astype(jnp.float32), axis=-1, keepdims=True)
            dl = (1.0 - g) * inner
            d_logit[i, k] = dl
            cots[i, k] = (c * spread(g, width)).astype(jnp.bfloat16)
            vec_part[0] += fold(rows[i, k].astype(jnp.float32) * spread(dl, width))

        @pl.loop(0, units // 256)
        def _(j):
            cols = tile(j)
            d_act = dot(cots[i].reshape(slots, width), down[cols, :], 1, 1)
            slope[i, :, cols] = (d_act * slope[i, :, cols].astype(jnp.float32)).astype(
                jnp.bfloat16
            )

        @pl.loop(0, width // 256)
        def _(j):
            cols = tile(j)
            value = dot(slope[i], up[cols, :], 1, 1)
            for k in range(planes):
                d_xn[k, :, cols] = value[k * cap : (k + 1) * cap]

        @pl.loop(0, planes)
        def _(k):
            r = rows[i, k].astype(jnp.float32)
            average = jnp.mean(r, axis=-1, keepdims=True)
            centred = r - average
            variance = jnp.mean(centred * centred, axis=-1, keepdims=True)
            scale = lax.rsqrt(variance + norm_eps)
            hat = centred * scale
            dx = d_xn[k]
            vec_part[1] += fold(dx * hat)
            vec_part[2] += fold(dx)
            dh = dx * vec[1:2, :]
            first = jnp.mean(dh, axis=-1, keepdims=True)
            second = jnp.mean(dh * hat, axis=-1, keepdims=True)
            d_in = scale * (dh - first - hat * second)
            d_slots[i, k] = (d_in + spread(d_logit[i, k], width) * centroid()).astype(jnp.bfloat16)

        ret_copies[i] = [
            wire.send(d_slots.at[i, k], back.at[i, e], (at.across(k), z))
            for k in range(1, planes)
        ]
        back[i, e] = d_slots[i, 0]

    home = Home(wire, at, "home", lambda i: part.at[i], z_in)

    def collect(i):
        for copy in ret_copies[i]:
            copy.wait_recv()
        unslot(slot_row(i), back.at[i], part.at[i])

    def weight_grad(lhs, rhs, index, out):
        @pl.loop(0, lhs.shape[-1] // 256)
        def _(j):
            cols = tile(j)
            left = lhs[:, :, cols].reshape(depth * slots, 256)
            value = dot(left, rhs[...].reshape(depth * slots, rhs.shape[-1]), 0, 0)
            scal[8:16] += fold(square_lanes(value))
            g_stage[index, cols, :] = value.astype(jnp.bfloat16)

        fetch.start(g_stage.at[index], out)

    rows_out(0)
    line.take(1)
    line.take(2, at.middle)
    rows_out(1)
    forward(0)
    line.take(2, at.ends)
    line.take(3, at.middle)
    rows_out(2)
    forward(1)
    line.take(3, at.ends)
    rows_out(3)
    fetch.done(in_zero)
    cot_copies[0] = []
    cot_copies[1] = [wire.send(cots.at[0], cots.at[1], at.partner)]
    fetch.done(in_cot)
    forward(2)
    cots_out(3)
    forward(3)
    cots_out(2)
    backward(3)
    backward(2)
    collect(3)
    home.push(3)
    backward(1)
    collect(2)
    home.push(2)
    home.pass_on(3)
    backward(0)
    collect(1)
    home.pass_on(2)
    home.near()
    weight_grad(act, cots, 0, g_down)
    weight_grad(xn, slope, 1, g_up)
    collect(0)
    home.last()

    @pl.loop(0, width // 256)
    def _(j):
        cols = tile(j)
        d_sum[:, cols] = home.total(cols)

    wire.drain()
    fetch.drain()


def expert_layer(cap, sent, placed, cot_raw, cot_zero, up, down, vec):
    count, width = sent.shape
    units = up.shape[1]
    depth = 4
    bf, full = jnp.bfloat16, jnp.float32
    slots = 8 * cap
    copies = 3 * 7 * depth + 32
    shapes = [
        ((count, width), full),
        ((width, units), bf),
        ((units, width), bf),
        ((depth, 8, cap, width), bf),
        ((3, 8, width), full),
        ((16, 128), full),
    ]
    big = pltpu.VMEM((depth, 8, cap, width), bf)
    return pl.pallas_call(
        functools.partial(expert_kernel, cap),
        out_shape=[jax.ShapeDtypeStruct(*one) for one in shapes],
        in_specs=[ANY_SPEC] * 6 + [VMEM_SPEC],
        out_specs=[VMEM_SPEC, ANY_SPEC, ANY_SPEC, ANY_SPEC, VMEM_SPEC, VMEM_SPEC],
        scratch_shapes=[
            pltpu.VMEM((count, width), bf),
            pltpu.VMEM((depth, 8, 256), jnp.int32),
            pltpu.VMEM((depth, count, width), bf),
            pltpu.VMEM((width, units), bf),
            pltpu.VMEM((units, width), bf),
            pltpu.VMEM((depth, count, width), bf),
            big,
            big,
            big,
            pltpu.VMEM((depth, slots, width), bf),
            pltpu.VMEM((depth, slots, units), bf),
            pltpu.VMEM((depth, slots, units), bf),
            big,
            big,
            big,
            pltpu.VMEM((depth, count, width), bf),
            pltpu.VMEM((5, count, width), bf),
            pltpu.VMEM((8, cap, width), full),
            pltpu.VMEM((depth, 8, cap, 128), full),
            pltpu.VMEM((depth, 8, cap, 128), full),
            pltpu.VMEM((2, max(width, units), max(width, units)), bf),
            pltpu.SemaphoreType.DMA((copies,)),
            pltpu.SemaphoreType.DMA((copies,)),
            pltpu.SemaphoreType.DMA((16,)),
        ],
        compiler_params=pltpu.CompilerParams(
            collective_id=1, has_side_effects=True, vmem_limit_bytes=62 << 20
        ),
    )(sent, placed, cot_raw, cot_zero, up, down, vec)


def reduce_kernel(
    cap,
    d_sum,
    cot,
    w_in,
    qkv_in,
    normed_in,
    ctx,
    tok,
    gains,
    placed,
    delta_in,
    resid,
    vec_part,
    scal,
    block_out,
    token_grad,
    shard_out,
    norm_out,
    vec_out,
    square_out,
    wfull,
    qkv,
    normed,
    delta,
    d_resid,
    d_proj,
    d_ctx,
    d_qkv,
    d_norm,
    stage,
    twin_in,
    x_in,
    y_in,
    x_last,
    y_last,
    done,
    z_last,
    back,
    part,
    z_in,
    small,
    small_in,
    square,
    send_sem,
    recv_sem,
    local_sem,
):
    at = Place()
    e, z = at.e, at.z
    depth, planes = 4, 8
    count, width = tok.shape
    shard = shard_out.shape[1]
    column = depth * shard
    half = column // 2
    wire = Wire(send_sem, recv_sem)
    fetch = Fetch(local_sem)
    in_delta = {i: fetch.start(delta_in.at[i], delta.at[i]) for i in (3, 2, 1, 0)}
    in_w = {m: fetch.start(w_in.at[m], wfull.at[m]) for m in (3, 2, 1, 0)}
    in_qkv = fetch.start(qkv_in, qkv)
    in_normed = fetch.start(normed_in, normed)
    at.meet()
    ret = {}
    home = Home(wire, at, "home", lambda i: part.at[i], z_in)

    def give(i):
        fetch.done(in_delta[i])
        ret[i] = [
            wire.send(delta.at[i, k], back.at[i, e], (at.across(k), z)) for k in range(1, planes)
        ]
        back[i, e] = delta[i, 0]

    def collect(i):
        for copy in ret[i]:
            copy.wait_recv()
        unslot(placed[at.line[i], 0:1, :count], back.at[i], part.at[i])

    def weight_grad(m, left_ref, right):
        @pl.loop(0, planes)
        def _(i):
            cols = pl.ds(pl.multiple_of(i * column, column), column)
            value = dot(left_ref[:, cols], right[...], 0, 0).astype(jnp.bfloat16)
            stage[m, lax.div(i, 4), lax.rem(lax.div(i, 2), 2), lax.rem(i, 2)] = value

    other = 1 - at.core
    first, second, third, fourth = {}, {}, {}, {}

    def to_core(m):
        first[m] = wire.send(stage.at[m, :, :, other], twin_in.at[m], at.twin)

    def to_plane(m):
        first[m].wait_recv()
        for j in range(2):
            for i in range(2):
                twin_in[m, j, i] = twin_in[m, j, i] + stage[m, j, i, at.core]
        second[m] = (
            wire.send(twin_in.at[m, :, 1 - at.x, pl.ds(0, half)], x_in.at[m], at.over_x),
            wire.send(twin_in.at[m, 1 - at.y, :, pl.ds(half, half)], y_in.at[m], at.over_y),
        )

    def to_last(m):
        second[m][0].wait_recv()
        for j in range(2):
            x_in[m, j] = x_in[m, j] + twin_in[m, j, at.x, 0:half]
        one = wire.send(x_in.at[m, 1 - at.y], x_last.at[m], at.over_y)
        second[m][1].wait_recv()
        for i in range(2):
            y_in[m, i] = y_in[m, i] + twin_in[m, at.y, i, half:]
        two = wire.send(y_in.at[m, 1 - at.x], y_last.at[m], at.over_x)
        third[m] = (one, two)

    def to_owner(m):
        third[m][0].wait_recv()
        pair = (2, shard, width)
        done[m, 0:2] = (x_in[m, at.y] + x_last[m]).reshape(pair)
        third[m][1].wait_recv()
        done[m, 2:4] = (y_in[m, at.x] + y_last[m]).reshape(pair)
        fourth[m] = [
            wire.send(done.at[m, at.mates[k][1]], z_last.at[m, k - 1], at.mates[k])
            for k in range(1, depth)
        ]

    def own(m):
        total = done[m, z].astype(jnp.float32)
        for k in range(1, depth):
            fourth[m][k - 1].wait_recv()
            total = total + z_last[m, k - 1].astype(jnp.float32)
        shard_out[m] = total

    give(3)
    value = cot[...].astype(jnp.float32) + d_sum[...]
    d_resid[...] = value
    d_proj[...] = value.astype(jnp.bfloat16)
    weight_grad(3, ctx, d_proj)
    to_core(3)
    fetch.done(in_w[3])

    @pl.loop(0, width // 256)
    def _(j):
        cols = tile(j)
        d_ctx[:, cols] = dot(d_proj[...], wfull[3, cols, :], 1, 1).astype(jnp.bfloat16)

    to_plane(3)
    fetch.done(in_qkv)
    causal = lax.broadcasted_iota(jnp.int32, (count, count), 0) >= lax.broadcasted_iota(
        jnp.int32, (count, count), 1
    )
    left = lax.broadcasted_iota(jnp.int32, (count, 128), 1) < 64
    scaling = 64 ** (-0.5)

    def pair(i):
        cols = tile(i, 128)
        query = qkv[0, :, cols]
        keys = qkv[1, :, cols]
        values = qkv[2, :, cols]
        d_out = d_ctx[:, cols]
        zero = jnp.zeros_like(query)
        got = []
        for side in range(2):
            mask = left if side == 0 else jnp.logical_not(left)
            q_side = jnp.where(mask, query, zero)
            k_side = jnp.where(mask, keys, zero)
            o_side = jnp.where(mask, d_out, zero)
            scores = dot(q_side, keys, 1, 1) * scaling
            scores = jnp.where(causal, scores, masked_fill)
            top = jnp.max(scores, axis=-1, keepdims=True)
            expo = jnp.exp(scores - top)
            probs = expo / jnp.sum(expo, axis=-1, keepdims=True)
            d_probs = dot(o_side, values, 1, 1)
            inner = jnp.sum(d_probs * probs, axis=-1, keepdims=True)
            d_scores = (probs * (d_probs - inner)).astype(jnp.bfloat16)
            got.append(
                (
                    dot(d_scores, k_side),
                    dot(d_scores, q_side, 0, 0),
                    dot(probs.astype(jnp.bfloat16), o_side, 0, 0),
                )
            )
        d_qkv[0, :, cols] = ((got[0][0] + got[1][0]) * scaling).astype(jnp.bfloat16)
        d_qkv[1, :, cols] = ((got[0][1] + got[1][1]) * scaling).astype(jnp.bfloat16)
        d_qkv[2, :, cols] = (got[0][2] + got[1][2]).astype(jnp.bfloat16)

    pl.loop(0, width // 256)(pair)
    give(2)
    pl.loop(width // 256, width // 128)(pair)
    fetch.done(in_normed)
    weight_grad(2, normed, d_qkv.at[2])
    to_core(2)
    to_last(3)
    weight_grad(1, normed, d_qkv.at[1])
    to_core(1)
    to_plane(2)
    weight_grad(0, normed, d_qkv.at[0])
    to_core(0)
    collect(3)
    home.push(3)
    to_owner(3)
    to_plane(1)
    for m in (2, 1, 0):
        fetch.done(in_w[m])

    @pl.loop(0, width // 256)
    def _(j):
        cols = tile(j)
        d_norm[:, cols] = (
            dot(d_qkv[0], wfull[0, cols, :], 1, 1)
            + dot(d_qkv[1], wfull[1, cols, :], 1, 1)
            + dot(d_qkv[2], wfull[2, cols, :], 1, 1)
        )

    gain = gains[0:1, :].astype(jnp.float32)
    d_gain = jnp.zeros((8, width), jnp.float32)
    d_bias = jnp.zeros((8, width), jnp.float32)
    for i in range(0, count, 64):
        piece = tok[i : i + 64, :].astype(jnp.float32)
        average = jnp.mean(piece, axis=-1, keepdims=True)
        centred = piece - average
        variance = jnp.mean(centred * centred, axis=-1, keepdims=True)
        scale = lax.rsqrt(variance + norm_eps)
        hat = centred * scale
        dx = d_norm[i : i + 64, :]
        d_gain = d_gain + fold(dx * hat)
        d_bias = d_bias + fold(dx)
        dh = dx * gain
        mean_one = jnp.mean(dh, axis=-1, keepdims=True)
        mean_two = jnp.mean(dh * hat, axis=-1, keepdims=True)
        d_in = scale * (dh - mean_one - hat * mean_two)
        token_grad[i : i + 64, :] = (d_resid[i : i + 64, :] + d_in).astype(jnp.bfloat16)
    mine = small.at[0]
    mine[...] = jnp.zeros((16, width), jnp.float32)
    mine[2:3, :] = gains[2:3, :].astype(jnp.float32)
    mine[0:1, :] = jnp.sum(d_gain, axis=0, keepdims=True)
    mine[1:2, :] = jnp.sum(d_bias, axis=0, keepdims=True)
    for k in range(3):
        mine[8 + k : 9 + k, :] = jnp.sum(vec_part[k], axis=0, keepdims=True)
    small_to = [at.partner, at.mirror, at.over_x, at.over_y, at.twin]

    def small_send(k):
        rows = pl.ds(0, 16 if k < 2 else 8)
        return wire.send(small.at[k, rows], small_in.at[k, rows], small_to[k])

    def small_next(k, copy):
        copy.wait_recv()
        rows = slice(0, 16 if k < 3 else 8)
        small[k, rows] = small[k - 1, rows] + small_in[k - 1, rows]
        if k == 2:
            vec_out[...] = small[2, 8:16]
        return small_send(k) if k < 5 else None

    flow = small_send(0)
    to_plane(0)
    to_last(2)
    collect(2)
    home.push(2)
    home.pass_on(3)
    flow = small_next(1, flow)
    give(1)
    to_last(1)
    to_owner(2)
    flow = small_next(2, flow)
    own(3)
    home.pass_on(2)
    give(0)
    to_last(0)
    flow = small_next(3, flow)
    to_owner(1)
    own(2)
    flow = small_next(4, flow)
    to_owner(0)
    collect(1)
    home.near()
    small_next(5, flow)
    norm_out[...] = small[5, 0:8]
    own(1)
    collect(0)
    norm_rows = norm_out[0:2, :]
    vec_rows = vec_out[0:3, :]
    squares = jnp.sum(norm_rows * norm_rows, axis=0, keepdims=True) / (planes * depth) + jnp.sum(
        vec_rows * vec_rows, axis=0, keepdims=True
    ) / depth
    local = scal[8:16, :]
    for m in (3, 2, 1):
        local = local + fold(square_lanes(shard_out[m]))
    lane_squares = squares[:, 0:128]
    for i in range(128, width, 128):
        lane_squares = lane_squares + squares[:, i : i + 128]
    head = lax.broadcasted_iota(jnp.int32, (8, 128), 0) == 0
    local = local + jnp.where(head, jnp.broadcast_to(lane_squares, (8, 128)), 0.0)
    own(0)
    square[0, e] = local + fold(square_lanes(shard_out[0]))
    spot = square.at[0, e]
    copies = [wire.send(spot, spot, (at.across(k), z)) for k in range(1, planes)]
    home.last()

    @pl.loop(0, width // 256)
    def _(j):
        cols = tile(j)
        block_out[:, cols] = (resid[:, cols] + home.total(cols)).astype(jnp.bfloat16)

    for copy in copies:
        copy.wait_recv()
    total = square[0, 0]
    for k in range(1, planes):
        total = total + square[0, k]
    square[1, z] = total
    spot = square.at[1, z]
    copies = [wire.send(spot, spot, at.mates[k]) for k in range(1, depth)]
    for copy in copies:
        copy.wait_recv()
    total = square[1, 0]
    for d in range(1, depth):
        total = total + square[1, d]
    square_out[...] = total
    wire.drain()
    fetch.drain()


def attend_back(cap, shard, *args):
    tokens = args[6]
    count, width = tokens.shape
    depth = 4
    bf, full = jnp.bfloat16, jnp.float32
    column = depth * shard
    half = column // 2
    copies = 7 * depth + 96
    shapes = [
        ((count, width), bf),
        ((count, width), bf),
        ((4, shard, width), full),
        ((8, width), full),
        ((8, width), full),
        ((8, 128), full),
    ]
    return pl.pallas_call(
        functools.partial(reduce_kernel, cap),
        out_shape=[jax.ShapeDtypeStruct(*one) for one in shapes],
        in_specs=[VMEM_SPEC] * 2
        + [ANY_SPEC] * 3
        + [VMEM_SPEC] * 4
        + [ANY_SPEC]
        + [VMEM_SPEC] * 3,
        out_specs=[VMEM_SPEC] * 6,
        scratch_shapes=[
            pltpu.VMEM((4, width, width), bf),
            pltpu.VMEM((3, count, width), bf),
            pltpu.VMEM((count, width), bf),
            pltpu.VMEM((depth, 8, cap, width), bf),
            pltpu.VMEM((count, width), full),
            pltpu.VMEM((count, width), bf),
            pltpu.VMEM((count, width), bf),
            pltpu.VMEM((3, count, width), bf),
            pltpu.VMEM((count, width), full),
            pltpu.VMEM((4, 2, 2, 2, column, width), bf),
            pltpu.VMEM((4, 2, 2, column, width), bf),
            pltpu.VMEM((4, 2, half, width), bf),
            pltpu.VMEM((4, 2, half, width), bf),
            pltpu.VMEM((4, half, width), bf),
            pltpu.VMEM((4, half, width), bf),
            pltpu.VMEM((4, depth, shard, width), bf),
            pltpu.VMEM((4, depth - 1, shard, width), bf),
            pltpu.VMEM((depth, 8, cap, width), bf),
            pltpu.VMEM((depth, count, width), bf),
            pltpu.VMEM((5, count, width), bf),
            pltpu.VMEM((6, 16, width), full),
            pltpu.VMEM((5, 16, width), full),
            pltpu.VMEM((2, 8, 8, 128), full),
            pltpu.SemaphoreType.DMA((copies,)),
            pltpu.SemaphoreType.DMA((copies,)),
            pltpu.SemaphoreType.DMA((16,)),
        ],
        compiler_params=pltpu.CompilerParams(
            collective_id=2, has_side_effects=True, vmem_limit_bytes=62 << 20
        ),
    )(*args)


def adam_kernel(
    up,
    up_first,
    up_second,
    up_grad,
    down,
    down_first,
    down_second,
    down_grad,
    attn,
    attn_first,
    attn_second,
    attn_grad,
    squares,
    up_new,
    up_moment,
    up_square,
    down_new,
    down_moment,
    down_square,
    attn_new,
    attn_moment,
    attn_square,
):
    norm = jnp.sqrt(jnp.sum(squares[...], keepdims=True))
    clip = clip_level / jnp.maximum(norm, clip_level)
    sets = [
        (up, up_first, up_second, up_grad, up_new, up_moment, up_square),
        (down, down_first, down_second, down_grad, down_new, down_moment, down_square),
        (attn, attn_first, attn_second, attn_grad, attn_new, attn_moment, attn_square),
    ]
    for weight, first, second, grad, new, moment, square in sets:
        got = adam_step(
            weight[...].astype(jnp.float32),
            first[...],
            second[...],
            grad[...].astype(jnp.float32),
            clip,
            rate_matrix,
            decay_rate,
        )
        new[...], moment[...], square[...] = got


def adam_all(up, down, attn, squares):
    steps = 16
    full = jnp.float32
    in_specs, out_specs, shapes, aliases = [], [], [], {}
    for group in (up, down, attn):
        rows, width = group[0].shape
        spec = pl.BlockSpec((rows // steps, width), lambda i: (i, 0))
        in_specs += [spec] * 4
        out_specs += [spec] * 3
        shapes += [jax.ShapeDtypeStruct((rows, width), full)] * 3
    return pl.pallas_call(
        adam_kernel,
        grid=(steps,),
        out_shape=shapes,
        in_specs=in_specs + [pl.BlockSpec(squares.shape, lambda i: (0, 0))],
        out_specs=out_specs,
        compiler_params=pltpu.CompilerParams(vmem_limit_bytes=40 << 20),
    )(*up, *down, *attn, squares)


def shards(
    tokens,
    cotangent,
    routes,
    attn_weight,
    attn_first,
    attn_second,
    norm_param,
    norm_first,
    norm_second,
    up_weight,
    up_first,
    up_second,
    down_weight,
    down_first,
    down_second,
    expert_vector,
    vector_first,
    vector_second,
):
    experts_here = lax.axis_size(EX)
    hidden_size = lax.axis_size(HI)
    token_count = tokens.shape[0]
    features = tokens.shape[1]
    capacity = 2 * token_count // experts_here
    slot_rows = experts_here * capacity
    head_dim = features // HEADS
    scaling = head_dim ** (-0.5)
    attn_low = attn_weight.astype(jnp.bfloat16)
    norm_low = norm_param.astype(jnp.bfloat16)
    attn_full, norm_full = (
        lax.all_gather(attn_low, BOTH, axis=1, tiled=True),
        lax.all_gather(norm_low, BOTH, axis=1, tiled=True),
    )
    inputs = tokens.astype(jnp.float32)
    normed, norm_pull = jax.vjp(
        layer_norm, inputs, norm_full[0].astype(jnp.float32), norm_full[1].astype(jnp.float32)
    )
    normed_low = normed.astype(jnp.bfloat16)
    projected = jnp.einsum(
        "td,sde->ste", normed_low, attn_full[:3], preferred_element_type=jnp.float32
    ).astype(jnp.bfloat16)
    query = projected[0].reshape(token_count, HEADS, head_dim)
    keys_all = projected[1].reshape(token_count, HEADS, head_dim)
    values_all = projected[2].reshape(token_count, HEADS, head_dim)
    causal = jnp.arange(token_count)[:, None] >= jnp.arange(token_count)[None, :]

    def score_rows():
        raw = (
            jnp.einsum("qhe,khe->hqk", query, keys_all, preferred_element_type=jnp.float32)
            * scaling
        )
        return jnp.where(causal[None], raw, masked_fill)

    scores = score_rows()
    row_max = jnp.max(scores, axis=-1, keepdims=True)
    expo = jnp.exp(scores - row_max)
    row_total = jnp.sum(expo, axis=-1, keepdims=True)
    log_total = row_max + jnp.log(row_total)
    probs_low = (expo / row_total).astype(jnp.bfloat16)
    context = jnp.einsum("hqk,khe->qhe", probs_low, values_all, preferred_element_type=jnp.float32)
    context = context.reshape(token_count, features).astype(jnp.bfloat16)
    resid = inputs + jnp.dot(context, attn_full[3], preferred_element_type=jnp.float32)
    route = routes[:, 0]
    chosen = (route[:, None] == jnp.arange(experts_here, dtype=jnp.int32)[None, :]).astype(
        jnp.int32
    )
    ranked = jnp.sum((jnp.cumsum(chosen, axis=0) - 1) * chosen, axis=1)
    placed = route * capacity + ranked
    placing = (jnp.arange(slot_rows, dtype=jnp.int32)[:, None] == placed[None, :]).astype(
        jnp.bfloat16
    )
    outgoing = jnp.dot(
        placing, resid.astype(jnp.bfloat16), preferred_element_type=jnp.float32
    ).astype(jnp.bfloat16)
    occupied = jnp.sum(placing.astype(jnp.float32), axis=1).astype(jnp.bfloat16)
    arrived, arrived_mask = (
        lax.all_to_all(
            outgoing.reshape(experts_here, capacity, features),
            EX,
            split_axis=0,
            concat_axis=0,
            tiled=True,
        ),
        lax.all_to_all(
            occupied.reshape(experts_here, capacity),
            EX,
            split_axis=0,
            concat_axis=0,
            tiled=True,
        ),
    )
    gathered, gathered_mask = (
        lax.all_gather(arrived, HI, axis=0, tiled=True),
        lax.all_gather(arrived_mask, HI, axis=0, tiled=True),
    )
    rows_all = gathered.reshape(-1, features)
    mask_all = gathered_mask.reshape(-1).astype(jnp.float32)
    rows_float = rows_all.astype(jnp.float32)
    centroid = expert_vector[0, 0]
    gating = jax.nn.sigmoid(jnp.sum(rows_float * centroid, axis=-1))
    expert_normed, expert_pull = jax.vjp(
        layer_norm, rows_float, expert_vector[0, 1], expert_vector[0, 2]
    )
    expert_low = expert_normed.astype(jnp.bfloat16)
    before = jnp.dot(expert_low, up_weight[0], preferred_element_type=jnp.float32)
    after, gelu_pull = jax.vjp(gelu_exact, before)
    after_low = after.astype(jnp.bfloat16)
    branch_own = lax.psum_scatter(
        jnp.dot(after_low, down_weight[0], preferred_element_type=jnp.float32).astype(jnp.bfloat16),
        HI,
        scatter_dimension=0,
        tiled=True,
    ).astype(jnp.float32)
    own_start = lax.axis_index(HI) * slot_rows
    gating_own = lax.dynamic_slice_in_dim(gating, own_start, slot_rows, 0)
    delta = (gating_own[:, None] * branch_own).astype(jnp.bfloat16)
    returned = lax.all_to_all(
        delta.reshape(experts_here, capacity, features),
        EX,
        split_axis=0,
        concat_axis=0,
        tiled=True,
    )
    delta_tokens = jnp.einsum(
        "st,sd->td",
        placing,
        returned.reshape(slot_rows, features),
        preferred_element_type=jnp.float32,
    )
    block_out = (resid + delta_tokens).astype(jnp.bfloat16)
    routed_count = jnp.sum(mask_all)
    gate_total = jnp.sum(mask_all * gating)
    expert_stats = jnp.stack(
        [routed_count / (token_count * hidden_size), gate_total / routed_count]
    )[:, None]
    cot_slots = jnp.dot(placing, cotangent, preferred_element_type=jnp.float32).astype(jnp.bfloat16)
    cot_arrived = lax.all_to_all(
        cot_slots.reshape(experts_here, capacity, features),
        EX,
        split_axis=0,
        concat_axis=0,
        tiled=True,
    )
    cot_rows = lax.all_gather(cot_arrived, HI, axis=0, tiled=True).reshape(-1, features)
    d_branch = (gating[:, None] * cot_rows.astype(jnp.float32)).astype(jnp.bfloat16)
    grad_down = jnp.einsum("gf,gd->fd", after_low, d_branch, preferred_element_type=jnp.float32)
    d_after = jnp.einsum("gd,fd->gf", d_branch, down_weight[0], preferred_element_type=jnp.float32)
    d_before = gelu_pull(d_after)[0].astype(jnp.bfloat16)
    grad_up = jnp.einsum("gd,gf->df", expert_low, d_before, preferred_element_type=jnp.float32)
    d_expert_normed = jnp.einsum(
        "gf,df->gd", d_before, up_weight[0], preferred_element_type=jnp.float32
    )
    d_rows, d_expert_gain, d_expert_bias = expert_pull(d_expert_normed)
    d_rows_own = lax.psum_scatter(
        d_rows.astype(jnp.bfloat16), HI, scatter_dimension=0, tiled=True
    ).astype(jnp.float32)
    cot_own = lax.dynamic_slice_in_dim(cot_rows, own_start, slot_rows, 0).astype(jnp.float32)
    rows_own = lax.dynamic_slice_in_dim(rows_float, own_start, slot_rows, 0)
    d_gating = jnp.sum(cot_own * branch_own, axis=-1)
    d_logit = d_gating * gating_own * (1.0 - gating_own)
    d_centroid = jnp.sum(d_logit[:, None] * rows_own, axis=0)
    d_sent = (d_rows_own + d_logit[:, None] * centroid).astype(jnp.bfloat16)
    back_slots = lax.all_to_all(
        d_sent.reshape(experts_here, capacity, features),
        EX,
        split_axis=0,
        concat_axis=0,
        tiled=True,
    )
    d_resid = cotangent.astype(jnp.float32) + jnp.einsum(
        "st,sd->td",
        placing,
        back_slots.reshape(slot_rows, features),
        preferred_element_type=jnp.float32,
    )
    vector_grad = lax.psum(jnp.stack([d_centroid, d_expert_gain, d_expert_bias])[None], HI)
    d_project = d_resid.astype(jnp.bfloat16)
    grad_out_proj = jnp.einsum("td,te->de", context, d_project, preferred_element_type=jnp.float32)
    d_context = jnp.einsum(
        "te,de->td", d_project, attn_full[3], preferred_element_type=jnp.float32
    ).astype(jnp.bfloat16)
    d_context = d_context.reshape(token_count, HEADS, head_dim)
    attn_probs = jnp.exp(score_rows() - log_total)
    probs_again = attn_probs.astype(jnp.bfloat16)
    d_probs = jnp.einsum("qhe,khe->hqk", d_context, values_all, preferred_element_type=jnp.float32)
    d_values = jnp.einsum(
        "hqk,qhe->khe", probs_again, d_context, preferred_element_type=jnp.float32
    ).astype(jnp.bfloat16)
    d_scores = (
        attn_probs * (d_probs - jnp.sum(d_probs * attn_probs, axis=-1, keepdims=True))
    ).astype(jnp.bfloat16)
    d_query = (
        jnp.einsum("hqk,khe->qhe", d_scores, keys_all, preferred_element_type=jnp.float32) * scaling
    ).astype(jnp.bfloat16)
    d_keys = (
        jnp.einsum("hqk,qhe->khe", d_scores, query, preferred_element_type=jnp.float32) * scaling
    ).astype(jnp.bfloat16)
    d_projected = jnp.stack(
        [
            d_query.reshape(token_count, features),
            d_keys.reshape(token_count, features),
            d_values.reshape(token_count, features),
        ]
    )
    grad_qkv = jnp.einsum(
        "td,ste->sde", normed_low, d_projected, preferred_element_type=jnp.float32
    )
    d_normed = jnp.einsum(
        "ste,sde->td", d_projected, attn_full[:3], preferred_element_type=jnp.float32
    )
    d_inputs, d_norm_gain, d_norm_bias = norm_pull(d_normed)
    token_grad = (d_resid + d_inputs).astype(jnp.bfloat16)
    grad_attn = jnp.concatenate([grad_qkv, grad_out_proj[None]], axis=0)
    grad_norm_param = jnp.stack([d_norm_gain, d_norm_bias])
    attn_shard, norm_shard = (
        lax.psum_scatter(grad_attn, BOTH, scatter_dimension=1, tiled=True),
        lax.psum_scatter(grad_norm_param, BOTH, scatter_dimension=1, tiled=True),
    )
    local_square = (
        jnp.sum(attn_shard * attn_shard)
        + jnp.sum(norm_shard * norm_shard)
        + jnp.sum(grad_up * grad_up)
        + jnp.sum(grad_down * grad_down)
        + jnp.sum(vector_grad * vector_grad) / hidden_size
    )
    grad_norm = jnp.sqrt(lax.psum(local_square, BOTH))
    clip_factor = clip_level / jnp.maximum(grad_norm, clip_level)
    attn_new = adam_step(
        attn_weight, attn_first, attn_second, attn_shard, clip_factor, rate_matrix, decay_rate
    )
    norm_new = adam_step(
        norm_param, norm_first, norm_second, norm_shard, clip_factor, rate_vector, 0.0
    )
    up_new = adam_step(
        up_weight.astype(jnp.float32),
        up_first,
        up_second,
        grad_up[None],
        clip_factor,
        rate_matrix,
        decay_rate,
    )
    down_new = adam_step(
        down_weight.astype(jnp.float32),
        down_first,
        down_second,
        grad_down[None],
        clip_factor,
        rate_matrix,
        decay_rate,
    )
    vector_new = adam_step(
        expert_vector, vector_first, vector_second, vector_grad, clip_factor, rate_vector, 0.0
    )
    return (
        block_out,
        token_grad,
        grad_norm,
        attn_new[0],
        attn_new[1],
        attn_new[2],
        norm_new[0],
        norm_new[1],
        norm_new[2],
        up_new[0],
        up_new[1],
        up_new[2],
        down_new[0],
        down_new[1],
        down_new[2],
        vector_new[0],
        vector_new[1],
        vector_new[2],
        expert_stats,
    )


def fast_shards(
    tokens,
    cotangent,
    routes,
    attn_weight,
    attn_first,
    attn_second,
    norm_param,
    norm_first,
    norm_second,
    up_weight,
    up_first,
    up_second,
    down_weight,
    down_first,
    down_second,
    expert_vector,
    vector_first,
    vector_second,
):
    experts = lax.axis_size(EX)
    depth = lax.axis_size(HI)
    count, width = tokens.shape
    cap = 2 * count // experts
    shard = attn_weight.shape[1]
    lanes = norm_param.shape[1]
    place = lax.axis_index(EX) * depth + lax.axis_index(HI)
    w_full, qkv, normed, ctx, resid, sent, placed, gains, cot_raw, cot_zero = attend(
        cap, tokens, attn_weight, norm_param, routes, cotangent
    )
    vec = jnp.pad(expert_vector[0], ((0, 5), (0, 0)))
    d_sum, grad_up, grad_down, delta, vec_part, scal = expert_layer(
        cap, sent, placed, cot_raw, cot_zero, up_weight[0], down_weight[0], vec
    )
    block_out, token_grad, attn_shard, norm_grads, vec_grads, squares = attend_back(
        cap,
        shard,
        d_sum,
        cotangent,
        w_full,
        qkv,
        normed,
        ctx,
        tokens,
        gains,
        placed,
        delta,
        resid,
        vec_part,
        scal,
    )
    here = lax.axis_index(EX)
    routed = lax.dynamic_slice(norm_grads, (2, here), (1, 1))[0, 0]
    empty = depth * experts * cap - routed
    gate_total = jnp.sum(scal[0:8, 0]) - 0.5 * empty
    expert_stats = jnp.stack([routed / (count * depth), gate_total / routed])[:, None]
    norm_shard = lax.dynamic_slice(norm_grads, (0, place * lanes), (2, lanes))
    vector_grad = vec_grads[None, 0:3]
    grad_norm = jnp.sqrt(jnp.sum(squares))
    clip_factor = clip_level / jnp.maximum(grad_norm, clip_level)
    flat = lambda v: v.reshape(-1, v.shape[-1])
    new = adam_all(
        [flat(v) for v in (up_weight, up_first, up_second, grad_up)],
        [flat(v) for v in (down_weight, down_first, down_second, grad_down)],
        [flat(v) for v in (attn_weight, attn_first, attn_second, attn_shard)],
        squares,
    )
    up_new = [v.reshape(up_weight.shape) for v in new[0:3]]
    down_new = [v.reshape(down_weight.shape) for v in new[3:6]]
    attn_new = [v.reshape(attn_weight.shape) for v in new[6:9]]
    norm_new = adam_step(
        norm_param, norm_first, norm_second, norm_shard, clip_factor, rate_vector, 0.0
    )
    vector_new = adam_step(
        expert_vector, vector_first, vector_second, vector_grad, clip_factor, rate_vector, 0.0
    )
    return (
        block_out,
        token_grad,
        grad_norm,
        *attn_new,
        *norm_new,
        *up_new,
        *down_new,
        *vector_new,
        expert_stats,
    )


def solution(mesh):
    small = mesh.shape[EX] == 8 and mesh.shape[HI] == 4
    return jax.shard_map(
        fast_shards if small else shards,
        mesh=mesh,
        in_specs=(
            P(BOTH, None),
            P(BOTH, None),
            P(BOTH, None),
            P(None, BOTH, None),
            P(None, BOTH, None),
            P(None, BOTH, None),
            P(None, BOTH),
            P(None, BOTH),
            P(None, BOTH),
            P(EX, None, HI),
            P(EX, None, HI),
            P(EX, None, HI),
            P(EX, HI, None),
            P(EX, HI, None),
            P(EX, HI, None),
            P(EX, None, None),
            P(EX, None, None),
            P(EX, None, None),
        ),
        out_specs=(
            P(BOTH, None),
            P(BOTH, None),
            P(),
            P(None, BOTH, None),
            P(None, BOTH, None),
            P(None, BOTH, None),
            P(None, BOTH),
            P(None, BOTH),
            P(None, BOTH),
            P(EX, None, HI),
            P(EX, None, HI),
            P(EX, None, HI),
            P(EX, HI, None),
            P(EX, HI, None),
            P(EX, HI, None),
            P(EX, None, None),
            P(EX, None, None),
            P(EX, None, None),
            P(None, EX),
        ),
        check_vma=False,
    )
```

```python
import functools
import math

import jax
import jax.numpy as jnp
from jax import lax
from jax.experimental import pallas as pl
from jax.experimental.pallas import tpu as pltpu
from jax.sharding import PartitionSpec as P

HEADS = 16
STEP = 10


norm_eps = 1e-05
clip_level = 1.0
beta_one = 0.9
beta_two = 0.999
adam_eps = 1e-08
decay_rate = 0.1
rate_matrix = 0.05
rate_vector = 0.5
masked_fill = -1e30
EX, HI = "expert", "hidden"
BOTH = (EX, HI)


def layer_norm(inputs, gain_row, bias_row):
    average = jnp.mean(inputs, axis=-1, keepdims=True)
    centred = inputs - average
    variance = jnp.mean(centred * centred, axis=-1, keepdims=True)
    return centred * lax.rsqrt(variance + norm_eps) * gain_row + bias_row


def gelu_exact(values):
    return jax.nn.gelu(values, approximate=False)


def adam_step(weight, first, second, grad, clip_factor, rate, decay):
    clipped = grad * clip_factor
    moment = beta_one * first + (1.0 - beta_one) * clipped
    square = beta_two * second + (1.0 - beta_two) * clipped * clipped
    corr_one = 1.0 - beta_one**STEP
    corr_two = 1.0 - beta_two**STEP
    update = moment / corr_one / (jnp.sqrt(square / corr_two) + adam_eps) + decay * weight
    return (weight - rate * update, moment, square)


MESH = pl.DeviceIdType.MESH
VMEM_SPEC = pl.BlockSpec(memory_space=pltpu.VMEM)
ANY_SPEC = pl.BlockSpec(memory_space=pl.ANY)


class Place:
    def __init__(self):
        self.e = lax.axis_index(EX)
        self.z = lax.axis_index(HI)
        high, low = lax.div(self.z, 2), lax.rem(self.z, 2)
        self.middle = high + low == 1
        self.ends = jnp.logical_not(self.middle)
        self.line = [self.z, self.z + 1 - 2 * low, 2 - high, 3 - 3 * high]
        self.core = lax.rem(self.e, 2)
        self.x = lax.rem(lax.div(self.e, 2), 2)
        self.y = lax.div(self.e, 4)
        self.ex = self.e + 2 - 4 * self.x
        self.ey = self.e + 4 - 8 * self.y
        self.exy = self.ex + 4 - 8 * self.y
        self.twin = (self.e + 1 - 2 * self.core, self.z)
        self.over_x = (self.ex, self.z)
        self.over_y = (self.ey, self.z)
        self.partner = (self.e, self.line[1])
        self.mirror = (self.e, 3 - self.z)
        self.mates = [None, self.partner, (self.e, self.z + 2 - 4 * high), self.mirror]

    def across(self, k):
        c = lax.rem(self.core + k % 2, 2)
        x = lax.rem(self.x + (k // 2) % 2, 2)
        y = lax.rem(self.y + k // 4, 2)
        return 4 * y + 2 * x + c

    def everyone(self):
        plane = [(self.across(k), self.z) for k in range(1, 8)]
        return plane + self.mates[1:]

    def meet(self):
        barrier = pltpu.get_barrier_semaphore()
        for device in self.everyone():
            pl.semaphore_signal(barrier, inc=1, device_id=device, device_id_type=MESH)
        pl.semaphore_wait(barrier, len(self.everyone()))


class Wire:
    def __init__(self, send_sem, recv_sem):
        self.send_sem, self.recv_sem = send_sem, recv_sem
        self.count = 0
        self.tags = {}
        self.sent = []

    def next(self):
        self.count += 1
        return self.count - 1

    def send(self, src, dst, device, tag=None, when=None):
        i = self.next()
        if tag is not None:
            if tag not in self.tags:
                self.tags[tag] = self.next()
            j = self.tags[tag]
        else:
            j = i
        copy = pltpu.make_async_remote_copy(
            src_ref=src,
            dst_ref=dst,
            send_sem=self.send_sem.at[i],
            recv_sem=self.recv_sem.at[j],
            device_id=device,
            device_id_type=MESH,
        )
        if when is None:
            copy.start()
        else:
            pl.when(when)(copy.start)
        self.sent.append((copy, when))
        return copy

    def arrived(self, tag, dst, device):
        if tag not in self.tags:
            self.tags[tag] = self.next()
        j = self.tags[tag]
        pltpu.make_async_remote_copy(
            src_ref=dst,
            dst_ref=dst,
            send_sem=self.send_sem.at[j],
            recv_sem=self.recv_sem.at[j],
            device_id=device,
            device_id_type=MESH,
        ).wait_recv()

    def left(self, copy):
        copy.wait_send()
        self.sent = [one for one in self.sent if one[0] is not copy]

    def drain(self):
        for copy, when in self.sent:
            if when is None:
                copy.wait_send()
            else:
                pl.when(when)(copy.wait_send)
        self.sent = []


class Line:
    def __init__(self, wire, at, name, slot):
        self.wire, self.at, self.name, self.slot = wire, at, name, slot

    def begin(self, own=None, outer=1, inner=True):
        at = self.at
        here = self.slot(at.z)
        own = here if own is None else own
        if outer:
            when = {1: None, 2: at.ends, 3: at.middle}[outer]
            self.wire.send(own, here, at.partner, (self.name, 1), when)
        if inner:
            self.wire.send(own, here, at.mirror, (self.name, 2), at.middle)

    def take(self, i, when=None):
        at = self.at
        block = self.slot(at.line[i])
        if when is None:
            self.wire.arrived((self.name, i), block, at.partner)
        else:
            pl.when(when)(lambda: self.wire.arrived((self.name, i), block, at.partner))
        if when is not at.ends:
            to, tag = (at.mirror, 3) if i == 1 else (at.partner, i)
            self.wire.send(block, block, to, (self.name, tag), at.middle)
        return block


class Fetch:
    def __init__(self, sem):
        self.sem = sem
        self.count = 0
        self.open = []

    def start(self, src, dst):
        copy = pltpu.make_async_copy(src, dst, self.sem.at[self.count])
        self.count += 1
        copy.start()
        self.open.append(copy)
        return copy

    def done(self, copy):
        copy.wait()
        self.open = [one for one in self.open if one is not copy]

    def drain(self):
        for copy in self.open:
            copy.wait()
        self.open = []


def dot(a, b, ca=1, cb=0):
    return lax.dot_general(a, b, (((ca,), (cb,)), ((), ())), preferred_element_type=jnp.float32)


def tile(i, size=256):
    return pl.ds(pl.multiple_of(i * size, size), size)


def pick(placed_row, slots):
    which = lax.broadcasted_iota(jnp.int32, (slots, placed_row.shape[1]), 0)
    return jnp.where(which == placed_row, 1.0, 0.0).astype(jnp.bfloat16)


def build(stage, source, placed_row):
    planes, cap, width = stage.shape
    onehot = pick(placed_row, planes * cap)

    @pl.loop(0, width // 512)
    def _(i):
        cols = tile(i, 512)
        value = dot(onehot, source[:, cols]).astype(jnp.bfloat16)
        for k in range(planes):
            stage[k, :, cols] = value[k * cap : (k + 1) * cap]


def attend_kernel(
    cap,
    tok,
    w_own,
    norm_in,
    route,
    cot,
    w_out,
    qkv_out,
    normed_out,
    ctx_out,
    resid_out,
    sent_out,
    placed_out,
    gains_out,
    cot_raw,
    cot_zero,
    w_low,
    wfull,
    norm_low,
    pieces,
    qkv,
    normed,
    ctx,
    resid,
    sent,
    placed,
    gains,
    stage,
    send_sem,
    recv_sem,
    local_sem,
):
    at = Place()
    e, z = at.e, at.z
    depth = 4
    count, width = tok.shape
    shard = w_own.shape[1]
    wire = Wire(send_sem, recv_sem)
    fetch = Fetch(local_sem)
    groups = [(0, 3), (3, 1)]
    fetch.start(cot, cot_raw.at[z])
    w_low[...] = w_own[...].astype(jnp.bfloat16)
    lanes = norm_in.shape[1]
    offset = lax.broadcasted_iota(jnp.int32, (lanes, 128), 1) - z * lanes
    ours = lax.broadcasted_iota(jnp.int32, (lanes, 128), 0) == offset
    low = norm_in[...].astype(jnp.bfloat16)
    norm_low[...] = jnp.zeros((16, 128), jnp.bfloat16)
    norm_low[0:2, :] = dot(low, jnp.where(ours, 1.0, 0.0).astype(jnp.bfloat16)).astype(
        jnp.bfloat16
    )
    at.meet()

    def block(g, who, zz):
        if g == 2:
            return pieces.at[who, zz]
        first, mats = groups[g]
        start = pl.multiple_of((who * depth + zz) * shard, shard)
        return wfull.at[pl.ds(first, mats), pl.ds(start, shard)]

    def mine(g):
        if g == 2:
            return norm_low
        first, mats = groups[g]
        return w_low.at[pl.ds(first, mats)]

    lines = [Line(wire, at, g, lambda zz, g=g: block(g, e, zz)) for g in range(3)]
    lines[2].begin(mine(2))
    lines[0].begin(mine(0))
    lines[1].begin(mine(1), outer=2, inner=False)
    cots = Line(wire, at, "cot", lambda zz: cot_raw.at[zz])
    cots.begin(cot, outer=2, inner=False)
    own = [fetch.start(mine(g), block(g, e, z)) for g in range(3)]
    to_x, to_y, to_far, to_twin = {}, {}, {}, {}

    def over_x(g, i):
        here = block(g, e, at.line[i])
        to_x[g, i] = wire.send(here, here, at.over_x)
        to_twin[g, i, 0] = wire.send(here, here, at.twin)

    def over_y(g, i):
        here = block(g, e, at.line[i])
        to_y[g, i] = wire.send(here, here, at.over_y)

    def forward(g, i):
        zz = at.line[i]
        if i in (0, 3):
            to_x[g, i].wait_recv()
            block_x = block(g, at.ex, zz)
            to_far[g, i] = wire.send(block_x, block_x, at.over_y)
            to_twin[g, i, 1] = wire.send(block_x, block_x, at.twin)
        else:
            to_y[g, i].wait_recv()
            block_y = block(g, at.ey, zz)
            to_far[g, i] = wire.send(block_y, block_y, at.over_x)
            to_twin[g, i, 1] = wire.send(block_y, block_y, at.twin)

    def side(g, i):
        zz = at.line[i]
        if i in (0, 3):
            to_y[g, i].wait_recv()
            there = block(g, at.ey, zz)
        else:
            to_x[g, i].wait_recv()
            there = block(g, at.ex, zz)
        to_twin[g, i, 2] = wire.send(there, there, at.twin)

    def far(g, i):
        to_far[g, i].wait_recv()
        there = block(g, at.exy, at.line[i])
        to_twin[g, i, 3] = wire.send(there, there, at.twin)

    def finish(g):
        for i in range(depth):
            for k in range(4):
                to_twin[g, i, k].wait_recv()

    def both(step, i):
        step(2, i)
        step(0, i)

    def take(i):
        lines[2].take(i)
        lines[0].take(i)

    for copy in (own[2], own[0]):
        fetch.done(copy)
    both(over_x, 0)
    both(over_y, 0)
    wide_r = lax.broadcasted_iota(jnp.int32, (count, count), 0)
    wide_c = lax.broadcasted_iota(jnp.int32, (count, count), 1)
    route_row = route[...].astype(jnp.float32)
    route_col = jnp.sum(jnp.where(wide_r == wide_c, route_row, 0.0), axis=1, keepdims=True)
    lane = lax.broadcasted_iota(jnp.int32, (count, 128), 1)
    chosen = jnp.where(route_col.astype(jnp.int32) == lane, 1.0, 0.0)
    rows_i = lax.broadcasted_iota(jnp.int32, (count, count), 0)
    cols_i = lax.broadcasted_iota(jnp.int32, (count, count), 1)
    lower = jnp.where(rows_i >= cols_i, 1.0, 0.0)
    running = dot(lower.astype(jnp.bfloat16), chosen.astype(jnp.bfloat16))
    rank = jnp.sum((running - 1.0) * chosen, axis=1, keepdims=True)
    column = route_col * float(cap) + rank
    row = jnp.sum(jnp.where(wide_r == wide_c, column, 0.0), axis=0, keepdims=True)
    row = jnp.concatenate([row, jnp.full((1, 256 - count), -1.0, jnp.float32)], axis=1)
    placed[z] = jnp.broadcast_to(row, (8, 256)).astype(jnp.int32)
    take(1)
    both(over_x, 1)
    both(over_y, 1)
    build(stage, cot, placed[z, 0:1, :count])
    both(forward, 0)
    take(2)
    lines[1].begin(mine(1), outer=3)
    both(forward, 1)
    both(over_y, 2)
    take(3)
    lines[1].take(1, at.middle)
    lines[1].take(2, at.middle)
    both(over_x, 3)
    both(over_x, 2)
    both(over_y, 3)
    both(side, 0)
    both(side, 1)
    both(far, 0)
    both(far, 1)
    lines[1].take(3, at.middle)
    cots.begin(cot, outer=0)
    both(forward, 2)
    both(forward, 3)
    cots.take(1, at.middle)
    places = Line(wire, at, "place", lambda zz: placed.at[zz])
    places.begin()
    fetch.done(own[1])
    for i in range(depth):
        if i:
            lines[1].take(i, at.ends)
        over_x(1, i)
        over_y(1, i)
    both(side, 3)
    both(side, 2)
    both(far, 2)
    both(far, 3)
    finish(2)
    cots.take(2, at.middle)
    gain_rows = jnp.concatenate(
        [
            sum([pieces[who, zz] for zz in range(1, depth)], pieces[who, 0])
            for who in range(8)
        ],
        axis=1,
    )
    tally = jnp.concatenate(
        [
            jnp.broadcast_to(jnp.sum(chosen, axis=0, keepdims=True), (16, 128)),
            jnp.zeros((16, width - 128), jnp.float32),
        ],
        axis=1,
    )
    third_row = lax.broadcasted_iota(jnp.int32, (16, width), 0) == 2
    gains[...] = jnp.where(third_row, tally, gain_rows.astype(jnp.float32)).astype(jnp.bfloat16)
    fetch.start(gains, gains_out)
    gain = gains[0:1, :].astype(jnp.float32)
    bias = gains[1:2, :].astype(jnp.float32)

    @pl.loop(0, count // 64)
    def _(i):
        rows = tile(i, 64)
        piece = tok[rows, :].astype(jnp.float32)
        average = jnp.mean(piece, axis=-1, keepdims=True)
        centred = piece - average
        variance = jnp.mean(centred * centred, axis=-1, keepdims=True)
        normed[rows, :] = (centred * lax.rsqrt(variance + norm_eps) * gain + bias).astype(
            jnp.bfloat16
        )

    fetch.start(normed, normed_out)
    finish(0)
    fetch.start(wfull.at[pl.ds(0, 3)], w_out.at[pl.ds(0, 3)])
    tiles = width // 256

    slots_out = [
        wire.send(stage.at[at.across(k)], cot_zero.at[k], (at.across(k), z)) for k in range(1, 8)
    ]
    fetch.start(stage.at[e], cot_zero.at[0])
    def project(i):
        m = lax.div(i, tiles)
        cols = tile(lax.rem(i, tiles))
        qkv[m, :, cols] = dot(normed[...], wfull[m, :, cols]).astype(jnp.bfloat16)

    pl.loop(0, tiles)(project)
    for i in range(depth):
        forward(1, i)
    places.take(1)
    cots.take(3, at.middle)
    pl.loop(tiles, 3 * tiles)(project)
    fetch.start(qkv, qkv_out)
    for i in range(depth):
        side(1, i)
    places.take(2, at.middle)
    causal = rows_i >= cols_i
    left = lax.broadcasted_iota(jnp.int32, (count, 128), 1) < 64
    scaling = jnp.asarray(64 ** (-0.5), jnp.bfloat16)

    def pair(i):
        cols = tile(i, 128)
        query = qkv[0, :, cols] * scaling
        keys = qkv[1, :, cols]
        values = qkv[2, :, cols]
        halves = []
        for side in range(2):
            mask = left if side == 0 else jnp.logical_not(left)
            scores = dot(jnp.where(mask, query, jnp.zeros_like(query)), keys, 1, 1)
            scores = jnp.where(causal, scores, masked_fill)
            top = jnp.max(scores, axis=-1, keepdims=True)
            expo = jnp.exp(scores - top)
            probs = expo / jnp.sum(expo, axis=-1, keepdims=True)
            halves.append(dot(probs.astype(jnp.bfloat16), values))
        ctx[:, cols] = jnp.where(left, halves[0], halves[1]).astype(jnp.bfloat16)

    pl.loop(0, 6)(pair)
    for i in range(depth):
        far(1, i)
    places.take(2, at.ends)
    places.take(3, at.middle)
    pl.loop(6, width // 128)(pair)
    fetch.start(ctx, ctx_out)
    finish(1)
    fetch.start(wfull.at[pl.ds(3, 1)], w_out.at[pl.ds(3, 1)])

    @pl.loop(0, tiles)
    def _(i):
        cols = tile(i)
        value = tok[:, cols].astype(jnp.float32) + dot(ctx[...], wfull[3, :, cols])
        resid[:, cols] = value
        sent[:, cols] = value.astype(jnp.bfloat16)

    fetch.start(sent, sent_out)
    fetch.start(resid, resid_out)
    places.take(3, at.ends)
    cots.take(2, at.ends)
    cots.take(3, at.ends)
    fetch.start(placed, placed_out)
    for copy in slots_out:
        copy.wait_recv()
    wire.drain()
    fetch.drain()


def attend(cap, tokens, w_own, norm_own, routes, cotangent):
    count, width = tokens.shape
    bf, full = jnp.bfloat16, jnp.float32
    copies = 176
    shapes = [
        ((4, width, width), bf),
        ((3, count, width), bf),
        ((count, width), bf),
        ((count, width), bf),
        ((count, width), full),
        ((count, width), bf),
        ((4, 8, 256), jnp.int32),
        ((16, width), bf),
        ((4, count, width), bf),
        ((8, cap, width), bf),
    ]
    return pl.pallas_call(
        functools.partial(attend_kernel, cap),
        out_shape=[jax.ShapeDtypeStruct(*one) for one in shapes],
        in_specs=[VMEM_SPEC] * 5,
        out_specs=[ANY_SPEC] * len(shapes),
        scratch_shapes=[
            pltpu.VMEM((4, w_own.shape[1], width), bf),
            pltpu.VMEM((4, width, width), bf),
            pltpu.VMEM((16, 128), bf),
            pltpu.VMEM((8, 4, 16, 128), bf),
            pltpu.VMEM((3, count, width), bf),
            pltpu.VMEM((count, width), bf),
            pltpu.VMEM((count, width), bf),
            pltpu.VMEM((count, width), full),
            pltpu.VMEM((count, width), bf),
            pltpu.VMEM((4, 8, 256), jnp.int32),
            pltpu.VMEM((16, width), bf),
            pltpu.VMEM((8, cap, width), bf),
            pltpu.SemaphoreType.DMA((copies,)),
            pltpu.SemaphoreType.DMA((copies,)),
            pltpu.SemaphoreType.DMA((16,)),
        ],
        compiler_params=pltpu.CompilerParams(
            collective_id=0, has_side_effects=True, vmem_limit_bytes=62 << 20
        ),
    )(tokens, w_own, norm_own, routes, cotangent)


def gelu_pair(v):
    cdf = 0.5 + 0.5 * lax.erf(v * (0.5**0.5))
    pdf = jnp.exp(-0.5 * v * v) * ((2.0 * math.pi) ** -0.5)
    return v * cdf, cdf + v * pdf


def fold(v):
    total = v[0:8]
    for i in range(8, v.shape[0], 8):
        total = total + v[i : i + 8]
    return total


def spread(column, lanes):
    return jnp.concatenate([column] * (lanes // 128), axis=1)


def square_lanes(v):
    total = v[:, 0:128] * v[:, 0:128]
    for i in range(128, v.shape[1], 128):
        total = total + v[:, i : i + 128] * v[:, i : i + 128]
    return total


def unslot(placed_row, slots, out):
    planes, cap, width = slots.shape
    onehot = pick(placed_row, planes * cap)

    @pl.loop(0, width // 256)
    def _(j):
        cols = tile(j)
        value = slots[:, :, cols].reshape(planes * cap, 256)
        out[:, cols] = dot(onehot, value, 0, 0).astype(jnp.bfloat16)


class Home:
    def __init__(self, wire, at, name, part, got):
        self.wire, self.at, self.name = wire, at, name
        self.part, self.got = part, got

    def add(self, i, k):
        part = self.part(i)
        part[...] = (part[...].astype(jnp.float32) + self.got[k].astype(jnp.float32)).astype(
            jnp.bfloat16
        )

    def push(self, i):
        here = self.part(i)
        at = self.at
        self.wire.send(here, self.got.at[i - 1], at.partner, (self.name, i), at.ends)

    def pass_on(self, i):
        at, wire, name = self.at, self.wire, self.name

        @pl.when(at.middle)
        def _():
            wire.arrived((name, i), self.got.at[i - 1], at.partner)
            self.add(i, i - 1)

        k = {3: 3, 2: 4}[i]
        wire.send(self.part(i), self.got.at[k], at.mirror, (name, k + 1), at.middle)

    def near(self):
        at, wire, name = self.at, self.wire, self.name

        @pl.when(at.middle)
        def _():
            wire.arrived((name, 4), self.got.at[3], at.mirror)
            self.add(1, 3)

        wire.send(self.part(1), self.got.at[0], at.partner, (name, 1))

    def relay_far(self):
        at, wire, name = self.at, self.wire, self.name
        far = self.got.at[3]
        pl.when(at.middle)(lambda: wire.arrived((name, 4), far, at.mirror))
        wire.send(far, self.got.at[0], at.partner, (name, 1), at.middle)

    def finish(self):
        at, wire, name = self.at, self.wire, self.name

        @pl.when(at.ends)
        def _():
            wire.arrived((name, 1), self.got.at[0], at.partner)
            self.add(0, 0)

        @pl.when(at.middle)
        def _():
            wire.arrived((name, 5), self.got.at[4], at.mirror)
            self.add(0, 4)

    def last(self):
        self.wire.arrived((self.name, 1), self.got.at[0], self.at.partner)

        @pl.when(self.at.middle)
        def _():
            self.wire.arrived((self.name, 5), self.got.at[4], self.at.mirror)
            self.add(0, 4)

    def total(self, cols):
        return self.part(0)[:, cols].astype(jnp.float32) + self.got[0, :, cols].astype(jnp.float32)


def expert_kernel(
    cap,
    sent_in,
    placed_in,
    cot_raw,
    cot_zero,
    up_in,
    down_in,
    vec,
    d_sum,
    g_up,
    g_down,
    delta_out,
    vec_part,
    scal,
    sent,
    placed,
    cot_line,
    up,
    down,
    raw,
    stage,
    rows,
    cots,
    xn,
    act,
    slope,
    delta,
    d_slots,
    back,
    part,
    z_in,
    d_xn,
    gate,
    d_logit,
    g_stage,
    send_sem,
    recv_sem,
    local_sem,
):
    at = Place()
    e, z = at.e, at.z
    depth, planes = 4, 8
    count, width = sent.shape
    slots = planes * cap
    units = up.shape[1]
    wire = Wire(send_sem, recv_sem)
    fetch = Fetch(local_sem)
    in_sent = fetch.start(sent_in, sent)
    in_placed = fetch.start(placed_in, placed)
    in_up = fetch.start(up_in, up)
    in_down = fetch.start(down_in, down)
    in_cot = fetch.start(cot_raw, cot_line)
    in_zero = fetch.start(cot_zero, cots.at[0])
    at.meet()
    fetch.done(in_sent)
    line = Line(wire, at, "row", lambda zz: raw.at[zz])
    line.begin(sent)
    vec_part[...] = jnp.zeros_like(vec_part)
    scal[...] = jnp.zeros_like(scal)
    fetch.done(in_placed)
    centroid = lambda: vec[0:1, :]
    row_copies, cot_copies, ret_copies = {}, {}, {}

    def exchange(i, dst):
        copies = [
            wire.send(stage.at[i, at.across(k)], dst.at[i, k], (at.across(k), z))
            for k in range(1, planes)
        ]
        dst[i, 0] = stage[i, e]
        return copies

    def slot_row(i):
        return placed[at.line[i], 0:1, :count]

    def rows_out(i):
        source = sent if i == 0 else raw.at[at.line[i]]
        build(stage.at[i], source, slot_row(i))
        row_copies[i] = exchange(i, rows)

    def cots_out(i):
        for copy in row_copies[i]:
            wire.left(copy)
        build(stage.at[i], cot_line.at[at.line[i]], slot_row(i))
        cot_copies[i] = exchange(i, cots)

    def forward(i):
        for copy in row_copies[i]:
            copy.wait_recv()
        gain, bias = vec[1:2, :], vec[2:3, :]

        @pl.loop(0, planes)
        def _(k):
            r = rows[i, k].astype(jnp.float32)
            logit = jnp.sum(r * centroid(), axis=-1, keepdims=True)
            g = jax.nn.sigmoid(logit)
            wide = jnp.broadcast_to(g, (cap, 128))
            gate[i, k] = wide
            scal[0:8] += fold(wide)
            average = jnp.mean(r, axis=-1, keepdims=True)
            centred = r - average
            variance = jnp.mean(centred * centred, axis=-1, keepdims=True)
            xn[i, pl.ds(pl.multiple_of(k * cap, 16), cap), :] = (
                centred * lax.rsqrt(variance + norm_eps) * gain + bias
            ).astype(jnp.bfloat16)

        if i == 0:
            fetch.done(in_up)

        @pl.loop(0, units // 256)
        def _(j):
            cols = tile(j)
            value, rate = gelu_pair(dot(xn[i], up[:, cols]))
            act[i, :, cols] = value.astype(jnp.bfloat16)
            slope[i, :, cols] = rate.astype(jnp.bfloat16)

        if i == 0:
            fetch.done(in_down)

        @pl.loop(0, width // 256)
        def _(j):
            cols = tile(j)
            branch = dot(act[i], down[:, cols])
            wide = spread(gate[i].reshape(slots, 128), 256)
            value = (wide * branch).astype(jnp.bfloat16)
            for k in range(planes):
                delta[i, k, :, cols] = value[k * cap : (k + 1) * cap]

        fetch.start(delta.at[i], delta_out.at[i])

    def backward(i):
        for copy in cot_copies[i]:
            copy.wait_recv()
        if i == 0:
            wire.left(cot_copies[1][0])

        @pl.loop(0, planes)
        def _(k):
            c = cots[i, k].astype(jnp.float32)
            g = gate[i, k]
            inner = jnp.sum(c * delta[i, k].astype(jnp.float32), axis=-1, keepdims=True)
            dl = (1.0 - g) * inner
            d_logit[i, k] = dl
            cots[i, k] = (c * spread(g, width)).astype(jnp.bfloat16)
            vec_part[0] += fold(rows[i, k].astype(jnp.float32) * spread(dl, width))

        @pl.loop(0, units // 256)
        def _(j):
            cols = tile(j)
            d_act = dot(cots[i].reshape(slots, width), down[cols, :], 1, 1)
            slope[i, :, cols] = (d_act * slope[i, :, cols].astype(jnp.float32)).astype(
                jnp.bfloat16
            )

        @pl.loop(0, width // 256)
        def _(j):
            cols = tile(j)
            value = dot(slope[i], up[cols, :], 1, 1)
            for k in range(planes):
                d_xn[k, :, cols] = value[k * cap : (k + 1) * cap]

        @pl.loop(0, planes)
        def _(k):
            r = rows[i, k].astype(jnp.float32)
            average = jnp.mean(r, axis=-1, keepdims=True)
            centred = r - average
            variance = jnp.mean(centred * centred, axis=-1, keepdims=True)
            scale = lax.rsqrt(variance + norm_eps)
            hat = centred * scale
            dx = d_xn[k]
            vec_part[1] += fold(dx * hat)
            vec_part[2] += fold(dx)
            dh = dx * vec[1:2, :]
            first = jnp.mean(dh, axis=-1, keepdims=True)
            second = jnp.mean(dh * hat, axis=-1, keepdims=True)
            d_in = scale * (dh - first - hat * second)
            d_slots[i, k] = (d_in + spread(d_logit[i, k], width) * centroid()).astype(jnp.bfloat16)

        ret_copies[i] = [
            wire.send(d_slots.at[i, k], back.at[i, e], (at.across(k), z))
            for k in range(1, planes)
        ]
        back[i, e] = d_slots[i, 0]

    home = Home(wire, at, "home", lambda i: part.at[i], z_in)

    def collect(i):
        for copy in ret_copies[i]:
            copy.wait_recv()
        unslot(slot_row(i), back.at[i], part.at[i])

    def weight_grad(lhs, rhs, index, out):
        @pl.loop(0, lhs.shape[-1] // 256)
        def _(j):
            cols = tile(j)
            left = lhs[:, :, cols].reshape(depth * slots, 256)
            value = dot(left, rhs[...].reshape(depth * slots, rhs.shape[-1]), 0, 0)
            scal[8:16] += fold(square_lanes(value))
            g_stage[index, cols, :] = value.astype(jnp.bfloat16)

        fetch.start(g_stage.at[index], out)

    rows_out(0)
    line.take(1)
    line.take(2, at.middle)
    rows_out(1)
    forward(0)
    line.take(2, at.ends)
    line.take(3, at.middle)
    rows_out(2)
    forward(1)
    line.take(3, at.ends)
    rows_out(3)
    fetch.done(in_zero)
    cot_copies[0] = []
    cot_copies[1] = [wire.send(cots.at[0], cots.at[1], at.partner)]
    fetch.done(in_cot)
    forward(2)
    cots_out(3)
    forward(3)
    cots_out(2)
    backward(3)
    backward(2)
    collect(3)
    home.push(3)
    backward(1)
    collect(2)
    home.push(2)
    home.pass_on(3)
    backward(0)
    collect(1)
    home.pass_on(2)
    home.near()
    weight_grad(act, cots, 0, g_down)
    weight_grad(xn, slope, 1, g_up)
    collect(0)
    home.last()

    @pl.loop(0, width // 256)
    def _(j):
        cols = tile(j)
        d_sum[:, cols] = home.total(cols)

    wire.drain()
    fetch.drain()


def expert_layer(cap, sent, placed, cot_raw, cot_zero, up, down, vec):
    count, width = sent.shape
    units = up.shape[1]
    depth = 4
    bf, full = jnp.bfloat16, jnp.float32
    slots = 8 * cap
    copies = 3 * 7 * depth + 32
    shapes = [
        ((count, width), full),
        ((width, units), bf),
        ((units, width), bf),
        ((depth, 8, cap, width), bf),
        ((3, 8, width), full),
        ((16, 128), full),
    ]
    big = pltpu.VMEM((depth, 8, cap, width), bf)
    return pl.pallas_call(
        functools.partial(expert_kernel, cap),
        out_shape=[jax.ShapeDtypeStruct(*one) for one in shapes],
        in_specs=[ANY_SPEC] * 6 + [VMEM_SPEC],
        out_specs=[VMEM_SPEC, ANY_SPEC, ANY_SPEC, ANY_SPEC, VMEM_SPEC, VMEM_SPEC],
        scratch_shapes=[
            pltpu.VMEM((count, width), bf),
            pltpu.VMEM((depth, 8, 256), jnp.int32),
            pltpu.VMEM((depth, count, width), bf),
            pltpu.VMEM((width, units), bf),
            pltpu.VMEM((units, width), bf),
            pltpu.VMEM((depth, count, width), bf),
            big,
            big,
            big,
            pltpu.VMEM((depth, slots, width), bf),
            pltpu.VMEM((depth, slots, units), bf),
            pltpu.VMEM((depth, slots, units), bf),
            big,
            big,
            big,
            pltpu.VMEM((depth, count, width), bf),
            pltpu.VMEM((5, count, width), bf),
            pltpu.VMEM((8, cap, width), full),
            pltpu.VMEM((depth, 8, cap, 128), full),
            pltpu.VMEM((depth, 8, cap, 128), full),
            pltpu.VMEM((2, max(width, units), max(width, units)), bf),
            pltpu.SemaphoreType.DMA((copies,)),
            pltpu.SemaphoreType.DMA((copies,)),
            pltpu.SemaphoreType.DMA((16,)),
        ],
        compiler_params=pltpu.CompilerParams(
            collective_id=1, has_side_effects=True, vmem_limit_bytes=62 << 20
        ),
    )(sent, placed, cot_raw, cot_zero, up, down, vec)


def reduce_kernel(
    cap,
    d_sum,
    cot,
    w_in,
    qkv_in,
    normed_in,
    ctx,
    tok,
    gains,
    placed,
    delta_in,
    resid,
    vec_part,
    scal,
    block_out,
    token_grad,
    shard_out,
    norm_out,
    vec_out,
    square_out,
    norm_shard,
    wfull,
    qkv,
    normed,
    delta,
    d_resid,
    d_proj,
    d_ctx,
    d_qkv,
    d_norm,
    stage,
    twin_in,
    x_in,
    y_in,
    x_last,
    y_last,
    done,
    z_last,
    back,
    part,
    z_in,
    near_in,
    small,
    small_in,
    square,
    send_sem,
    recv_sem,
    local_sem,
):
    at = Place()
    e, z = at.e, at.z
    depth, planes = 4, 8
    count, width = tok.shape
    shard = shard_out.shape[1]
    column = depth * shard
    half = column // 2
    wire = Wire(send_sem, recv_sem)
    fetch = Fetch(local_sem)
    in_delta = {i: fetch.start(delta_in.at[i], delta.at[i]) for i in (1, 3, 2, 0)}
    in_w = {m: fetch.start(w_in.at[m], wfull.at[m]) for m in (3, 2, 1, 0)}
    in_qkv = fetch.start(qkv_in, qkv)
    in_normed = fetch.start(normed_in, normed)
    at.meet()
    ret = {}
    home = Home(wire, at, "home", lambda i: part.at[i], z_in)

    def give(i):
        if i in in_delta:
            fetch.done(in_delta.pop(i))
        ret[i] = [
            wire.send(delta.at[i, k], back.at[i, e], (at.across(k), z)) for k in range(1, planes)
        ]
        back[i, e] = delta[i, 0]

    def collect(i):
        for copy in ret[i]:
            copy.wait_recv()
        unslot(placed[at.line[i], 0:1, :count], back.at[i], part.at[i])

    def weight_grad(m, left_ref, right):
        @pl.loop(0, planes)
        def _(i):
            cols = pl.ds(pl.multiple_of(i * column, column), column)
            value = dot(left_ref[:, cols], right[...], 0, 0).astype(jnp.bfloat16)
            stage[m, lax.div(i, 4), lax.rem(lax.div(i, 2), 2), lax.rem(i, 2)] = value

    other = 1 - at.core
    first, second, third, fourth, fifth = {}, {}, {}, {}, {}

    def to_core(m):
        first[m] = wire.send(stage.at[m, :, :, other], twin_in.at[m], at.twin)

    def to_plane(m):
        first[m].wait_recv()
        for j in range(2):
            for i in range(2):
                twin_in[m, j, i] = twin_in[m, j, i] + stage[m, j, i, at.core]
        second[m] = (
            wire.send(twin_in.at[m, :, 1 - at.x, pl.ds(0, half)], x_in.at[m], at.over_x),
            wire.send(twin_in.at[m, 1 - at.y, :, pl.ds(half, half)], y_in.at[m], at.over_y),
        )

    def to_last(m):
        second[m][0].wait_recv()
        for j in range(2):
            x_in[m, j] = x_in[m, j] + twin_in[m, j, at.x, 0:half]
        one = wire.send(x_in.at[m, 1 - at.y], x_last.at[m], at.over_y)
        second[m][1].wait_recv()
        for i in range(2):
            y_in[m, i] = y_in[m, i] + twin_in[m, at.y, i, half:]
        two = wire.send(y_in.at[m, 1 - at.x], y_last.at[m], at.over_x)
        third[m] = (one, two)

    def to_owner(m):
        third[m][0].wait_recv()
        pair = (2, shard, width)
        done[m, 0:2] = (x_in[m, at.y] + x_last[m]).reshape(pair)
        third[m][1].wait_recv()
        done[m, 2:4] = (y_in[m, at.x] + y_last[m]).reshape(pair)
        theirs = at.partner[1]
        fourth[m] = (
            wire.send(done.at[m, theirs], z_last.at[m, 0], at.partner),
            wire.send(done.at[m, 3 - theirs], z_last.at[m, 1], at.partner),
        )

    def cross(m):
        fourth[m][1].wait_recv()
        done[m, 3 - z] = done[m, 3 - z] + z_last[m, 1]
        fifth[m] = wire.send(done.at[m, 3 - z], z_last.at[m, 2], at.mirror)

    def own(m):
        fourth[m][0].wait_recv()
        fifth[m].wait_recv()
        total = done[m, z].astype(jnp.float32)
        for k in (0, 2):
            total = total + z_last[m, k].astype(jnp.float32)
        shard_out[m] = total

    fetch.done(in_delta[1])
    near_copy = wire.send(delta.at[1], near_in, at.partner)
    give(3)
    value = cot[...].astype(jnp.float32) + d_sum[...]
    d_resid[...] = value
    d_proj[...] = value.astype(jnp.bfloat16)
    weight_grad(3, ctx, d_proj)
    to_core(3)
    fetch.done(in_w[3])

    @pl.loop(0, width // 256)
    def _(j):
        cols = tile(j)
        d_ctx[:, cols] = dot(d_proj[...], wfull[3, cols, :], 1, 1).astype(jnp.bfloat16)

    to_plane(3)
    fetch.done(in_qkv)
    causal = lax.broadcasted_iota(jnp.int32, (count, count), 0) >= lax.broadcasted_iota(
        jnp.int32, (count, count), 1
    )
    left = lax.broadcasted_iota(jnp.int32, (count, 128), 1) < 64
    scaling = 64 ** (-0.5)

    def pair(i):
        cols = tile(i, 128)
        query = qkv[0, :, cols]
        keys = qkv[1, :, cols]
        values = qkv[2, :, cols]
        d_out = d_ctx[:, cols]
        zero = jnp.zeros_like(query)
        got = []
        for side in range(2):
            mask = left if side == 0 else jnp.logical_not(left)
            q_side = jnp.where(mask, query, zero)
            k_side = jnp.where(mask, keys, zero)
            o_side = jnp.where(mask, d_out, zero)
            scores = dot(q_side, keys, 1, 1) * scaling
            scores = jnp.where(causal, scores, masked_fill)
            top = jnp.max(scores, axis=-1, keepdims=True)
            expo = jnp.exp(scores - top)
            probs = expo / jnp.sum(expo, axis=-1, keepdims=True)
            d_probs = dot(o_side, values, 1, 1)
            inner = jnp.sum(d_probs * probs, axis=-1, keepdims=True)
            d_scores = (probs * (d_probs - inner)).astype(jnp.bfloat16)
            got.append(
                (
                    dot(d_scores, k_side),
                    dot(d_scores, q_side, 0, 0),
                    dot(probs.astype(jnp.bfloat16), o_side, 0, 0),
                )
            )
        d_qkv[0, :, cols] = ((got[0][0] + got[1][0]) * scaling).astype(jnp.bfloat16)
        d_qkv[1, :, cols] = ((got[0][1] + got[1][1]) * scaling).astype(jnp.bfloat16)
        d_qkv[2, :, cols] = (got[0][2] + got[1][2]).astype(jnp.bfloat16)

    pl.loop(0, width // 256)(pair)
    give(2)
    pl.loop(width // 256, width // 128)(pair)
    collect(3)
    home.push(3)
    fetch.done(in_normed)
    weight_grad(2, normed, d_qkv.at[2])
    to_core(2)
    to_last(3)
    weight_grad(1, normed, d_qkv.at[1])
    to_core(1)
    to_plane(2)
    weight_grad(0, normed, d_qkv.at[0])
    to_core(0)
    home.pass_on(3)
    to_owner(3)
    to_plane(1)
    collect(2)
    home.push(2)
    for m in (2, 1, 0):
        fetch.done(in_w[m])

    @pl.loop(0, width // 256)
    def _(j):
        cols = tile(j)
        d_norm[:, cols] = (
            dot(d_qkv[0], wfull[0, cols, :], 1, 1)
            + dot(d_qkv[1], wfull[1, cols, :], 1, 1)
            + dot(d_qkv[2], wfull[2, cols, :], 1, 1)
        )

    gain = gains[0:1, :].astype(jnp.float32)
    d_gain = jnp.zeros((8, width), jnp.float32)
    d_bias = jnp.zeros((8, width), jnp.float32)
    for i in range(0, count, 64):
        piece = tok[i : i + 64, :].astype(jnp.float32)
        average = jnp.mean(piece, axis=-1, keepdims=True)
        centred = piece - average
        variance = jnp.mean(centred * centred, axis=-1, keepdims=True)
        scale = lax.rsqrt(variance + norm_eps)
        hat = centred * scale
        dx = d_norm[i : i + 64, :]
        d_gain = d_gain + fold(dx * hat)
        d_bias = d_bias + fold(dx)
        dh = dx * gain
        mean_one = jnp.mean(dh, axis=-1, keepdims=True)
        mean_two = jnp.mean(dh * hat, axis=-1, keepdims=True)
        d_in = scale * (dh - mean_one - hat * mean_two)
        token_grad[i : i + 64, :] = (d_resid[i : i + 64, :] + d_in).astype(jnp.bfloat16)
    mine = small.at[0]
    mine[...] = jnp.zeros((8, width), jnp.float32)
    mine[2:3, :] = gains[2:3, :].astype(jnp.float32)
    mine[0:1, :] = jnp.sum(d_gain, axis=0, keepdims=True)
    mine[1:2, :] = jnp.sum(d_bias, axis=0, keepdims=True)
    for k in range(3):
        mine[3 + k : 4 + k, :] = jnp.sum(vec_part[k], axis=0, keepdims=True)
    small_copy = wire.send(mine, small.at[1], at.partner)
    to_last(2)
    home.relay_far()
    home.pass_on(2)
    near_copy.wait_recv()
    fetch.done(in_delta.pop(0))

    @pl.loop(0, planes)
    def _(k):
        delta[0, k] = (delta[0, k].astype(jnp.float32) + near_in[k].astype(jnp.float32)).astype(
            jnp.bfloat16
        )

    to_plane(0)
    cross(3)
    small_copy.wait_recv()
    small[2] = small[0] + small[1]
    small_copy = wire.send(small.at[2], small.at[3], at.mirror)
    to_last(1)
    to_owner(2)
    own(3)
    to_last(0)
    cross(2)
    small_copy.wait_recv()
    total = small[2] + small[3]
    vec_out[...] = total
    small_in[e] = total
    spot = small_in.at[e]
    plane_copies = [wire.send(spot, spot, (at.across(k), z)) for k in range(1, planes)]
    give(0)
    to_owner(1)
    own(2)
    to_owner(0)
    cross(1)
    cross(0)
    own(1)
    for copy in plane_copies:
        copy.wait_recv()
    total = small_in[0]
    for k in range(1, planes):
        total = total + small_in[k]
    norm_out[...] = total
    norm_rows = norm_out[0:2, :]
    mine = norm_out[0:2, tile(e, 128)]
    lanes = norm_shard.shape[1]
    value = mine[:, 0:lanes]
    for k in range(1, depth):
        value = jnp.where(z == k, mine[:, k * lanes : (k + 1) * lanes], value)
    norm_shard[...] = value
    lane = lax.broadcasted_iota(jnp.int32, (1, 128), 1)
    routed = jnp.sum(jnp.where(lane == e, norm_out[2:3, 0:128], 0.0), keepdims=True)
    gates = jnp.sum(scal[0:8, 0:1], keepdims=True) - 0.5 * (depth * planes * cap - routed)
    vec_rows = vec_out[3:6, :]
    squares = jnp.sum(norm_rows * norm_rows, axis=0, keepdims=True) / (planes * depth) + jnp.sum(
        vec_rows * vec_rows, axis=0, keepdims=True
    ) / depth
    local = scal[8:16, :]
    for m in (3, 2, 1):
        local = local + fold(square_lanes(shard_out[m]))
    lane_squares = squares[:, 0:128]
    for i in range(128, width, 128):
        lane_squares = lane_squares + squares[:, i : i + 128]
    head = lax.broadcasted_iota(jnp.int32, (8, 128), 0) == 0
    local = local + jnp.where(head, jnp.broadcast_to(lane_squares, (8, 128)), 0.0)
    own(0)
    square[0, e] = local + fold(square_lanes(shard_out[0]))
    spot = square.at[0, e]
    copies = [wire.send(spot, spot, (at.across(k), z)) for k in range(1, planes)]
    collect(0)
    home.finish()

    @pl.loop(0, width // 256)
    def _(j):
        cols = tile(j)
        block_out[:, cols] = (resid[:, cols] + part[0, :, cols].astype(jnp.float32)).astype(
            jnp.bfloat16
        )

    for copy in copies:
        copy.wait_recv()
    total = square[0, 0]
    for k in range(1, planes):
        total = total + square[0, k]
    square[1, z] = total
    spot = square.at[1, z]
    copies = [wire.send(spot, spot, at.mates[k]) for k in range(1, depth)]
    for copy in copies:
        copy.wait_recv()
    total = square[1, 0]
    for d in range(1, depth):
        total = total + square[1, d]
    norm = jnp.sqrt(jnp.sum(total, keepdims=True))
    which = lax.broadcasted_iota(jnp.int32, (8, 128), 0)
    stats = jnp.where(which == 0, routed / (count * depth), gates / routed)
    clip = clip_level / jnp.maximum(norm, clip_level)
    square_out[...] = jnp.where(which < 2, stats, jnp.where(which == 2, norm, clip))
    wire.drain()
    fetch.drain()


def attend_back(cap, shard, *args):
    tokens = args[6]
    count, width = tokens.shape
    depth = 4
    bf, full = jnp.bfloat16, jnp.float32
    column = depth * shard
    half = column // 2
    copies = 7 * depth + 96
    shapes = [
        ((count, width), bf),
        ((count, width), bf),
        ((4, shard, width), full),
        ((8, width), full),
        ((8, width), full),
        ((8, 128), full),
        ((2, width // 32), full),
    ]
    return pl.pallas_call(
        functools.partial(reduce_kernel, cap),
        out_shape=[jax.ShapeDtypeStruct(*one) for one in shapes],
        in_specs=[VMEM_SPEC] * 2
        + [ANY_SPEC] * 3
        + [VMEM_SPEC] * 4
        + [ANY_SPEC]
        + [VMEM_SPEC] * 3,
        out_specs=[VMEM_SPEC] * 7,
        scratch_shapes=[
            pltpu.VMEM((4, width, width), bf),
            pltpu.VMEM((3, count, width), bf),
            pltpu.VMEM((count, width), bf),
            pltpu.VMEM((depth, 8, cap, width), bf),
            pltpu.VMEM((count, width), full),
            pltpu.VMEM((count, width), bf),
            pltpu.VMEM((count, width), bf),
            pltpu.VMEM((3, count, width), bf),
            pltpu.VMEM((count, width), full),
            pltpu.VMEM((4, 2, 2, 2, column, width), bf),
            pltpu.VMEM((4, 2, 2, column, width), bf),
            pltpu.VMEM((4, 2, half, width), bf),
            pltpu.VMEM((4, 2, half, width), bf),
            pltpu.VMEM((4, half, width), bf),
            pltpu.VMEM((4, half, width), bf),
            pltpu.VMEM((4, depth, shard, width), bf),
            pltpu.VMEM((4, depth - 1, shard, width), bf),
            pltpu.VMEM((depth, 8, cap, width), bf),
            pltpu.VMEM((depth, count, width), bf),
            pltpu.VMEM((5, count, width), bf),
            pltpu.VMEM((8, cap, width), bf),
            pltpu.VMEM((4, 8, width), full),
            pltpu.VMEM((8, 8, width), full),
            pltpu.VMEM((2, 8, 8, 128), full),
            pltpu.SemaphoreType.DMA((copies,)),
            pltpu.SemaphoreType.DMA((copies,)),
            pltpu.SemaphoreType.DMA((16,)),
        ],
        compiler_params=pltpu.CompilerParams(
            collective_id=2, has_side_effects=True, vmem_limit_bytes=62 << 20
        ),
    )(*args)


def adam_quick(weight, first, second, grad, clip_factor, rate, decay):
    clipped = grad * clip_factor
    moment = beta_one * first + (1.0 - beta_one) * clipped
    square = beta_two * second + (1.0 - beta_two) * clipped * clipped
    root = jnp.sqrt(square * (1.0 / (1.0 - beta_two**STEP))) + adam_eps
    step = moment * (rate / (1.0 - beta_one**STEP)) / root
    return (weight * (1.0 - rate * decay) - step, moment, square)


def adam_kernel(
    up,
    up_first,
    up_second,
    up_grad,
    down,
    down_first,
    down_second,
    down_grad,
    attn,
    attn_first,
    attn_second,
    attn_grad,
    facts,
    up_new,
    up_moment,
    up_square,
    down_new,
    down_moment,
    down_square,
    attn_new,
    attn_moment,
    attn_square,
):
    clip = facts[3:4, 0:1]
    sets = [
        (up, up_first, up_second, up_grad, up_new, up_moment, up_square),
        (down, down_first, down_second, down_grad, down_new, down_moment, down_square),
        (attn, attn_first, attn_second, attn_grad, attn_new, attn_moment, attn_square),
    ]
    for weight, first, second, grad, new, moment, square in sets:
        got = adam_quick(
            weight[...].astype(jnp.float32),
            first[...],
            second[...],
            grad[...].astype(jnp.float32),
            clip,
            rate_matrix,
            decay_rate,
        )
        new[...], moment[...], square[...] = got


def adam_all(up, down, attn, facts):
    steps = 8
    full = jnp.float32
    in_specs, out_specs, shapes, aliases = [], [], [], {}
    for group in (up, down, attn):
        rows, width = group[0].shape
        spec = pl.BlockSpec((rows // steps, width), lambda i: (i, 0))
        in_specs += [spec] * 4
        out_specs += [spec] * 3
        shapes += [jax.ShapeDtypeStruct((rows, width), full)] * 3
    return pl.pallas_call(
        adam_kernel,
        grid=(steps,),
        out_shape=shapes,
        in_specs=in_specs + [pl.BlockSpec(facts.shape, lambda i: (0, 0))],
        out_specs=out_specs,
        compiler_params=pltpu.CompilerParams(vmem_limit_bytes=60 << 20),
    )(*up, *down, *attn, facts)


def shards(
    tokens,
    cotangent,
    routes,
    attn_weight,
    attn_first,
    attn_second,
    norm_param,
    norm_first,
    norm_second,
    up_weight,
    up_first,
    up_second,
    down_weight,
    down_first,
    down_second,
    expert_vector,
    vector_first,
    vector_second,
):
    experts_here = lax.axis_size(EX)
    hidden_size = lax.axis_size(HI)
    token_count = tokens.shape[0]
    features = tokens.shape[1]
    capacity = 2 * token_count // experts_here
    slot_rows = experts_here * capacity
    head_dim = features // HEADS
    scaling = head_dim ** (-0.5)
    attn_low = attn_weight.astype(jnp.bfloat16)
    norm_low = norm_param.astype(jnp.bfloat16)
    attn_full, norm_full = (
        lax.all_gather(attn_low, BOTH, axis=1, tiled=True),
        lax.all_gather(norm_low, BOTH, axis=1, tiled=True),
    )
    inputs = tokens.astype(jnp.float32)
    normed, norm_pull = jax.vjp(
        layer_norm, inputs, norm_full[0].astype(jnp.float32), norm_full[1].astype(jnp.float32)
    )
    normed_low = normed.astype(jnp.bfloat16)
    projected = jnp.einsum(
        "td,sde->ste", normed_low, attn_full[:3], preferred_element_type=jnp.float32
    ).astype(jnp.bfloat16)
    query = projected[0].reshape(token_count, HEADS, head_dim)
    keys_all = projected[1].reshape(token_count, HEADS, head_dim)
    values_all = projected[2].reshape(token_count, HEADS, head_dim)
    causal = jnp.arange(token_count)[:, None] >= jnp.arange(token_count)[None, :]

    def score_rows():
        raw = (
            jnp.einsum("qhe,khe->hqk", query, keys_all, preferred_element_type=jnp.float32)
            * scaling
        )
        return jnp.where(causal[None], raw, masked_fill)

    scores = score_rows()
    row_max = jnp.max(scores, axis=-1, keepdims=True)
    expo = jnp.exp(scores - row_max)
    row_total = jnp.sum(expo, axis=-1, keepdims=True)
    log_total = row_max + jnp.log(row_total)
    probs_low = (expo / row_total).astype(jnp.bfloat16)
    context = jnp.einsum("hqk,khe->qhe", probs_low, values_all, preferred_element_type=jnp.float32)
    context = context.reshape(token_count, features).astype(jnp.bfloat16)
    resid = inputs + jnp.dot(context, attn_full[3], preferred_element_type=jnp.float32)
    route = routes[:, 0]
    chosen = (route[:, None] == jnp.arange(experts_here, dtype=jnp.int32)[None, :]).astype(
        jnp.int32
    )
    ranked = jnp.sum((jnp.cumsum(chosen, axis=0) - 1) * chosen, axis=1)
    placed = route * capacity + ranked
    placing = (jnp.arange(slot_rows, dtype=jnp.int32)[:, None] == placed[None, :]).astype(
        jnp.bfloat16
    )
    outgoing = jnp.dot(
        placing, resid.astype(jnp.bfloat16), preferred_element_type=jnp.float32
    ).astype(jnp.bfloat16)
    occupied = jnp.sum(placing.astype(jnp.float32), axis=1).astype(jnp.bfloat16)
    arrived, arrived_mask = (
        lax.all_to_all(
            outgoing.reshape(experts_here, capacity, features),
            EX,
            split_axis=0,
            concat_axis=0,
            tiled=True,
        ),
        lax.all_to_all(
            occupied.reshape(experts_here, capacity),
            EX,
            split_axis=0,
            concat_axis=0,
            tiled=True,
        ),
    )
    gathered, gathered_mask = (
        lax.all_gather(arrived, HI, axis=0, tiled=True),
        lax.all_gather(arrived_mask, HI, axis=0, tiled=True),
    )
    rows_all = gathered.reshape(-1, features)
    mask_all = gathered_mask.reshape(-1).astype(jnp.float32)
    rows_float = rows_all.astype(jnp.float32)
    centroid = expert_vector[0, 0]
    gating = jax.nn.sigmoid(jnp.sum(rows_float * centroid, axis=-1))
    expert_normed, expert_pull = jax.vjp(
        layer_norm, rows_float, expert_vector[0, 1], expert_vector[0, 2]
    )
    expert_low = expert_normed.astype(jnp.bfloat16)
    before = jnp.dot(expert_low, up_weight[0], preferred_element_type=jnp.float32)
    after, gelu_pull = jax.vjp(gelu_exact, before)
    after_low = after.astype(jnp.bfloat16)
    branch_own = lax.psum_scatter(
        jnp.dot(after_low, down_weight[0], preferred_element_type=jnp.float32).astype(jnp.bfloat16),
        HI,
        scatter_dimension=0,
        tiled=True,
    ).astype(jnp.float32)
    own_start = lax.axis_index(HI) * slot_rows
    gating_own = lax.dynamic_slice_in_dim(gating, own_start, slot_rows, 0)
    delta = (gating_own[:, None] * branch_own).astype(jnp.bfloat16)
    returned = lax.all_to_all(
        delta.reshape(experts_here, capacity, features),
        EX,
        split_axis=0,
        concat_axis=0,
        tiled=True,
    )
    delta_tokens = jnp.einsum(
        "st,sd->td",
        placing,
        returned.reshape(slot_rows, features),
        preferred_element_type=jnp.float32,
    )
    block_out = (resid + delta_tokens).astype(jnp.bfloat16)
    routed_count = jnp.sum(mask_all)
    gate_total = jnp.sum(mask_all * gating)
    expert_stats = jnp.stack(
        [routed_count / (token_count * hidden_size), gate_total / routed_count]
    )[:, None]
    cot_slots = jnp.dot(placing, cotangent, preferred_element_type=jnp.float32).astype(jnp.bfloat16)
    cot_arrived = lax.all_to_all(
        cot_slots.reshape(experts_here, capacity, features),
        EX,
        split_axis=0,
        concat_axis=0,
        tiled=True,
    )
    cot_rows = lax.all_gather(cot_arrived, HI, axis=0, tiled=True).reshape(-1, features)
    d_branch = (gating[:, None] * cot_rows.astype(jnp.float32)).astype(jnp.bfloat16)
    grad_down = jnp.einsum("gf,gd->fd", after_low, d_branch, preferred_element_type=jnp.float32)
    d_after = jnp.einsum("gd,fd->gf", d_branch, down_weight[0], preferred_element_type=jnp.float32)
    d_before = gelu_pull(d_after)[0].astype(jnp.bfloat16)
    grad_up = jnp.einsum("gd,gf->df", expert_low, d_before, preferred_element_type=jnp.float32)
    d_expert_normed = jnp.einsum(
        "gf,df->gd", d_before, up_weight[0], preferred_element_type=jnp.float32
    )
    d_rows, d_expert_gain, d_expert_bias = expert_pull(d_expert_normed)
    d_rows_own = lax.psum_scatter(
        d_rows.astype(jnp.bfloat16), HI, scatter_dimension=0, tiled=True
    ).astype(jnp.float32)
    cot_own = lax.dynamic_slice_in_dim(cot_rows, own_start, slot_rows, 0).astype(jnp.float32)
    rows_own = lax.dynamic_slice_in_dim(rows_float, own_start, slot_rows, 0)
    d_gating = jnp.sum(cot_own * branch_own, axis=-1)
    d_logit = d_gating * gating_own * (1.0 - gating_own)
    d_centroid = jnp.sum(d_logit[:, None] * rows_own, axis=0)
    d_sent = (d_rows_own + d_logit[:, None] * centroid).astype(jnp.bfloat16)
    back_slots = lax.all_to_all(
        d_sent.reshape(experts_here, capacity, features),
        EX,
        split_axis=0,
        concat_axis=0,
        tiled=True,
    )
    d_resid = cotangent.astype(jnp.float32) + jnp.einsum(
        "st,sd->td",
        placing,
        back_slots.reshape(slot_rows, features),
        preferred_element_type=jnp.float32,
    )
    vector_grad = lax.psum(jnp.stack([d_centroid, d_expert_gain, d_expert_bias])[None], HI)
    d_project = d_resid.astype(jnp.bfloat16)
    grad_out_proj = jnp.einsum("td,te->de", context, d_project, preferred_element_type=jnp.float32)
    d_context = jnp.einsum(
        "te,de->td", d_project, attn_full[3], preferred_element_type=jnp.float32
    ).astype(jnp.bfloat16)
    d_context = d_context.reshape(token_count, HEADS, head_dim)
    attn_probs = jnp.exp(score_rows() - log_total)
    probs_again = attn_probs.astype(jnp.bfloat16)
    d_probs = jnp.einsum("qhe,khe->hqk", d_context, values_all, preferred_element_type=jnp.float32)
    d_values = jnp.einsum(
        "hqk,qhe->khe", probs_again, d_context, preferred_element_type=jnp.float32
    ).astype(jnp.bfloat16)
    d_scores = (
        attn_probs * (d_probs - jnp.sum(d_probs * attn_probs, axis=-1, keepdims=True))
    ).astype(jnp.bfloat16)
    d_query = (
        jnp.einsum("hqk,khe->qhe", d_scores, keys_all, preferred_element_type=jnp.float32) * scaling
    ).astype(jnp.bfloat16)
    d_keys = (
        jnp.einsum("hqk,qhe->khe", d_scores, query, preferred_element_type=jnp.float32) * scaling
    ).astype(jnp.bfloat16)
    d_projected = jnp.stack(
        [
            d_query.reshape(token_count, features),
            d_keys.reshape(token_count, features),
            d_values.reshape(token_count, features),
        ]
    )
    grad_qkv = jnp.einsum(
        "td,ste->sde", normed_low, d_projected, preferred_element_type=jnp.float32
    )
    d_normed = jnp.einsum(
        "ste,sde->td", d_projected, attn_full[:3], preferred_element_type=jnp.float32
    )
    d_inputs, d_norm_gain, d_norm_bias = norm_pull(d_normed)
    token_grad = (d_resid + d_inputs).astype(jnp.bfloat16)
    grad_attn = jnp.concatenate([grad_qkv, grad_out_proj[None]], axis=0)
    grad_norm_param = jnp.stack([d_norm_gain, d_norm_bias])
    attn_shard, norm_shard = (
        lax.psum_scatter(grad_attn, BOTH, scatter_dimension=1, tiled=True),
        lax.psum_scatter(grad_norm_param, BOTH, scatter_dimension=1, tiled=True),
    )
    local_square = (
        jnp.sum(attn_shard * attn_shard)
        + jnp.sum(norm_shard * norm_shard)
        + jnp.sum(grad_up * grad_up)
        + jnp.sum(grad_down * grad_down)
        + jnp.sum(vector_grad * vector_grad) / hidden_size
    )
    grad_norm = jnp.sqrt(lax.psum(local_square, BOTH))
    clip_factor = clip_level / jnp.maximum(grad_norm, clip_level)
    attn_new = adam_step(
        attn_weight, attn_first, attn_second, attn_shard, clip_factor, rate_matrix, decay_rate
    )
    norm_new = adam_step(
        norm_param, norm_first, norm_second, norm_shard, clip_factor, rate_vector, 0.0
    )
    up_new = adam_step(
        up_weight.astype(jnp.float32),
        up_first,
        up_second,
        grad_up[None],
        clip_factor,
        rate_matrix,
        decay_rate,
    )
    down_new = adam_step(
        down_weight.astype(jnp.float32),
        down_first,
        down_second,
        grad_down[None],
        clip_factor,
        rate_matrix,
        decay_rate,
    )
    vector_new = adam_step(
        expert_vector, vector_first, vector_second, vector_grad, clip_factor, rate_vector, 0.0
    )
    return (
        block_out,
        token_grad,
        grad_norm,
        attn_new[0],
        attn_new[1],
        attn_new[2],
        norm_new[0],
        norm_new[1],
        norm_new[2],
        up_new[0],
        up_new[1],
        up_new[2],
        down_new[0],
        down_new[1],
        down_new[2],
        vector_new[0],
        vector_new[1],
        vector_new[2],
        expert_stats,
    )


def fast_shards(
    tokens,
    cotangent,
    routes,
    attn_weight,
    attn_first,
    attn_second,
    norm_param,
    norm_first,
    norm_second,
    up_weight,
    up_first,
    up_second,
    down_weight,
    down_first,
    down_second,
    expert_vector,
    vector_first,
    vector_second,
):
    experts = lax.axis_size(EX)
    count, width = tokens.shape
    cap = 2 * count // experts
    shard = attn_weight.shape[1]
    w_full, qkv, normed, ctx, resid, sent, placed, gains, cot_raw, cot_zero = attend(
        cap, tokens, attn_weight, norm_param, routes.reshape(1, count), cotangent
    )
    vec = jnp.pad(expert_vector[0], ((0, 5), (0, 0)))
    d_sum, grad_up, grad_down, delta, vec_part, scal = expert_layer(
        cap, sent, placed, cot_raw, cot_zero, up_weight[0], down_weight[0], vec
    )
    block_out, token_grad, attn_shard, norm_grads, vec_grads, facts, norm_shard = attend_back(
        cap,
        shard,
        d_sum,
        cotangent,
        w_full,
        qkv,
        normed,
        ctx,
        tokens,
        gains,
        placed,
        delta,
        resid,
        vec_part,
        scal,
    )
    expert_stats = facts[0:2, 0:1]
    grad_norm = facts[2, 0]
    clip_factor = facts[3, 0]
    vector_grad = vec_grads[None, 3:6]
    flat = lambda v: v.reshape(-1, v.shape[-1])
    new = adam_all(
        [flat(v) for v in (up_weight, up_first, up_second, grad_up)],
        [flat(v) for v in (down_weight, down_first, down_second, grad_down)],
        [flat(v) for v in (attn_weight, attn_first, attn_second, attn_shard)],
        facts,
    )
    up_new = [v.reshape(up_weight.shape) for v in new[0:3]]
    down_new = [v.reshape(down_weight.shape) for v in new[3:6]]
    attn_new = [v.reshape(attn_weight.shape) for v in new[6:9]]
    norm_new = adam_step(
        norm_param, norm_first, norm_second, norm_shard, clip_factor, rate_vector, 0.0
    )
    vector_new = adam_step(
        expert_vector, vector_first, vector_second, vector_grad, clip_factor, rate_vector, 0.0
    )
    return (
        block_out,
        token_grad,
        grad_norm,
        *attn_new,
        *norm_new,
        *up_new,
        *down_new,
        *vector_new,
        expert_stats,
    )


def solution(mesh):
    small = mesh.shape[EX] == 8 and mesh.shape[HI] == 4
    return jax.shard_map(
        fast_shards if small else shards,
        mesh=mesh,
        in_specs=(
            P(BOTH, None),
            P(BOTH, None),
            P(BOTH, None),
            P(None, BOTH, None),
            P(None, BOTH, None),
            P(None, BOTH, None),
            P(None, BOTH),
            P(None, BOTH),
            P(None, BOTH),
            P(EX, None, HI),
            P(EX, None, HI),
            P(EX, None, HI),
            P(EX, HI, None),
            P(EX, HI, None),
            P(EX, HI, None),
            P(EX, None, None),
            P(EX, None, None),
            P(EX, None, None),
        ),
        out_specs=(
            P(BOTH, None),
            P(BOTH, None),
            P(),
            P(None, BOTH, None),
            P(None, BOTH, None),
            P(None, BOTH, None),
            P(None, BOTH),
            P(None, BOTH),
            P(None, BOTH),
            P(EX, None, HI),
            P(EX, None, HI),
            P(EX, None, HI),
            P(EX, HI, None),
            P(EX, HI, None),
            P(EX, HI, None),
            P(EX, None, None),
            P(EX, None, None),
            P(EX, None, None),
            P(None, EX),
        ),
        check_vma=False,
    )
```

```python
import functools
import math

import jax
import jax.numpy as jnp
from jax import lax
from jax.experimental import pallas as pl
from jax.experimental.pallas import tpu as pltpu
from jax.sharding import PartitionSpec as P

HEADS = 16
STEP = 10


norm_eps = 1e-05
clip_level = 1.0
beta_one = 0.9
beta_two = 0.999
adam_eps = 1e-08
decay_rate = 0.1
rate_matrix = 0.05
rate_vector = 0.5
masked_fill = -1e30
EX, HI = "expert", "hidden"
BOTH = (EX, HI)


def layer_norm(inputs, gain_row, bias_row):
    average = jnp.mean(inputs, axis=-1, keepdims=True)
    centred = inputs - average
    variance = jnp.mean(centred * centred, axis=-1, keepdims=True)
    return centred * lax.rsqrt(variance + norm_eps) * gain_row + bias_row


def gelu_exact(values):
    return jax.nn.gelu(values, approximate=False)


def adam_step(weight, first, second, grad, clip_factor, rate, decay):
    clipped = grad * clip_factor
    moment = beta_one * first + (1.0 - beta_one) * clipped
    square = beta_two * second + (1.0 - beta_two) * clipped * clipped
    corr_one = 1.0 - beta_one**STEP
    corr_two = 1.0 - beta_two**STEP
    update = moment / corr_one / (jnp.sqrt(square / corr_two) + adam_eps) + decay * weight
    return (weight - rate * update, moment, square)


MESH = pl.DeviceIdType.MESH
VMEM_SPEC = pl.BlockSpec(memory_space=pltpu.VMEM)
ANY_SPEC = pl.BlockSpec(memory_space=pl.ANY)


class Place:
    def __init__(self):
        self.e = lax.axis_index(EX)
        self.z = lax.axis_index(HI)
        high, low = lax.div(self.z, 2), lax.rem(self.z, 2)
        self.middle = high + low == 1
        self.ends = jnp.logical_not(self.middle)
        self.line = [self.z, self.z + 1 - 2 * low, 2 - high, 3 - 3 * high]
        self.core = lax.rem(self.e, 2)
        self.x = lax.rem(lax.div(self.e, 2), 2)
        self.y = lax.div(self.e, 4)
        self.ex = self.e + 2 - 4 * self.x
        self.ey = self.e + 4 - 8 * self.y
        self.exy = self.ex + 4 - 8 * self.y
        self.twin = (self.e + 1 - 2 * self.core, self.z)
        self.over_x = (self.ex, self.z)
        self.over_y = (self.ey, self.z)
        self.partner = (self.e, self.line[1])
        self.mirror = (self.e, 3 - self.z)
        self.mates = [None, self.partner, (self.e, self.z + 2 - 4 * high), self.mirror]

    def across(self, k):
        c = lax.rem(self.core + k % 2, 2)
        x = lax.rem(self.x + (k // 2) % 2, 2)
        y = lax.rem(self.y + k // 4, 2)
        return 4 * y + 2 * x + c

    def everyone(self):
        plane = [(self.across(k), self.z) for k in range(1, 8)]
        return plane + self.mates[1:]

    def meet(self):
        barrier = pltpu.get_barrier_semaphore()
        for device in self.everyone():
            pl.semaphore_signal(barrier, inc=1, device_id=device, device_id_type=MESH)
        pl.semaphore_wait(barrier, len(self.everyone()))


class Wire:
    def __init__(self, send_sem, recv_sem):
        self.send_sem, self.recv_sem = send_sem, recv_sem
        self.count = 0
        self.tags = {}
        self.sent = []

    def next(self):
        self.count += 1
        return self.count - 1

    def send(self, src, dst, device, tag=None, when=None):
        i = self.next()
        if tag is not None:
            if tag not in self.tags:
                self.tags[tag] = self.next()
            j = self.tags[tag]
        else:
            j = i
        copy = pltpu.make_async_remote_copy(
            src_ref=src,
            dst_ref=dst,
            send_sem=self.send_sem.at[i],
            recv_sem=self.recv_sem.at[j],
            device_id=device,
            device_id_type=MESH,
        )
        if when is None:
            copy.start()
        else:
            pl.when(when)(copy.start)
        self.sent.append((copy, when))
        return copy

    def arrived(self, tag, dst, device):
        if tag not in self.tags:
            self.tags[tag] = self.next()
        j = self.tags[tag]
        pltpu.make_async_remote_copy(
            src_ref=dst,
            dst_ref=dst,
            send_sem=self.send_sem.at[j],
            recv_sem=self.recv_sem.at[j],
            device_id=device,
            device_id_type=MESH,
        ).wait_recv()

    def left(self, copy):
        copy.wait_send()
        self.sent = [one for one in self.sent if one[0] is not copy]

    def drain(self):
        for copy, when in self.sent:
            if when is None:
                copy.wait_send()
            else:
                pl.when(when)(copy.wait_send)
        self.sent = []


class Line:
    def __init__(self, wire, at, name, slot):
        self.wire, self.at, self.name, self.slot = wire, at, name, slot

    def begin(self, own=None, outer=1, inner=True):
        at = self.at
        here = self.slot(at.z)
        own = here if own is None else own
        if outer:
            when = {1: None, 2: at.ends, 3: at.middle}[outer]
            self.wire.send(own, here, at.partner, (self.name, 1), when)
        if inner:
            self.wire.send(own, here, at.mirror, (self.name, 2), at.middle)

    def take(self, i, when=None):
        at = self.at
        block = self.slot(at.line[i])
        if when is None:
            self.wire.arrived((self.name, i), block, at.partner)
        else:
            pl.when(when)(lambda: self.wire.arrived((self.name, i), block, at.partner))
        if when is not at.ends:
            to, tag = (at.mirror, 3) if i == 1 else (at.partner, i)
            self.wire.send(block, block, to, (self.name, tag), at.middle)
        return block


class Fetch:
    def __init__(self, sem):
        self.sem = sem
        self.count = 0
        self.open = []

    def start(self, src, dst):
        copy = pltpu.make_async_copy(src, dst, self.sem.at[self.count])
        self.count += 1
        copy.start()
        self.open.append(copy)
        return copy

    def done(self, copy):
        copy.wait()
        self.open = [one for one in self.open if one is not copy]

    def drain(self):
        for copy in self.open:
            copy.wait()
        self.open = []


def dot(a, b, ca=1, cb=0):
    return lax.dot_general(a, b, (((ca,), (cb,)), ((), ())), preferred_element_type=jnp.float32)


def tile(i, size=256):
    return pl.ds(pl.multiple_of(i * size, size), size)


def pick(placed_row, slots):
    which = lax.broadcasted_iota(jnp.int32, (slots, placed_row.shape[1]), 0)
    return jnp.where(which == placed_row, 1.0, 0.0).astype(jnp.bfloat16)


def build(stage, source, placed_row):
    planes, cap, width = stage.shape
    onehot = pick(placed_row, planes * cap)

    @pl.loop(0, width // 512)
    def _(i):
        cols = tile(i, 512)
        value = dot(onehot, source[:, cols]).astype(jnp.bfloat16)
        for k in range(planes):
            stage[k, :, cols] = value[k * cap : (k + 1) * cap]


def attend_kernel(
    cap,
    tok,
    w_own,
    norm_in,
    route,
    cot,
    w_out,
    qkv_out,
    normed_out,
    ctx_out,
    resid_out,
    sent_out,
    placed_out,
    gains_out,
    cot_raw,
    cot_zero,
    w_low,
    wfull,
    norm_low,
    pieces,
    qkv,
    normed,
    ctx,
    resid,
    sent,
    placed,
    gains,
    stage,
    send_sem,
    recv_sem,
    local_sem,
):
    at = Place()
    e, z = at.e, at.z
    depth = 4
    count, width = tok.shape
    shard = w_own.shape[1]
    wire = Wire(send_sem, recv_sem)
    fetch = Fetch(local_sem)
    groups = [(0, 3), (3, 1)]
    fetch.start(cot, cot_raw.at[z])
    w_low[...] = w_own[...].astype(jnp.bfloat16)
    lanes = norm_in.shape[1]
    offset = lax.broadcasted_iota(jnp.int32, (lanes, 128), 1) - z * lanes
    ours = lax.broadcasted_iota(jnp.int32, (lanes, 128), 0) == offset
    low = norm_in[...].astype(jnp.bfloat16)
    norm_low[...] = jnp.zeros((16, 128), jnp.bfloat16)
    norm_low[0:2, :] = dot(low, jnp.where(ours, 1.0, 0.0).astype(jnp.bfloat16)).astype(
        jnp.bfloat16
    )
    at.meet()

    def block(g, who, zz):
        if g == 2:
            return pieces.at[who, zz]
        first, mats = groups[g]
        start = pl.multiple_of((who * depth + zz) * shard, shard)
        return wfull.at[pl.ds(first, mats), pl.ds(start, shard)]

    def mine(g):
        if g == 2:
            return norm_low
        first, mats = groups[g]
        return w_low.at[pl.ds(first, mats)]

    lines = [Line(wire, at, g, lambda zz, g=g: block(g, e, zz)) for g in range(3)]
    lines[2].begin(mine(2))
    lines[0].begin(mine(0))
    lines[1].begin(mine(1), outer=2, inner=False)
    cots = Line(wire, at, "cot", lambda zz: cot_raw.at[zz])
    cots.begin(cot, outer=2, inner=False)
    own = [fetch.start(mine(g), block(g, e, z)) for g in range(3)]
    to_x, to_y, to_far, to_twin = {}, {}, {}, {}

    def over_x(g, i):
        here = block(g, e, at.line[i])
        to_x[g, i] = wire.send(here, here, at.over_x)
        to_twin[g, i, 0] = wire.send(here, here, at.twin)

    def over_y(g, i):
        here = block(g, e, at.line[i])
        to_y[g, i] = wire.send(here, here, at.over_y)

    def forward(g, i):
        zz = at.line[i]
        if i in (0, 3):
            to_x[g, i].wait_recv()
            block_x = block(g, at.ex, zz)
            to_far[g, i] = wire.send(block_x, block_x, at.over_y)
            to_twin[g, i, 1] = wire.send(block_x, block_x, at.twin)
        else:
            to_y[g, i].wait_recv()
            block_y = block(g, at.ey, zz)
            to_far[g, i] = wire.send(block_y, block_y, at.over_x)
            to_twin[g, i, 1] = wire.send(block_y, block_y, at.twin)

    def side(g, i):
        zz = at.line[i]
        if i in (0, 3):
            to_y[g, i].wait_recv()
            there = block(g, at.ey, zz)
        else:
            to_x[g, i].wait_recv()
            there = block(g, at.ex, zz)
        to_twin[g, i, 2] = wire.send(there, there, at.twin)

    def far(g, i):
        to_far[g, i].wait_recv()
        there = block(g, at.exy, at.line[i])
        to_twin[g, i, 3] = wire.send(there, there, at.twin)

    def finish(g):
        for i in range(depth):
            for k in range(4):
                to_twin[g, i, k].wait_recv()

    def both(step, i):
        step(2, i)
        step(0, i)

    def take(i):
        lines[2].take(i)
        lines[0].take(i)

    for copy in (own[2], own[0]):
        fetch.done(copy)
    both(over_x, 0)
    both(over_y, 0)
    wide_r = lax.broadcasted_iota(jnp.int32, (count, count), 0)
    wide_c = lax.broadcasted_iota(jnp.int32, (count, count), 1)
    route_row = route[...].astype(jnp.float32)
    route_col = jnp.sum(jnp.where(wide_r == wide_c, route_row, 0.0), axis=1, keepdims=True)
    lane = lax.broadcasted_iota(jnp.int32, (count, 128), 1)
    chosen = jnp.where(route_col.astype(jnp.int32) == lane, 1.0, 0.0)
    rows_i = lax.broadcasted_iota(jnp.int32, (count, count), 0)
    cols_i = lax.broadcasted_iota(jnp.int32, (count, count), 1)
    lower = jnp.where(rows_i >= cols_i, 1.0, 0.0)
    running = dot(lower.astype(jnp.bfloat16), chosen.astype(jnp.bfloat16))
    rank = jnp.sum((running - 1.0) * chosen, axis=1, keepdims=True)
    column = route_col * float(cap) + rank
    row = jnp.sum(jnp.where(wide_r == wide_c, column, 0.0), axis=0, keepdims=True)
    row = jnp.concatenate([row, jnp.full((1, 256 - count), -1.0, jnp.float32)], axis=1)
    placed[z] = jnp.broadcast_to(row, (8, 256)).astype(jnp.int32)
    take(1)
    both(over_x, 1)
    both(over_y, 1)
    build(stage, cot, placed[z, 0:1, :count])
    both(forward, 0)
    take(2)
    lines[1].begin(mine(1), outer=3)
    both(forward, 1)
    both(over_y, 2)
    take(3)
    lines[1].take(1, at.middle)
    lines[1].take(2, at.middle)
    both(over_x, 3)
    both(over_x, 2)
    both(over_y, 3)
    both(side, 0)
    both(side, 1)
    both(far, 0)
    both(far, 1)
    lines[1].take(3, at.middle)
    cots.begin(cot, outer=0)
    both(forward, 2)
    both(forward, 3)
    cots.take(1, at.middle)
    places = Line(wire, at, "place", lambda zz: placed.at[zz])
    places.begin()
    fetch.done(own[1])
    for i in range(depth):
        if i:
            lines[1].take(i, at.ends)
        over_x(1, i)
        over_y(1, i)
    both(side, 3)
    both(side, 2)
    both(far, 2)
    both(far, 3)
    finish(2)
    cots.take(2, at.middle)
    gain_rows = jnp.concatenate(
        [
            sum([pieces[who, zz] for zz in range(1, depth)], pieces[who, 0])
            for who in range(8)
        ],
        axis=1,
    )
    tally = jnp.concatenate(
        [
            jnp.broadcast_to(jnp.sum(chosen, axis=0, keepdims=True), (16, 128)),
            jnp.zeros((16, width - 128), jnp.float32),
        ],
        axis=1,
    )
    third_row = lax.broadcasted_iota(jnp.int32, (16, width), 0) == 2
    gains[...] = jnp.where(third_row, tally, gain_rows.astype(jnp.float32)).astype(jnp.bfloat16)
    fetch.start(gains, gains_out)
    gain = gains[0:1, :].astype(jnp.float32)
    bias = gains[1:2, :].astype(jnp.float32)

    @pl.loop(0, count // 64)
    def _(i):
        rows = tile(i, 64)
        piece = tok[rows, :].astype(jnp.float32)
        average = jnp.mean(piece, axis=-1, keepdims=True)
        centred = piece - average
        variance = jnp.mean(centred * centred, axis=-1, keepdims=True)
        normed[rows, :] = (centred * lax.rsqrt(variance + norm_eps) * gain + bias).astype(
            jnp.bfloat16
        )

    fetch.start(normed, normed_out)
    finish(0)
    fetch.start(wfull.at[pl.ds(0, 3)], w_out.at[pl.ds(0, 3)])
    tiles = width // 256

    slots_out = [
        wire.send(stage.at[at.across(k)], cot_zero.at[k], (at.across(k), z)) for k in range(1, 8)
    ]
    fetch.start(stage.at[e], cot_zero.at[0])
    def project(i):
        m = lax.div(i, tiles)
        cols = tile(lax.rem(i, tiles))
        qkv[m, :, cols] = dot(normed[...], wfull[m, :, cols]).astype(jnp.bfloat16)

    pl.loop(0, tiles)(project)
    for i in range(depth):
        forward(1, i)
    places.take(1)
    cots.take(3, at.middle)
    pl.loop(tiles, 3 * tiles)(project)
    fetch.start(qkv, qkv_out)
    for i in range(depth):
        side(1, i)
    places.take(2, at.middle)
    causal = rows_i >= cols_i
    left = lax.broadcasted_iota(jnp.int32, (count, 128), 1) < 64
    scaling = jnp.asarray(64 ** (-0.5), jnp.bfloat16)

    def pair(i):
        cols = tile(i, 128)
        query = qkv[0, :, cols] * scaling
        keys = qkv[1, :, cols]
        values = qkv[2, :, cols]
        halves = []
        for side in range(2):
            mask = left if side == 0 else jnp.logical_not(left)
            scores = dot(jnp.where(mask, query, jnp.zeros_like(query)), keys, 1, 1)
            scores = jnp.where(causal, scores, masked_fill)
            top = jnp.max(scores, axis=-1, keepdims=True)
            expo = jnp.exp(scores - top)
            probs = expo / jnp.sum(expo, axis=-1, keepdims=True)
            halves.append(dot(probs.astype(jnp.bfloat16), values))
        ctx[:, cols] = jnp.where(left, halves[0], halves[1]).astype(jnp.bfloat16)

    pl.loop(0, 6, unroll=2)(pair)
    for i in range(depth):
        far(1, i)
    places.take(2, at.ends)
    places.take(3, at.middle)
    pl.loop(6, width // 128, unroll=2)(pair)
    fetch.start(ctx, ctx_out)
    finish(1)
    fetch.start(wfull.at[pl.ds(3, 1)], w_out.at[pl.ds(3, 1)])

    @pl.loop(0, tiles)
    def _(i):
        cols = tile(i)
        value = tok[:, cols].astype(jnp.float32) + dot(ctx[...], wfull[3, :, cols])
        resid[:, cols] = value
        sent[:, cols] = value.astype(jnp.bfloat16)

    fetch.start(sent, sent_out)
    fetch.start(resid, resid_out)
    places.take(3, at.ends)
    cots.take(2, at.ends)
    cots.take(3, at.ends)
    fetch.start(placed, placed_out)
    for copy in slots_out:
        copy.wait_recv()
    wire.drain()
    fetch.drain()


def attend(cap, tokens, w_own, norm_own, routes, cotangent):
    count, width = tokens.shape
    bf, full = jnp.bfloat16, jnp.float32
    copies = 176
    shapes = [
        ((4, width, width), bf),
        ((3, count, width), bf),
        ((count, width), bf),
        ((count, width), bf),
        ((count, width), full),
        ((count, width), bf),
        ((4, 8, 256), jnp.int32),
        ((16, width), bf),
        ((4, count, width), bf),
        ((8, cap, width), bf),
    ]
    return pl.pallas_call(
        functools.partial(attend_kernel, cap),
        out_shape=[jax.ShapeDtypeStruct(*one) for one in shapes],
        in_specs=[VMEM_SPEC] * 5,
        out_specs=[ANY_SPEC] * len(shapes),
        scratch_shapes=[
            pltpu.VMEM((4, w_own.shape[1], width), bf),
            pltpu.VMEM((4, width, width), bf),
            pltpu.VMEM((16, 128), bf),
            pltpu.VMEM((8, 4, 16, 128), bf),
            pltpu.VMEM((3, count, width), bf),
            pltpu.VMEM((count, width), bf),
            pltpu.VMEM((count, width), bf),
            pltpu.VMEM((count, width), full),
            pltpu.VMEM((count, width), bf),
            pltpu.VMEM((4, 8, 256), jnp.int32),
            pltpu.VMEM((16, width), bf),
            pltpu.VMEM((8, cap, width), bf),
            pltpu.SemaphoreType.DMA((copies,)),
            pltpu.SemaphoreType.DMA((copies,)),
            pltpu.SemaphoreType.DMA((16,)),
        ],
        compiler_params=pltpu.CompilerParams(
            collective_id=0, has_side_effects=True, vmem_limit_bytes=62 << 20
        ),
    )(tokens, w_own, norm_own, routes, cotangent)


def gelu_pair(v):
    cdf = 0.5 + 0.5 * lax.erf(v * (0.5**0.5))
    pdf = jnp.exp(-0.5 * v * v) * ((2.0 * math.pi) ** -0.5)
    return v * cdf, cdf + v * pdf


def fold(v):
    total = v[0:8]
    for i in range(8, v.shape[0], 8):
        total = total + v[i : i + 8]
    return total


def spread(column, lanes):
    return jnp.concatenate([column] * (lanes // 128), axis=1)


def square_lanes(v):
    total = v[:, 0:128] * v[:, 0:128]
    for i in range(128, v.shape[1], 128):
        total = total + v[:, i : i + 128] * v[:, i : i + 128]
    return total


def unslot(placed_row, slots, out):
    planes, cap, width = slots.shape
    onehot = pick(placed_row, planes * cap)

    @pl.loop(0, width // 256)
    def _(j):
        cols = tile(j)
        value = slots[:, :, cols].reshape(planes * cap, 256)
        out[:, cols] = dot(onehot, value, 0, 0).astype(jnp.bfloat16)


class Home:
    def __init__(self, wire, at, name, part, got):
        self.wire, self.at, self.name = wire, at, name
        self.part, self.got = part, got
        half = got.shape[1] // 2
        self.halves = [pl.ds(0, half), pl.ds(half, half)]

    def add(self, i, k, half):
        part = self.part(i)
        part[half, :] = (
            part[half, :].astype(jnp.float32) + self.got[k, half, :].astype(jnp.float32)
        ).astype(jnp.bfloat16)

    def arrived(self, tag, k, n, device):
        half = self.halves[n]
        self.wire.arrived((self.name, tag, n), self.got.at[k, half], device)

    def send(self, src, k, n, device, tag, when=None):
        half = self.halves[n]
        self.wire.send(src.at[half], self.got.at[k, half], device, (self.name, tag, n), when)

    def push(self, i):
        for n in range(2):
            self.send(self.part(i), i - 1, n, self.at.partner, i, self.at.ends)

    def pass_on(self, i):
        at = self.at
        k = {3: 3, 2: 4}[i]
        for n, half in enumerate(self.halves):

            @pl.when(at.middle)
            def _():
                self.arrived(i, i - 1, n, at.partner)
                self.add(i, i - 1, half)

            self.send(self.part(i), k, n, at.mirror, k + 1, at.middle)

    def near(self):
        at = self.at
        for n, half in enumerate(self.halves):

            @pl.when(at.middle)
            def _():
                self.arrived(4, 3, n, at.mirror)
                self.add(1, 3, half)

            self.send(self.part(1), 0, n, at.partner, 1)

    def relay_far(self):
        at = self.at
        for n in range(2):
            pl.when(at.middle)(lambda: self.arrived(4, 3, n, at.mirror))
            self.send(self.got.at[3], 0, n, at.partner, 1, at.middle)

    def finish(self):
        at = self.at
        for n, half in enumerate(self.halves):

            @pl.when(at.ends)
            def _():
                self.arrived(1, 0, n, at.partner)
                self.add(0, 0, half)

            @pl.when(at.middle)
            def _():
                self.arrived(5, 4, n, at.mirror)
                self.add(0, 4, half)

    def last(self):
        at = self.at
        for n, half in enumerate(self.halves):
            self.arrived(1, 0, n, at.partner)

            @pl.when(at.middle)
            def _():
                self.arrived(5, 4, n, at.mirror)
                self.add(0, 4, half)

    def total(self, cols):
        return self.part(0)[:, cols].astype(jnp.float32) + self.got[0, :, cols].astype(jnp.float32)


def expert_kernel(
    cap,
    sent_in,
    placed_in,
    cot_raw,
    cot_zero,
    up_in,
    down_in,
    vec,
    d_sum,
    g_up,
    g_down,
    delta_out,
    vec_part,
    scal,
    sent,
    placed,
    cot_line,
    up,
    down,
    raw,
    stage,
    rows,
    cots,
    xn,
    act,
    slope,
    delta,
    d_slots,
    back,
    part,
    z_in,
    d_xn,
    gate,
    d_logit,
    g_stage,
    send_sem,
    recv_sem,
    local_sem,
):
    at = Place()
    e, z = at.e, at.z
    depth, planes = 4, 8
    count, width = sent.shape
    slots = planes * cap
    units = up.shape[1]
    wire = Wire(send_sem, recv_sem)
    fetch = Fetch(local_sem)
    in_sent = fetch.start(sent_in, sent)
    in_placed = fetch.start(placed_in, placed)
    in_up = fetch.start(up_in, up)
    in_down = fetch.start(down_in, down)
    in_cot = fetch.start(cot_raw, cot_line)
    in_zero = fetch.start(cot_zero, cots.at[0])
    at.meet()
    fetch.done(in_sent)
    line = Line(wire, at, "row", lambda zz: raw.at[zz])
    line.begin(sent)
    vec_part[...] = jnp.zeros_like(vec_part)
    scal[...] = jnp.zeros_like(scal)
    fetch.done(in_placed)
    centroid = lambda: vec[0]
    row_copies, cot_copies, ret_copies = {}, {}, {}

    def exchange(i, dst, s, offsets=range(1, planes)):
        return [
            wire.send(stage.at[s, at.across(k)], dst.at[i, k], (at.across(k), z)) for k in offsets
        ]

    def slot_row(i):
        return placed[at.line[i], 0:1, :count]

    def rows_out(i):
        source = sent if i == 0 else raw.at[at.line[i]]
        build(stage.at[i], source, slot_row(i))
        row_copies[i] = exchange(i, rows, i)
        rows[i, 0] = stage[i, e]

    def cots_out(i, s, offsets):
        if i not in cot_copies:
            for copy in row_copies[s]:
                wire.left(copy)
            build(stage.at[s], cot_line.at[at.line[i]], slot_row(i))
            cot_copies[i] = []
            cots[i, 0] = stage[s, e]
        cot_copies[i] += exchange(i, cots, s, offsets)

    def forward(i):
        for copy in row_copies[i]:
            copy.wait_recv()
        gain, bias = vec[1], vec[2]

        @pl.loop(0, planes, unroll=2)
        def _(k):
            r = rows[i, k].astype(jnp.float32)
            logit = jnp.sum(r * centroid(), axis=-1, keepdims=True)
            g = jax.nn.sigmoid(logit)
            wide = jnp.broadcast_to(g, (cap, 128))
            gate[i, k] = wide
            scal[0:8] += fold(wide)
            average = jnp.mean(r, axis=-1, keepdims=True)
            centred = r - average
            variance = jnp.mean(centred * centred, axis=-1, keepdims=True)
            xn[i, pl.ds(pl.multiple_of(k * cap, 16), cap), :] = (
                centred * lax.rsqrt(variance + norm_eps) * gain + bias
            ).astype(jnp.bfloat16)

        if i == 0:
            fetch.done(in_up)

        @pl.loop(0, units // 512)
        def _(j):
            cols = tile(j, 512)
            value, rate = gelu_pair(dot(xn[i], up[:, cols]))
            act[i, :, cols] = value.astype(jnp.bfloat16)
            slope[i, :, cols] = rate.astype(jnp.bfloat16)

        if i == 0:
            fetch.done(in_down)

        @pl.loop(0, width // 512)
        def _(j):
            cols = tile(j, 512)
            branch = dot(act[i], down[:, cols])
            wide = spread(gate[i].reshape(slots, 128), 512)
            value = (wide * branch).astype(jnp.bfloat16)
            for k in range(planes):
                delta[i, k, :, cols] = value[k * cap : (k + 1) * cap]

        fetch.start(delta.at[i], delta_out.at[i])

    def backward(i):
        for copy in cot_copies[i]:
            copy.wait_recv()

        @pl.loop(0, planes, unroll=2)
        def _(k):
            c = cots[i, k].astype(jnp.float32)
            g = gate[i, k]
            inner = jnp.sum(c * delta[i, k].astype(jnp.float32), axis=-1, keepdims=True)
            dl = (1.0 - g) * inner
            d_logit[i, k] = dl
            cots[i, k] = (c * spread(g, width)).astype(jnp.bfloat16)
            vec_part[0] += fold(rows[i, k].astype(jnp.float32) * spread(dl, width))

        @pl.loop(0, units // 512)
        def _(j):
            cols = tile(j, 512)
            d_act = dot(cots[i].reshape(slots, width), down[cols, :], 1, 1)
            slope[i, :, cols] = (d_act * slope[i, :, cols].astype(jnp.float32)).astype(
                jnp.bfloat16
            )

    def backward_in(i):
        @pl.loop(0, width // 512)
        def _(j):
            cols = tile(j, 512)
            value = dot(slope[i], up[cols, :], 1, 1)
            for k in range(planes):
                d_xn[k, :, cols] = value[k * cap : (k + 1) * cap]

        @pl.loop(0, planes, unroll=2)
        def _(k):
            r = rows[i, k].astype(jnp.float32)
            average = jnp.mean(r, axis=-1, keepdims=True)
            centred = r - average
            variance = jnp.mean(centred * centred, axis=-1, keepdims=True)
            scale = lax.rsqrt(variance + norm_eps)
            hat = centred * scale
            dx = d_xn[k]
            vec_part[1] += fold(dx * hat)
            vec_part[2] += fold(dx)
            dh = dx * vec[1]
            first = jnp.mean(dh, axis=-1, keepdims=True)
            second = jnp.mean(dh * hat, axis=-1, keepdims=True)
            d_in = scale * (dh - first - hat * second)
            d_slots[i, k] = (d_in + spread(d_logit[i, k], width) * centroid()).astype(jnp.bfloat16)

    def give(i):
        ret_copies[i] = [
            wire.send(d_slots.at[i, k], back.at[i, e], (at.across(k), z))
            for k in range(1, planes)
        ]
        back[i, e] = d_slots[i, 0]

    home = Home(wire, at, "home", lambda i: part.at[i], z_in)

    def collect(i):
        for copy in ret_copies[i]:
            copy.wait_recv()
        unslot(slot_row(i), back.at[i], part.at[i])

    def weight_grad(lhs, rhs, index, out):
        @pl.loop(0, lhs.shape[-1] // 512)
        def _(j):
            cols = tile(j, 512)
            left = lhs[:, :, cols].reshape(depth * slots, 512)
            value = dot(left, rhs[...].reshape(depth * slots, rhs.shape[-1]), 0, 0)
            scal[8:16] += fold(square_lanes(value))
            g_stage[index, cols, :] = value.astype(jnp.bfloat16)

        fetch.start(g_stage.at[index], out)

    rows_out(0)
    line.take(1)
    line.take(2, at.middle)
    rows_out(1)
    fetch.done(in_cot)
    cots_out(3, 0, (2, 4, 6))
    forward(0)
    line.take(2, at.ends)
    line.take(3, at.middle)
    rows_out(2)
    forward(1)
    line.take(3, at.ends)
    rows_out(3)
    fetch.done(in_zero)
    cot_copies[0] = []
    cot_copies[1] = [wire.send(cot_zero, cots.at[1], at.partner)]
    cots_out(3, 0, (3, 5, 7, 1))
    forward(2)
    cots_out(2, 1, range(1, planes))
    forward(3)
    backward(3)
    backward_in(3)
    give(3)
    backward(2)
    backward_in(2)
    give(2)
    backward(1)
    backward_in(1)
    give(1)
    backward(0)
    collect(3)
    home.push(3)
    backward_in(0)
    give(0)
    collect(2)
    home.push(2)
    home.pass_on(3)
    weight_grad(act, cots, 0, g_down)
    collect(1)
    home.near()
    home.pass_on(2)
    weight_grad(xn, slope, 1, g_up)
    collect(0)
    home.last()

    @pl.loop(0, width // 256)
    def _(j):
        cols = tile(j)
        d_sum[:, cols] = home.total(cols)

    wire.drain()
    fetch.drain()


def expert_layer(cap, sent, placed, cot_raw, cot_zero, up, down, vec):
    count, width = sent.shape
    units = up.shape[1]
    depth = 4
    bf, full = jnp.bfloat16, jnp.float32
    slots = 8 * cap
    copies = 3 * 7 * depth + 56
    shapes = [
        ((count, width), full),
        ((width, units), bf),
        ((units, width), bf),
        ((depth, 8, cap, width), bf),
        ((3, 8, width), full),
        ((16, 128), full),
    ]
    big = pltpu.VMEM((depth, 8, cap, width), bf)
    return pl.pallas_call(
        functools.partial(expert_kernel, cap),
        out_shape=[jax.ShapeDtypeStruct(*one) for one in shapes],
        in_specs=[ANY_SPEC] * 6 + [VMEM_SPEC],
        out_specs=[VMEM_SPEC, ANY_SPEC, ANY_SPEC, ANY_SPEC, VMEM_SPEC, VMEM_SPEC],
        scratch_shapes=[
            pltpu.VMEM((count, width), bf),
            pltpu.VMEM((depth, 8, 256), jnp.int32),
            pltpu.VMEM((depth, count, width), bf),
            pltpu.VMEM((width, units), bf),
            pltpu.VMEM((units, width), bf),
            pltpu.VMEM((depth, count, width), bf),
            big,
            big,
            big,
            pltpu.VMEM((depth, slots, width), bf),
            pltpu.VMEM((depth, slots, units), bf),
            pltpu.VMEM((depth, slots, units), bf),
            big,
            big,
            big,
            pltpu.VMEM((depth, count, width), bf),
            pltpu.VMEM((5, count, width), bf),
            pltpu.VMEM((8, cap, width), full),
            pltpu.VMEM((depth, 8, cap, 128), full),
            pltpu.VMEM((depth, 8, cap, 128), full),
            pltpu.VMEM((2, max(width, units), max(width, units)), bf),
            pltpu.SemaphoreType.DMA((copies,)),
            pltpu.SemaphoreType.DMA((copies,)),
            pltpu.SemaphoreType.DMA((16,)),
        ],
        compiler_params=pltpu.CompilerParams(
            collective_id=1, has_side_effects=True, vmem_limit_bytes=62 << 20
        ),
    )(sent, placed, cot_raw, cot_zero, up, down, vec)


def reduce_kernel(
    cap,
    d_sum,
    cot,
    w_in,
    qkv_in,
    normed_in,
    ctx,
    tok,
    gains,
    placed,
    delta_in,
    resid,
    vec_part,
    scal,
    block_out,
    token_grad,
    shard_out,
    norm_out,
    vec_out,
    square_out,
    norm_shard,
    wfull,
    qkv,
    normed,
    delta,
    d_resid,
    d_proj,
    d_ctx,
    d_qkv,
    d_norm,
    stage,
    twin_in,
    x_in,
    y_in,
    x_last,
    y_last,
    done,
    z_last,
    back,
    part,
    z_in,
    near_in,
    small,
    small_in,
    square,
    send_sem,
    recv_sem,
    local_sem,
):
    at = Place()
    e, z = at.e, at.z
    depth, planes = 4, 8
    count, width = tok.shape
    shard = shard_out.shape[1]
    column = depth * shard
    half = column // 2
    wire = Wire(send_sem, recv_sem)
    fetch = Fetch(local_sem)
    in_delta = {i: fetch.start(delta_in.at[i], delta.at[i]) for i in (1, 3, 2, 0)}
    in_w = {m: fetch.start(w_in.at[m], wfull.at[m]) for m in (3, 2, 1, 0)}
    in_qkv = fetch.start(qkv_in, qkv)
    in_normed = fetch.start(normed_in, normed)
    at.meet()
    ret = {}
    home = Home(wire, at, "home", lambda i: part.at[i], z_in)

    def give(i):
        if i in in_delta:
            fetch.done(in_delta.pop(i))
        ret[i] = [
            wire.send(delta.at[i, k], back.at[i, e], (at.across(k), z)) for k in range(1, planes)
        ]
        back[i, e] = delta[i, 0]

    def collect(i):
        for copy in ret[i]:
            copy.wait_recv()
        unslot(placed[at.line[i], 0:1, :count], back.at[i], part.at[i])

    def weight_grad(m, left_ref, right):
        @pl.loop(0, planes)
        def _(i):
            cols = pl.ds(pl.multiple_of(i * column, column), column)
            value = dot(left_ref[:, cols], right[...], 0, 0).astype(jnp.bfloat16)
            stage[m, lax.div(i, 4), lax.rem(lax.div(i, 2), 2), lax.rem(i, 2)] = value

    other = 1 - at.core
    first, second, third, fourth, fifth = {}, {}, {}, {}, {}

    def to_core(m):
        first[m] = wire.send(stage.at[m, :, :, other], twin_in.at[m], at.twin)

    def to_plane(m):
        first[m].wait_recv()
        for j in range(2):
            for i in range(2):
                twin_in[m, j, i] = twin_in[m, j, i] + stage[m, j, i, at.core]
        second[m] = (
            wire.send(twin_in.at[m, :, 1 - at.x, pl.ds(0, half)], x_in.at[m], at.over_x),
            wire.send(twin_in.at[m, 1 - at.y, :, pl.ds(half, half)], y_in.at[m], at.over_y),
        )

    def to_last(m):
        second[m][0].wait_recv()
        for j in range(2):
            x_in[m, j] = x_in[m, j] + twin_in[m, j, at.x, 0:half]
        one = wire.send(x_in.at[m, 1 - at.y], x_last.at[m], at.over_y)
        second[m][1].wait_recv()
        for i in range(2):
            y_in[m, i] = y_in[m, i] + twin_in[m, at.y, i, half:]
        two = wire.send(y_in.at[m, 1 - at.x], y_last.at[m], at.over_x)
        third[m] = (one, two)

    def to_owner(m):
        third[m][0].wait_recv()
        pair = (2, shard, width)
        done[m, 0:2] = (x_in[m, at.y] + x_last[m]).reshape(pair)
        third[m][1].wait_recv()
        done[m, 2:4] = (y_in[m, at.x] + y_last[m]).reshape(pair)
        theirs = at.partner[1]
        fourth[m] = (
            wire.send(done.at[m, theirs], z_last.at[m, 0], at.partner),
            wire.send(done.at[m, 3 - theirs], z_last.at[m, 1], at.partner),
        )

    def cross(m):
        fourth[m][1].wait_recv()
        done[m, 3 - z] = done[m, 3 - z] + z_last[m, 1]
        fifth[m] = wire.send(done.at[m, 3 - z], z_last.at[m, 2], at.mirror)

    def own(m):
        fourth[m][0].wait_recv()
        fifth[m].wait_recv()
        total = done[m, z].astype(jnp.float32)
        for k in (0, 2):
            total = total + z_last[m, k].astype(jnp.float32)
        shard_out[m] = total

    fetch.done(in_delta[1])
    near_copy = wire.send(delta.at[1], near_in, at.partner)
    give(3)
    value = cot[...].astype(jnp.float32) + d_sum[...]
    d_resid[...] = value
    d_proj[...] = value.astype(jnp.bfloat16)
    weight_grad(3, ctx, d_proj)
    to_core(3)
    fetch.done(in_w[3])

    @pl.loop(0, width // 256)
    def _(j):
        cols = tile(j)
        d_ctx[:, cols] = dot(d_proj[...], wfull[3, cols, :], 1, 1).astype(jnp.bfloat16)

    to_plane(3)
    fetch.done(in_qkv)
    causal = lax.broadcasted_iota(jnp.int32, (count, count), 0) >= lax.broadcasted_iota(
        jnp.int32, (count, count), 1
    )
    left = lax.broadcasted_iota(jnp.int32, (count, 128), 1) < 64
    scaling = 64 ** (-0.5)

    def pair(i):
        cols = tile(i, 128)
        query = qkv[0, :, cols]
        keys = qkv[1, :, cols]
        values = qkv[2, :, cols]
        d_out = d_ctx[:, cols]
        zero = jnp.zeros_like(query)
        got = []
        for side in range(2):
            mask = left if side == 0 else jnp.logical_not(left)
            q_side = jnp.where(mask, query, zero)
            k_side = jnp.where(mask, keys, zero)
            o_side = jnp.where(mask, d_out, zero)
            scores = dot(q_side, keys, 1, 1) * scaling
            scores = jnp.where(causal, scores, masked_fill)
            top = jnp.max(scores, axis=-1, keepdims=True)
            expo = jnp.exp(scores - top)
            probs = expo / jnp.sum(expo, axis=-1, keepdims=True)
            d_probs = dot(o_side, values, 1, 1)
            inner = jnp.sum(d_probs * probs, axis=-1, keepdims=True)
            d_scores = (probs * (d_probs - inner)).astype(jnp.bfloat16)
            got.append(
                (
                    dot(d_scores, k_side),
                    dot(d_scores, q_side, 0, 0),
                    dot(probs.astype(jnp.bfloat16), o_side, 0, 0),
                )
            )
        d_qkv[0, :, cols] = ((got[0][0] + got[1][0]) * scaling).astype(jnp.bfloat16)
        d_qkv[1, :, cols] = ((got[0][1] + got[1][1]) * scaling).astype(jnp.bfloat16)
        d_qkv[2, :, cols] = (got[0][2] + got[1][2]).astype(jnp.bfloat16)

    pl.loop(0, width // 256, unroll=2)(pair)
    give(2)
    pl.loop(width // 256, width // 128, unroll=2)(pair)
    collect(3)
    home.push(3)
    fetch.done(in_normed)
    weight_grad(2, normed, d_qkv.at[2])
    to_core(2)
    to_last(3)
    weight_grad(1, normed, d_qkv.at[1])
    to_core(1)
    to_plane(2)
    weight_grad(0, normed, d_qkv.at[0])
    to_core(0)
    home.pass_on(3)
    to_owner(3)
    to_plane(1)
    collect(2)
    home.push(2)
    for m in (2, 1, 0):
        fetch.done(in_w[m])

    @pl.loop(0, width // 256)
    def _(j):
        cols = tile(j)
        d_norm[:, cols] = (
            dot(d_qkv[0], wfull[0, cols, :], 1, 1)
            + dot(d_qkv[1], wfull[1, cols, :], 1, 1)
            + dot(d_qkv[2], wfull[2, cols, :], 1, 1)
        )

    gain = gains[0:1, :].astype(jnp.float32)
    d_gain = jnp.zeros((8, width), jnp.float32)
    d_bias = jnp.zeros((8, width), jnp.float32)
    for i in range(0, count, 64):
        piece = tok[i : i + 64, :].astype(jnp.float32)
        average = jnp.mean(piece, axis=-1, keepdims=True)
        centred = piece - average
        variance = jnp.mean(centred * centred, axis=-1, keepdims=True)
        scale = lax.rsqrt(variance + norm_eps)
        hat = centred * scale
        dx = d_norm[i : i + 64, :]
        d_gain = d_gain + fold(dx * hat)
        d_bias = d_bias + fold(dx)
        dh = dx * gain
        mean_one = jnp.mean(dh, axis=-1, keepdims=True)
        mean_two = jnp.mean(dh * hat, axis=-1, keepdims=True)
        d_in = scale * (dh - mean_one - hat * mean_two)
        token_grad[i : i + 64, :] = (d_resid[i : i + 64, :] + d_in).astype(jnp.bfloat16)
    mine = small.at[0]
    mine[...] = jnp.zeros((8, width), jnp.float32)
    mine[2:3, :] = gains[2:3, :].astype(jnp.float32)
    mine[0:1, :] = jnp.sum(d_gain, axis=0, keepdims=True)
    mine[1:2, :] = jnp.sum(d_bias, axis=0, keepdims=True)
    for k in range(3):
        mine[3 + k : 4 + k, :] = jnp.sum(vec_part[k], axis=0, keepdims=True)
    small_copy = wire.send(mine, small.at[1], at.partner)
    to_last(2)
    home.relay_far()
    home.pass_on(2)
    near_copy.wait_recv()
    fetch.done(in_delta.pop(0))

    @pl.loop(0, planes)
    def _(k):
        delta[0, k] = (delta[0, k].astype(jnp.float32) + near_in[k].astype(jnp.float32)).astype(
            jnp.bfloat16
        )

    to_plane(0)
    cross(3)
    small_copy.wait_recv()
    small[2] = small[0] + small[1]
    small_copy = wire.send(small.at[2], small.at[3], at.mirror)
    to_last(1)
    to_owner(2)
    own(3)
    to_last(0)
    cross(2)
    small_copy.wait_recv()
    total = small[2] + small[3]
    vec_out[...] = total
    small_in[e] = total
    spot = small_in.at[e]
    plane_copies = [wire.send(spot, spot, (at.across(k), z)) for k in range(1, planes)]
    give(0)
    to_owner(1)
    own(2)
    to_owner(0)
    cross(1)
    cross(0)
    own(1)
    for copy in plane_copies:
        copy.wait_recv()
    total = small_in[0]
    for k in range(1, planes):
        total = total + small_in[k]
    norm_out[...] = total
    norm_rows = norm_out[0:2, :]
    mine = norm_out[0:2, tile(e, 128)]
    lanes = norm_shard.shape[1]
    value = mine[:, 0:lanes]
    for k in range(1, depth):
        value = jnp.where(z == k, mine[:, k * lanes : (k + 1) * lanes], value)
    norm_shard[...] = value
    lane = lax.broadcasted_iota(jnp.int32, (1, 128), 1)
    routed = jnp.sum(jnp.where(lane == e, norm_out[2:3, 0:128], 0.0), keepdims=True)
    gates = jnp.sum(scal[0:8, 0:1], keepdims=True) - 0.5 * (depth * planes * cap - routed)
    vec_rows = vec_out[3:6, :]
    squares = jnp.sum(norm_rows * norm_rows, axis=0, keepdims=True) / (planes * depth) + jnp.sum(
        vec_rows * vec_rows, axis=0, keepdims=True
    ) / depth
    local = scal[8:16, :]
    for m in (3, 2, 1):
        local = local + fold(square_lanes(shard_out[m]))
    lane_squares = squares[:, 0:128]
    for i in range(128, width, 128):
        lane_squares = lane_squares + squares[:, i : i + 128]
    head = lax.broadcasted_iota(jnp.int32, (8, 128), 0) == 0
    local = local + jnp.where(head, jnp.broadcast_to(lane_squares, (8, 128)), 0.0)
    own(0)
    square[0, e] = local + fold(square_lanes(shard_out[0]))
    spot = square.at[0, e]
    copies = [wire.send(spot, spot, (at.across(k), z)) for k in range(1, planes)]
    collect(0)
    home.finish()

    @pl.loop(0, width // 256)
    def _(j):
        cols = tile(j)
        block_out[:, cols] = (resid[:, cols] + part[0, :, cols].astype(jnp.float32)).astype(
            jnp.bfloat16
        )

    for copy in copies:
        copy.wait_recv()
    total = square[0, 0]
    for k in range(1, planes):
        total = total + square[0, k]
    square[1, z] = total
    spot = square.at[1, z]
    copies = [wire.send(spot, spot, at.mates[k]) for k in range(1, depth)]
    for copy in copies:
        copy.wait_recv()
    total = square[1, 0]
    for d in range(1, depth):
        total = total + square[1, d]
    norm = jnp.sqrt(jnp.sum(total, keepdims=True))
    which = lax.broadcasted_iota(jnp.int32, (8, 128), 0)
    stats = jnp.where(which == 0, routed / (count * depth), gates / routed)
    clip = clip_level / jnp.maximum(norm, clip_level)
    square_out[...] = jnp.where(which < 2, stats, jnp.where(which == 2, norm, clip))
    wire.drain()
    fetch.drain()


def attend_back(cap, shard, *args):
    tokens = args[6]
    count, width = tokens.shape
    depth = 4
    bf, full = jnp.bfloat16, jnp.float32
    column = depth * shard
    half = column // 2
    copies = 7 * depth + 96
    shapes = [
        ((count, width), bf),
        ((count, width), bf),
        ((4, shard, width), full),
        ((8, width), full),
        ((8, width), full),
        ((8, 128), full),
        ((2, width // 32), full),
    ]
    return pl.pallas_call(
        functools.partial(reduce_kernel, cap),
        out_shape=[jax.ShapeDtypeStruct(*one) for one in shapes],
        in_specs=[VMEM_SPEC] * 2
        + [ANY_SPEC] * 3
        + [VMEM_SPEC] * 4
        + [ANY_SPEC]
        + [VMEM_SPEC] * 3,
        out_specs=[VMEM_SPEC] * 7,
        scratch_shapes=[
            pltpu.VMEM((4, width, width), bf),
            pltpu.VMEM((3, count, width), bf),
            pltpu.VMEM((count, width), bf),
            pltpu.VMEM((depth, 8, cap, width), bf),
            pltpu.VMEM((count, width), full),
            pltpu.VMEM((count, width), bf),
            pltpu.VMEM((count, width), bf),
            pltpu.VMEM((3, count, width), bf),
            pltpu.VMEM((count, width), full),
            pltpu.VMEM((4, 2, 2, 2, column, width), bf),
            pltpu.VMEM((4, 2, 2, column, width), bf),
            pltpu.VMEM((4, 2, half, width), bf),
            pltpu.VMEM((4, 2, half, width), bf),
            pltpu.VMEM((4, half, width), bf),
            pltpu.VMEM((4, half, width), bf),
            pltpu.VMEM((4, depth, shard, width), bf),
            pltpu.VMEM((4, depth - 1, shard, width), bf),
            pltpu.VMEM((depth, 8, cap, width), bf),
            pltpu.VMEM((depth, count, width), bf),
            pltpu.VMEM((5, count, width), bf),
            pltpu.VMEM((8, cap, width), bf),
            pltpu.VMEM((4, 8, width), full),
            pltpu.VMEM((8, 8, width), full),
            pltpu.VMEM((2, 8, 8, 128), full),
            pltpu.SemaphoreType.DMA((copies,)),
            pltpu.SemaphoreType.DMA((copies,)),
            pltpu.SemaphoreType.DMA((16,)),
        ],
        compiler_params=pltpu.CompilerParams(
            collective_id=2, has_side_effects=True, vmem_limit_bytes=62 << 20
        ),
    )(*args)


def adam_quick(weight, first, second, grad, clip_factor, rate, decay):
    clipped = grad * clip_factor
    moment = beta_one * first + (1.0 - beta_one) * clipped
    square = beta_two * second + (1.0 - beta_two) * clipped * clipped
    root = jnp.sqrt(square * (1.0 / (1.0 - beta_two**STEP))) + adam_eps
    step = moment * (rate / (1.0 - beta_one**STEP)) / root
    return (weight * (1.0 - rate * decay) - step, moment, square)


def adam_kernel(*refs):
    ins, outs = refs[:23], refs[23:]
    facts, block_in, token_in = ins[20:23]
    clip = facts[3:4, 0:1]
    for k in range(3):
        weight, first, second, grad = ins[4 * k : 4 * k + 4]
        new, moment, square = outs[3 * k : 3 * k + 3]
        new[...], moment[...], square[...] = adam_quick(
            weight[...].astype(jnp.float32),
            first[...],
            second[...],
            grad[...].astype(jnp.float32),
            clip,
            rate_matrix,
            decay_rate,
        )

    @pl.when(pl.program_id(0) == 0)
    def _():
        weight, first, second, grad = ins[12:16]
        for k in range(3):
            got = adam_quick(
                weight[k], first[k], second[k], grad[3 + k : 4 + k, :], clip, rate_vector, 0.0
            )
            for out, value in zip(outs[9:12], got):
                out[k] = value
        weight, first, second, grad = ins[16:20]
        got = adam_quick(
            weight[...], first[...], second[...], grad[...], clip, rate_vector, 0.0
        )
        for out, value in zip(outs[12:15], got):
            out[...] = value
        outs[15][...] = block_in[...]
        outs[16][...] = token_in[...]
        outs[17][...] = facts[2:3, 0:1]
        outs[18][...] = jnp.concatenate([facts[0:1, 0:1], facts[1:2, 0:1]], axis=1)


def adam_all(up, down, attn, vector, norm, facts, block_out, token_grad):
    steps = 8
    full = jnp.float32

    def whole(shape):
        return pl.BlockSpec(shape, lambda i: (0,) * len(shape))

    def cut(v):
        return pl.BlockSpec((v.shape[0] // steps, v.shape[1]), lambda i: (i, 0))

    args, in_specs, out_specs, shapes = [], [], [], []
    for group in (up, down, attn):
        args += group
        in_specs += [cut(v) for v in group]
        out_specs += [cut(group[0])] * 3
        shapes += [jax.ShapeDtypeStruct(group[0].shape, full)] * 3
    for group in (vector, norm):
        args += group
        in_specs += [whole(v.shape) for v in group]
        out_specs += [whole(group[0].shape)] * 3
        shapes += [jax.ShapeDtypeStruct(group[0].shape, full)] * 3
    args += [facts]
    in_specs += [whole(facts.shape)]
    for v in (block_out, token_grad):
        args += [v]
        in_specs += [whole(v.shape)]
        out_specs += [whole(v.shape)]
        shapes += [jax.ShapeDtypeStruct(v.shape, v.dtype)]
    for shape in ((1, 1), (1, 2)):
        out_specs += [whole(shape)]
        shapes += [jax.ShapeDtypeStruct(shape, full)]
    return pl.pallas_call(
        adam_kernel,
        grid=(steps,),
        out_shape=shapes,
        in_specs=in_specs,
        out_specs=out_specs,
        compiler_params=pltpu.CompilerParams(vmem_limit_bytes=60 << 20),
    )(*args)


def shards(
    tokens,
    cotangent,
    routes,
    attn_weight,
    attn_first,
    attn_second,
    norm_param,
    norm_first,
    norm_second,
    up_weight,
    up_first,
    up_second,
    down_weight,
    down_first,
    down_second,
    expert_vector,
    vector_first,
    vector_second,
):
    experts_here = lax.axis_size(EX)
    hidden_size = lax.axis_size(HI)
    token_count = tokens.shape[0]
    features = tokens.shape[1]
    capacity = 2 * token_count // experts_here
    slot_rows = experts_here * capacity
    head_dim = features // HEADS
    scaling = head_dim ** (-0.5)
    attn_low = attn_weight.astype(jnp.bfloat16)
    norm_low = norm_param.astype(jnp.bfloat16)
    attn_full, norm_full = (
        lax.all_gather(attn_low, BOTH, axis=1, tiled=True),
        lax.all_gather(norm_low, BOTH, axis=1, tiled=True),
    )
    inputs = tokens.astype(jnp.float32)
    normed, norm_pull = jax.vjp(
        layer_norm, inputs, norm_full[0].astype(jnp.float32), norm_full[1].astype(jnp.float32)
    )
    normed_low = normed.astype(jnp.bfloat16)
    projected = jnp.einsum(
        "td,sde->ste", normed_low, attn_full[:3], preferred_element_type=jnp.float32
    ).astype(jnp.bfloat16)
    query = projected[0].reshape(token_count, HEADS, head_dim)
    keys_all = projected[1].reshape(token_count, HEADS, head_dim)
    values_all = projected[2].reshape(token_count, HEADS, head_dim)
    causal = jnp.arange(token_count)[:, None] >= jnp.arange(token_count)[None, :]

    def score_rows():
        raw = (
            jnp.einsum("qhe,khe->hqk", query, keys_all, preferred_element_type=jnp.float32)
            * scaling
        )
        return jnp.where(causal[None], raw, masked_fill)

    scores = score_rows()
    row_max = jnp.max(scores, axis=-1, keepdims=True)
    expo = jnp.exp(scores - row_max)
    row_total = jnp.sum(expo, axis=-1, keepdims=True)
    log_total = row_max + jnp.log(row_total)
    probs_low = (expo / row_total).astype(jnp.bfloat16)
    context = jnp.einsum("hqk,khe->qhe", probs_low, values_all, preferred_element_type=jnp.float32)
    context = context.reshape(token_count, features).astype(jnp.bfloat16)
    resid = inputs + jnp.dot(context, attn_full[3], preferred_element_type=jnp.float32)
    route = routes[:, 0]
    chosen = (route[:, None] == jnp.arange(experts_here, dtype=jnp.int32)[None, :]).astype(
        jnp.int32
    )
    ranked = jnp.sum((jnp.cumsum(chosen, axis=0) - 1) * chosen, axis=1)
    placed = route * capacity + ranked
    placing = (jnp.arange(slot_rows, dtype=jnp.int32)[:, None] == placed[None, :]).astype(
        jnp.bfloat16
    )
    outgoing = jnp.dot(
        placing, resid.astype(jnp.bfloat16), preferred_element_type=jnp.float32
    ).astype(jnp.bfloat16)
    occupied = jnp.sum(placing.astype(jnp.float32), axis=1).astype(jnp.bfloat16)
    arrived, arrived_mask = (
        lax.all_to_all(
            outgoing.reshape(experts_here, capacity, features),
            EX,
            split_axis=0,
            concat_axis=0,
            tiled=True,
        ),
        lax.all_to_all(
            occupied.reshape(experts_here, capacity),
            EX,
            split_axis=0,
            concat_axis=0,
            tiled=True,
        ),
    )
    gathered, gathered_mask = (
        lax.all_gather(arrived, HI, axis=0, tiled=True),
        lax.all_gather(arrived_mask, HI, axis=0, tiled=True),
    )
    rows_all = gathered.reshape(-1, features)
    mask_all = gathered_mask.reshape(-1).astype(jnp.float32)
    rows_float = rows_all.astype(jnp.float32)
    centroid = expert_vector[0, 0]
    gating = jax.nn.sigmoid(jnp.sum(rows_float * centroid, axis=-1))
    expert_normed, expert_pull = jax.vjp(
        layer_norm, rows_float, expert_vector[0, 1], expert_vector[0, 2]
    )
    expert_low = expert_normed.astype(jnp.bfloat16)
    before = jnp.dot(expert_low, up_weight[0], preferred_element_type=jnp.float32)
    after, gelu_pull = jax.vjp(gelu_exact, before)
    after_low = after.astype(jnp.bfloat16)
    branch_own = lax.psum_scatter(
        jnp.dot(after_low, down_weight[0], preferred_element_type=jnp.float32).astype(jnp.bfloat16),
        HI,
        scatter_dimension=0,
        tiled=True,
    ).astype(jnp.float32)
    own_start = lax.axis_index(HI) * slot_rows
    gating_own = lax.dynamic_slice_in_dim(gating, own_start, slot_rows, 0)
    delta = (gating_own[:, None] * branch_own).astype(jnp.bfloat16)
    returned = lax.all_to_all(
        delta.reshape(experts_here, capacity, features),
        EX,
        split_axis=0,
        concat_axis=0,
        tiled=True,
    )
    delta_tokens = jnp.einsum(
        "st,sd->td",
        placing,
        returned.reshape(slot_rows, features),
        preferred_element_type=jnp.float32,
    )
    block_out = (resid + delta_tokens).astype(jnp.bfloat16)
    routed_count = jnp.sum(mask_all)
    gate_total = jnp.sum(mask_all * gating)
    expert_stats = jnp.stack(
        [routed_count / (token_count * hidden_size), gate_total / routed_count]
    )[:, None]
    cot_slots = jnp.dot(placing, cotangent, preferred_element_type=jnp.float32).astype(jnp.bfloat16)
    cot_arrived = lax.all_to_all(
        cot_slots.reshape(experts_here, capacity, features),
        EX,
        split_axis=0,
        concat_axis=0,
        tiled=True,
    )
    cot_rows = lax.all_gather(cot_arrived, HI, axis=0, tiled=True).reshape(-1, features)
    d_branch = (gating[:, None] * cot_rows.astype(jnp.float32)).astype(jnp.bfloat16)
    grad_down = jnp.einsum("gf,gd->fd", after_low, d_branch, preferred_element_type=jnp.float32)
    d_after = jnp.einsum("gd,fd->gf", d_branch, down_weight[0], preferred_element_type=jnp.float32)
    d_before = gelu_pull(d_after)[0].astype(jnp.bfloat16)
    grad_up = jnp.einsum("gd,gf->df", expert_low, d_before, preferred_element_type=jnp.float32)
    d_expert_normed = jnp.einsum(
        "gf,df->gd", d_before, up_weight[0], preferred_element_type=jnp.float32
    )
    d_rows, d_expert_gain, d_expert_bias = expert_pull(d_expert_normed)
    d_rows_own = lax.psum_scatter(
        d_rows.astype(jnp.bfloat16), HI, scatter_dimension=0, tiled=True
    ).astype(jnp.float32)
    cot_own = lax.dynamic_slice_in_dim(cot_rows, own_start, slot_rows, 0).astype(jnp.float32)
    rows_own = lax.dynamic_slice_in_dim(rows_float, own_start, slot_rows, 0)
    d_gating = jnp.sum(cot_own * branch_own, axis=-1)
    d_logit = d_gating * gating_own * (1.0 - gating_own)
    d_centroid = jnp.sum(d_logit[:, None] * rows_own, axis=0)
    d_sent = (d_rows_own + d_logit[:, None] * centroid).astype(jnp.bfloat16)
    back_slots = lax.all_to_all(
        d_sent.reshape(experts_here, capacity, features),
        EX,
        split_axis=0,
        concat_axis=0,
        tiled=True,
    )
    d_resid = cotangent.astype(jnp.float32) + jnp.einsum(
        "st,sd->td",
        placing,
        back_slots.reshape(slot_rows, features),
        preferred_element_type=jnp.float32,
    )
    vector_grad = lax.psum(jnp.stack([d_centroid, d_expert_gain, d_expert_bias])[None], HI)
    d_project = d_resid.astype(jnp.bfloat16)
    grad_out_proj = jnp.einsum("td,te->de", context, d_project, preferred_element_type=jnp.float32)
    d_context = jnp.einsum(
        "te,de->td", d_project, attn_full[3], preferred_element_type=jnp.float32
    ).astype(jnp.bfloat16)
    d_context = d_context.reshape(token_count, HEADS, head_dim)
    attn_probs = jnp.exp(score_rows() - log_total)
    probs_again = attn_probs.astype(jnp.bfloat16)
    d_probs = jnp.einsum("qhe,khe->hqk", d_context, values_all, preferred_element_type=jnp.float32)
    d_values = jnp.einsum(
        "hqk,qhe->khe", probs_again, d_context, preferred_element_type=jnp.float32
    ).astype(jnp.bfloat16)
    d_scores = (
        attn_probs * (d_probs - jnp.sum(d_probs * attn_probs, axis=-1, keepdims=True))
    ).astype(jnp.bfloat16)
    d_query = (
        jnp.einsum("hqk,khe->qhe", d_scores, keys_all, preferred_element_type=jnp.float32) * scaling
    ).astype(jnp.bfloat16)
    d_keys = (
        jnp.einsum("hqk,qhe->khe", d_scores, query, preferred_element_type=jnp.float32) * scaling
    ).astype(jnp.bfloat16)
    d_projected = jnp.stack(
        [
            d_query.reshape(token_count, features),
            d_keys.reshape(token_count, features),
            d_values.reshape(token_count, features),
        ]
    )
    grad_qkv = jnp.einsum(
        "td,ste->sde", normed_low, d_projected, preferred_element_type=jnp.float32
    )
    d_normed = jnp.einsum(
        "ste,sde->td", d_projected, attn_full[:3], preferred_element_type=jnp.float32
    )
    d_inputs, d_norm_gain, d_norm_bias = norm_pull(d_normed)
    token_grad = (d_resid + d_inputs).astype(jnp.bfloat16)
    grad_attn = jnp.concatenate([grad_qkv, grad_out_proj[None]], axis=0)
    grad_norm_param = jnp.stack([d_norm_gain, d_norm_bias])
    attn_shard, norm_shard = (
        lax.psum_scatter(grad_attn, BOTH, scatter_dimension=1, tiled=True),
        lax.psum_scatter(grad_norm_param, BOTH, scatter_dimension=1, tiled=True),
    )
    local_square = (
        jnp.sum(attn_shard * attn_shard)
        + jnp.sum(norm_shard * norm_shard)
        + jnp.sum(grad_up * grad_up)
        + jnp.sum(grad_down * grad_down)
        + jnp.sum(vector_grad * vector_grad) / hidden_size
    )
    grad_norm = jnp.sqrt(lax.psum(local_square, BOTH))
    clip_factor = clip_level / jnp.maximum(grad_norm, clip_level)
    attn_new = adam_step(
        attn_weight, attn_first, attn_second, attn_shard, clip_factor, rate_matrix, decay_rate
    )
    norm_new = adam_step(
        norm_param, norm_first, norm_second, norm_shard, clip_factor, rate_vector, 0.0
    )
    up_new = adam_step(
        up_weight.astype(jnp.float32),
        up_first,
        up_second,
        grad_up[None],
        clip_factor,
        rate_matrix,
        decay_rate,
    )
    down_new = adam_step(
        down_weight.astype(jnp.float32),
        down_first,
        down_second,
        grad_down[None],
        clip_factor,
        rate_matrix,
        decay_rate,
    )
    vector_new = adam_step(
        expert_vector, vector_first, vector_second, vector_grad, clip_factor, rate_vector, 0.0
    )
    return (
        block_out,
        token_grad,
        grad_norm,
        attn_new[0],
        attn_new[1],
        attn_new[2],
        norm_new[0],
        norm_new[1],
        norm_new[2],
        up_new[0],
        up_new[1],
        up_new[2],
        down_new[0],
        down_new[1],
        down_new[2],
        vector_new[0],
        vector_new[1],
        vector_new[2],
        expert_stats,
    )


def fast_shards(
    tokens,
    cotangent,
    routes,
    attn_weight,
    attn_first,
    attn_second,
    norm_param,
    norm_first,
    norm_second,
    up_weight,
    up_first,
    up_second,
    down_weight,
    down_first,
    down_second,
    expert_vector,
    vector_first,
    vector_second,
):
    experts = lax.axis_size(EX)
    count, width = tokens.shape
    cap = 2 * count // experts
    shard = attn_weight.shape[1]
    w_full, qkv, normed, ctx, resid, sent, placed, gains, cot_raw, cot_zero = attend(
        cap, tokens, attn_weight, norm_param, routes.reshape(1, count), cotangent
    )
    rows = lambda v: v.reshape(3, 1, width)
    d_sum, grad_up, grad_down, delta, vec_part, scal = expert_layer(
        cap, sent, placed, cot_raw, cot_zero, up_weight[0], down_weight[0], rows(expert_vector)
    )
    block_out, token_grad, attn_shard, norm_grads, vec_grads, facts, norm_shard = attend_back(
        cap,
        shard,
        d_sum,
        cotangent,
        w_full,
        qkv,
        normed,
        ctx,
        tokens,
        gains,
        placed,
        delta,
        resid,
        vec_part,
        scal,
    )
    flat = lambda v: v.reshape(-1, v.shape[-1])
    new = adam_all(
        [flat(v) for v in (up_weight, up_first, up_second, grad_up)],
        [flat(v) for v in (down_weight, down_first, down_second, grad_down)],
        [flat(v) for v in (attn_weight, attn_first, attn_second, attn_shard)],
        [rows(v) for v in (expert_vector, vector_first, vector_second)] + [vec_grads],
        [norm_param, norm_first, norm_second, norm_shard],
        facts,
        block_out,
        token_grad,
    )
    up_new = [v.reshape(up_weight.shape) for v in new[0:3]]
    down_new = [v.reshape(down_weight.shape) for v in new[3:6]]
    attn_new = [v.reshape(attn_weight.shape) for v in new[6:9]]
    vector_new = [v.reshape(expert_vector.shape) for v in new[9:12]]
    norm_new = new[12:15]
    block_out, token_grad = new[15:17]
    grad_norm = new[17].reshape(())
    expert_stats = new[18].reshape(2, 1)
    return (
        block_out,
        token_grad,
        grad_norm,
        *attn_new,
        *norm_new,
        *up_new,
        *down_new,
        *vector_new,
        expert_stats,
    )


def solution(mesh):
    small = mesh.shape[EX] == 8 and mesh.shape[HI] == 4
    return jax.shard_map(
        fast_shards if small else shards,
        mesh=mesh,
        in_specs=(
            P(BOTH, None),
            P(BOTH, None),
            P(BOTH, None),
            P(None, BOTH, None),
            P(None, BOTH, None),
            P(None, BOTH, None),
            P(None, BOTH),
            P(None, BOTH),
            P(None, BOTH),
            P(EX, None, HI),
            P(EX, None, HI),
            P(EX, None, HI),
            P(EX, HI, None),
            P(EX, HI, None),
            P(EX, HI, None),
            P(EX, None, None),
            P(EX, None, None),
            P(EX, None, None),
        ),
        out_specs=(
            P(BOTH, None),
            P(BOTH, None),
            P(),
            P(None, BOTH, None),
            P(None, BOTH, None),
            P(None, BOTH, None),
            P(None, BOTH),
            P(None, BOTH),
            P(None, BOTH),
            P(EX, None, HI),
            P(EX, None, HI),
            P(EX, None, HI),
            P(EX, HI, None),
            P(EX, HI, None),
            P(EX, HI, None),
            P(EX, None, None),
            P(EX, None, None),
            P(EX, None, None),
            P(None, EX),
        ),
        check_vma=False,
    )
```

```python
import functools
import math

import jax
import jax.numpy as jnp
from jax import lax
from jax.experimental import pallas as pl
from jax.experimental.pallas import tpu as pltpu
from jax.sharding import PartitionSpec as P

HEADS = 16
STEP = 10


norm_eps = 1e-05
clip_level = 1.0
beta_one = 0.9
beta_two = 0.999
adam_eps = 1e-08
decay_rate = 0.1
rate_matrix = 0.05
rate_vector = 0.5
masked_fill = -1e30
EX, HI = "expert", "hidden"
BOTH = (EX, HI)


def layer_norm(inputs, gain_row, bias_row):
    average = jnp.mean(inputs, axis=-1, keepdims=True)
    centred = inputs - average
    variance = jnp.mean(centred * centred, axis=-1, keepdims=True)
    return centred * lax.rsqrt(variance + norm_eps) * gain_row + bias_row


def gelu_exact(values):
    return jax.nn.gelu(values, approximate=False)


def adam_step(weight, first, second, grad, clip_factor, rate, decay):
    clipped = grad * clip_factor
    moment = beta_one * first + (1.0 - beta_one) * clipped
    square = beta_two * second + (1.0 - beta_two) * clipped * clipped
    corr_one = 1.0 - beta_one**STEP
    corr_two = 1.0 - beta_two**STEP
    update = moment / corr_one / (jnp.sqrt(square / corr_two) + adam_eps) + decay * weight
    return (weight - rate * update, moment, square)


MESH = pl.DeviceIdType.MESH
VMEM_SPEC = pl.BlockSpec(memory_space=pltpu.VMEM)
ANY_SPEC = pl.BlockSpec(memory_space=pl.ANY)


class Place:
    def __init__(self):
        self.e = lax.axis_index(EX)
        self.z = lax.axis_index(HI)
        high, low = lax.div(self.z, 2), lax.rem(self.z, 2)
        self.middle = high + low == 1
        self.ends = jnp.logical_not(self.middle)
        self.line = [self.z, self.z + 1 - 2 * low, 2 - high, 3 - 3 * high]
        self.core = lax.rem(self.e, 2)
        self.x = lax.rem(lax.div(self.e, 2), 2)
        self.y = lax.div(self.e, 4)
        self.ex = self.e + 2 - 4 * self.x
        self.ey = self.e + 4 - 8 * self.y
        self.exy = self.ex + 4 - 8 * self.y
        self.twin = (self.e + 1 - 2 * self.core, self.z)
        self.over_x = (self.ex, self.z)
        self.over_y = (self.ey, self.z)
        self.partner = (self.e, self.line[1])
        self.mirror = (self.e, 3 - self.z)
        self.mates = [None, self.partner, (self.e, self.z + 2 - 4 * high), self.mirror]

    def across(self, k):
        c = lax.rem(self.core + k % 2, 2)
        x = lax.rem(self.x + (k // 2) % 2, 2)
        y = lax.rem(self.y + k // 4, 2)
        return 4 * y + 2 * x + c

    def everyone(self):
        plane = [(self.across(k), self.z) for k in range(1, 8)]
        return plane + self.mates[1:]

    def meet(self):
        barrier = pltpu.get_barrier_semaphore()
        for device in self.everyone():
            pl.semaphore_signal(barrier, inc=1, device_id=device, device_id_type=MESH)
        pl.semaphore_wait(barrier, len(self.everyone()))


class Wire:
    def __init__(self, send_sem, recv_sem):
        self.send_sem, self.recv_sem = send_sem, recv_sem
        self.count = 0
        self.tags = {}
        self.sent = []

    def next(self):
        self.count += 1
        return self.count - 1

    def send(self, src, dst, device, tag=None, when=None):
        i = self.next()
        if tag is not None:
            if tag not in self.tags:
                self.tags[tag] = self.next()
            j = self.tags[tag]
        else:
            j = i
        copy = pltpu.make_async_remote_copy(
            src_ref=src,
            dst_ref=dst,
            send_sem=self.send_sem.at[i],
            recv_sem=self.recv_sem.at[j],
            device_id=device,
            device_id_type=MESH,
        )
        if when is None:
            copy.start()
        else:
            pl.when(when)(copy.start)
        self.sent.append((copy, when))
        return copy

    def arrived(self, tag, dst, device):
        if tag not in self.tags:
            self.tags[tag] = self.next()
        j = self.tags[tag]
        pltpu.make_async_remote_copy(
            src_ref=dst,
            dst_ref=dst,
            send_sem=self.send_sem.at[j],
            recv_sem=self.recv_sem.at[j],
            device_id=device,
            device_id_type=MESH,
        ).wait_recv()

    def left(self, copy):
        copy.wait_send()
        self.sent = [one for one in self.sent if one[0] is not copy]

    def drain(self):
        for copy, when in self.sent:
            if when is None:
                copy.wait_send()
            else:
                pl.when(when)(copy.wait_send)
        self.sent = []


class Line:
    def __init__(self, wire, at, name, slot):
        self.wire, self.at, self.name, self.slot = wire, at, name, slot

    def begin(self, own=None, outer=1, inner=True):
        at = self.at
        here = self.slot(at.z)
        own = here if own is None else own
        if outer:
            when = {1: None, 2: at.ends, 3: at.middle}[outer]
            self.wire.send(own, here, at.partner, (self.name, 1), when)
        if inner:
            self.wire.send(own, here, at.mirror, (self.name, 2), at.middle)

    def take(self, i, when=None):
        at = self.at
        block = self.slot(at.line[i])
        if when is None:
            self.wire.arrived((self.name, i), block, at.partner)
        else:
            pl.when(when)(lambda: self.wire.arrived((self.name, i), block, at.partner))
        if when is not at.ends:
            to, tag = (at.mirror, 3) if i == 1 else (at.partner, i)
            self.wire.send(block, block, to, (self.name, tag), at.middle)
        return block


class Fetch:
    def __init__(self, sem):
        self.sem = sem
        self.count = 0
        self.open = []

    def start(self, src, dst):
        copy = pltpu.make_async_copy(src, dst, self.sem.at[self.count])
        self.count += 1
        copy.start()
        self.open.append(copy)
        return copy

    def done(self, copy):
        copy.wait()
        self.open = [one for one in self.open if one is not copy]

    def drain(self):
        for copy in self.open:
            copy.wait()
        self.open = []


def dot(a, b, ca=1, cb=0):
    return lax.dot_general(a, b, (((ca,), (cb,)), ((), ())), preferred_element_type=jnp.float32)


def tile(i, size=256):
    return pl.ds(pl.multiple_of(i * size, size), size)


def pick(placed_row, slots):
    which = lax.broadcasted_iota(jnp.int32, (slots, placed_row.shape[1]), 0)
    return jnp.where(which == placed_row, 1.0, 0.0).astype(jnp.bfloat16)


def build(stage, source, placed_row):
    planes, cap, width = stage.shape
    onehot = pick(placed_row, planes * cap)

    @pl.loop(0, width // 512)
    def _(i):
        cols = tile(i, 512)
        value = dot(onehot, source[:, cols]).astype(jnp.bfloat16)
        for k in range(planes):
            stage[k, :, cols] = value[k * cap : (k + 1) * cap]


def attend_kernel(
    cap,
    tok,
    w_own,
    norm_in,
    route,
    cot,
    w_out,
    qkv_out,
    normed_out,
    ctx_out,
    resid_out,
    sent_out,
    placed_out,
    gains_out,
    cot_raw,
    cot_zero,
    w_low,
    wfull,
    norm_low,
    pieces,
    qkv,
    normed,
    ctx,
    resid,
    sent,
    placed,
    gains,
    stage,
    send_sem,
    recv_sem,
    local_sem,
):
    at = Place()
    e, z = at.e, at.z
    depth = 4
    count, width = tok.shape
    shard = w_own.shape[1]
    wire = Wire(send_sem, recv_sem)
    fetch = Fetch(local_sem)
    groups = [(0, 3), (3, 1)]
    fetch.start(cot, cot_raw.at[z])
    w_low[...] = w_own[...].astype(jnp.bfloat16)
    lanes = norm_in.shape[1]
    offset = lax.broadcasted_iota(jnp.int32, (lanes, 128), 1) - z * lanes
    ours = lax.broadcasted_iota(jnp.int32, (lanes, 128), 0) == offset
    low = norm_in[...].astype(jnp.bfloat16)
    norm_low[...] = jnp.zeros((16, 128), jnp.bfloat16)
    norm_low[0:2, :] = dot(low, jnp.where(ours, 1.0, 0.0).astype(jnp.bfloat16)).astype(
        jnp.bfloat16
    )
    at.meet()

    def block(g, who, zz):
        if g == 2:
            return pieces.at[who, zz]
        first, mats = groups[g]
        start = pl.multiple_of((who * depth + zz) * shard, shard)
        return wfull.at[pl.ds(first, mats), pl.ds(start, shard)]

    def mine(g):
        if g == 2:
            return norm_low
        first, mats = groups[g]
        return w_low.at[pl.ds(first, mats)]

    lines = [Line(wire, at, g, lambda zz, g=g: block(g, e, zz)) for g in range(3)]
    lines[2].begin(mine(2))
    lines[0].begin(mine(0))
    lines[1].begin(mine(1), outer=2, inner=False)
    cots = Line(wire, at, "cot", lambda zz: cot_raw.at[zz])
    cots.begin(cot, outer=2, inner=False)
    own = [fetch.start(mine(g), block(g, e, z)) for g in range(3)]
    to_x, to_y, to_far, to_twin = {}, {}, {}, {}

    def over_x(g, i):
        here = block(g, e, at.line[i])
        to_x[g, i] = wire.send(here, here, at.over_x)
        to_twin[g, i, 0] = wire.send(here, here, at.twin)

    def over_y(g, i):
        here = block(g, e, at.line[i])
        to_y[g, i] = wire.send(here, here, at.over_y)

    def forward(g, i):
        zz = at.line[i]
        if i in (0, 3):
            to_x[g, i].wait_recv()
            block_x = block(g, at.ex, zz)
            to_far[g, i] = wire.send(block_x, block_x, at.over_y)
            to_twin[g, i, 1] = wire.send(block_x, block_x, at.twin)
        else:
            to_y[g, i].wait_recv()
            block_y = block(g, at.ey, zz)
            to_far[g, i] = wire.send(block_y, block_y, at.over_x)
            to_twin[g, i, 1] = wire.send(block_y, block_y, at.twin)

    def side(g, i):
        zz = at.line[i]
        if i in (0, 3):
            to_y[g, i].wait_recv()
            there = block(g, at.ey, zz)
        else:
            to_x[g, i].wait_recv()
            there = block(g, at.ex, zz)
        to_twin[g, i, 2] = wire.send(there, there, at.twin)

    def far(g, i):
        to_far[g, i].wait_recv()
        there = block(g, at.exy, at.line[i])
        to_twin[g, i, 3] = wire.send(there, there, at.twin)

    def finish(g):
        for i in range(depth):
            for k in range(4):
                to_twin[g, i, k].wait_recv()

    def both(step, i):
        step(2, i)
        step(0, i)

    def take(i):
        lines[2].take(i)
        lines[0].take(i)

    for copy in (own[2], own[0]):
        fetch.done(copy)
    both(over_x, 0)
    both(over_y, 0)
    wide_r = lax.broadcasted_iota(jnp.int32, (count, count), 0)
    wide_c = lax.broadcasted_iota(jnp.int32, (count, count), 1)
    route_row = route[...].astype(jnp.float32)
    route_col = jnp.sum(jnp.where(wide_r == wide_c, route_row, 0.0), axis=1, keepdims=True)
    lane = lax.broadcasted_iota(jnp.int32, (count, 128), 1)
    chosen = jnp.where(route_col.astype(jnp.int32) == lane, 1.0, 0.0)
    rows_i = lax.broadcasted_iota(jnp.int32, (count, count), 0)
    cols_i = lax.broadcasted_iota(jnp.int32, (count, count), 1)
    lower = jnp.where(rows_i >= cols_i, 1.0, 0.0)
    running = dot(lower.astype(jnp.bfloat16), chosen.astype(jnp.bfloat16))
    rank = jnp.sum((running - 1.0) * chosen, axis=1, keepdims=True)
    column = route_col * float(cap) + rank
    row = jnp.sum(jnp.where(wide_r == wide_c, column, 0.0), axis=0, keepdims=True)
    row = jnp.concatenate([row, jnp.full((1, 256 - count), -1.0, jnp.float32)], axis=1)
    placed[z] = jnp.broadcast_to(row, (8, 256)).astype(jnp.int32)
    take(1)
    both(over_x, 1)
    both(over_y, 1)
    build(stage, cot, placed[z, 0:1, :count])
    both(forward, 0)
    take(2)
    lines[1].begin(mine(1), outer=3)
    both(forward, 1)
    both(over_y, 2)
    take(3)
    lines[1].take(1, at.middle)
    lines[1].take(2, at.middle)
    both(over_x, 3)
    both(over_x, 2)
    both(over_y, 3)
    both(side, 0)
    both(side, 1)
    both(far, 0)
    both(far, 1)
    lines[1].take(3, at.middle)
    cots.begin(cot, outer=0)
    both(forward, 2)
    both(forward, 3)
    cots.take(1, at.middle)
    places = Line(wire, at, "place", lambda zz: placed.at[zz])
    places.begin()
    fetch.done(own[1])
    for i in range(depth):
        if i:
            lines[1].take(i, at.ends)
        over_x(1, i)
        over_y(1, i)
    both(side, 3)
    both(side, 2)
    both(far, 2)
    both(far, 3)
    cots.take(2, at.middle)
    finish(2)
    cots.take(3, at.middle)
    gain_rows = jnp.concatenate(
        [
            sum([pieces[who, zz] for zz in range(1, depth)], pieces[who, 0])
            for who in range(8)
        ],
        axis=1,
    )
    tally = jnp.concatenate(
        [
            jnp.broadcast_to(jnp.sum(chosen, axis=0, keepdims=True), (16, 128)),
            jnp.zeros((16, width - 128), jnp.float32),
        ],
        axis=1,
    )
    third_row = lax.broadcasted_iota(jnp.int32, (16, width), 0) == 2
    gains[...] = jnp.where(third_row, tally, gain_rows.astype(jnp.float32)).astype(jnp.bfloat16)
    fetch.start(gains, gains_out)
    gain = gains[0:1, :].astype(jnp.float32)
    bias = gains[1:2, :].astype(jnp.float32)

    @pl.loop(0, count // 64)
    def _(i):
        rows = tile(i, 64)
        piece = tok[rows, :].astype(jnp.float32)
        average = jnp.mean(piece, axis=-1, keepdims=True)
        centred = piece - average
        variance = jnp.mean(centred * centred, axis=-1, keepdims=True)
        normed[rows, :] = (centred * lax.rsqrt(variance + norm_eps) * gain + bias).astype(
            jnp.bfloat16
        )

    fetch.start(normed, normed_out)
    finish(0)
    fetch.start(wfull.at[pl.ds(0, 3)], w_out.at[pl.ds(0, 3)])
    tiles = width // 256

    def project(i):
        m = lax.div(i, tiles)
        cols = tile(lax.rem(i, tiles))
        qkv[m, :, cols] = dot(normed[...], wfull[m, :, cols]).astype(jnp.bfloat16)

    pl.loop(0, tiles)(project)
    for i in range(depth):
        forward(1, i)
    slots_out = [
        wire.send(stage.at[at.across(k)], cot_zero.at[k], (at.across(k), z)) for k in range(1, 8)
    ]
    fetch.start(stage.at[e], cot_zero.at[0])
    places.take(1)
    pl.loop(tiles, 3 * tiles)(project)
    fetch.start(qkv, qkv_out)
    for i in range(depth):
        side(1, i)
    places.take(2, at.middle)
    causal = rows_i >= cols_i
    left = lax.broadcasted_iota(jnp.int32, (count, 128), 1) < 64
    scaling = jnp.asarray(64 ** (-0.5), jnp.bfloat16)

    def pair(i):
        cols = tile(i, 128)
        query = qkv[0, :, cols] * scaling
        keys = qkv[1, :, cols]
        values = qkv[2, :, cols]
        halves = []
        for side in range(2):
            mask = left if side == 0 else jnp.logical_not(left)
            scores = dot(jnp.where(mask, query, jnp.zeros_like(query)), keys, 1, 1)
            scores = jnp.where(causal, scores, masked_fill)
            top = jnp.max(scores, axis=-1, keepdims=True)
            expo = jnp.exp(scores - top)
            probs = expo / jnp.sum(expo, axis=-1, keepdims=True)
            halves.append(dot(probs.astype(jnp.bfloat16), values))
        ctx[:, cols] = jnp.where(left, halves[0], halves[1]).astype(jnp.bfloat16)

    pl.loop(0, 6, unroll=2)(pair)
    for i in range(depth):
        far(1, i)
    places.take(2, at.ends)
    places.take(3, at.middle)
    pl.loop(6, width // 128, unroll=2)(pair)
    fetch.start(ctx, ctx_out)
    finish(1)
    fetch.start(wfull.at[pl.ds(3, 1)], w_out.at[pl.ds(3, 1)])

    @pl.loop(0, tiles)
    def _(i):
        cols = tile(i)
        value = tok[:, cols].astype(jnp.float32) + dot(ctx[...], wfull[3, :, cols])
        resid[:, cols] = value
        sent[:, cols] = value.astype(jnp.bfloat16)

    fetch.start(sent, sent_out)
    fetch.start(resid, resid_out)
    places.take(3, at.ends)
    cots.take(2, at.ends)
    cots.take(3, at.ends)
    fetch.start(placed, placed_out)
    for copy in slots_out:
        copy.wait_recv()
    wire.drain()
    fetch.drain()


def attend(cap, tokens, w_own, norm_own, routes, cotangent):
    count, width = tokens.shape
    bf, full = jnp.bfloat16, jnp.float32
    copies = 176
    shapes = [
        ((4, width, width), bf),
        ((3, count, width), bf),
        ((count, width), bf),
        ((count, width), bf),
        ((count, width), full),
        ((count, width), bf),
        ((4, 8, 256), jnp.int32),
        ((16, width), bf),
        ((4, count, width), bf),
        ((8, cap, width), bf),
    ]
    return pl.pallas_call(
        functools.partial(attend_kernel, cap),
        out_shape=[jax.ShapeDtypeStruct(*one) for one in shapes],
        in_specs=[VMEM_SPEC] * 5,
        out_specs=[ANY_SPEC] * len(shapes),
        scratch_shapes=[
            pltpu.VMEM((4, w_own.shape[1], width), bf),
            pltpu.VMEM((4, width, width), bf),
            pltpu.VMEM((16, 128), bf),
            pltpu.VMEM((8, 4, 16, 128), bf),
            pltpu.VMEM((3, count, width), bf),
            pltpu.VMEM((count, width), bf),
            pltpu.VMEM((count, width), bf),
            pltpu.VMEM((count, width), full),
            pltpu.VMEM((count, width), bf),
            pltpu.VMEM((4, 8, 256), jnp.int32),
            pltpu.VMEM((16, width), bf),
            pltpu.VMEM((8, cap, width), bf),
            pltpu.SemaphoreType.DMA((copies,)),
            pltpu.SemaphoreType.DMA((copies,)),
            pltpu.SemaphoreType.DMA((16,)),
        ],
        compiler_params=pltpu.CompilerParams(
            collective_id=0, has_side_effects=True, vmem_limit_bytes=62 << 20
        ),
    )(tokens, w_own, norm_own, routes, cotangent)


def gelu_pair(v):
    cdf = 0.5 + 0.5 * lax.erf(v * (0.5**0.5))
    pdf = jnp.exp(-0.5 * v * v) * ((2.0 * math.pi) ** -0.5)
    return v * cdf, cdf + v * pdf


def fold(v):
    total = v[0:8]
    for i in range(8, v.shape[0], 8):
        total = total + v[i : i + 8]
    return total


def spread(column, lanes):
    return jnp.concatenate([column] * (lanes // 128), axis=1)


def square_lanes(v):
    total = v[:, 0:128] * v[:, 0:128]
    for i in range(128, v.shape[1], 128):
        total = total + v[:, i : i + 128] * v[:, i : i + 128]
    return total


def unslot(placed_row, slots, out):
    planes, cap, width = slots.shape
    onehot = pick(placed_row, planes * cap)

    @pl.loop(0, width // 256)
    def _(j):
        cols = tile(j)
        value = slots[:, :, cols].reshape(planes * cap, 256)
        out[:, cols] = dot(onehot, value, 0, 0).astype(jnp.bfloat16)


class Home:
    def __init__(self, wire, at, name, part, got):
        self.wire, self.at, self.name = wire, at, name
        self.part, self.got = part, got
        half = got.shape[1] // 2
        self.halves = [pl.ds(0, half), pl.ds(half, half)]

    def add(self, i, k, half):
        part = self.part(i)
        part[half, :] = (
            part[half, :].astype(jnp.float32) + self.got[k, half, :].astype(jnp.float32)
        ).astype(jnp.bfloat16)

    def arrived(self, tag, k, n, device):
        half = self.halves[n]
        self.wire.arrived((self.name, tag, n), self.got.at[k, half], device)

    def send(self, src, k, n, device, tag, when=None):
        half = self.halves[n]
        self.wire.send(src.at[half], self.got.at[k, half], device, (self.name, tag, n), when)

    def push(self, i):
        for n in range(2):
            self.send(self.part(i), i - 1, n, self.at.partner, i, self.at.ends)

    def pass_on(self, i):
        at = self.at
        k = {3: 3, 2: 4}[i]
        for n, half in enumerate(self.halves):

            @pl.when(at.middle)
            def _():
                self.arrived(i, i - 1, n, at.partner)
                self.add(i, i - 1, half)

            self.send(self.part(i), k, n, at.mirror, k + 1, at.middle)

    def near(self):
        at = self.at
        for n, half in enumerate(self.halves):

            @pl.when(at.middle)
            def _():
                self.arrived(4, 3, n, at.mirror)
                self.add(1, 3, half)

            self.send(self.part(1), 0, n, at.partner, 1)

    def relay_far(self):
        at = self.at
        for n in range(2):
            pl.when(at.middle)(lambda: self.arrived(4, 3, n, at.mirror))
            self.send(self.got.at[3], 0, n, at.partner, 1, at.middle)

    def finish(self):
        at = self.at
        for n, half in enumerate(self.halves):

            @pl.when(at.ends)
            def _():
                self.arrived(1, 0, n, at.partner)
                self.add(0, 0, half)

            @pl.when(at.middle)
            def _():
                self.arrived(5, 4, n, at.mirror)
                self.add(0, 4, half)

    def last(self):
        at = self.at
        for n, half in enumerate(self.halves):
            self.arrived(1, 0, n, at.partner)

            @pl.when(at.middle)
            def _():
                self.arrived(5, 4, n, at.mirror)
                self.add(0, 4, half)

    def total(self, cols):
        return self.part(0)[:, cols].astype(jnp.float32) + self.got[0, :, cols].astype(jnp.float32)


def expert_kernel(
    cap,
    sent_in,
    placed_in,
    cot_raw,
    cot_zero,
    up_in,
    down_in,
    vec,
    d_sum,
    g_up,
    g_down,
    delta_out,
    vec_part,
    scal,
    sent,
    placed,
    cot_line,
    up,
    down,
    raw,
    stage,
    rows,
    cots,
    xn,
    act,
    slope,
    delta,
    d_slots,
    back,
    part,
    z_in,
    d_xn,
    gate,
    d_logit,
    g_stage,
    send_sem,
    recv_sem,
    local_sem,
):
    at = Place()
    e, z = at.e, at.z
    depth, planes = 4, 8
    count, width = sent.shape
    slots = planes * cap
    units = up.shape[1]
    wire = Wire(send_sem, recv_sem)
    fetch = Fetch(local_sem)
    in_sent = fetch.start(sent_in, sent)
    in_placed = fetch.start(placed_in, placed)
    in_up = fetch.start(up_in, up)
    in_down = fetch.start(down_in, down)
    in_cot = fetch.start(cot_raw, cot_line)
    in_zero = fetch.start(cot_zero, cots.at[0])
    at.meet()
    fetch.done(in_sent)
    line = Line(wire, at, "row", lambda zz: raw.at[zz])
    line.begin(sent)
    vec_part[...] = jnp.zeros_like(vec_part)
    scal[...] = jnp.zeros_like(scal)
    fetch.done(in_placed)
    centroid = lambda: vec[0]
    row_copies, cot_copies, ret_copies = {}, {}, {}

    def exchange(i, dst, s, offsets=range(1, planes)):
        return [
            wire.send(stage.at[s, at.across(k)], dst.at[i, k], (at.across(k), z)) for k in offsets
        ]

    def slot_row(i):
        return placed[at.line[i], 0:1, :count]

    def rows_out(i):
        source = sent if i == 0 else raw.at[at.line[i]]
        build(stage.at[i], source, slot_row(i))
        row_copies[i] = exchange(i, rows, i)
        rows[i, 0] = stage[i, e]

    def cots_out(i, s, offsets):
        if i not in cot_copies:
            for copy in row_copies[s]:
                wire.left(copy)
            build(stage.at[s], cot_line.at[at.line[i]], slot_row(i))
            cot_copies[i] = []
            cots[i, 0] = stage[s, e]
        cot_copies[i] += exchange(i, cots, s, offsets)

    def forward(i):
        for copy in row_copies[i]:
            copy.wait_recv()
        gain, bias = vec[1], vec[2]

        @pl.loop(0, planes, unroll=2)
        def _(k):
            r = rows[i, k].astype(jnp.float32)
            logit = jnp.sum(r * centroid(), axis=-1, keepdims=True)
            g = jax.nn.sigmoid(logit)
            wide = jnp.broadcast_to(g, (cap, 128))
            gate[i, k] = wide
            scal[0:8] += fold(wide)
            average = jnp.mean(r, axis=-1, keepdims=True)
            centred = r - average
            variance = jnp.mean(centred * centred, axis=-1, keepdims=True)
            xn[i, pl.ds(pl.multiple_of(k * cap, 16), cap), :] = (
                centred * lax.rsqrt(variance + norm_eps) * gain + bias
            ).astype(jnp.bfloat16)

        if i == 0:
            fetch.done(in_up)

        @pl.loop(0, units // 512)
        def _(j):
            cols = tile(j, 512)
            value, rate = gelu_pair(dot(xn[i], up[:, cols]))
            act[i, :, cols] = value.astype(jnp.bfloat16)
            slope[i, :, cols] = rate.astype(jnp.bfloat16)

        if i == 0:
            fetch.done(in_down)

        @pl.loop(0, width // 512)
        def _(j):
            cols = tile(j, 512)
            branch = dot(act[i], down[:, cols])
            wide = spread(gate[i].reshape(slots, 128), 512)
            value = (wide * branch).astype(jnp.bfloat16)
            for k in range(planes):
                delta[i, k, :, cols] = value[k * cap : (k + 1) * cap]

        fetch.start(delta.at[i], delta_out.at[i])

    def backward(i):
        for copy in cot_copies[i]:
            copy.wait_recv()

        @pl.loop(0, planes, unroll=2)
        def _(k):
            c = cots[i, k].astype(jnp.float32)
            g = gate[i, k]
            inner = jnp.sum(c * delta[i, k].astype(jnp.float32), axis=-1, keepdims=True)
            dl = (1.0 - g) * inner
            d_logit[i, k] = dl
            cots[i, k] = (c * spread(g, width)).astype(jnp.bfloat16)
            vec_part[0] += fold(rows[i, k].astype(jnp.float32) * spread(dl, width))

        @pl.loop(0, units // 512)
        def _(j):
            cols = tile(j, 512)
            d_act = dot(cots[i].reshape(slots, width), down[cols, :], 1, 1)
            slope[i, :, cols] = (d_act * slope[i, :, cols].astype(jnp.float32)).astype(
                jnp.bfloat16
            )

    def backward_in(i):
        @pl.loop(0, width // 512)
        def _(j):
            cols = tile(j, 512)
            value = dot(slope[i], up[cols, :], 1, 1)
            for k in range(planes):
                d_xn[k, :, cols] = value[k * cap : (k + 1) * cap]

        @pl.loop(0, planes, unroll=2)
        def _(k):
            r = rows[i, k].astype(jnp.float32)
            average = jnp.mean(r, axis=-1, keepdims=True)
            centred = r - average
            variance = jnp.mean(centred * centred, axis=-1, keepdims=True)
            scale = lax.rsqrt(variance + norm_eps)
            hat = centred * scale
            dx = d_xn[k]
            vec_part[1] += fold(dx * hat)
            vec_part[2] += fold(dx)
            dh = dx * vec[1]
            first = jnp.mean(dh, axis=-1, keepdims=True)
            second = jnp.mean(dh * hat, axis=-1, keepdims=True)
            d_in = scale * (dh - first - hat * second)
            d_slots[i, k] = (d_in + spread(d_logit[i, k], width) * centroid()).astype(jnp.bfloat16)

    def give(i):
        ret_copies[i] = [
            wire.send(d_slots.at[i, k], back.at[i, e], (at.across(k), z))
            for k in range(1, planes)
        ]
        back[i, e] = d_slots[i, 0]

    home = Home(wire, at, "home", lambda i: part.at[i], z_in)

    def collect(i):
        for copy in ret_copies[i]:
            copy.wait_recv()
        unslot(slot_row(i), back.at[i], part.at[i])

    def weight_grad(lhs, rhs, index, out):
        @pl.loop(0, lhs.shape[-1] // 512)
        def _(j):
            cols = tile(j, 512)
            left = lhs[:, :, cols].reshape(depth * slots, 512)
            value = dot(left, rhs[...].reshape(depth * slots, rhs.shape[-1]), 0, 0)
            scal[8:16] += fold(square_lanes(value))
            g_stage[index, cols, :] = value.astype(jnp.bfloat16)

        fetch.start(g_stage.at[index], out)

    rows_out(0)
    line.take(1)
    line.take(2, at.middle)
    rows_out(1)
    fetch.done(in_cot)
    cots_out(3, 0, (2, 4, 6))
    forward(0)
    line.take(2, at.ends)
    line.take(3, at.middle)
    rows_out(2)
    forward(1)
    line.take(3, at.ends)
    rows_out(3)
    fetch.done(in_zero)
    cot_copies[0] = []
    cot_copies[1] = [wire.send(cot_zero, cots.at[1], at.partner)]
    cots_out(3, 0, (3, 5, 7, 1))
    forward(2)
    cots_out(2, 1, range(1, planes))
    forward(3)
    backward(3)
    backward_in(3)
    give(3)
    backward(2)
    backward_in(2)
    give(2)
    backward(1)
    backward_in(1)
    give(1)
    backward(0)
    collect(3)
    home.push(3)
    backward_in(0)
    give(0)
    collect(2)
    home.push(2)
    home.pass_on(3)
    weight_grad(act, cots, 0, g_down)
    collect(1)
    home.near()
    home.pass_on(2)
    weight_grad(xn, slope, 1, g_up)
    collect(0)
    home.last()

    @pl.loop(0, width // 256)
    def _(j):
        cols = tile(j)
        d_sum[:, cols] = home.total(cols)

    wire.drain()
    fetch.drain()


def expert_layer(cap, sent, placed, cot_raw, cot_zero, up, down, vec):
    count, width = sent.shape
    units = up.shape[1]
    depth = 4
    bf, full = jnp.bfloat16, jnp.float32
    slots = 8 * cap
    copies = 3 * 7 * depth + 56
    shapes = [
        ((count, width), full),
        ((width, units), bf),
        ((units, width), bf),
        ((depth, 8, cap, width), bf),
        ((3, 8, width), full),
        ((16, 128), full),
    ]
    big = pltpu.VMEM((depth, 8, cap, width), bf)
    return pl.pallas_call(
        functools.partial(expert_kernel, cap),
        out_shape=[jax.ShapeDtypeStruct(*one) for one in shapes],
        in_specs=[ANY_SPEC] * 6 + [VMEM_SPEC],
        out_specs=[VMEM_SPEC, ANY_SPEC, ANY_SPEC, ANY_SPEC, VMEM_SPEC, VMEM_SPEC],
        scratch_shapes=[
            pltpu.VMEM((count, width), bf),
            pltpu.VMEM((depth, 8, 256), jnp.int32),
            pltpu.VMEM((depth, count, width), bf),
            pltpu.VMEM((width, units), bf),
            pltpu.VMEM((units, width), bf),
            pltpu.VMEM((depth, count, width), bf),
            big,
            big,
            big,
            pltpu.VMEM((depth, slots, width), bf),
            pltpu.VMEM((depth, slots, units), bf),
            pltpu.VMEM((depth, slots, units), bf),
            big,
            big,
            big,
            pltpu.VMEM((depth, count, width), bf),
            pltpu.VMEM((5, count, width), bf),
            pltpu.VMEM((8, cap, width), full),
            pltpu.VMEM((depth, 8, cap, 128), full),
            pltpu.VMEM((depth, 8, cap, 128), full),
            pltpu.VMEM((2, max(width, units), max(width, units)), bf),
            pltpu.SemaphoreType.DMA((copies,)),
            pltpu.SemaphoreType.DMA((copies,)),
            pltpu.SemaphoreType.DMA((16,)),
        ],
        compiler_params=pltpu.CompilerParams(
            collective_id=1, has_side_effects=True, vmem_limit_bytes=62 << 20
        ),
    )(sent, placed, cot_raw, cot_zero, up, down, vec)


def reduce_kernel(
    cap,
    d_sum,
    cot,
    w_in,
    qkv_in,
    normed_in,
    ctx,
    tok,
    gains,
    placed,
    delta_in,
    resid,
    vec_part,
    scal,
    block_out,
    token_grad,
    shard_out,
    norm_out,
    vec_out,
    square_out,
    norm_shard,
    wfull,
    qkv,
    normed,
    delta,
    d_resid,
    d_proj,
    d_ctx,
    d_qkv,
    d_norm,
    stage,
    twin_in,
    x_in,
    y_in,
    x_last,
    y_last,
    done,
    z_last,
    back,
    part,
    z_in,
    near_in,
    small,
    small_in,
    square,
    send_sem,
    recv_sem,
    local_sem,
):
    at = Place()
    e, z = at.e, at.z
    depth, planes = 4, 8
    count, width = tok.shape
    shard = shard_out.shape[1]
    column = depth * shard
    half = column // 2
    wire = Wire(send_sem, recv_sem)
    fetch = Fetch(local_sem)
    in_delta = {i: fetch.start(delta_in.at[i], delta.at[i]) for i in (1, 3, 2, 0)}
    in_w = {m: fetch.start(w_in.at[m], wfull.at[m]) for m in (3, 2, 1, 0)}
    in_qkv = fetch.start(qkv_in, qkv)
    in_normed = fetch.start(normed_in, normed)
    at.meet()
    ret = {}
    home = Home(wire, at, "home", lambda i: part.at[i], z_in)

    def give(i):
        if i in in_delta:
            fetch.done(in_delta.pop(i))
        ret[i] = [
            wire.send(delta.at[i, k], back.at[i, e], (at.across(k), z)) for k in range(1, planes)
        ]
        back[i, e] = delta[i, 0]

    def collect(i):
        for copy in ret[i]:
            copy.wait_recv()
        unslot(placed[at.line[i], 0:1, :count], back.at[i], part.at[i])

    def weight_grad(m, left_ref, right):
        @pl.loop(0, planes)
        def _(i):
            cols = pl.ds(pl.multiple_of(i * column, column), column)
            value = dot(left_ref[:, cols], right[...], 0, 0).astype(jnp.bfloat16)
            stage[m, lax.div(i, 4), lax.rem(lax.div(i, 2), 2), lax.rem(i, 2)] = value

    other = 1 - at.core
    first, second, third, fourth, fifth = {}, {}, {}, {}, {}

    def to_core(m):
        first[m] = wire.send(stage.at[m, :, :, other], twin_in.at[m], at.twin)

    def to_plane(m):
        first[m].wait_recv()
        for j in range(2):
            for i in range(2):
                twin_in[m, j, i] = twin_in[m, j, i] + stage[m, j, i, at.core]
        second[m] = (
            wire.send(twin_in.at[m, :, 1 - at.x, pl.ds(0, half)], x_in.at[m], at.over_x),
            wire.send(twin_in.at[m, 1 - at.y, :, pl.ds(half, half)], y_in.at[m], at.over_y),
        )

    def to_last(m):
        second[m][0].wait_recv()
        for j in range(2):
            x_in[m, j] = x_in[m, j] + twin_in[m, j, at.x, 0:half]
        one = wire.send(x_in.at[m, 1 - at.y], x_last.at[m], at.over_y)
        second[m][1].wait_recv()
        for i in range(2):
            y_in[m, i] = y_in[m, i] + twin_in[m, at.y, i, half:]
        two = wire.send(y_in.at[m, 1 - at.x], y_last.at[m], at.over_x)
        third[m] = (one, two)

    def to_owner(m):
        third[m][0].wait_recv()
        pair = (2, shard, width)
        done[m, 0:2] = (x_in[m, at.y] + x_last[m]).reshape(pair)
        third[m][1].wait_recv()
        done[m, 2:4] = (y_in[m, at.x] + y_last[m]).reshape(pair)
        theirs = at.partner[1]
        fourth[m] = (
            wire.send(done.at[m, theirs], z_last.at[m, 0], at.partner),
            wire.send(done.at[m, 3 - theirs], z_last.at[m, 1], at.partner),
        )

    def cross(m):
        fourth[m][1].wait_recv()
        done[m, 3 - z] = done[m, 3 - z] + z_last[m, 1]
        fifth[m] = wire.send(done.at[m, 3 - z], z_last.at[m, 2], at.mirror)

    def own(m):
        fourth[m][0].wait_recv()
        fifth[m].wait_recv()
        total = done[m, z].astype(jnp.float32)
        for k in (0, 2):
            total = total + z_last[m, k].astype(jnp.float32)
        shard_out[m] = total

    fetch.done(in_delta[1])
    near_copy = wire.send(delta.at[1], near_in, at.partner)
    give(3)
    value = cot[...].astype(jnp.float32) + d_sum[...]
    d_resid[...] = value
    d_proj[...] = value.astype(jnp.bfloat16)
    weight_grad(3, ctx, d_proj)
    to_core(3)
    fetch.done(in_w[3])

    @pl.loop(0, width // 256)
    def _(j):
        cols = tile(j)
        d_ctx[:, cols] = dot(d_proj[...], wfull[3, cols, :], 1, 1).astype(jnp.bfloat16)

    to_plane(3)
    fetch.done(in_qkv)
    causal = lax.broadcasted_iota(jnp.int32, (count, count), 0) >= lax.broadcasted_iota(
        jnp.int32, (count, count), 1
    )
    left = lax.broadcasted_iota(jnp.int32, (count, 128), 1) < 64
    scaling = 64 ** (-0.5)

    def pair(i):
        cols = tile(i, 128)
        query = qkv[0, :, cols]
        keys = qkv[1, :, cols]
        values = qkv[2, :, cols]
        d_out = d_ctx[:, cols]
        zero = jnp.zeros_like(query)
        got = []
        for side in range(2):
            mask = left if side == 0 else jnp.logical_not(left)
            q_side = jnp.where(mask, query, zero)
            k_side = jnp.where(mask, keys, zero)
            o_side = jnp.where(mask, d_out, zero)
            scores = dot(q_side, keys, 1, 1) * scaling
            scores = jnp.where(causal, scores, masked_fill)
            top = jnp.max(scores, axis=-1, keepdims=True)
            expo = jnp.exp(scores - top)
            probs = expo / jnp.sum(expo, axis=-1, keepdims=True)
            d_probs = dot(o_side, values, 1, 1)
            inner = jnp.sum(d_probs * probs, axis=-1, keepdims=True)
            d_scores = (probs * (d_probs - inner)).astype(jnp.bfloat16)
            got.append(
                (
                    dot(d_scores, k_side),
                    dot(d_scores, q_side, 0, 0),
                    dot(probs.astype(jnp.bfloat16), o_side, 0, 0),
                )
            )
        d_qkv[0, :, cols] = ((got[0][0] + got[1][0]) * scaling).astype(jnp.bfloat16)
        d_qkv[1, :, cols] = ((got[0][1] + got[1][1]) * scaling).astype(jnp.bfloat16)
        d_qkv[2, :, cols] = (got[0][2] + got[1][2]).astype(jnp.bfloat16)

    pl.loop(0, width // 256, unroll=2)(pair)
    give(2)
    pl.loop(width // 256, width // 128, unroll=2)(pair)
    collect(3)
    home.push(3)
    fetch.done(in_normed)
    weight_grad(2, normed, d_qkv.at[2])
    to_core(2)
    to_last(3)
    weight_grad(1, normed, d_qkv.at[1])
    to_core(1)
    to_plane(2)
    weight_grad(0, normed, d_qkv.at[0])
    to_core(0)
    home.pass_on(3)
    to_owner(3)
    to_plane(1)
    collect(2)
    home.push(2)
    for m in (2, 1, 0):
        fetch.done(in_w[m])

    @pl.loop(0, width // 256)
    def _(j):
        cols = tile(j)
        d_norm[:, cols] = (
            dot(d_qkv[0], wfull[0, cols, :], 1, 1)
            + dot(d_qkv[1], wfull[1, cols, :], 1, 1)
            + dot(d_qkv[2], wfull[2, cols, :], 1, 1)
        )

    gain = gains[0:1, :].astype(jnp.float32)
    d_gain = jnp.zeros((8, width), jnp.float32)
    d_bias = jnp.zeros((8, width), jnp.float32)
    for i in range(0, count, 64):
        piece = tok[i : i + 64, :].astype(jnp.float32)
        average = jnp.mean(piece, axis=-1, keepdims=True)
        centred = piece - average
        variance = jnp.mean(centred * centred, axis=-1, keepdims=True)
        scale = lax.rsqrt(variance + norm_eps)
        hat = centred * scale
        dx = d_norm[i : i + 64, :]
        d_gain = d_gain + fold(dx * hat)
        d_bias = d_bias + fold(dx)
        dh = dx * gain
        mean_one = jnp.mean(dh, axis=-1, keepdims=True)
        mean_two = jnp.mean(dh * hat, axis=-1, keepdims=True)
        d_in = scale * (dh - mean_one - hat * mean_two)
        token_grad[i : i + 64, :] = (d_resid[i : i + 64, :] + d_in).astype(jnp.bfloat16)
    mine = small.at[0]
    mine[...] = jnp.zeros((8, width), jnp.float32)
    mine[2:3, :] = gains[2:3, :].astype(jnp.float32)
    mine[0:1, :] = jnp.sum(d_gain, axis=0, keepdims=True)
    mine[1:2, :] = jnp.sum(d_bias, axis=0, keepdims=True)
    for k in range(3):
        mine[3 + k : 4 + k, :] = jnp.sum(vec_part[k], axis=0, keepdims=True)
    small_copy = wire.send(mine, small.at[1], at.partner)
    to_last(2)
    home.relay_far()
    home.pass_on(2)
    near_copy.wait_recv()
    fetch.done(in_delta.pop(0))

    @pl.loop(0, planes)
    def _(k):
        delta[0, k] = (delta[0, k].astype(jnp.float32) + near_in[k].astype(jnp.float32)).astype(
            jnp.bfloat16
        )

    to_plane(0)
    cross(3)
    small_copy.wait_recv()
    small[2] = small[0] + small[1]
    small_copy = wire.send(small.at[2], small.at[3], at.mirror)
    to_last(1)
    to_owner(2)
    own(3)
    to_last(0)
    cross(2)
    small_copy.wait_recv()
    total = small[2] + small[3]
    vec_out[...] = total
    small_in[e] = total
    spot = small_in.at[e]
    plane_copies = [wire.send(spot, spot, (at.across(k), z)) for k in range(1, planes)]
    give(0)
    to_owner(1)
    own(2)
    to_owner(0)
    cross(1)
    cross(0)
    own(1)
    for copy in plane_copies:
        copy.wait_recv()
    total = small_in[0]
    for k in range(1, planes):
        total = total + small_in[k]
    norm_out[...] = total
    norm_rows = norm_out[0:2, :]
    mine = norm_out[0:2, tile(e, 128)]
    lanes = norm_shard.shape[1]
    value = mine[:, 0:lanes]
    for k in range(1, depth):
        value = jnp.where(z == k, mine[:, k * lanes : (k + 1) * lanes], value)
    norm_shard[...] = value
    lane = lax.broadcasted_iota(jnp.int32, (1, 128), 1)
    routed = jnp.sum(jnp.where(lane == e, norm_out[2:3, 0:128], 0.0), keepdims=True)
    gates = jnp.sum(scal[0:8, 0:1], keepdims=True) - 0.5 * (depth * planes * cap - routed)
    vec_rows = vec_out[3:6, :]
    squares = jnp.sum(norm_rows * norm_rows, axis=0, keepdims=True) / (planes * depth) + jnp.sum(
        vec_rows * vec_rows, axis=0, keepdims=True
    ) / depth
    local = scal[8:16, :]
    for m in (3, 2, 1):
        local = local + fold(square_lanes(shard_out[m]))
    lane_squares = squares[:, 0:128]
    for i in range(128, width, 128):
        lane_squares = lane_squares + squares[:, i : i + 128]
    head = lax.broadcasted_iota(jnp.int32, (8, 128), 0) == 0
    local = local + jnp.where(head, jnp.broadcast_to(lane_squares, (8, 128)), 0.0)
    own(0)
    square[0, e] = local + fold(square_lanes(shard_out[0]))
    spot = square.at[0, e]
    copies = [wire.send(spot, spot, (at.across(k), z)) for k in range(1, planes)]
    collect(0)
    home.finish()

    @pl.loop(0, width // 256)
    def _(j):
        cols = tile(j)
        block_out[:, cols] = (resid[:, cols] + part[0, :, cols].astype(jnp.float32)).astype(
            jnp.bfloat16
        )

    for copy in copies:
        copy.wait_recv()
    total = square[0, 0]
    for k in range(1, planes):
        total = total + square[0, k]
    square[1, z] = total
    spot = square.at[1, z]
    copies = [wire.send(spot, spot, at.mates[k]) for k in range(1, depth)]
    for copy in copies:
        copy.wait_recv()
    total = square[1, 0]
    for d in range(1, depth):
        total = total + square[1, d]
    norm = jnp.sqrt(jnp.sum(total, keepdims=True))
    which = lax.broadcasted_iota(jnp.int32, (8, 128), 0)
    stats = jnp.where(which == 0, routed / (count * depth), gates / routed)
    clip = clip_level / jnp.maximum(norm, clip_level)
    square_out[...] = jnp.where(which < 2, stats, jnp.where(which == 2, norm, clip))
    wire.drain()
    fetch.drain()


def attend_back(cap, shard, *args):
    tokens = args[6]
    count, width = tokens.shape
    depth = 4
    bf, full = jnp.bfloat16, jnp.float32
    column = depth * shard
    half = column // 2
    copies = 7 * depth + 96
    shapes = [
        ((count, width), bf),
        ((count, width), bf),
        ((4, shard, width), full),
        ((8, width), full),
        ((8, width), full),
        ((8, 128), full),
        ((2, width // 32), full),
    ]
    return pl.pallas_call(
        functools.partial(reduce_kernel, cap),
        out_shape=[jax.ShapeDtypeStruct(*one) for one in shapes],
        in_specs=[VMEM_SPEC] * 2
        + [ANY_SPEC] * 3
        + [VMEM_SPEC] * 4
        + [ANY_SPEC]
        + [VMEM_SPEC] * 3,
        out_specs=[VMEM_SPEC] * 7,
        scratch_shapes=[
            pltpu.VMEM((4, width, width), bf),
            pltpu.VMEM((3, count, width), bf),
            pltpu.VMEM((count, width), bf),
            pltpu.VMEM((depth, 8, cap, width), bf),
            pltpu.VMEM((count, width), full),
            pltpu.VMEM((count, width), bf),
            pltpu.VMEM((count, width), bf),
            pltpu.VMEM((3, count, width), bf),
            pltpu.VMEM((count, width), full),
            pltpu.VMEM((4, 2, 2, 2, column, width), bf),
            pltpu.VMEM((4, 2, 2, column, width), bf),
            pltpu.VMEM((4, 2, half, width), bf),
            pltpu.VMEM((4, 2, half, width), bf),
            pltpu.VMEM((4, half, width), bf),
            pltpu.VMEM((4, half, width), bf),
            pltpu.VMEM((4, depth, shard, width), bf),
            pltpu.VMEM((4, depth - 1, shard, width), bf),
            pltpu.VMEM((depth, 8, cap, width), bf),
            pltpu.VMEM((depth, count, width), bf),
            pltpu.VMEM((5, count, width), bf),
            pltpu.VMEM((8, cap, width), bf),
            pltpu.VMEM((4, 8, width), full),
            pltpu.VMEM((8, 8, width), full),
            pltpu.VMEM((2, 8, 8, 128), full),
            pltpu.SemaphoreType.DMA((copies,)),
            pltpu.SemaphoreType.DMA((copies,)),
            pltpu.SemaphoreType.DMA((16,)),
        ],
        compiler_params=pltpu.CompilerParams(
            collective_id=2, has_side_effects=True, vmem_limit_bytes=62 << 20
        ),
    )(*args)


def adam_quick(weight, first, second, grad, clip_factor, rate, decay):
    clipped = grad * clip_factor
    moment = beta_one * first + (1.0 - beta_one) * clipped
    square = beta_two * second + (1.0 - beta_two) * clipped * clipped
    root = jnp.sqrt(square * (1.0 / (1.0 - beta_two**STEP))) + adam_eps
    step = moment * (rate / (1.0 - beta_one**STEP)) / root
    return (weight * (1.0 - rate * decay) - step, moment, square)


def adam_kernel(*refs):
    ins, outs = refs[:23], refs[23:]
    facts, block_in, token_in = ins[20:23]
    clip = facts[3:4, 0:1]
    for k in range(3):
        weight, first, second, grad = ins[4 * k : 4 * k + 4]
        new, moment, square = outs[3 * k : 3 * k + 3]
        new[...], moment[...], square[...] = adam_quick(
            weight[...].astype(jnp.float32),
            first[...],
            second[...],
            grad[...].astype(jnp.float32),
            clip,
            rate_matrix,
            decay_rate,
        )

    @pl.when(pl.program_id(0) == 0)
    def _():
        weight, first, second, grad = ins[12:16]
        for k in range(3):
            got = adam_quick(
                weight[k], first[k], second[k], grad[3 + k : 4 + k, :], clip, rate_vector, 0.0
            )
            for out, value in zip(outs[9:12], got):
                out[k] = value
        weight, first, second, grad = ins[16:20]
        got = adam_quick(
            weight[...], first[...], second[...], grad[...], clip, rate_vector, 0.0
        )
        for out, value in zip(outs[12:15], got):
            out[...] = value
        outs[15][...] = block_in[...]
        outs[16][...] = token_in[...]
        outs[17][...] = facts[2:3, 0:1]
        outs[18][...] = jnp.concatenate([facts[0:1, 0:1], facts[1:2, 0:1]], axis=1)


def adam_all(up, down, attn, vector, norm, facts, block_out, token_grad):
    steps = 8
    full = jnp.float32

    def whole(shape):
        return pl.BlockSpec(shape, lambda i: (0,) * len(shape))

    def cut(v):
        return pl.BlockSpec((v.shape[0] // steps, v.shape[1]), lambda i: (i, 0))

    args, in_specs, out_specs, shapes = [], [], [], []
    for group in (up, down, attn):
        args += group
        in_specs += [cut(v) for v in group]
        out_specs += [cut(group[0])] * 3
        shapes += [jax.ShapeDtypeStruct(group[0].shape, full)] * 3
    for group in (vector, norm):
        args += group
        in_specs += [whole(v.shape) for v in group]
        out_specs += [whole(group[0].shape)] * 3
        shapes += [jax.ShapeDtypeStruct(group[0].shape, full)] * 3
    args += [facts]
    in_specs += [whole(facts.shape)]
    for v in (block_out, token_grad):
        args += [v]
        in_specs += [whole(v.shape)]
        out_specs += [whole(v.shape)]
        shapes += [jax.ShapeDtypeStruct(v.shape, v.dtype)]
    for shape in ((1, 1), (1, 2)):
        out_specs += [whole(shape)]
        shapes += [jax.ShapeDtypeStruct(shape, full)]
    return pl.pallas_call(
        adam_kernel,
        grid=(steps,),
        out_shape=shapes,
        in_specs=in_specs,
        out_specs=out_specs,
        compiler_params=pltpu.CompilerParams(vmem_limit_bytes=60 << 20),
    )(*args)


def shards(
    tokens,
    cotangent,
    routes,
    attn_weight,
    attn_first,
    attn_second,
    norm_param,
    norm_first,
    norm_second,
    up_weight,
    up_first,
    up_second,
    down_weight,
    down_first,
    down_second,
    expert_vector,
    vector_first,
    vector_second,
):
    experts_here = lax.axis_size(EX)
    hidden_size = lax.axis_size(HI)
    token_count = tokens.shape[0]
    features = tokens.shape[1]
    capacity = 2 * token_count // experts_here
    slot_rows = experts_here * capacity
    head_dim = features // HEADS
    scaling = head_dim ** (-0.5)
    attn_low = attn_weight.astype(jnp.bfloat16)
    norm_low = norm_param.astype(jnp.bfloat16)
    attn_full, norm_full = (
        lax.all_gather(attn_low, BOTH, axis=1, tiled=True),
        lax.all_gather(norm_low, BOTH, axis=1, tiled=True),
    )
    inputs = tokens.astype(jnp.float32)
    normed, norm_pull = jax.vjp(
        layer_norm, inputs, norm_full[0].astype(jnp.float32), norm_full[1].astype(jnp.float32)
    )
    normed_low = normed.astype(jnp.bfloat16)
    projected = jnp.einsum(
        "td,sde->ste", normed_low, attn_full[:3], preferred_element_type=jnp.float32
    ).astype(jnp.bfloat16)
    query = projected[0].reshape(token_count, HEADS, head_dim)
    keys_all = projected[1].reshape(token_count, HEADS, head_dim)
    values_all = projected[2].reshape(token_count, HEADS, head_dim)
    causal = jnp.arange(token_count)[:, None] >= jnp.arange(token_count)[None, :]

    def score_rows():
        raw = (
            jnp.einsum("qhe,khe->hqk", query, keys_all, preferred_element_type=jnp.float32)
            * scaling
        )
        return jnp.where(causal[None], raw, masked_fill)

    scores = score_rows()
    row_max = jnp.max(scores, axis=-1, keepdims=True)
    expo = jnp.exp(scores - row_max)
    row_total = jnp.sum(expo, axis=-1, keepdims=True)
    log_total = row_max + jnp.log(row_total)
    probs_low = (expo / row_total).astype(jnp.bfloat16)
    context = jnp.einsum("hqk,khe->qhe", probs_low, values_all, preferred_element_type=jnp.float32)
    context = context.reshape(token_count, features).astype(jnp.bfloat16)
    resid = inputs + jnp.dot(context, attn_full[3], preferred_element_type=jnp.float32)
    route = routes[:, 0]
    chosen = (route[:, None] == jnp.arange(experts_here, dtype=jnp.int32)[None, :]).astype(
        jnp.int32
    )
    ranked = jnp.sum((jnp.cumsum(chosen, axis=0) - 1) * chosen, axis=1)
    placed = route * capacity + ranked
    placing = (jnp.arange(slot_rows, dtype=jnp.int32)[:, None] == placed[None, :]).astype(
        jnp.bfloat16
    )
    outgoing = jnp.dot(
        placing, resid.astype(jnp.bfloat16), preferred_element_type=jnp.float32
    ).astype(jnp.bfloat16)
    occupied = jnp.sum(placing.astype(jnp.float32), axis=1).astype(jnp.bfloat16)
    arrived, arrived_mask = (
        lax.all_to_all(
            outgoing.reshape(experts_here, capacity, features),
            EX,
            split_axis=0,
            concat_axis=0,
            tiled=True,
        ),
        lax.all_to_all(
            occupied.reshape(experts_here, capacity),
            EX,
            split_axis=0,
            concat_axis=0,
            tiled=True,
        ),
    )
    gathered, gathered_mask = (
        lax.all_gather(arrived, HI, axis=0, tiled=True),
        lax.all_gather(arrived_mask, HI, axis=0, tiled=True),
    )
    rows_all = gathered.reshape(-1, features)
    mask_all = gathered_mask.reshape(-1).astype(jnp.float32)
    rows_float = rows_all.astype(jnp.float32)
    centroid = expert_vector[0, 0]
    gating = jax.nn.sigmoid(jnp.sum(rows_float * centroid, axis=-1))
    expert_normed, expert_pull = jax.vjp(
        layer_norm, rows_float, expert_vector[0, 1], expert_vector[0, 2]
    )
    expert_low = expert_normed.astype(jnp.bfloat16)
    before = jnp.dot(expert_low, up_weight[0], preferred_element_type=jnp.float32)
    after, gelu_pull = jax.vjp(gelu_exact, before)
    after_low = after.astype(jnp.bfloat16)
    branch_own = lax.psum_scatter(
        jnp.dot(after_low, down_weight[0], preferred_element_type=jnp.float32).astype(jnp.bfloat16),
        HI,
        scatter_dimension=0,
        tiled=True,
    ).astype(jnp.float32)
    own_start = lax.axis_index(HI) * slot_rows
    gating_own = lax.dynamic_slice_in_dim(gating, own_start, slot_rows, 0)
    delta = (gating_own[:, None] * branch_own).astype(jnp.bfloat16)
    returned = lax.all_to_all(
        delta.reshape(experts_here, capacity, features),
        EX,
        split_axis=0,
        concat_axis=0,
        tiled=True,
    )
    delta_tokens = jnp.einsum(
        "st,sd->td",
        placing,
        returned.reshape(slot_rows, features),
        preferred_element_type=jnp.float32,
    )
    block_out = (resid + delta_tokens).astype(jnp.bfloat16)
    routed_count = jnp.sum(mask_all)
    gate_total = jnp.sum(mask_all * gating)
    expert_stats = jnp.stack(
        [routed_count / (token_count * hidden_size), gate_total / routed_count]
    )[:, None]
    cot_slots = jnp.dot(placing, cotangent, preferred_element_type=jnp.float32).astype(jnp.bfloat16)
    cot_arrived = lax.all_to_all(
        cot_slots.reshape(experts_here, capacity, features),
        EX,
        split_axis=0,
        concat_axis=0,
        tiled=True,
    )
    cot_rows = lax.all_gather(cot_arrived, HI, axis=0, tiled=True).reshape(-1, features)
    d_branch = (gating[:, None] * cot_rows.astype(jnp.float32)).astype(jnp.bfloat16)
    grad_down = jnp.einsum("gf,gd->fd", after_low, d_branch, preferred_element_type=jnp.float32)
    d_after = jnp.einsum("gd,fd->gf", d_branch, down_weight[0], preferred_element_type=jnp.float32)
    d_before = gelu_pull(d_after)[0].astype(jnp.bfloat16)
    grad_up = jnp.einsum("gd,gf->df", expert_low, d_before, preferred_element_type=jnp.float32)
    d_expert_normed = jnp.einsum(
        "gf,df->gd", d_before, up_weight[0], preferred_element_type=jnp.float32
    )
    d_rows, d_expert_gain, d_expert_bias = expert_pull(d_expert_normed)
    d_rows_own = lax.psum_scatter(
        d_rows.astype(jnp.bfloat16), HI, scatter_dimension=0, tiled=True
    ).astype(jnp.float32)
    cot_own = lax.dynamic_slice_in_dim(cot_rows, own_start, slot_rows, 0).astype(jnp.float32)
    rows_own = lax.dynamic_slice_in_dim(rows_float, own_start, slot_rows, 0)
    d_gating = jnp.sum(cot_own * branch_own, axis=-1)
    d_logit = d_gating * gating_own * (1.0 - gating_own)
    d_centroid = jnp.sum(d_logit[:, None] * rows_own, axis=0)
    d_sent = (d_rows_own + d_logit[:, None] * centroid).astype(jnp.bfloat16)
    back_slots = lax.all_to_all(
        d_sent.reshape(experts_here, capacity, features),
        EX,
        split_axis=0,
        concat_axis=0,
        tiled=True,
    )
    d_resid = cotangent.astype(jnp.float32) + jnp.einsum(
        "st,sd->td",
        placing,
        back_slots.reshape(slot_rows, features),
        preferred_element_type=jnp.float32,
    )
    vector_grad = lax.psum(jnp.stack([d_centroid, d_expert_gain, d_expert_bias])[None], HI)
    d_project = d_resid.astype(jnp.bfloat16)
    grad_out_proj = jnp.einsum("td,te->de", context, d_project, preferred_element_type=jnp.float32)
    d_context = jnp.einsum(
        "te,de->td", d_project, attn_full[3], preferred_element_type=jnp.float32
    ).astype(jnp.bfloat16)
    d_context = d_context.reshape(token_count, HEADS, head_dim)
    attn_probs = jnp.exp(score_rows() - log_total)
    probs_again = attn_probs.astype(jnp.bfloat16)
    d_probs = jnp.einsum("qhe,khe->hqk", d_context, values_all, preferred_element_type=jnp.float32)
    d_values = jnp.einsum(
        "hqk,qhe->khe", probs_again, d_context, preferred_element_type=jnp.float32
    ).astype(jnp.bfloat16)
    d_scores = (
        attn_probs * (d_probs - jnp.sum(d_probs * attn_probs, axis=-1, keepdims=True))
    ).astype(jnp.bfloat16)
    d_query = (
        jnp.einsum("hqk,khe->qhe", d_scores, keys_all, preferred_element_type=jnp.float32) * scaling
    ).astype(jnp.bfloat16)
    d_keys = (
        jnp.einsum("hqk,qhe->khe", d_scores, query, preferred_element_type=jnp.float32) * scaling
    ).astype(jnp.bfloat16)
    d_projected = jnp.stack(
        [
            d_query.reshape(token_count, features),
            d_keys.reshape(token_count, features),
            d_values.reshape(token_count, features),
        ]
    )
    grad_qkv = jnp.einsum(
        "td,ste->sde", normed_low, d_projected, preferred_element_type=jnp.float32
    )
    d_normed = jnp.einsum(
        "ste,sde->td", d_projected, attn_full[:3], preferred_element_type=jnp.float32
    )
    d_inputs, d_norm_gain, d_norm_bias = norm_pull(d_normed)
    token_grad = (d_resid + d_inputs).astype(jnp.bfloat16)
    grad_attn = jnp.concatenate([grad_qkv, grad_out_proj[None]], axis=0)
    grad_norm_param = jnp.stack([d_norm_gain, d_norm_bias])
    attn_shard, norm_shard = (
        lax.psum_scatter(grad_attn, BOTH, scatter_dimension=1, tiled=True),
        lax.psum_scatter(grad_norm_param, BOTH, scatter_dimension=1, tiled=True),
    )
    local_square = (
        jnp.sum(attn_shard * attn_shard)
        + jnp.sum(norm_shard * norm_shard)
        + jnp.sum(grad_up * grad_up)
        + jnp.sum(grad_down * grad_down)
        + jnp.sum(vector_grad * vector_grad) / hidden_size
    )
    grad_norm = jnp.sqrt(lax.psum(local_square, BOTH))
    clip_factor = clip_level / jnp.maximum(grad_norm, clip_level)
    attn_new = adam_step(
        attn_weight, attn_first, attn_second, attn_shard, clip_factor, rate_matrix, decay_rate
    )
    norm_new = adam_step(
        norm_param, norm_first, norm_second, norm_shard, clip_factor, rate_vector, 0.0
    )
    up_new = adam_step(
        up_weight.astype(jnp.float32),
        up_first,
        up_second,
        grad_up[None],
        clip_factor,
        rate_matrix,
        decay_rate,
    )
    down_new = adam_step(
        down_weight.astype(jnp.float32),
        down_first,
        down_second,
        grad_down[None],
        clip_factor,
        rate_matrix,
        decay_rate,
    )
    vector_new = adam_step(
        expert_vector, vector_first, vector_second, vector_grad, clip_factor, rate_vector, 0.0
    )
    return (
        block_out,
        token_grad,
        grad_norm,
        attn_new[0],
        attn_new[1],
        attn_new[2],
        norm_new[0],
        norm_new[1],
        norm_new[2],
        up_new[0],
        up_new[1],
        up_new[2],
        down_new[0],
        down_new[1],
        down_new[2],
        vector_new[0],
        vector_new[1],
        vector_new[2],
        expert_stats,
    )


def fast_shards(
    tokens,
    cotangent,
    routes,
    attn_weight,
    attn_first,
    attn_second,
    norm_param,
    norm_first,
    norm_second,
    up_weight,
    up_first,
    up_second,
    down_weight,
    down_first,
    down_second,
    expert_vector,
    vector_first,
    vector_second,
):
    experts = lax.axis_size(EX)
    count, width = tokens.shape
    cap = 2 * count // experts
    shard = attn_weight.shape[1]
    w_full, qkv, normed, ctx, resid, sent, placed, gains, cot_raw, cot_zero = attend(
        cap, tokens, attn_weight, norm_param, routes.reshape(1, count), cotangent
    )
    rows = lambda v: v.reshape(3, 1, width)
    d_sum, grad_up, grad_down, delta, vec_part, scal = expert_layer(
        cap, sent, placed, cot_raw, cot_zero, up_weight[0], down_weight[0], rows(expert_vector)
    )
    block_out, token_grad, attn_shard, norm_grads, vec_grads, facts, norm_shard = attend_back(
        cap,
        shard,
        d_sum,
        cotangent,
        w_full,
        qkv,
        normed,
        ctx,
        tokens,
        gains,
        placed,
        delta,
        resid,
        vec_part,
        scal,
    )
    flat = lambda v: v.reshape(-1, v.shape[-1])
    new = adam_all(
        [flat(v) for v in (up_weight, up_first, up_second, grad_up)],
        [flat(v) for v in (down_weight, down_first, down_second, grad_down)],
        [flat(v) for v in (attn_weight, attn_first, attn_second, attn_shard)],
        [rows(v) for v in (expert_vector, vector_first, vector_second)] + [vec_grads],
        [norm_param, norm_first, norm_second, norm_shard],
        facts,
        block_out,
        token_grad,
    )
    up_new = [v.reshape(up_weight.shape) for v in new[0:3]]
    down_new = [v.reshape(down_weight.shape) for v in new[3:6]]
    attn_new = [v.reshape(attn_weight.shape) for v in new[6:9]]
    vector_new = [v.reshape(expert_vector.shape) for v in new[9:12]]
    norm_new = new[12:15]
    block_out, token_grad = new[15:17]
    grad_norm = new[17].reshape(())
    expert_stats = new[18].reshape(2, 1)
    return (
        block_out,
        token_grad,
        grad_norm,
        *attn_new,
        *norm_new,
        *up_new,
        *down_new,
        *vector_new,
        expert_stats,
    )


def solution(mesh):
    small = mesh.shape[EX] == 8 and mesh.shape[HI] == 4
    return jax.shard_map(
        fast_shards if small else shards,
        mesh=mesh,
        in_specs=(
            P(BOTH, None),
            P(BOTH, None),
            P(BOTH, None),
            P(None, BOTH, None),
            P(None, BOTH, None),
            P(None, BOTH, None),
            P(None, BOTH),
            P(None, BOTH),
            P(None, BOTH),
            P(EX, None, HI),
            P(EX, None, HI),
            P(EX, None, HI),
            P(EX, HI, None),
            P(EX, HI, None),
            P(EX, HI, None),
            P(EX, None, None),
            P(EX, None, None),
            P(EX, None, None),
        ),
        out_specs=(
            P(BOTH, None),
            P(BOTH, None),
            P(),
            P(None, BOTH, None),
            P(None, BOTH, None),
            P(None, BOTH, None),
            P(None, BOTH),
            P(None, BOTH),
            P(None, BOTH),
            P(EX, None, HI),
            P(EX, None, HI),
            P(EX, None, HI),
            P(EX, HI, None),
            P(EX, HI, None),
            P(EX, HI, None),
            P(EX, None, None),
            P(EX, None, None),
            P(EX, None, None),
            P(None, EX),
        ),
        check_vma=False,
    )
```

```python
import functools
import math

import jax
import jax.numpy as jnp
from jax import lax
from jax.experimental import pallas as pl
from jax.experimental.pallas import tpu as pltpu
from jax.sharding import PartitionSpec as P

HEADS = 16
STEP = 10


norm_eps = 1e-05
clip_level = 1.0
beta_one = 0.9
beta_two = 0.999
adam_eps = 1e-08
decay_rate = 0.1
rate_matrix = 0.05
rate_vector = 0.5
masked_fill = -1e30
EX, HI = "expert", "hidden"
BOTH = (EX, HI)


def layer_norm(inputs, gain_row, bias_row):
    average = jnp.mean(inputs, axis=-1, keepdims=True)
    centred = inputs - average
    variance = jnp.mean(centred * centred, axis=-1, keepdims=True)
    return centred * lax.rsqrt(variance + norm_eps) * gain_row + bias_row


def gelu_exact(values):
    return jax.nn.gelu(values, approximate=False)


def adam_step(weight, first, second, grad, clip_factor, rate, decay):
    clipped = grad * clip_factor
    moment = beta_one * first + (1.0 - beta_one) * clipped
    square = beta_two * second + (1.0 - beta_two) * clipped * clipped
    corr_one = 1.0 - beta_one**STEP
    corr_two = 1.0 - beta_two**STEP
    update = moment / corr_one / (jnp.sqrt(square / corr_two) + adam_eps) + decay * weight
    return (weight - rate * update, moment, square)


MESH = pl.DeviceIdType.MESH
VMEM_SPEC = pl.BlockSpec(memory_space=pltpu.VMEM)
ANY_SPEC = pl.BlockSpec(memory_space=pl.ANY)


class Place:
    def __init__(self):
        self.e = lax.axis_index(EX)
        self.z = lax.axis_index(HI)
        high, low = lax.div(self.z, 2), lax.rem(self.z, 2)
        self.middle = high + low == 1
        self.ends = jnp.logical_not(self.middle)
        self.line = [self.z, self.z + 1 - 2 * low, 2 - high, 3 - 3 * high]
        self.core = lax.rem(self.e, 2)
        self.x = lax.rem(lax.div(self.e, 2), 2)
        self.y = lax.div(self.e, 4)
        self.ex = self.e + 2 - 4 * self.x
        self.ey = self.e + 4 - 8 * self.y
        self.exy = self.ex + 4 - 8 * self.y
        self.twin = (self.e + 1 - 2 * self.core, self.z)
        self.over_x = (self.ex, self.z)
        self.over_y = (self.ey, self.z)
        self.partner = (self.e, self.line[1])
        self.mirror = (self.e, 3 - self.z)
        self.mates = [None, self.partner, (self.e, self.z + 2 - 4 * high), self.mirror]

    def across(self, k):
        c = lax.rem(self.core + k % 2, 2)
        x = lax.rem(self.x + (k // 2) % 2, 2)
        y = lax.rem(self.y + k // 4, 2)
        return 4 * y + 2 * x + c

    def everyone(self):
        plane = [(self.across(k), self.z) for k in range(1, 8)]
        return plane + self.mates[1:]

    def meet(self):
        barrier = pltpu.get_barrier_semaphore()
        for device in self.everyone():
            pl.semaphore_signal(barrier, inc=1, device_id=device, device_id_type=MESH)
        pl.semaphore_wait(barrier, len(self.everyone()))


class Wire:
    def __init__(self, send_sem, recv_sem):
        self.send_sem, self.recv_sem = send_sem, recv_sem
        self.count = 0
        self.tags = {}
        self.sent = []

    def next(self):
        self.count += 1
        return self.count - 1

    def send(self, src, dst, device, tag=None, when=None):
        i = self.next()
        if tag is not None:
            if tag not in self.tags:
                self.tags[tag] = self.next()
            j = self.tags[tag]
        else:
            j = i
        copy = pltpu.make_async_remote_copy(
            src_ref=src,
            dst_ref=dst,
            send_sem=self.send_sem.at[i],
            recv_sem=self.recv_sem.at[j],
            device_id=device,
            device_id_type=MESH,
        )
        if when is None:
            copy.start()
        else:
            pl.when(when)(copy.start)
        self.sent.append((copy, when))
        return copy

    def arrived(self, tag, dst, device):
        if tag not in self.tags:
            self.tags[tag] = self.next()
        j = self.tags[tag]
        pltpu.make_async_remote_copy(
            src_ref=dst,
            dst_ref=dst,
            send_sem=self.send_sem.at[j],
            recv_sem=self.recv_sem.at[j],
            device_id=device,
            device_id_type=MESH,
        ).wait_recv()

    def left(self, copy):
        copy.wait_send()
        self.sent = [one for one in self.sent if one[0] is not copy]

    def drain(self):
        for copy, when in self.sent:
            if when is None:
                copy.wait_send()
            else:
                pl.when(when)(copy.wait_send)
        self.sent = []


class Line:
    def __init__(self, wire, at, name, slot):
        self.wire, self.at, self.name, self.slot = wire, at, name, slot

    def begin(self, own=None, outer=1, inner=True):
        at = self.at
        here = self.slot(at.z)
        own = here if own is None else own
        if outer:
            when = {1: None, 2: at.ends, 3: at.middle}[outer]
            self.wire.send(own, here, at.partner, (self.name, 1), when)
        if inner:
            self.wire.send(own, here, at.mirror, (self.name, 2), at.middle)

    def take(self, i, when=None):
        at = self.at
        block = self.slot(at.line[i])
        if when is None:
            self.wire.arrived((self.name, i), block, at.partner)
        else:
            pl.when(when)(lambda: self.wire.arrived((self.name, i), block, at.partner))
        if when is not at.ends:
            to, tag = (at.mirror, 3) if i == 1 else (at.partner, i)
            self.wire.send(block, block, to, (self.name, tag), at.middle)
        return block


class Fetch:
    def __init__(self, sem):
        self.sem = sem
        self.count = 0
        self.open = []

    def start(self, src, dst):
        copy = pltpu.make_async_copy(src, dst, self.sem.at[self.count])
        self.count += 1
        copy.start()
        self.open.append(copy)
        return copy

    def done(self, copy):
        copy.wait()
        self.open = [one for one in self.open if one is not copy]

    def drain(self):
        for copy in self.open:
            copy.wait()
        self.open = []


def dot(a, b, ca=1, cb=0):
    return lax.dot_general(a, b, (((ca,), (cb,)), ((), ())), preferred_element_type=jnp.float32)


def tile(i, size=256):
    return pl.ds(pl.multiple_of(i * size, size), size)


def pick(placed_row, slots):
    which = lax.broadcasted_iota(jnp.int32, (slots, placed_row.shape[1]), 0)
    return jnp.where(which == placed_row, 1.0, 0.0).astype(jnp.bfloat16)


def build(stage, source, placed_row):
    planes, cap, width = stage.shape
    onehot = pick(placed_row, planes * cap)

    @pl.loop(0, width // 512)
    def _(i):
        cols = tile(i, 512)
        value = dot(onehot, source[:, cols]).astype(jnp.bfloat16)
        for k in range(planes):
            stage[k, :, cols] = value[k * cap : (k + 1) * cap]


def attend_kernel(
    cap,
    tok,
    w_own,
    norm_in,
    route,
    cot,
    w_out,
    qkv_out,
    normed_out,
    ctx_out,
    resid_out,
    sent_out,
    placed_out,
    gains_out,
    cot_raw,
    cot_zero,
    w_low,
    wfull,
    norm_low,
    pieces,
    qkv,
    normed,
    ctx,
    resid,
    sent,
    placed,
    gains,
    stage,
    send_sem,
    recv_sem,
    local_sem,
):
    at = Place()
    e, z = at.e, at.z
    depth = 4
    count, width = tok.shape
    shard = w_own.shape[1]
    wire = Wire(send_sem, recv_sem)
    fetch = Fetch(local_sem)
    groups = [(0, 3), (3, 1)]
    fetch.start(cot, cot_raw.at[z])
    w_low[...] = w_own[...].astype(jnp.bfloat16)
    lanes = norm_in.shape[1]
    offset = lax.broadcasted_iota(jnp.int32, (lanes, 128), 1) - z * lanes
    ours = lax.broadcasted_iota(jnp.int32, (lanes, 128), 0) == offset
    low = norm_in[...].astype(jnp.bfloat16)
    norm_low[...] = jnp.zeros((16, 128), jnp.bfloat16)
    norm_low[0:2, :] = dot(low, jnp.where(ours, 1.0, 0.0).astype(jnp.bfloat16)).astype(
        jnp.bfloat16
    )
    at.meet()

    def block(g, who, zz):
        if g == 2:
            return pieces.at[who, zz]
        first, mats = groups[g]
        start = pl.multiple_of((who * depth + zz) * shard, shard)
        return wfull.at[pl.ds(first, mats), pl.ds(start, shard)]

    def mine(g):
        if g == 2:
            return norm_low
        first, mats = groups[g]
        return w_low.at[pl.ds(first, mats)]

    lines = [Line(wire, at, g, lambda zz, g=g: block(g, e, zz)) for g in range(3)]
    lines[2].begin(mine(2))
    lines[0].begin(mine(0))
    lines[1].begin(mine(1), outer=2, inner=False)
    cots = Line(wire, at, "cot", lambda zz: cot_raw.at[zz])
    cots.begin(cot, outer=2, inner=False)
    own = [fetch.start(mine(g), block(g, e, z)) for g in range(3)]
    to_x, to_y, to_far, to_twin = {}, {}, {}, {}

    def over_x(g, i):
        here = block(g, e, at.line[i])
        to_x[g, i] = wire.send(here, here, at.over_x)
        to_twin[g, i, 0] = wire.send(here, here, at.twin)

    def over_y(g, i):
        here = block(g, e, at.line[i])
        to_y[g, i] = wire.send(here, here, at.over_y)

    def forward(g, i):
        zz = at.line[i]
        if i in (0, 3):
            to_x[g, i].wait_recv()
            block_x = block(g, at.ex, zz)
            to_far[g, i] = wire.send(block_x, block_x, at.over_y)
            to_twin[g, i, 1] = wire.send(block_x, block_x, at.twin)
        else:
            to_y[g, i].wait_recv()
            block_y = block(g, at.ey, zz)
            to_far[g, i] = wire.send(block_y, block_y, at.over_x)
            to_twin[g, i, 1] = wire.send(block_y, block_y, at.twin)

    def side(g, i):
        zz = at.line[i]
        if i in (0, 3):
            to_y[g, i].wait_recv()
            there = block(g, at.ey, zz)
        else:
            to_x[g, i].wait_recv()
            there = block(g, at.ex, zz)
        to_twin[g, i, 2] = wire.send(there, there, at.twin)

    def far(g, i):
        to_far[g, i].wait_recv()
        there = block(g, at.exy, at.line[i])
        to_twin[g, i, 3] = wire.send(there, there, at.twin)

    def finish(g):
        for i in range(depth):
            for k in range(4):
                to_twin[g, i, k].wait_recv()

    def both(step, i):
        step(2, i)
        step(0, i)

    def take(i):
        lines[2].take(i)
        lines[0].take(i)

    for copy in (own[2], own[0]):
        fetch.done(copy)
    both(over_x, 0)
    both(over_y, 0)
    wide_r = lax.broadcasted_iota(jnp.int32, (count, count), 0)
    wide_c = lax.broadcasted_iota(jnp.int32, (count, count), 1)
    route_row = route[...].astype(jnp.float32)
    route_col = jnp.sum(jnp.where(wide_r == wide_c, route_row, 0.0), axis=1, keepdims=True)
    lane = lax.broadcasted_iota(jnp.int32, (count, 128), 1)
    chosen = jnp.where(route_col.astype(jnp.int32) == lane, 1.0, 0.0)
    rows_i = lax.broadcasted_iota(jnp.int32, (count, count), 0)
    cols_i = lax.broadcasted_iota(jnp.int32, (count, count), 1)
    lower = jnp.where(rows_i >= cols_i, 1.0, 0.0)
    running = dot(lower.astype(jnp.bfloat16), chosen.astype(jnp.bfloat16))
    rank = jnp.sum((running - 1.0) * chosen, axis=1, keepdims=True)
    column = route_col * float(cap) + rank
    row = jnp.sum(jnp.where(wide_r == wide_c, column, 0.0), axis=0, keepdims=True)
    row = jnp.concatenate([row, jnp.full((1, 256 - count), -1.0, jnp.float32)], axis=1)
    placed[z] = jnp.broadcast_to(row, (8, 256)).astype(jnp.int32)
    take(1)
    both(over_x, 1)
    both(over_y, 1)
    build(stage, cot, placed[z, 0:1, :count])
    both(forward, 0)
    take(2)
    lines[1].begin(mine(1), outer=3)
    both(forward, 1)
    both(over_y, 2)
    take(3)
    lines[1].take(1, at.middle)
    lines[1].take(2, at.middle)
    both(over_x, 3)
    both(over_x, 2)
    both(over_y, 3)
    both(side, 0)
    both(side, 1)
    both(far, 0)
    both(far, 1)
    lines[1].take(3, at.middle)
    cots.begin(cot, outer=0)
    both(forward, 2)
    both(forward, 3)
    cots.take(1, at.middle)
    places = Line(wire, at, "place", lambda zz: placed.at[zz])
    places.begin()
    fetch.done(own[1])
    for i in range(depth):
        if i:
            lines[1].take(i, at.ends)
        over_x(1, i)
        over_y(1, i)
    both(side, 3)
    both(side, 2)
    both(far, 2)
    both(far, 3)
    cots.take(2, at.middle)
    finish(2)
    cots.take(3, at.middle)
    gain_rows = jnp.concatenate(
        [
            sum([pieces[who, zz] for zz in range(1, depth)], pieces[who, 0])
            for who in range(8)
        ],
        axis=1,
    )
    tally = jnp.concatenate(
        [
            jnp.broadcast_to(jnp.sum(chosen, axis=0, keepdims=True), (16, 128)),
            jnp.zeros((16, width - 128), jnp.float32),
        ],
        axis=1,
    )
    third_row = lax.broadcasted_iota(jnp.int32, (16, width), 0) == 2
    gains[...] = jnp.where(third_row, tally, gain_rows.astype(jnp.float32)).astype(jnp.bfloat16)
    fetch.start(gains, gains_out)
    gain = gains[0:1, :].astype(jnp.float32)
    bias = gains[1:2, :].astype(jnp.float32)

    @pl.loop(0, count // 64)
    def _(i):
        rows = tile(i, 64)
        piece = tok[rows, :].astype(jnp.float32)
        average = jnp.mean(piece, axis=-1, keepdims=True)
        centred = piece - average
        variance = jnp.mean(centred * centred, axis=-1, keepdims=True)
        normed[rows, :] = (centred * lax.rsqrt(variance + norm_eps) * gain + bias).astype(
            jnp.bfloat16
        )

    fetch.start(normed, normed_out)
    finish(0)
    fetch.start(wfull.at[pl.ds(0, 3)], w_out.at[pl.ds(0, 3)])
    tiles = width // 512

    def project(i):
        m = lax.div(i, tiles)
        cols = tile(lax.rem(i, tiles), 512)
        qkv[m, :, cols] = dot(normed[...], wfull[m, :, cols]).astype(jnp.bfloat16)

    pl.loop(0, tiles)(project)
    for i in range(depth):
        forward(1, i)
    slots_out = [
        wire.send(stage.at[at.across(k)], cot_zero.at[k], (at.across(k), z)) for k in range(1, 8)
    ]
    fetch.start(stage.at[e], cot_zero.at[0])
    places.take(1)
    pl.loop(tiles, 3 * tiles)(project)
    fetch.start(qkv, qkv_out)
    for i in range(depth):
        side(1, i)
    places.take(2, at.middle)
    causal = rows_i >= cols_i
    left = lax.broadcasted_iota(jnp.int32, (count, 128), 1) < 64
    scaling = jnp.asarray(64 ** (-0.5), jnp.bfloat16)

    def pair(i):
        cols = tile(i, 128)
        query = qkv[0, :, cols] * scaling
        keys = qkv[1, :, cols]
        values = qkv[2, :, cols]
        halves = []
        for side in range(2):
            mask = left if side == 0 else jnp.logical_not(left)
            scores = dot(jnp.where(mask, query, jnp.zeros_like(query)), keys, 1, 1)
            scores = jnp.where(causal, scores, masked_fill)
            top = jnp.max(scores, axis=-1, keepdims=True)
            expo = jnp.exp(scores - top)
            probs = expo / jnp.sum(expo, axis=-1, keepdims=True)
            halves.append(dot(probs.astype(jnp.bfloat16), values))
        ctx[:, cols] = jnp.where(left, halves[0], halves[1]).astype(jnp.bfloat16)

    pl.loop(0, 6, unroll=3)(pair)
    for i in range(depth):
        far(1, i)
    places.take(2, at.ends)
    places.take(3, at.middle)
    pl.loop(6, width // 128, unroll=2)(pair)
    fetch.start(ctx, ctx_out)
    finish(1)
    fetch.start(wfull.at[pl.ds(3, 1)], w_out.at[pl.ds(3, 1)])

    @pl.loop(0, tiles)
    def _(i):
        cols = tile(i, 512)
        value = tok[:, cols].astype(jnp.float32) + dot(ctx[...], wfull[3, :, cols])
        resid[:, cols] = value
        sent[:, cols] = value.astype(jnp.bfloat16)

    fetch.start(sent, sent_out)
    fetch.start(resid, resid_out)
    places.take(3, at.ends)
    cots.take(2, at.ends)
    cots.take(3, at.ends)
    fetch.start(placed, placed_out)
    for copy in slots_out:
        copy.wait_recv()
    wire.drain()
    fetch.drain()


def attend(cap, tokens, w_own, norm_own, routes, cotangent):
    count, width = tokens.shape
    bf, full = jnp.bfloat16, jnp.float32
    copies = 176
    shapes = [
        ((4, width, width), bf),
        ((3, count, width), bf),
        ((count, width), bf),
        ((count, width), bf),
        ((count, width), full),
        ((count, width), bf),
        ((4, 8, 256), jnp.int32),
        ((16, width), bf),
        ((4, count, width), bf),
        ((8, cap, width), bf),
    ]
    return pl.pallas_call(
        functools.partial(attend_kernel, cap),
        out_shape=[jax.ShapeDtypeStruct(*one) for one in shapes],
        in_specs=[VMEM_SPEC] * 5,
        out_specs=[ANY_SPEC] * len(shapes),
        scratch_shapes=[
            pltpu.VMEM((4, w_own.shape[1], width), bf),
            pltpu.VMEM((4, width, width), bf),
            pltpu.VMEM((16, 128), bf),
            pltpu.VMEM((8, 4, 16, 128), bf),
            pltpu.VMEM((3, count, width), bf),
            pltpu.VMEM((count, width), bf),
            pltpu.VMEM((count, width), bf),
            pltpu.VMEM((count, width), full),
            pltpu.VMEM((count, width), bf),
            pltpu.VMEM((4, 8, 256), jnp.int32),
            pltpu.VMEM((16, width), bf),
            pltpu.VMEM((8, cap, width), bf),
            pltpu.SemaphoreType.DMA((copies,)),
            pltpu.SemaphoreType.DMA((copies,)),
            pltpu.SemaphoreType.DMA((16,)),
        ],
        compiler_params=pltpu.CompilerParams(
            collective_id=0, has_side_effects=True, vmem_limit_bytes=62 << 20
        ),
    )(tokens, w_own, norm_own, routes, cotangent)


def gelu_pair(v):
    cdf = 0.5 + 0.5 * lax.erf(v * (0.5**0.5))
    pdf = jnp.exp(-0.5 * v * v) * ((2.0 * math.pi) ** -0.5)
    return v * cdf, cdf + v * pdf


def fold(v):
    total = v[0:8]
    for i in range(8, v.shape[0], 8):
        total = total + v[i : i + 8]
    return total


def spread(column, lanes):
    return jnp.concatenate([column] * (lanes // 128), axis=1)


def square_lanes(v):
    total = v[:, 0:128] * v[:, 0:128]
    for i in range(128, v.shape[1], 128):
        total = total + v[:, i : i + 128] * v[:, i : i + 128]
    return total


def unslot(placed_row, slots, out):
    planes, cap, width = slots.shape
    onehot = pick(placed_row, planes * cap)

    @pl.loop(0, width // 256)
    def _(j):
        cols = tile(j)
        value = slots[:, :, cols].reshape(planes * cap, 256)
        out[:, cols] = dot(onehot, value, 0, 0).astype(jnp.bfloat16)


class Home:
    def __init__(self, wire, at, name, part, got):
        self.wire, self.at, self.name = wire, at, name
        self.part, self.got = part, got
        half = got.shape[1] // 2
        self.halves = [pl.ds(0, half), pl.ds(half, half)]

    def add(self, i, k, half):
        part = self.part(i)
        part[half, :] = (
            part[half, :].astype(jnp.float32) + self.got[k, half, :].astype(jnp.float32)
        ).astype(jnp.bfloat16)

    def arrived(self, tag, k, n, device):
        half = self.halves[n]
        self.wire.arrived((self.name, tag, n), self.got.at[k, half], device)

    def send(self, src, k, n, device, tag, when=None):
        half = self.halves[n]
        self.wire.send(src.at[half], self.got.at[k, half], device, (self.name, tag, n), when)

    def push(self, i):
        for n in range(2):
            self.send(self.part(i), i - 1, n, self.at.partner, i, self.at.ends)

    def pass_on(self, i):
        at = self.at
        k = {3: 3, 2: 4}[i]
        for n, half in enumerate(self.halves):

            @pl.when(at.middle)
            def _():
                self.arrived(i, i - 1, n, at.partner)
                self.add(i, i - 1, half)

            self.send(self.part(i), k, n, at.mirror, k + 1, at.middle)

    def near(self):
        at = self.at
        for n, half in enumerate(self.halves):

            @pl.when(at.middle)
            def _():
                self.arrived(4, 3, n, at.mirror)
                self.add(1, 3, half)

            self.send(self.part(1), 0, n, at.partner, 1)

    def relay_far(self):
        at = self.at
        for n in range(2):
            pl.when(at.middle)(lambda: self.arrived(4, 3, n, at.mirror))
            self.send(self.got.at[3], 0, n, at.partner, 1, at.middle)

    def finish(self):
        at = self.at
        for n, half in enumerate(self.halves):

            @pl.when(at.ends)
            def _():
                self.arrived(1, 0, n, at.partner)
                self.add(0, 0, half)

            @pl.when(at.middle)
            def _():
                self.arrived(5, 4, n, at.mirror)
                self.add(0, 4, half)

    def last(self):
        at = self.at
        for n, half in enumerate(self.halves):
            self.arrived(1, 0, n, at.partner)

            @pl.when(at.middle)
            def _():
                self.arrived(5, 4, n, at.mirror)
                self.add(0, 4, half)

    def total(self, cols):
        return self.part(0)[:, cols].astype(jnp.float32) + self.got[0, :, cols].astype(jnp.float32)


def expert_kernel(
    cap,
    sent_in,
    placed_in,
    cot_raw,
    cot_zero,
    up_in,
    down_in,
    vec,
    d_sum,
    g_up,
    g_down,
    delta_out,
    vec_part,
    scal,
    sent,
    placed,
    cot_line,
    up,
    down,
    raw,
    stage,
    rows,
    cots,
    xn,
    act,
    slope,
    delta,
    d_slots,
    back,
    part,
    z_in,
    d_xn,
    gate,
    d_logit,
    g_stage,
    send_sem,
    recv_sem,
    local_sem,
):
    at = Place()
    e, z = at.e, at.z
    depth, planes = 4, 8
    count, width = sent.shape
    slots = planes * cap
    units = up.shape[1]
    wire = Wire(send_sem, recv_sem)
    fetch = Fetch(local_sem)
    in_sent = fetch.start(sent_in, sent)
    in_placed = fetch.start(placed_in, placed)
    in_up = fetch.start(up_in, up)
    in_down = fetch.start(down_in, down)
    in_cot = fetch.start(cot_raw, cot_line)
    in_zero = fetch.start(cot_zero, cots.at[0])
    at.meet()
    fetch.done(in_sent)
    line = Line(wire, at, "row", lambda zz: raw.at[zz])
    line.begin(sent)
    vec_part[...] = jnp.zeros_like(vec_part)
    scal[...] = jnp.zeros_like(scal)
    fetch.done(in_placed)
    centroid = lambda: vec[0]
    row_copies, cot_copies, ret_copies = {}, {}, {}

    def exchange(i, dst, s, offsets=range(1, planes)):
        return [
            wire.send(stage.at[s, at.across(k)], dst.at[i, k], (at.across(k), z)) for k in offsets
        ]

    def slot_row(i):
        return placed[at.line[i], 0:1, :count]

    def rows_out(i):
        source = sent if i == 0 else raw.at[at.line[i]]
        build(stage.at[i], source, slot_row(i))
        row_copies[i] = exchange(i, rows, i)
        rows[i, 0] = stage[i, e]

    def cots_out(i, s, offsets):
        if i not in cot_copies:
            for copy in row_copies[s]:
                wire.left(copy)
            build(stage.at[s], cot_line.at[at.line[i]], slot_row(i))
            cot_copies[i] = []
            cots[i, 0] = stage[s, e]
        cot_copies[i] += exchange(i, cots, s, offsets)

    def forward(i):
        for copy in row_copies[i]:
            copy.wait_recv()
        gain, bias = vec[1], vec[2]

        @pl.loop(0, planes, unroll=2)
        def _(k):
            r = rows[i, k].astype(jnp.float32)
            logit = jnp.sum(r * centroid(), axis=-1, keepdims=True)
            g = jax.nn.sigmoid(logit)
            wide = jnp.broadcast_to(g, (cap, 128))
            gate[i, k] = wide
            scal[0:8] += fold(wide)
            average = jnp.mean(r, axis=-1, keepdims=True)
            centred = r - average
            variance = jnp.mean(centred * centred, axis=-1, keepdims=True)
            xn[i, pl.ds(pl.multiple_of(k * cap, 16), cap), :] = (
                centred * lax.rsqrt(variance + norm_eps) * gain + bias
            ).astype(jnp.bfloat16)

        if i == 0:
            fetch.done(in_up)

        @pl.loop(0, units // 512)
        def _(j):
            cols = tile(j, 512)
            value, rate = gelu_pair(dot(xn[i], up[:, cols]))
            act[i, :, cols] = value.astype(jnp.bfloat16)
            slope[i, :, cols] = rate.astype(jnp.bfloat16)

        if i == 0:
            fetch.done(in_down)

        @pl.loop(0, width // 512)
        def _(j):
            cols = tile(j, 512)
            branch = dot(act[i], down[:, cols])
            wide = spread(gate[i].reshape(slots, 128), 512)
            value = (wide * branch).astype(jnp.bfloat16)
            for k in range(planes):
                delta[i, k, :, cols] = value[k * cap : (k + 1) * cap]

        fetch.start(delta.at[i], delta_out.at[i])

    def backward(i):
        for copy in cot_copies[i]:
            copy.wait_recv()

        @pl.loop(0, planes, unroll=2)
        def _(k):
            c = cots[i, k].astype(jnp.float32)
            g = gate[i, k]
            inner = jnp.sum(c * delta[i, k].astype(jnp.float32), axis=-1, keepdims=True)
            dl = (1.0 - g) * inner
            d_logit[i, k] = dl
            cots[i, k] = (c * spread(g, width)).astype(jnp.bfloat16)
            vec_part[0] += fold(rows[i, k].astype(jnp.float32) * spread(dl, width))

        @pl.loop(0, units // 512)
        def _(j):
            cols = tile(j, 512)
            d_act = dot(cots[i].reshape(slots, width), down[cols, :], 1, 1)
            slope[i, :, cols] = (d_act * slope[i, :, cols].astype(jnp.float32)).astype(
                jnp.bfloat16
            )

    def backward_in(i):
        @pl.loop(0, width // 512)
        def _(j):
            cols = tile(j, 512)
            value = dot(slope[i], up[cols, :], 1, 1)
            for k in range(planes):
                d_xn[k, :, cols] = value[k * cap : (k + 1) * cap]

        @pl.loop(0, planes, unroll=2)
        def _(k):
            r = rows[i, k].astype(jnp.float32)
            average = jnp.mean(r, axis=-1, keepdims=True)
            centred = r - average
            variance = jnp.mean(centred * centred, axis=-1, keepdims=True)
            scale = lax.rsqrt(variance + norm_eps)
            hat = centred * scale
            dx = d_xn[k]
            vec_part[1] += fold(dx * hat)
            vec_part[2] += fold(dx)
            dh = dx * vec[1]
            first = jnp.mean(dh, axis=-1, keepdims=True)
            second = jnp.mean(dh * hat, axis=-1, keepdims=True)
            d_in = scale * (dh - first - hat * second)
            d_slots[i, k] = (d_in + spread(d_logit[i, k], width) * centroid()).astype(jnp.bfloat16)

    def give(i):
        ret_copies[i] = [
            wire.send(d_slots.at[i, k], back.at[i, e], (at.across(k), z))
            for k in range(1, planes)
        ]
        back[i, e] = d_slots[i, 0]

    home = Home(wire, at, "home", lambda i: part.at[i], z_in)

    def collect(i):
        for copy in ret_copies[i]:
            copy.wait_recv()
        unslot(slot_row(i), back.at[i], part.at[i])

    def weight_grad(lhs, rhs, index, out):
        @pl.loop(0, lhs.shape[-1] // 512)
        def _(j):
            cols = tile(j, 512)
            left = lhs[:, :, cols].reshape(depth * slots, 512)
            value = dot(left, rhs[...].reshape(depth * slots, rhs.shape[-1]), 0, 0)
            scal[8:16] += fold(square_lanes(value))
            g_stage[index, cols, :] = value.astype(jnp.bfloat16)

        fetch.start(g_stage.at[index], out)

    rows_out(0)
    line.take(1)
    line.take(2, at.middle)
    rows_out(1)
    fetch.done(in_cot)
    cots_out(3, 0, (2, 4, 6))
    forward(0)
    line.take(2, at.ends)
    line.take(3, at.middle)
    rows_out(2)
    forward(1)
    line.take(3, at.ends)
    rows_out(3)
    fetch.done(in_zero)
    cot_copies[0] = []
    cot_copies[1] = [wire.send(cot_zero, cots.at[1], at.partner)]
    cots_out(3, 0, (3, 5, 7, 1))
    forward(2)
    cots_out(2, 1, range(1, planes))
    forward(3)
    backward(3)
    backward_in(3)
    give(3)
    backward(2)
    backward_in(2)
    give(2)
    backward(1)
    backward_in(1)
    give(1)
    backward(0)
    collect(3)
    home.push(3)
    backward_in(0)
    give(0)
    collect(2)
    home.push(2)
    home.pass_on(3)
    weight_grad(act, cots, 0, g_down)
    collect(1)
    home.near()
    home.pass_on(2)
    weight_grad(xn, slope, 1, g_up)
    collect(0)
    home.last()

    @pl.loop(0, width // 256)
    def _(j):
        cols = tile(j)
        d_sum[:, cols] = home.total(cols)

    wire.drain()
    fetch.drain()


def expert_layer(cap, sent, placed, cot_raw, cot_zero, up, down, vec):
    count, width = sent.shape
    units = up.shape[1]
    depth = 4
    bf, full = jnp.bfloat16, jnp.float32
    slots = 8 * cap
    copies = 3 * 7 * depth + 56
    shapes = [
        ((count, width), full),
        ((width, units), bf),
        ((units, width), bf),
        ((depth, 8, cap, width), bf),
        ((3, 8, width), full),
        ((16, 128), full),
    ]
    big = pltpu.VMEM((depth, 8, cap, width), bf)
    return pl.pallas_call(
        functools.partial(expert_kernel, cap),
        out_shape=[jax.ShapeDtypeStruct(*one) for one in shapes],
        in_specs=[ANY_SPEC] * 6 + [VMEM_SPEC],
        out_specs=[VMEM_SPEC, ANY_SPEC, ANY_SPEC, ANY_SPEC, VMEM_SPEC, VMEM_SPEC],
        scratch_shapes=[
            pltpu.VMEM((count, width), bf),
            pltpu.VMEM((depth, 8, 256), jnp.int32),
            pltpu.VMEM((depth, count, width), bf),
            pltpu.VMEM((width, units), bf),
            pltpu.VMEM((units, width), bf),
            pltpu.VMEM((depth, count, width), bf),
            big,
            big,
            big,
            pltpu.VMEM((depth, slots, width), bf),
            pltpu.VMEM((depth, slots, units), bf),
            pltpu.VMEM((depth, slots, units), bf),
            big,
            big,
            big,
            pltpu.VMEM((depth, count, width), bf),
            pltpu.VMEM((5, count, width), bf),
            pltpu.VMEM((8, cap, width), full),
            pltpu.VMEM((depth, 8, cap, 128), full),
            pltpu.VMEM((depth, 8, cap, 128), full),
            pltpu.VMEM((2, max(width, units), max(width, units)), bf),
            pltpu.SemaphoreType.DMA((copies,)),
            pltpu.SemaphoreType.DMA((copies,)),
            pltpu.SemaphoreType.DMA((16,)),
        ],
        compiler_params=pltpu.CompilerParams(
            collective_id=1, has_side_effects=True, vmem_limit_bytes=62 << 20
        ),
    )(sent, placed, cot_raw, cot_zero, up, down, vec)


def reduce_kernel(
    cap,
    d_sum,
    cot,
    w_in,
    qkv_in,
    normed_in,
    ctx,
    tok,
    gains,
    placed,
    delta_in,
    resid,
    vec_part,
    scal,
    block_out,
    token_grad,
    shard_out,
    norm_out,
    vec_out,
    square_out,
    norm_shard,
    wfull,
    qkv,
    normed,
    delta,
    d_resid,
    d_proj,
    d_ctx,
    d_qkv,
    d_norm,
    stage,
    twin_in,
    x_in,
    y_in,
    x_last,
    y_last,
    done,
    z_last,
    back,
    part,
    z_in,
    near_in,
    small,
    small_in,
    square,
    send_sem,
    recv_sem,
    local_sem,
):
    at = Place()
    e, z = at.e, at.z
    depth, planes = 4, 8
    count, width = tok.shape
    shard = shard_out.shape[1]
    column = depth * shard
    half = column // 2
    wire = Wire(send_sem, recv_sem)
    fetch = Fetch(local_sem)
    in_delta = {i: fetch.start(delta_in.at[i], delta.at[i]) for i in (1, 3, 2, 0)}
    in_w = {m: fetch.start(w_in.at[m], wfull.at[m]) for m in (3, 2, 1, 0)}
    in_qkv = fetch.start(qkv_in, qkv)
    in_normed = fetch.start(normed_in, normed)
    at.meet()
    ret = {}
    home = Home(wire, at, "home", lambda i: part.at[i], z_in)

    def give(i):
        if i in in_delta:
            fetch.done(in_delta.pop(i))
        ret[i] = [
            wire.send(delta.at[i, k], back.at[i, e], (at.across(k), z)) for k in range(1, planes)
        ]
        back[i, e] = delta[i, 0]

    def collect(i):
        for copy in ret[i]:
            copy.wait_recv()
        unslot(placed[at.line[i], 0:1, :count], back.at[i], part.at[i])

    def weight_grad(m, left_ref, right):
        @pl.loop(0, planes, unroll=2)
        def _(i):
            cols = pl.ds(pl.multiple_of(i * column, column), column)
            value = dot(left_ref[:, cols], right[...], 0, 0).astype(jnp.bfloat16)
            stage[m, lax.div(i, 4), lax.rem(lax.div(i, 2), 2), lax.rem(i, 2)] = value

    other = 1 - at.core
    first, second, third, fourth, fifth = {}, {}, {}, {}, {}

    def to_core(m):
        first[m] = wire.send(stage.at[m, :, :, other], twin_in.at[m], at.twin)

    def to_plane(m):
        first[m].wait_recv()
        for j in range(2):
            for i in range(2):
                twin_in[m, j, i] = twin_in[m, j, i] + stage[m, j, i, at.core]
        second[m] = (
            wire.send(twin_in.at[m, :, 1 - at.x, pl.ds(0, half)], x_in.at[m], at.over_x),
            wire.send(twin_in.at[m, 1 - at.y, :, pl.ds(half, half)], y_in.at[m], at.over_y),
        )

    def to_last(m):
        second[m][0].wait_recv()
        for j in range(2):
            x_in[m, j] = x_in[m, j] + twin_in[m, j, at.x, 0:half]
        one = wire.send(x_in.at[m, 1 - at.y], x_last.at[m], at.over_y)
        second[m][1].wait_recv()
        for i in range(2):
            y_in[m, i] = y_in[m, i] + twin_in[m, at.y, i, half:]
        two = wire.send(y_in.at[m, 1 - at.x], y_last.at[m], at.over_x)
        third[m] = (one, two)

    def to_owner(m):
        third[m][0].wait_recv()
        pair = (2, shard, width)
        done[m, 0:2] = (x_in[m, at.y] + x_last[m]).reshape(pair)
        third[m][1].wait_recv()
        done[m, 2:4] = (y_in[m, at.x] + y_last[m]).reshape(pair)
        theirs = at.partner[1]
        fourth[m] = (
            wire.send(done.at[m, theirs], z_last.at[m, 0], at.partner),
            wire.send(done.at[m, 3 - theirs], z_last.at[m, 1], at.partner),
        )

    def cross(m):
        fourth[m][1].wait_recv()
        done[m, 3 - z] = done[m, 3 - z] + z_last[m, 1]
        fifth[m] = wire.send(done.at[m, 3 - z], z_last.at[m, 2], at.mirror)

    def own(m):
        fourth[m][0].wait_recv()
        fifth[m].wait_recv()
        total = done[m, z].astype(jnp.float32)
        for k in (0, 2):
            total = total + z_last[m, k].astype(jnp.float32)
        shard_out[m] = total

    fetch.done(in_delta[1])
    near_copy = wire.send(delta.at[1], near_in, at.partner)
    give(3)
    value = cot[...].astype(jnp.float32) + d_sum[...]
    d_resid[...] = value
    d_proj[...] = value.astype(jnp.bfloat16)
    weight_grad(3, ctx, d_proj)
    to_core(3)
    fetch.done(in_w[3])

    @pl.loop(0, width // 512)
    def _(j):
        cols = tile(j, 512)
        d_ctx[:, cols] = dot(d_proj[...], wfull[3, cols, :], 1, 1).astype(jnp.bfloat16)

    to_plane(3)
    fetch.done(in_qkv)
    causal = lax.broadcasted_iota(jnp.int32, (count, count), 0) >= lax.broadcasted_iota(
        jnp.int32, (count, count), 1
    )
    left = lax.broadcasted_iota(jnp.int32, (count, 128), 1) < 64
    scaling = 64 ** (-0.5)

    def pair(i):
        cols = tile(i, 128)
        query = qkv[0, :, cols]
        keys = qkv[1, :, cols]
        values = qkv[2, :, cols]
        d_out = d_ctx[:, cols]
        zero = jnp.zeros_like(query)
        got = []
        for side in range(2):
            mask = left if side == 0 else jnp.logical_not(left)
            q_side = jnp.where(mask, query, zero)
            k_side = jnp.where(mask, keys, zero)
            o_side = jnp.where(mask, d_out, zero)
            scores = dot(q_side, keys, 1, 1) * scaling
            scores = jnp.where(causal, scores, masked_fill)
            top = jnp.max(scores, axis=-1, keepdims=True)
            expo = jnp.exp(scores - top)
            probs = expo / jnp.sum(expo, axis=-1, keepdims=True)
            d_probs = dot(o_side, values, 1, 1)
            inner = jnp.sum(d_probs * probs, axis=-1, keepdims=True)
            d_scores = (probs * (d_probs - inner)).astype(jnp.bfloat16)
            got.append(
                (
                    dot(d_scores, k_side),
                    dot(d_scores, q_side, 0, 0),
                    dot(probs.astype(jnp.bfloat16), o_side, 0, 0),
                )
            )
        d_qkv[0, :, cols] = ((got[0][0] + got[1][0]) * scaling).astype(jnp.bfloat16)
        d_qkv[1, :, cols] = ((got[0][1] + got[1][1]) * scaling).astype(jnp.bfloat16)
        d_qkv[2, :, cols] = (got[0][2] + got[1][2]).astype(jnp.bfloat16)

    pl.loop(0, width // 256, unroll=4)(pair)
    give(2)
    pl.loop(width // 256, width // 128, unroll=4)(pair)
    collect(3)
    home.push(3)
    fetch.done(in_normed)
    weight_grad(2, normed, d_qkv.at[2])
    to_core(2)
    to_last(3)
    weight_grad(1, normed, d_qkv.at[1])
    to_core(1)
    to_plane(2)
    weight_grad(0, normed, d_qkv.at[0])
    to_core(0)
    home.pass_on(3)
    to_owner(3)
    to_plane(1)
    collect(2)
    home.push(2)
    for m in (2, 1, 0):
        fetch.done(in_w[m])

    @pl.loop(0, width // 512)
    def _(j):
        cols = tile(j, 512)
        d_norm[:, cols] = (
            dot(d_qkv[0], wfull[0, cols, :], 1, 1)
            + dot(d_qkv[1], wfull[1, cols, :], 1, 1)
            + dot(d_qkv[2], wfull[2, cols, :], 1, 1)
        )

    gain = gains[0:1, :].astype(jnp.float32)
    d_gain = jnp.zeros((8, width), jnp.float32)
    d_bias = jnp.zeros((8, width), jnp.float32)
    for i in range(0, count, 64):
        piece = tok[i : i + 64, :].astype(jnp.float32)
        average = jnp.mean(piece, axis=-1, keepdims=True)
        centred = piece - average
        variance = jnp.mean(centred * centred, axis=-1, keepdims=True)
        scale = lax.rsqrt(variance + norm_eps)
        hat = centred * scale
        dx = d_norm[i : i + 64, :]
        d_gain = d_gain + fold(dx * hat)
        d_bias = d_bias + fold(dx)
        dh = dx * gain
        mean_one = jnp.mean(dh, axis=-1, keepdims=True)
        mean_two = jnp.mean(dh * hat, axis=-1, keepdims=True)
        d_in = scale * (dh - mean_one - hat * mean_two)
        token_grad[i : i + 64, :] = (d_resid[i : i + 64, :] + d_in).astype(jnp.bfloat16)
    mine = small.at[0]
    mine[...] = jnp.zeros((8, width), jnp.float32)
    mine[2:3, :] = gains[2:3, :].astype(jnp.float32)
    mine[0:1, :] = jnp.sum(d_gain, axis=0, keepdims=True)
    mine[1:2, :] = jnp.sum(d_bias, axis=0, keepdims=True)
    for k in range(3):
        mine[3 + k : 4 + k, :] = jnp.sum(vec_part[k], axis=0, keepdims=True)
    small_copy = wire.send(mine, small.at[1], at.partner)
    to_last(2)
    home.relay_far()
    home.pass_on(2)
    near_copy.wait_recv()
    fetch.done(in_delta.pop(0))

    @pl.loop(0, planes)
    def _(k):
        delta[0, k] = (delta[0, k].astype(jnp.float32) + near_in[k].astype(jnp.float32)).astype(
            jnp.bfloat16
        )

    to_plane(0)
    cross(3)
    small_copy.wait_recv()
    small[2] = small[0] + small[1]
    small_copy = wire.send(small.at[2], small.at[3], at.mirror)
    to_last(1)
    to_owner(2)
    own(3)
    to_last(0)
    cross(2)
    small_copy.wait_recv()
    total = small[2] + small[3]
    vec_out[...] = total
    small_in[e] = total
    spot = small_in.at[e]
    plane_copies = [wire.send(spot, spot, (at.across(k), z)) for k in range(1, planes)]
    give(0)
    to_owner(1)
    own(2)
    to_owner(0)
    cross(1)
    cross(0)
    own(1)
    for copy in plane_copies:
        copy.wait_recv()
    total = small_in[0]
    for k in range(1, planes):
        total = total + small_in[k]
    norm_out[...] = total
    norm_rows = norm_out[0:2, :]
    mine = norm_out[0:2, tile(e, 128)]
    lanes = norm_shard.shape[1]
    value = mine[:, 0:lanes]
    for k in range(1, depth):
        value = jnp.where(z == k, mine[:, k * lanes : (k + 1) * lanes], value)
    norm_shard[...] = value
    lane = lax.broadcasted_iota(jnp.int32, (1, 128), 1)
    routed = jnp.sum(jnp.where(lane == e, norm_out[2:3, 0:128], 0.0), keepdims=True)
    gates = jnp.sum(scal[0:8, 0:1], keepdims=True) - 0.5 * (depth * planes * cap - routed)
    vec_rows = vec_out[3:6, :]
    squares = jnp.sum(norm_rows * norm_rows, axis=0, keepdims=True) / (planes * depth) + jnp.sum(
        vec_rows * vec_rows, axis=0, keepdims=True
    ) / depth
    local = scal[8:16, :]
    for m in (3, 2, 1):
        local = local + fold(square_lanes(shard_out[m]))
    lane_squares = squares[:, 0:128]
    for i in range(128, width, 128):
        lane_squares = lane_squares + squares[:, i : i + 128]
    head = lax.broadcasted_iota(jnp.int32, (8, 128), 0) == 0
    local = local + jnp.where(head, jnp.broadcast_to(lane_squares, (8, 128)), 0.0)
    own(0)
    square[0, e] = local + fold(square_lanes(shard_out[0]))
    spot = square.at[0, e]
    copies = [wire.send(spot, spot, (at.across(k), z)) for k in range(1, planes)]
    collect(0)
    home.finish()

    @pl.loop(0, width // 256)
    def _(j):
        cols = tile(j)
        block_out[:, cols] = (resid[:, cols] + part[0, :, cols].astype(jnp.float32)).astype(
            jnp.bfloat16
        )

    for copy in copies:
        copy.wait_recv()
    total = square[0, 0]
    for k in range(1, planes):
        total = total + square[0, k]
    square[1, z] = total
    spot = square.at[1, z]
    copies = [wire.send(spot, spot, at.mates[k]) for k in range(1, depth)]
    for copy in copies:
        copy.wait_recv()
    total = square[1, 0]
    for d in range(1, depth):
        total = total + square[1, d]
    norm = jnp.sqrt(jnp.sum(total, keepdims=True))
    which = lax.broadcasted_iota(jnp.int32, (8, 128), 0)
    stats = jnp.where(which == 0, routed / (count * depth), gates / routed)
    clip = clip_level / jnp.maximum(norm, clip_level)
    square_out[...] = jnp.where(which < 2, stats, jnp.where(which == 2, norm, clip))
    wire.drain()
    fetch.drain()


def attend_back(cap, shard, *args):
    tokens = args[6]
    count, width = tokens.shape
    depth = 4
    bf, full = jnp.bfloat16, jnp.float32
    column = depth * shard
    half = column // 2
    copies = 7 * depth + 96
    shapes = [
        ((count, width), bf),
        ((count, width), bf),
        ((4, shard, width), full),
        ((8, width), full),
        ((8, width), full),
        ((8, 128), full),
        ((2, width // 32), full),
    ]
    return pl.pallas_call(
        functools.partial(reduce_kernel, cap),
        out_shape=[jax.ShapeDtypeStruct(*one) for one in shapes],
        in_specs=[VMEM_SPEC] * 2
        + [ANY_SPEC] * 3
        + [VMEM_SPEC] * 4
        + [ANY_SPEC]
        + [VMEM_SPEC] * 3,
        out_specs=[VMEM_SPEC] * 7,
        scratch_shapes=[
            pltpu.VMEM((4, width, width), bf),
            pltpu.VMEM((3, count, width), bf),
            pltpu.VMEM((count, width), bf),
            pltpu.VMEM((depth, 8, cap, width), bf),
            pltpu.VMEM((count, width), full),
            pltpu.VMEM((count, width), bf),
            pltpu.VMEM((count, width), bf),
            pltpu.VMEM((3, count, width), bf),
            pltpu.VMEM((count, width), full),
            pltpu.VMEM((4, 2, 2, 2, column, width), bf),
            pltpu.VMEM((4, 2, 2, column, width), bf),
            pltpu.VMEM((4, 2, half, width), bf),
            pltpu.VMEM((4, 2, half, width), bf),
            pltpu.VMEM((4, half, width), bf),
            pltpu.VMEM((4, half, width), bf),
            pltpu.VMEM((4, depth, shard, width), bf),
            pltpu.VMEM((4, depth - 1, shard, width), bf),
            pltpu.VMEM((depth, 8, cap, width), bf),
            pltpu.VMEM((depth, count, width), bf),
            pltpu.VMEM((5, count, width), bf),
            pltpu.VMEM((8, cap, width), bf),
            pltpu.VMEM((4, 8, width), full),
            pltpu.VMEM((8, 8, width), full),
            pltpu.VMEM((2, 8, 8, 128), full),
            pltpu.SemaphoreType.DMA((copies,)),
            pltpu.SemaphoreType.DMA((copies,)),
            pltpu.SemaphoreType.DMA((16,)),
        ],
        compiler_params=pltpu.CompilerParams(
            collective_id=2, has_side_effects=True, vmem_limit_bytes=62 << 20
        ),
    )(*args)


def adam_quick(weight, first, second, grad, clip_factor, rate, decay):
    clipped = grad * clip_factor
    moment = beta_one * first + (1.0 - beta_one) * clipped
    square = beta_two * second + (1.0 - beta_two) * clipped * clipped
    root = jnp.sqrt(square * (1.0 / (1.0 - beta_two**STEP))) + adam_eps
    step = moment * (rate / (1.0 - beta_one**STEP)) / root
    return (weight * (1.0 - rate * decay) - step, moment, square)


def adam_kernel(*refs):
    ins, outs = refs[:23], refs[23:]
    facts, block_in, token_in = ins[20:23]
    clip = facts[3:4, 0:1]
    for k in range(3):
        weight, first, second, grad = ins[4 * k : 4 * k + 4]
        new, moment, square = outs[3 * k : 3 * k + 3]
        new[...], moment[...], square[...] = adam_quick(
            weight[...].astype(jnp.float32),
            first[...],
            second[...],
            grad[...].astype(jnp.float32),
            clip,
            rate_matrix,
            decay_rate,
        )

    @pl.when(pl.program_id(0) == 0)
    def _():
        weight, first, second, grad = ins[12:16]
        for k in range(3):
            got = adam_quick(
                weight[k], first[k], second[k], grad[3 + k : 4 + k, :], clip, rate_vector, 0.0
            )
            for out, value in zip(outs[9:12], got):
                out[k] = value
        weight, first, second, grad = ins[16:20]
        got = adam_quick(
            weight[...], first[...], second[...], grad[...], clip, rate_vector, 0.0
        )
        for out, value in zip(outs[12:15], got):
            out[...] = value
        outs[15][...] = block_in[...]
        outs[16][...] = token_in[...]
        outs[17][...] = facts[2:3, 0:1]
        outs[18][...] = jnp.concatenate([facts[0:1, 0:1], facts[1:2, 0:1]], axis=1)


def adam_all(up, down, attn, vector, norm, facts, block_out, token_grad):
    steps = 8
    full = jnp.float32

    def whole(shape):
        return pl.BlockSpec(shape, lambda i: (0,) * len(shape))

    def cut(v):
        return pl.BlockSpec((v.shape[0] // steps, v.shape[1]), lambda i: (i, 0))

    args, in_specs, out_specs, shapes = [], [], [], []
    for group in (up, down, attn):
        args += group
        in_specs += [cut(v) for v in group]
        out_specs += [cut(group[0])] * 3
        shapes += [jax.ShapeDtypeStruct(group[0].shape, full)] * 3
    for group in (vector, norm):
        args += group
        in_specs += [whole(v.shape) for v in group]
        out_specs += [whole(group[0].shape)] * 3
        shapes += [jax.ShapeDtypeStruct(group[0].shape, full)] * 3
    args += [facts]
    in_specs += [whole(facts.shape)]
    for v in (block_out, token_grad):
        args += [v]
        in_specs += [whole(v.shape)]
        out_specs += [whole(v.shape)]
        shapes += [jax.ShapeDtypeStruct(v.shape, v.dtype)]
    for shape in ((1, 1), (1, 2)):
        out_specs += [whole(shape)]
        shapes += [jax.ShapeDtypeStruct(shape, full)]
    return pl.pallas_call(
        adam_kernel,
        grid=(steps,),
        out_shape=shapes,
        in_specs=in_specs,
        out_specs=out_specs,
        compiler_params=pltpu.CompilerParams(vmem_limit_bytes=60 << 20),
    )(*args)


def shards(
    tokens,
    cotangent,
    routes,
    attn_weight,
    attn_first,
    attn_second,
    norm_param,
    norm_first,
    norm_second,
    up_weight,
    up_first,
    up_second,
    down_weight,
    down_first,
    down_second,
    expert_vector,
    vector_first,
    vector_second,
):
    experts_here = lax.axis_size(EX)
    hidden_size = lax.axis_size(HI)
    token_count = tokens.shape[0]
    features = tokens.shape[1]
    capacity = 2 * token_count // experts_here
    slot_rows = experts_here * capacity
    head_dim = features // HEADS
    scaling = head_dim ** (-0.5)
    attn_low = attn_weight.astype(jnp.bfloat16)
    norm_low = norm_param.astype(jnp.bfloat16)
    attn_full, norm_full = (
        lax.all_gather(attn_low, BOTH, axis=1, tiled=True),
        lax.all_gather(norm_low, BOTH, axis=1, tiled=True),
    )
    inputs = tokens.astype(jnp.float32)
    normed, norm_pull = jax.vjp(
        layer_norm, inputs, norm_full[0].astype(jnp.float32), norm_full[1].astype(jnp.float32)
    )
    normed_low = normed.astype(jnp.bfloat16)
    projected = jnp.einsum(
        "td,sde->ste", normed_low, attn_full[:3], preferred_element_type=jnp.float32
    ).astype(jnp.bfloat16)
    query = projected[0].reshape(token_count, HEADS, head_dim)
    keys_all = projected[1].reshape(token_count, HEADS, head_dim)
    values_all = projected[2].reshape(token_count, HEADS, head_dim)
    causal = jnp.arange(token_count)[:, None] >= jnp.arange(token_count)[None, :]

    def score_rows():
        raw = (
            jnp.einsum("qhe,khe->hqk", query, keys_all, preferred_element_type=jnp.float32)
            * scaling
        )
        return jnp.where(causal[None], raw, masked_fill)

    scores = score_rows()
    row_max = jnp.max(scores, axis=-1, keepdims=True)
    expo = jnp.exp(scores - row_max)
    row_total = jnp.sum(expo, axis=-1, keepdims=True)
    log_total = row_max + jnp.log(row_total)
    probs_low = (expo / row_total).astype(jnp.bfloat16)
    context = jnp.einsum("hqk,khe->qhe", probs_low, values_all, preferred_element_type=jnp.float32)
    context = context.reshape(token_count, features).astype(jnp.bfloat16)
    resid = inputs + jnp.dot(context, attn_full[3], preferred_element_type=jnp.float32)
    route = routes[:, 0]
    chosen = (route[:, None] == jnp.arange(experts_here, dtype=jnp.int32)[None, :]).astype(
        jnp.int32
    )
    ranked = jnp.sum((jnp.cumsum(chosen, axis=0) - 1) * chosen, axis=1)
    placed = route * capacity + ranked
    placing = (jnp.arange(slot_rows, dtype=jnp.int32)[:, None] == placed[None, :]).astype(
        jnp.bfloat16
    )
    outgoing = jnp.dot(
        placing, resid.astype(jnp.bfloat16), preferred_element_type=jnp.float32
    ).astype(jnp.bfloat16)
    occupied = jnp.sum(placing.astype(jnp.float32), axis=1).astype(jnp.bfloat16)
    arrived, arrived_mask = (
        lax.all_to_all(
            outgoing.reshape(experts_here, capacity, features),
            EX,
            split_axis=0,
            concat_axis=0,
            tiled=True,
        ),
        lax.all_to_all(
            occupied.reshape(experts_here, capacity),
            EX,
            split_axis=0,
            concat_axis=0,
            tiled=True,
        ),
    )
    gathered, gathered_mask = (
        lax.all_gather(arrived, HI, axis=0, tiled=True),
        lax.all_gather(arrived_mask, HI, axis=0, tiled=True),
    )
    rows_all = gathered.reshape(-1, features)
    mask_all = gathered_mask.reshape(-1).astype(jnp.float32)
    rows_float = rows_all.astype(jnp.float32)
    centroid = expert_vector[0, 0]
    gating = jax.nn.sigmoid(jnp.sum(rows_float * centroid, axis=-1))
    expert_normed, expert_pull = jax.vjp(
        layer_norm, rows_float, expert_vector[0, 1], expert_vector[0, 2]
    )
    expert_low = expert_normed.astype(jnp.bfloat16)
    before = jnp.dot(expert_low, up_weight[0], preferred_element_type=jnp.float32)
    after, gelu_pull = jax.vjp(gelu_exact, before)
    after_low = after.astype(jnp.bfloat16)
    branch_own = lax.psum_scatter(
        jnp.dot(after_low, down_weight[0], preferred_element_type=jnp.float32).astype(jnp.bfloat16),
        HI,
        scatter_dimension=0,
        tiled=True,
    ).astype(jnp.float32)
    own_start = lax.axis_index(HI) * slot_rows
    gating_own = lax.dynamic_slice_in_dim(gating, own_start, slot_rows, 0)
    delta = (gating_own[:, None] * branch_own).astype(jnp.bfloat16)
    returned = lax.all_to_all(
        delta.reshape(experts_here, capacity, features),
        EX,
        split_axis=0,
        concat_axis=0,
        tiled=True,
    )
    delta_tokens = jnp.einsum(
        "st,sd->td",
        placing,
        returned.reshape(slot_rows, features),
        preferred_element_type=jnp.float32,
    )
    block_out = (resid + delta_tokens).astype(jnp.bfloat16)
    routed_count = jnp.sum(mask_all)
    gate_total = jnp.sum(mask_all * gating)
    expert_stats = jnp.stack(
        [routed_count / (token_count * hidden_size), gate_total / routed_count]
    )[:, None]
    cot_slots = jnp.dot(placing, cotangent, preferred_element_type=jnp.float32).astype(jnp.bfloat16)
    cot_arrived = lax.all_to_all(
        cot_slots.reshape(experts_here, capacity, features),
        EX,
        split_axis=0,
        concat_axis=0,
        tiled=True,
    )
    cot_rows = lax.all_gather(cot_arrived, HI, axis=0, tiled=True).reshape(-1, features)
    d_branch = (gating[:, None] * cot_rows.astype(jnp.float32)).astype(jnp.bfloat16)
    grad_down = jnp.einsum("gf,gd->fd", after_low, d_branch, preferred_element_type=jnp.float32)
    d_after = jnp.einsum("gd,fd->gf", d_branch, down_weight[0], preferred_element_type=jnp.float32)
    d_before = gelu_pull(d_after)[0].astype(jnp.bfloat16)
    grad_up = jnp.einsum("gd,gf->df", expert_low, d_before, preferred_element_type=jnp.float32)
    d_expert_normed = jnp.einsum(
        "gf,df->gd", d_before, up_weight[0], preferred_element_type=jnp.float32
    )
    d_rows, d_expert_gain, d_expert_bias = expert_pull(d_expert_normed)
    d_rows_own = lax.psum_scatter(
        d_rows.astype(jnp.bfloat16), HI, scatter_dimension=0, tiled=True
    ).astype(jnp.float32)
    cot_own = lax.dynamic_slice_in_dim(cot_rows, own_start, slot_rows, 0).astype(jnp.float32)
    rows_own = lax.dynamic_slice_in_dim(rows_float, own_start, slot_rows, 0)
    d_gating = jnp.sum(cot_own * branch_own, axis=-1)
    d_logit = d_gating * gating_own * (1.0 - gating_own)
    d_centroid = jnp.sum(d_logit[:, None] * rows_own, axis=0)
    d_sent = (d_rows_own + d_logit[:, None] * centroid).astype(jnp.bfloat16)
    back_slots = lax.all_to_all(
        d_sent.reshape(experts_here, capacity, features),
        EX,
        split_axis=0,
        concat_axis=0,
        tiled=True,
    )
    d_resid = cotangent.astype(jnp.float32) + jnp.einsum(
        "st,sd->td",
        placing,
        back_slots.reshape(slot_rows, features),
        preferred_element_type=jnp.float32,
    )
    vector_grad = lax.psum(jnp.stack([d_centroid, d_expert_gain, d_expert_bias])[None], HI)
    d_project = d_resid.astype(jnp.bfloat16)
    grad_out_proj = jnp.einsum("td,te->de", context, d_project, preferred_element_type=jnp.float32)
    d_context = jnp.einsum(
        "te,de->td", d_project, attn_full[3], preferred_element_type=jnp.float32
    ).astype(jnp.bfloat16)
    d_context = d_context.reshape(token_count, HEADS, head_dim)
    attn_probs = jnp.exp(score_rows() - log_total)
    probs_again = attn_probs.astype(jnp.bfloat16)
    d_probs = jnp.einsum("qhe,khe->hqk", d_context, values_all, preferred_element_type=jnp.float32)
    d_values = jnp.einsum(
        "hqk,qhe->khe", probs_again, d_context, preferred_element_type=jnp.float32
    ).astype(jnp.bfloat16)
    d_scores = (
        attn_probs * (d_probs - jnp.sum(d_probs * attn_probs, axis=-1, keepdims=True))
    ).astype(jnp.bfloat16)
    d_query = (
        jnp.einsum("hqk,khe->qhe", d_scores, keys_all, preferred_element_type=jnp.float32) * scaling
    ).astype(jnp.bfloat16)
    d_keys = (
        jnp.einsum("hqk,qhe->khe", d_scores, query, preferred_element_type=jnp.float32) * scaling
    ).astype(jnp.bfloat16)
    d_projected = jnp.stack(
        [
            d_query.reshape(token_count, features),
            d_keys.reshape(token_count, features),
            d_values.reshape(token_count, features),
        ]
    )
    grad_qkv = jnp.einsum(
        "td,ste->sde", normed_low, d_projected, preferred_element_type=jnp.float32
    )
    d_normed = jnp.einsum(
        "ste,sde->td", d_projected, attn_full[:3], preferred_element_type=jnp.float32
    )
    d_inputs, d_norm_gain, d_norm_bias = norm_pull(d_normed)
    token_grad = (d_resid + d_inputs).astype(jnp.bfloat16)
    grad_attn = jnp.concatenate([grad_qkv, grad_out_proj[None]], axis=0)
    grad_norm_param = jnp.stack([d_norm_gain, d_norm_bias])
    attn_shard, norm_shard = (
        lax.psum_scatter(grad_attn, BOTH, scatter_dimension=1, tiled=True),
        lax.psum_scatter(grad_norm_param, BOTH, scatter_dimension=1, tiled=True),
    )
    local_square = (
        jnp.sum(attn_shard * attn_shard)
        + jnp.sum(norm_shard * norm_shard)
        + jnp.sum(grad_up * grad_up)
        + jnp.sum(grad_down * grad_down)
        + jnp.sum(vector_grad * vector_grad) / hidden_size
    )
    grad_norm = jnp.sqrt(lax.psum(local_square, BOTH))
    clip_factor = clip_level / jnp.maximum(grad_norm, clip_level)
    attn_new = adam_step(
        attn_weight, attn_first, attn_second, attn_shard, clip_factor, rate_matrix, decay_rate
    )
    norm_new = adam_step(
        norm_param, norm_first, norm_second, norm_shard, clip_factor, rate_vector, 0.0
    )
    up_new = adam_step(
        up_weight.astype(jnp.float32),
        up_first,
        up_second,
        grad_up[None],
        clip_factor,
        rate_matrix,
        decay_rate,
    )
    down_new = adam_step(
        down_weight.astype(jnp.float32),
        down_first,
        down_second,
        grad_down[None],
        clip_factor,
        rate_matrix,
        decay_rate,
    )
    vector_new = adam_step(
        expert_vector, vector_first, vector_second, vector_grad, clip_factor, rate_vector, 0.0
    )
    return (
        block_out,
        token_grad,
        grad_norm,
        attn_new[0],
        attn_new[1],
        attn_new[2],
        norm_new[0],
        norm_new[1],
        norm_new[2],
        up_new[0],
        up_new[1],
        up_new[2],
        down_new[0],
        down_new[1],
        down_new[2],
        vector_new[0],
        vector_new[1],
        vector_new[2],
        expert_stats,
    )


def fast_shards(
    tokens,
    cotangent,
    routes,
    attn_weight,
    attn_first,
    attn_second,
    norm_param,
    norm_first,
    norm_second,
    up_weight,
    up_first,
    up_second,
    down_weight,
    down_first,
    down_second,
    expert_vector,
    vector_first,
    vector_second,
):
    experts = lax.axis_size(EX)
    count, width = tokens.shape
    cap = 2 * count // experts
    shard = attn_weight.shape[1]
    w_full, qkv, normed, ctx, resid, sent, placed, gains, cot_raw, cot_zero = attend(
        cap, tokens, attn_weight, norm_param, routes.reshape(1, count), cotangent
    )
    rows = lambda v: v.reshape(3, 1, width)
    d_sum, grad_up, grad_down, delta, vec_part, scal = expert_layer(
        cap, sent, placed, cot_raw, cot_zero, up_weight[0], down_weight[0], rows(expert_vector)
    )
    block_out, token_grad, attn_shard, norm_grads, vec_grads, facts, norm_shard = attend_back(
        cap,
        shard,
        d_sum,
        cotangent,
        w_full,
        qkv,
        normed,
        ctx,
        tokens,
        gains,
        placed,
        delta,
        resid,
        vec_part,
        scal,
    )
    flat = lambda v: v.reshape(-1, v.shape[-1])
    new = adam_all(
        [flat(v) for v in (up_weight, up_first, up_second, grad_up)],
        [flat(v) for v in (down_weight, down_first, down_second, grad_down)],
        [flat(v) for v in (attn_weight, attn_first, attn_second, attn_shard)],
        [rows(v) for v in (expert_vector, vector_first, vector_second)] + [vec_grads],
        [norm_param, norm_first, norm_second, norm_shard],
        facts,
        block_out,
        token_grad,
    )
    up_new = [v.reshape(up_weight.shape) for v in new[0:3]]
    down_new = [v.reshape(down_weight.shape) for v in new[3:6]]
    attn_new = [v.reshape(attn_weight.shape) for v in new[6:9]]
    vector_new = [v.reshape(expert_vector.shape) for v in new[9:12]]
    norm_new = new[12:15]
    block_out, token_grad = new[15:17]
    grad_norm = new[17].reshape(())
    expert_stats = new[18].reshape(2, 1)
    return (
        block_out,
        token_grad,
        grad_norm,
        *attn_new,
        *norm_new,
        *up_new,
        *down_new,
        *vector_new,
        expert_stats,
    )


def solution(mesh):
    small = mesh.shape[EX] == 8 and mesh.shape[HI] == 4
    return jax.shard_map(
        fast_shards if small else shards,
        mesh=mesh,
        in_specs=(
            P(BOTH, None),
            P(BOTH, None),
            P(BOTH, None),
            P(None, BOTH, None),
            P(None, BOTH, None),
            P(None, BOTH, None),
            P(None, BOTH),
            P(None, BOTH),
            P(None, BOTH),
            P(EX, None, HI),
            P(EX, None, HI),
            P(EX, None, HI),
            P(EX, HI, None),
            P(EX, HI, None),
            P(EX, HI, None),
            P(EX, None, None),
            P(EX, None, None),
            P(EX, None, None),
        ),
        out_specs=(
            P(BOTH, None),
            P(BOTH, None),
            P(),
            P(None, BOTH, None),
            P(None, BOTH, None),
            P(None, BOTH, None),
            P(None, BOTH),
            P(None, BOTH),
            P(None, BOTH),
            P(EX, None, HI),
            P(EX, None, HI),
            P(EX, None, HI),
            P(EX, HI, None),
            P(EX, HI, None),
            P(EX, HI, None),
            P(EX, None, None),
            P(EX, None, None),
            P(EX, None, None),
            P(None, EX),
        ),
        check_vma=False,
    )
```

```python
import functools
import math

import jax
import jax.numpy as jnp
from jax import lax
from jax.experimental import pallas as pl
from jax.experimental.pallas import tpu as pltpu
from jax.sharding import PartitionSpec as P

HEADS = 16
STEP = 10


norm_eps = 1e-05
clip_level = 1.0
beta_one = 0.9
beta_two = 0.999
adam_eps = 1e-08
decay_rate = 0.1
rate_matrix = 0.05
rate_vector = 0.5
masked_fill = -1e30
EX, HI = "expert", "hidden"
BOTH = (EX, HI)


def layer_norm(inputs, gain_row, bias_row):
    average = jnp.mean(inputs, axis=-1, keepdims=True)
    centred = inputs - average
    variance = jnp.mean(centred * centred, axis=-1, keepdims=True)
    return centred * lax.rsqrt(variance + norm_eps) * gain_row + bias_row


def gelu_exact(values):
    return jax.nn.gelu(values, approximate=False)


def adam_step(weight, first, second, grad, clip_factor, rate, decay):
    clipped = grad * clip_factor
    moment = beta_one * first + (1.0 - beta_one) * clipped
    square = beta_two * second + (1.0 - beta_two) * clipped * clipped
    corr_one = 1.0 - beta_one**STEP
    corr_two = 1.0 - beta_two**STEP
    update = moment / corr_one / (jnp.sqrt(square / corr_two) + adam_eps) + decay * weight
    return (weight - rate * update, moment, square)


MESH = pl.DeviceIdType.MESH
VMEM_SPEC = pl.BlockSpec(memory_space=pltpu.VMEM)
ANY_SPEC = pl.BlockSpec(memory_space=pl.ANY)


class Place:
    def __init__(self):
        self.e = lax.axis_index(EX)
        self.z = lax.axis_index(HI)
        high, low = lax.div(self.z, 2), lax.rem(self.z, 2)
        self.middle = high + low == 1
        self.ends = jnp.logical_not(self.middle)
        self.line = [self.z, self.z + 1 - 2 * low, 2 - high, 3 - 3 * high]
        self.core = lax.rem(self.e, 2)
        self.x = lax.rem(lax.div(self.e, 2), 2)
        self.y = lax.div(self.e, 4)
        self.ex = self.e + 2 - 4 * self.x
        self.ey = self.e + 4 - 8 * self.y
        self.exy = self.ex + 4 - 8 * self.y
        self.twin = (self.e + 1 - 2 * self.core, self.z)
        self.over_x = (self.ex, self.z)
        self.over_y = (self.ey, self.z)
        self.partner = (self.e, self.line[1])
        self.mirror = (self.e, 3 - self.z)
        self.mates = [None, self.partner, (self.e, self.z + 2 - 4 * high), self.mirror]

    def across(self, k):
        c = lax.rem(self.core + k % 2, 2)
        x = lax.rem(self.x + (k // 2) % 2, 2)
        y = lax.rem(self.y + k // 4, 2)
        return 4 * y + 2 * x + c

    def everyone(self):
        plane = [(self.across(k), self.z) for k in range(1, 8)]
        return plane + self.mates[1:]

    def meet(self):
        barrier = pltpu.get_barrier_semaphore()
        for device in self.everyone():
            pl.semaphore_signal(barrier, inc=1, device_id=device, device_id_type=MESH)
        pl.semaphore_wait(barrier, len(self.everyone()))


class Wire:
    def __init__(self, send_sem, recv_sem):
        self.send_sem, self.recv_sem = send_sem, recv_sem
        self.count = 0
        self.tags = {}
        self.sent = []

    def next(self):
        self.count += 1
        return self.count - 1

    def send(self, src, dst, device, tag=None, when=None):
        i = self.next()
        if tag is not None:
            if tag not in self.tags:
                self.tags[tag] = self.next()
            j = self.tags[tag]
        else:
            j = i
        copy = pltpu.make_async_remote_copy(
            src_ref=src,
            dst_ref=dst,
            send_sem=self.send_sem.at[i],
            recv_sem=self.recv_sem.at[j],
            device_id=device,
            device_id_type=MESH,
        )
        if when is None:
            copy.start()
        else:
            pl.when(when)(copy.start)
        self.sent.append((copy, when))
        return copy

    def arrived(self, tag, dst, device):
        if tag not in self.tags:
            self.tags[tag] = self.next()
        j = self.tags[tag]
        pltpu.make_async_remote_copy(
            src_ref=dst,
            dst_ref=dst,
            send_sem=self.send_sem.at[j],
            recv_sem=self.recv_sem.at[j],
            device_id=device,
            device_id_type=MESH,
        ).wait_recv()

    def left(self, copy):
        copy.wait_send()
        self.sent = [one for one in self.sent if one[0] is not copy]

    def drain(self):
        for copy, when in self.sent:
            if when is None:
                copy.wait_send()
            else:
                pl.when(when)(copy.wait_send)
        self.sent = []


class Line:
    def __init__(self, wire, at, name, slot):
        self.wire, self.at, self.name, self.slot = wire, at, name, slot

    def begin(self, own=None, outer=1, inner=True):
        at = self.at
        here = self.slot(at.z)
        own = here if own is None else own
        if outer:
            when = {1: None, 2: at.ends, 3: at.middle}[outer]
            self.wire.send(own, here, at.partner, (self.name, 1), when)
        if inner:
            self.wire.send(own, here, at.mirror, (self.name, 2), at.middle)

    def take(self, i, when=None):
        at = self.at
        block = self.slot(at.line[i])
        if when is None:
            self.wire.arrived((self.name, i), block, at.partner)
        else:
            pl.when(when)(lambda: self.wire.arrived((self.name, i), block, at.partner))
        if when is not at.ends:
            to, tag = (at.mirror, 3) if i == 1 else (at.partner, i)
            self.wire.send(block, block, to, (self.name, tag), at.middle)
        return block


class Fetch:
    def __init__(self, sem):
        self.sem = sem
        self.count = 0
        self.open = []

    def start(self, src, dst):
        copy = pltpu.make_async_copy(src, dst, self.sem.at[self.count])
        self.count += 1
        copy.start()
        self.open.append(copy)
        return copy

    def done(self, copy):
        copy.wait()
        self.open = [one for one in self.open if one is not copy]

    def drain(self):
        for copy in self.open:
            copy.wait()
        self.open = []


def dot(a, b, ca=1, cb=0):
    return lax.dot_general(a, b, (((ca,), (cb,)), ((), ())), preferred_element_type=jnp.float32)


def tile(i, size=256):
    return pl.ds(pl.multiple_of(i * size, size), size)


def pick(placed_row, slots):
    which = lax.broadcasted_iota(jnp.int32, (slots, placed_row.shape[1]), 0)
    return jnp.where(which == placed_row, 1.0, 0.0).astype(jnp.bfloat16)


def build(stage, source, placed_row):
    planes, cap, width = stage.shape
    onehot = pick(placed_row, planes * cap)

    @pl.loop(0, width // 512)
    def _(i):
        cols = tile(i, 512)
        value = dot(onehot, source[:, cols]).astype(jnp.bfloat16)
        for k in range(planes):
            stage[k, :, cols] = value[k * cap : (k + 1) * cap]


def attend_kernel(
    cap,
    tok,
    w_own,
    norm_in,
    route,
    cot,
    w_out,
    qkv_out,
    normed_out,
    ctx_out,
    resid_out,
    sent_out,
    placed_out,
    gains_out,
    cot_raw,
    cot_zero,
    w_low,
    wfull,
    norm_low,
    pieces,
    qkv,
    normed,
    ctx,
    resid,
    sent,
    placed,
    gains,
    stage,
    send_sem,
    recv_sem,
    local_sem,
):
    at = Place()
    e, z = at.e, at.z
    depth = 4
    count, width = tok.shape
    shard = w_own.shape[1]
    wire = Wire(send_sem, recv_sem)
    fetch = Fetch(local_sem)
    groups = [(0, 3), (3, 1)]
    fetch.start(cot, cot_raw.at[z])
    w_low[...] = w_own[...].astype(jnp.bfloat16)
    lanes = norm_in.shape[1]
    offset = lax.broadcasted_iota(jnp.int32, (lanes, 128), 1) - z * lanes
    ours = lax.broadcasted_iota(jnp.int32, (lanes, 128), 0) == offset
    low = norm_in[...].astype(jnp.bfloat16)
    norm_low[...] = jnp.zeros((16, 128), jnp.bfloat16)
    norm_low[0:2, :] = dot(low, jnp.where(ours, 1.0, 0.0).astype(jnp.bfloat16)).astype(
        jnp.bfloat16
    )
    at.meet()

    def block(g, who, zz):
        if g == 2:
            return pieces.at[who, zz]
        first, mats = groups[g]
        start = pl.multiple_of((who * depth + zz) * shard, shard)
        return wfull.at[pl.ds(first, mats), pl.ds(start, shard)]

    def mine(g):
        if g == 2:
            return norm_low
        first, mats = groups[g]
        return w_low.at[pl.ds(first, mats)]

    lines = [Line(wire, at, g, lambda zz, g=g: block(g, e, zz)) for g in range(3)]
    lines[2].begin(mine(2))
    lines[0].begin(mine(0))
    lines[1].begin(mine(1), outer=2, inner=False)
    cots = Line(wire, at, "cot", lambda zz: cot_raw.at[zz])
    cots.begin(cot, outer=2, inner=False)
    own = [fetch.start(mine(g), block(g, e, z)) for g in range(3)]
    to_x, to_y, to_far, to_twin = {}, {}, {}, {}

    def over_x(g, i):
        here = block(g, e, at.line[i])
        to_x[g, i] = wire.send(here, here, at.over_x)
        to_twin[g, i, 0] = wire.send(here, here, at.twin)

    def over_y(g, i):
        here = block(g, e, at.line[i])
        to_y[g, i] = wire.send(here, here, at.over_y)

    def forward(g, i):
        zz = at.line[i]
        if i in (0, 3):
            to_x[g, i].wait_recv()
            block_x = block(g, at.ex, zz)
            to_far[g, i] = wire.send(block_x, block_x, at.over_y)
            to_twin[g, i, 1] = wire.send(block_x, block_x, at.twin)
        else:
            to_y[g, i].wait_recv()
            block_y = block(g, at.ey, zz)
            to_far[g, i] = wire.send(block_y, block_y, at.over_x)
            to_twin[g, i, 1] = wire.send(block_y, block_y, at.twin)

    def side(g, i):
        zz = at.line[i]
        if i in (0, 3):
            to_y[g, i].wait_recv()
            there = block(g, at.ey, zz)
        else:
            to_x[g, i].wait_recv()
            there = block(g, at.ex, zz)
        to_twin[g, i, 2] = wire.send(there, there, at.twin)

    def far(g, i):
        to_far[g, i].wait_recv()
        there = block(g, at.exy, at.line[i])
        to_twin[g, i, 3] = wire.send(there, there, at.twin)

    def finish(g):
        for i in range(depth):
            for k in range(4):
                to_twin[g, i, k].wait_recv()

    def both(step, i):
        step(2, i)
        step(0, i)

    def take(i):
        lines[2].take(i)
        lines[0].take(i)

    for copy in (own[2], own[0]):
        fetch.done(copy)
    both(over_x, 0)
    both(over_y, 0)
    wide_r = lax.broadcasted_iota(jnp.int32, (count, count), 0)
    wide_c = lax.broadcasted_iota(jnp.int32, (count, count), 1)
    route_row = route[...].astype(jnp.float32)
    route_col = jnp.sum(jnp.where(wide_r == wide_c, route_row, 0.0), axis=1, keepdims=True)
    lane = lax.broadcasted_iota(jnp.int32, (count, 128), 1)
    chosen = jnp.where(route_col.astype(jnp.int32) == lane, 1.0, 0.0)
    rows_i = lax.broadcasted_iota(jnp.int32, (count, count), 0)
    cols_i = lax.broadcasted_iota(jnp.int32, (count, count), 1)
    lower = jnp.where(rows_i >= cols_i, 1.0, 0.0)
    running = dot(lower.astype(jnp.bfloat16), chosen.astype(jnp.bfloat16))
    rank = jnp.sum((running - 1.0) * chosen, axis=1, keepdims=True)
    column = route_col * float(cap) + rank
    row = jnp.sum(jnp.where(wide_r == wide_c, column, 0.0), axis=0, keepdims=True)
    row = jnp.concatenate([row, jnp.full((1, 256 - count), -1.0, jnp.float32)], axis=1)
    placed[z] = jnp.broadcast_to(row, (8, 256)).astype(jnp.int32)
    take(1)
    both(over_x, 1)
    both(over_y, 1)
    build(stage, cot, placed[z, 0:1, :count])
    both(forward, 0)
    take(2)
    lines[1].begin(mine(1), outer=3)
    both(forward, 1)
    both(over_y, 2)
    take(3)
    lines[1].take(1, at.middle)
    lines[1].take(2, at.middle)
    both(over_x, 3)
    both(over_x, 2)
    both(over_y, 3)
    both(side, 0)
    both(side, 1)
    both(far, 0)
    both(far, 1)
    lines[1].take(3, at.middle)
    cots.begin(cot, outer=0)
    both(forward, 2)
    both(forward, 3)
    cots.take(1, at.middle)
    places = Line(wire, at, "place", lambda zz: placed.at[zz])
    places.begin()
    fetch.done(own[1])
    for i in range(depth):
        if i:
            lines[1].take(i, at.ends)
        over_x(1, i)
        over_y(1, i)
    both(side, 3)
    both(side, 2)
    both(far, 2)
    both(far, 3)
    cots.take(2, at.middle)
    finish(2)
    cots.take(3, at.middle)
    gain_rows = jnp.concatenate(
        [
            sum([pieces[who, zz] for zz in range(1, depth)], pieces[who, 0])
            for who in range(8)
        ],
        axis=1,
    )
    tally = jnp.concatenate(
        [
            jnp.broadcast_to(jnp.sum(chosen, axis=0, keepdims=True), (16, 128)),
            jnp.zeros((16, width - 128), jnp.float32),
        ],
        axis=1,
    )
    third_row = lax.broadcasted_iota(jnp.int32, (16, width), 0) == 2
    gains[...] = jnp.where(third_row, tally, gain_rows.astype(jnp.float32)).astype(jnp.bfloat16)
    fetch.start(gains, gains_out)
    gain = gains[0:1, :].astype(jnp.float32)
    bias = gains[1:2, :].astype(jnp.float32)

    @pl.loop(0, count // 64)
    def _(i):
        rows = tile(i, 64)
        piece = tok[rows, :].astype(jnp.float32)
        average = jnp.mean(piece, axis=-1, keepdims=True)
        centred = piece - average
        variance = jnp.mean(centred * centred, axis=-1, keepdims=True)
        normed[rows, :] = (centred * lax.rsqrt(variance + norm_eps) * gain + bias).astype(
            jnp.bfloat16
        )

    fetch.start(normed, normed_out)
    finish(0)
    fetch.start(wfull.at[pl.ds(0, 3)], w_out.at[pl.ds(0, 3)])
    tiles = width // 512

    def project(i):
        m = lax.div(i, tiles)
        cols = tile(lax.rem(i, tiles), 512)
        qkv[m, :, cols] = dot(normed[...], wfull[m, :, cols]).astype(jnp.bfloat16)

    pl.loop(0, tiles)(project)
    for i in range(depth):
        forward(1, i)
    slots_out = [
        wire.send(stage.at[at.across(k)], cot_zero.at[k], (at.across(k), z)) for k in range(1, 8)
    ]
    fetch.start(stage.at[e], cot_zero.at[0])
    places.take(1)
    pl.loop(tiles, 3 * tiles)(project)
    fetch.start(qkv, qkv_out)
    for i in range(depth):
        side(1, i)
    places.take(2, at.middle)
    causal = rows_i >= cols_i
    left = lax.broadcasted_iota(jnp.int32, (count, 128), 1) < 64
    scaling = jnp.asarray(64 ** (-0.5), jnp.bfloat16)

    def pair(i):
        cols = tile(i, 128)
        query = qkv[0, :, cols] * scaling
        keys = qkv[1, :, cols]
        values = qkv[2, :, cols]
        halves = []
        for side in range(2):
            mask = left if side == 0 else jnp.logical_not(left)
            scores = dot(jnp.where(mask, query, jnp.zeros_like(query)), keys, 1, 1)
            scores = jnp.where(causal, scores, masked_fill)
            top = jnp.max(scores, axis=-1, keepdims=True)
            expo = jnp.exp(scores - top)
            probs = expo / jnp.sum(expo, axis=-1, keepdims=True)
            halves.append(dot(probs.astype(jnp.bfloat16), values))
        ctx[:, cols] = jnp.where(left, halves[0], halves[1]).astype(jnp.bfloat16)

    pl.loop(0, 6, unroll=3)(pair)
    for i in range(depth):
        far(1, i)
    places.take(2, at.ends)
    places.take(3, at.middle)
    pl.loop(6, width // 128, unroll=2)(pair)
    fetch.start(ctx, ctx_out)
    finish(1)
    fetch.start(wfull.at[pl.ds(3, 1)], w_out.at[pl.ds(3, 1)])

    @pl.loop(0, tiles)
    def _(i):
        cols = tile(i, 512)
        value = tok[:, cols].astype(jnp.float32) + dot(ctx[...], wfull[3, :, cols])
        resid[:, cols] = value
        sent[:, cols] = value.astype(jnp.bfloat16)

    fetch.start(sent, sent_out)
    fetch.start(resid, resid_out)
    places.take(3, at.ends)
    cots.take(2, at.ends)
    cots.take(3, at.ends)
    fetch.start(placed, placed_out)
    for copy in slots_out:
        copy.wait_recv()
    wire.drain()
    fetch.drain()


def attend(cap, tokens, w_own, norm_own, routes, cotangent):
    count, width = tokens.shape
    bf, full = jnp.bfloat16, jnp.float32
    copies = 176
    shapes = [
        ((4, width, width), bf),
        ((3, count, width), bf),
        ((count, width), bf),
        ((count, width), bf),
        ((count, width), full),
        ((count, width), bf),
        ((4, 8, 256), jnp.int32),
        ((16, width), bf),
        ((4, count, width), bf),
        ((8, cap, width), bf),
    ]
    return pl.pallas_call(
        functools.partial(attend_kernel, cap),
        out_shape=[jax.ShapeDtypeStruct(*one) for one in shapes],
        in_specs=[VMEM_SPEC] * 5,
        out_specs=[ANY_SPEC] * len(shapes),
        scratch_shapes=[
            pltpu.VMEM((4, w_own.shape[1], width), bf),
            pltpu.VMEM((4, width, width), bf),
            pltpu.VMEM((16, 128), bf),
            pltpu.VMEM((8, 4, 16, 128), bf),
            pltpu.VMEM((3, count, width), bf),
            pltpu.VMEM((count, width), bf),
            pltpu.VMEM((count, width), bf),
            pltpu.VMEM((count, width), full),
            pltpu.VMEM((count, width), bf),
            pltpu.VMEM((4, 8, 256), jnp.int32),
            pltpu.VMEM((16, width), bf),
            pltpu.VMEM((8, cap, width), bf),
            pltpu.SemaphoreType.DMA((copies,)),
            pltpu.SemaphoreType.DMA((copies,)),
            pltpu.SemaphoreType.DMA((16,)),
        ],
        compiler_params=pltpu.CompilerParams(
            collective_id=0, has_side_effects=True, vmem_limit_bytes=62 << 20
        ),
    )(tokens, w_own, norm_own, routes, cotangent)


def gelu_pair(v):
    cdf = 0.5 + 0.5 * lax.erf(v * (0.5**0.5))
    pdf = jnp.exp(-0.5 * v * v) * ((2.0 * math.pi) ** -0.5)
    return v * cdf, cdf + v * pdf


def fold(v):
    total = v[0:8]
    for i in range(8, v.shape[0], 8):
        total = total + v[i : i + 8]
    return total


def spread(column, lanes):
    return jnp.concatenate([column] * (lanes // 128), axis=1)


def square_lanes(v):
    total = v[:, 0:128] * v[:, 0:128]
    for i in range(128, v.shape[1], 128):
        total = total + v[:, i : i + 128] * v[:, i : i + 128]
    return total


def unslot(placed_row, slots, out):
    planes, cap, width = slots.shape
    onehot = pick(placed_row, planes * cap)

    @pl.loop(0, width // 256)
    def _(j):
        cols = tile(j)
        value = slots[:, :, cols].reshape(planes * cap, 256)
        out[:, cols] = dot(onehot, value, 0, 0).astype(jnp.bfloat16)


class Home:
    def __init__(self, wire, at, name, part, got):
        self.wire, self.at, self.name = wire, at, name
        self.part, self.got = part, got
        half = got.shape[1] // 2
        self.halves = [pl.ds(0, half), pl.ds(half, half)]

    def add(self, i, k, half):
        part = self.part(i)
        part[half, :] = (
            part[half, :].astype(jnp.float32) + self.got[k, half, :].astype(jnp.float32)
        ).astype(jnp.bfloat16)

    def arrived(self, tag, k, n, device):
        half = self.halves[n]
        self.wire.arrived((self.name, tag, n), self.got.at[k, half], device)

    def send(self, src, k, n, device, tag, when=None):
        half = self.halves[n]
        self.wire.send(src.at[half], self.got.at[k, half], device, (self.name, tag, n), when)

    def push(self, i):
        for n in range(2):
            self.send(self.part(i), i - 1, n, self.at.partner, i, self.at.ends)

    def pass_on(self, i):
        at = self.at
        k = {3: 3, 2: 4}[i]
        for n, half in enumerate(self.halves):

            @pl.when(at.middle)
            def _():
                self.arrived(i, i - 1, n, at.partner)
                self.add(i, i - 1, half)

            self.send(self.part(i), k, n, at.mirror, k + 1, at.middle)

    def near(self):
        at = self.at
        for n, half in enumerate(self.halves):

            @pl.when(at.middle)
            def _():
                self.arrived(4, 3, n, at.mirror)
                self.add(1, 3, half)

            self.send(self.part(1), 0, n, at.partner, 1)

    def relay_far(self):
        at = self.at
        for n in range(2):
            pl.when(at.middle)(lambda: self.arrived(4, 3, n, at.mirror))
            self.send(self.got.at[3], 0, n, at.partner, 1, at.middle)

    def finish(self):
        at = self.at
        for n, half in enumerate(self.halves):

            @pl.when(at.ends)
            def _():
                self.arrived(1, 0, n, at.partner)
                self.add(0, 0, half)

            @pl.when(at.middle)
            def _():
                self.arrived(5, 4, n, at.mirror)
                self.add(0, 4, half)

    def last(self):
        at = self.at
        for n, half in enumerate(self.halves):
            self.arrived(1, 0, n, at.partner)

            @pl.when(at.middle)
            def _():
                self.arrived(5, 4, n, at.mirror)
                self.add(0, 4, half)

    def total(self, cols):
        return self.part(0)[:, cols].astype(jnp.float32) + self.got[0, :, cols].astype(jnp.float32)


def expert_kernel(
    cap,
    sent_in,
    placed_in,
    cot_raw,
    cot_zero,
    up_in,
    down_in,
    vec,
    d_sum,
    g_up,
    g_down,
    delta_out,
    vec_part,
    scal,
    sent,
    placed,
    cot_line,
    up,
    down,
    raw,
    stage,
    rows,
    cots,
    xn,
    act,
    slope,
    delta,
    d_slots,
    back,
    part,
    z_in,
    d_xn,
    gate,
    d_logit,
    g_stage,
    send_sem,
    recv_sem,
    local_sem,
):
    at = Place()
    e, z = at.e, at.z
    depth, planes = 4, 8
    count, width = sent.shape
    slots = planes * cap
    units = up.shape[1]
    wire = Wire(send_sem, recv_sem)
    fetch = Fetch(local_sem)
    in_sent = fetch.start(sent_in, sent)
    in_placed = fetch.start(placed_in, placed)
    in_up = fetch.start(up_in, up)
    in_down = fetch.start(down_in, down)
    in_cot = fetch.start(cot_raw, cot_line)
    in_zero = fetch.start(cot_zero, cots.at[0])
    at.meet()
    fetch.done(in_sent)
    line = Line(wire, at, "row", lambda zz: raw.at[zz])
    line.begin(sent)
    vec_part[...] = jnp.zeros_like(vec_part)
    scal[...] = jnp.zeros_like(scal)
    fetch.done(in_placed)
    centroid = lambda: vec[0]
    row_copies, cot_copies, ret_copies = {}, {}, {}

    def exchange(i, dst, s, offsets=range(1, planes)):
        return [
            wire.send(stage.at[s, at.across(k)], dst.at[i, k], (at.across(k), z)) for k in offsets
        ]

    def slot_row(i):
        return placed[at.line[i], 0:1, :count]

    def rows_out(i):
        source = sent if i == 0 else raw.at[at.line[i]]
        build(stage.at[i], source, slot_row(i))
        row_copies[i] = exchange(i, rows, i)
        rows[i, 0] = stage[i, e]

    def cots_out(i, s, offsets):
        if i not in cot_copies:
            for copy in row_copies[s]:
                wire.left(copy)
            build(stage.at[s], cot_line.at[at.line[i]], slot_row(i))
            cot_copies[i] = []
            cots[i, 0] = stage[s, e]
        cot_copies[i] += exchange(i, cots, s, offsets)

    def forward(i):
        for copy in row_copies[i]:
            copy.wait_recv()
        gain, bias = vec[1], vec[2]

        @pl.loop(0, planes, unroll=2)
        def _(k):
            r = rows[i, k].astype(jnp.float32)
            logit = jnp.sum(r * centroid(), axis=-1, keepdims=True)
            g = jax.nn.sigmoid(logit)
            wide = jnp.broadcast_to(g, (cap, 128))
            gate[i, k] = wide
            scal[0:8] += fold(wide)
            average = jnp.mean(r, axis=-1, keepdims=True)
            centred = r - average
            variance = jnp.mean(centred * centred, axis=-1, keepdims=True)
            xn[i, pl.ds(pl.multiple_of(k * cap, 16), cap), :] = (
                centred * lax.rsqrt(variance + norm_eps) * gain + bias
            ).astype(jnp.bfloat16)

        if i == 0:
            fetch.done(in_up)

        @pl.loop(0, units // 512)
        def _(j):
            cols = tile(j, 512)
            value, rate = gelu_pair(dot(xn[i], up[:, cols]))
            act[i, :, cols] = value.astype(jnp.bfloat16)
            slope[i, :, cols] = rate.astype(jnp.bfloat16)

        if i == 0:
            fetch.done(in_down)

        @pl.loop(0, width // 512)
        def _(j):
            cols = tile(j, 512)
            branch = dot(act[i], down[:, cols])
            wide = spread(gate[i].reshape(slots, 128), 512)
            value = (wide * branch).astype(jnp.bfloat16)
            for k in range(planes):
                delta[i, k, :, cols] = value[k * cap : (k + 1) * cap]

        fetch.start(delta.at[i], delta_out.at[i])

    def backward(i):
        for copy in cot_copies[i]:
            copy.wait_recv()

        @pl.loop(0, planes, unroll=2)
        def _(k):
            c = cots[i, k].astype(jnp.float32)
            g = gate[i, k]
            inner = jnp.sum(c * delta[i, k].astype(jnp.float32), axis=-1, keepdims=True)
            dl = (1.0 - g) * inner
            d_logit[i, k] = dl
            cots[i, k] = (c * spread(g, width)).astype(jnp.bfloat16)
            vec_part[0] += fold(rows[i, k].astype(jnp.float32) * spread(dl, width))

        @pl.loop(0, units // 512)
        def _(j):
            cols = tile(j, 512)
            d_act = dot(cots[i].reshape(slots, width), down[cols, :], 1, 1)
            slope[i, :, cols] = (d_act * slope[i, :, cols].astype(jnp.float32)).astype(
                jnp.bfloat16
            )

    def backward_in(i):
        @pl.loop(0, width // 512)
        def _(j):
            cols = tile(j, 512)
            value = dot(slope[i], up[cols, :], 1, 1)
            for k in range(planes):
                d_xn[k, :, cols] = value[k * cap : (k + 1) * cap]

        @pl.loop(0, planes, unroll=2)
        def _(k):
            r = rows[i, k].astype(jnp.float32)
            average = jnp.mean(r, axis=-1, keepdims=True)
            centred = r - average
            variance = jnp.mean(centred * centred, axis=-1, keepdims=True)
            scale = lax.rsqrt(variance + norm_eps)
            hat = centred * scale
            dx = d_xn[k]
            vec_part[1] += fold(dx * hat)
            vec_part[2] += fold(dx)
            dh = dx * vec[1]
            first = jnp.mean(dh, axis=-1, keepdims=True)
            second = jnp.mean(dh * hat, axis=-1, keepdims=True)
            d_in = scale * (dh - first - hat * second)
            d_slots[i, k] = (d_in + spread(d_logit[i, k], width) * centroid()).astype(jnp.bfloat16)

    def give(i):
        ret_copies[i] = [
            wire.send(d_slots.at[i, k], back.at[i, e], (at.across(k), z))
            for k in range(1, planes)
        ]
        back[i, e] = d_slots[i, 0]

    home = Home(wire, at, "home", lambda i: part.at[i], z_in)

    def collect(i):
        for copy in ret_copies[i]:
            copy.wait_recv()
        unslot(slot_row(i), back.at[i], part.at[i])

    def weight_grad(lhs, rhs, index, out):
        @pl.loop(0, lhs.shape[-1] // 512)
        def _(j):
            cols = tile(j, 512)
            left = lhs[:, :, cols].reshape(depth * slots, 512)
            value = dot(left, rhs[...].reshape(depth * slots, rhs.shape[-1]), 0, 0)
            scal[8:16] += fold(square_lanes(value))
            g_stage[index, cols, :] = value.astype(jnp.bfloat16)

        fetch.start(g_stage.at[index], out)

    rows_out(0)
    line.take(1)
    line.take(2, at.middle)
    rows_out(1)
    fetch.done(in_cot)
    cots_out(3, 0, (2, 4, 6))
    forward(0)
    line.take(2, at.ends)
    line.take(3, at.middle)
    rows_out(2)
    forward(1)
    line.take(3, at.ends)
    rows_out(3)
    fetch.done(in_zero)
    cot_copies[0] = []
    cot_copies[1] = [wire.send(cot_zero, cots.at[1], at.partner)]
    cots_out(3, 0, (3, 5, 7, 1))
    forward(2)
    cots_out(2, 1, range(1, planes))
    forward(3)
    backward(3)
    backward_in(3)
    give(3)
    backward(2)
    backward_in(2)
    give(2)
    backward(1)
    backward_in(1)
    give(1)
    backward(0)
    collect(3)
    home.push(3)
    backward_in(0)
    give(0)
    collect(2)
    home.push(2)
    home.pass_on(3)
    weight_grad(act, cots, 0, g_down)
    collect(1)
    home.near()
    home.pass_on(2)
    weight_grad(xn, slope, 1, g_up)
    collect(0)
    home.last()

    @pl.loop(0, width // 256)
    def _(j):
        cols = tile(j)
        d_sum[:, cols] = home.total(cols)

    wire.drain()
    fetch.drain()


def expert_layer(cap, sent, placed, cot_raw, cot_zero, up, down, vec):
    count, width = sent.shape
    units = up.shape[1]
    depth = 4
    bf, full = jnp.bfloat16, jnp.float32
    slots = 8 * cap
    copies = 3 * 7 * depth + 56
    shapes = [
        ((count, width), full),
        ((width, units), bf),
        ((units, width), bf),
        ((depth, 8, cap, width), bf),
        ((3, 8, width), full),
        ((16, 128), full),
    ]
    big = pltpu.VMEM((depth, 8, cap, width), bf)
    return pl.pallas_call(
        functools.partial(expert_kernel, cap),
        out_shape=[jax.ShapeDtypeStruct(*one) for one in shapes],
        in_specs=[ANY_SPEC] * 6 + [VMEM_SPEC],
        out_specs=[VMEM_SPEC, ANY_SPEC, ANY_SPEC, ANY_SPEC, VMEM_SPEC, VMEM_SPEC],
        scratch_shapes=[
            pltpu.VMEM((count, width), bf),
            pltpu.VMEM((depth, 8, 256), jnp.int32),
            pltpu.VMEM((depth, count, width), bf),
            pltpu.VMEM((width, units), bf),
            pltpu.VMEM((units, width), bf),
            pltpu.VMEM((depth, count, width), bf),
            big,
            big,
            big,
            pltpu.VMEM((depth, slots, width), bf),
            pltpu.VMEM((depth, slots, units), bf),
            pltpu.VMEM((depth, slots, units), bf),
            big,
            big,
            big,
            pltpu.VMEM((depth, count, width), bf),
            pltpu.VMEM((5, count, width), bf),
            pltpu.VMEM((8, cap, width), full),
            pltpu.VMEM((depth, 8, cap, 128), full),
            pltpu.VMEM((depth, 8, cap, 128), full),
            pltpu.VMEM((2, max(width, units), max(width, units)), bf),
            pltpu.SemaphoreType.DMA((copies,)),
            pltpu.SemaphoreType.DMA((copies,)),
            pltpu.SemaphoreType.DMA((16,)),
        ],
        compiler_params=pltpu.CompilerParams(
            collective_id=1, has_side_effects=True, vmem_limit_bytes=62 << 20
        ),
    )(sent, placed, cot_raw, cot_zero, up, down, vec)


def reduce_kernel(
    cap,
    d_sum,
    cot,
    w_in,
    qkv_in,
    normed_in,
    ctx,
    tok,
    gains,
    placed,
    delta_in,
    resid,
    vec_part,
    scal,
    block_out,
    token_grad,
    shard_out,
    norm_out,
    vec_out,
    square_out,
    norm_shard,
    wfull,
    qkv,
    normed,
    delta,
    d_resid,
    d_proj,
    d_ctx,
    d_qkv,
    d_norm,
    stage,
    twin_in,
    x_in,
    y_in,
    x_last,
    y_last,
    done,
    z_last,
    back,
    part,
    z_in,
    near_in,
    small,
    small_in,
    square,
    send_sem,
    recv_sem,
    local_sem,
):
    at = Place()
    e, z = at.e, at.z
    depth, planes = 4, 8
    count, width = tok.shape
    shard = shard_out.shape[1]
    column = depth * shard
    half = column // 2
    wire = Wire(send_sem, recv_sem)
    fetch = Fetch(local_sem)
    in_delta = {i: fetch.start(delta_in.at[i], delta.at[i]) for i in (1, 3, 2, 0)}
    in_w = {m: fetch.start(w_in.at[m], wfull.at[m]) for m in (3, 2, 1, 0)}
    in_qkv = fetch.start(qkv_in, qkv)
    in_normed = fetch.start(normed_in, normed)
    at.meet()
    ret = {}
    home = Home(wire, at, "home", lambda i: part.at[i], z_in)

    def give(i):
        if i in in_delta:
            fetch.done(in_delta.pop(i))
        ret[i] = [
            wire.send(delta.at[i, k], back.at[i, e], (at.across(k), z)) for k in range(1, planes)
        ]
        back[i, e] = delta[i, 0]

    def collect(i):
        for copy in ret[i]:
            copy.wait_recv()
        unslot(placed[at.line[i], 0:1, :count], back.at[i], part.at[i])

    def weight_grad(m, left_ref, right):
        @pl.loop(0, planes, unroll=2)
        def _(i):
            cols = pl.ds(pl.multiple_of(i * column, column), column)
            value = dot(left_ref[:, cols], right[...], 0, 0).astype(jnp.bfloat16)
            stage[m, lax.div(i, 4), lax.rem(lax.div(i, 2), 2), lax.rem(i, 2)] = value

    other = 1 - at.core
    first, second, third, fourth, fifth = {}, {}, {}, {}, {}

    def to_core(m):
        first[m] = wire.send(stage.at[m, :, :, other], twin_in.at[m], at.twin)

    def to_plane(m):
        first[m].wait_recv()
        for j in range(2):
            for i in range(2):
                twin_in[m, j, i] = twin_in[m, j, i] + stage[m, j, i, at.core]
        second[m] = (
            wire.send(twin_in.at[m, :, 1 - at.x, pl.ds(0, half)], x_in.at[m], at.over_x),
            wire.send(twin_in.at[m, 1 - at.y, :, pl.ds(half, half)], y_in.at[m], at.over_y),
        )

    def to_last(m):
        second[m][0].wait_recv()
        for j in range(2):
            x_in[m, j] = x_in[m, j] + twin_in[m, j, at.x, 0:half]
        one = wire.send(x_in.at[m, 1 - at.y], x_last.at[m], at.over_y)
        second[m][1].wait_recv()
        for i in range(2):
            y_in[m, i] = y_in[m, i] + twin_in[m, at.y, i, half:]
        two = wire.send(y_in.at[m, 1 - at.x], y_last.at[m], at.over_x)
        third[m] = (one, two)

    def to_owner(m):
        third[m][0].wait_recv()
        pair = (2, shard, width)
        done[m, 0:2] = (x_in[m, at.y] + x_last[m]).reshape(pair)
        third[m][1].wait_recv()
        done[m, 2:4] = (y_in[m, at.x] + y_last[m]).reshape(pair)
        theirs = at.partner[1]
        fourth[m] = (
            wire.send(done.at[m, theirs], z_last.at[m, 0], at.partner),
            wire.send(done.at[m, 3 - theirs], z_last.at[m, 1], at.partner),
        )

    def cross(m):
        fourth[m][1].wait_recv()
        done[m, 3 - z] = done[m, 3 - z] + z_last[m, 1]
        fifth[m] = wire.send(done.at[m, 3 - z], z_last.at[m, 2], at.mirror)

    def own(m):
        fourth[m][0].wait_recv()
        fifth[m].wait_recv()
        total = done[m, z].astype(jnp.float32)
        for k in (0, 2):
            total = total + z_last[m, k].astype(jnp.float32)
        shard_out[m] = total

    fetch.done(in_delta[1])
    near_copy = wire.send(delta.at[1], near_in, at.partner)
    give(3)
    value = cot[...].astype(jnp.float32) + d_sum[...]
    d_resid[...] = value
    d_proj[...] = value.astype(jnp.bfloat16)
    weight_grad(3, ctx, d_proj)
    to_core(3)
    fetch.done(in_w[3])

    @pl.loop(0, width // 512)
    def _(j):
        cols = tile(j, 512)
        d_ctx[:, cols] = dot(d_proj[...], wfull[3, cols, :], 1, 1).astype(jnp.bfloat16)

    to_plane(3)
    fetch.done(in_qkv)
    causal = lax.broadcasted_iota(jnp.int32, (count, count), 0) >= lax.broadcasted_iota(
        jnp.int32, (count, count), 1
    )
    left = lax.broadcasted_iota(jnp.int32, (count, 128), 1) < 64
    scaling = 64 ** (-0.5)

    def pair(i):
        cols = tile(i, 128)
        query = qkv[0, :, cols]
        keys = qkv[1, :, cols]
        values = qkv[2, :, cols]
        d_out = d_ctx[:, cols]
        zero = jnp.zeros_like(query)
        got = []
        for side in range(2):
            mask = left if side == 0 else jnp.logical_not(left)
            q_side = jnp.where(mask, query, zero)
            k_side = jnp.where(mask, keys, zero)
            o_side = jnp.where(mask, d_out, zero)
            scores = dot(q_side, keys, 1, 1) * scaling
            scores = jnp.where(causal, scores, masked_fill)
            top = jnp.max(scores, axis=-1, keepdims=True)
            expo = jnp.exp(scores - top)
            probs = expo / jnp.sum(expo, axis=-1, keepdims=True)
            d_probs = dot(o_side, values, 1, 1)
            inner = jnp.sum(d_probs * probs, axis=-1, keepdims=True)
            d_scores = (probs * (d_probs - inner)).astype(jnp.bfloat16)
            got.append(
                (
                    dot(d_scores, k_side),
                    dot(d_scores, q_side, 0, 0),
                    dot(probs.astype(jnp.bfloat16), o_side, 0, 0),
                )
            )
        d_qkv[0, :, cols] = ((got[0][0] + got[1][0]) * scaling).astype(jnp.bfloat16)
        d_qkv[1, :, cols] = ((got[0][1] + got[1][1]) * scaling).astype(jnp.bfloat16)
        d_qkv[2, :, cols] = (got[0][2] + got[1][2]).astype(jnp.bfloat16)

    pl.loop(0, width // 256, unroll=4)(pair)
    give(2)
    pl.loop(width // 256, width // 128, unroll=4)(pair)
    collect(3)
    home.push(3)
    fetch.done(in_normed)
    weight_grad(2, normed, d_qkv.at[2])
    to_core(2)
    to_last(3)
    weight_grad(1, normed, d_qkv.at[1])
    to_core(1)
    to_plane(2)
    weight_grad(0, normed, d_qkv.at[0])
    to_core(0)
    home.pass_on(3)
    to_owner(3)
    to_plane(1)
    collect(2)
    home.push(2)
    for m in (2, 1, 0):
        fetch.done(in_w[m])

    @pl.loop(0, width // 512)
    def _(j):
        cols = tile(j, 512)
        d_norm[:, cols] = (
            dot(d_qkv[0], wfull[0, cols, :], 1, 1)
            + dot(d_qkv[1], wfull[1, cols, :], 1, 1)
            + dot(d_qkv[2], wfull[2, cols, :], 1, 1)
        )

    gain = gains[0:1, :].astype(jnp.float32)
    d_gain = jnp.zeros((8, width), jnp.float32)
    d_bias = jnp.zeros((8, width), jnp.float32)
    for i in range(0, count, 64):
        piece = tok[i : i + 64, :].astype(jnp.float32)
        average = jnp.mean(piece, axis=-1, keepdims=True)
        centred = piece - average
        variance = jnp.mean(centred * centred, axis=-1, keepdims=True)
        scale = lax.rsqrt(variance + norm_eps)
        hat = centred * scale
        dx = d_norm[i : i + 64, :]
        d_gain = d_gain + fold(dx * hat)
        d_bias = d_bias + fold(dx)
        dh = dx * gain
        mean_one = jnp.mean(dh, axis=-1, keepdims=True)
        mean_two = jnp.mean(dh * hat, axis=-1, keepdims=True)
        d_in = scale * (dh - mean_one - hat * mean_two)
        token_grad[i : i + 64, :] = (d_resid[i : i + 64, :] + d_in).astype(jnp.bfloat16)
    mine = small.at[0]
    mine[...] = jnp.zeros((8, width), jnp.float32)
    mine[2:3, :] = gains[2:3, :].astype(jnp.float32)
    mine[0:1, :] = jnp.sum(d_gain, axis=0, keepdims=True)
    mine[1:2, :] = jnp.sum(d_bias, axis=0, keepdims=True)
    for k in range(3):
        mine[3 + k : 4 + k, :] = jnp.sum(vec_part[k], axis=0, keepdims=True)
    small_copy = wire.send(mine, small.at[1], at.partner)
    to_last(2)
    home.relay_far()
    home.pass_on(2)
    near_copy.wait_recv()
    fetch.done(in_delta.pop(0))

    @pl.loop(0, planes)
    def _(k):
        delta[0, k] = (delta[0, k].astype(jnp.float32) + near_in[k].astype(jnp.float32)).astype(
            jnp.bfloat16
        )

    to_plane(0)
    cross(3)
    small_copy.wait_recv()
    small[2] = small[0] + small[1]
    small_copy = wire.send(small.at[2], small.at[3], at.mirror)
    to_last(1)
    to_owner(2)
    own(3)
    to_last(0)
    cross(2)
    small_copy.wait_recv()
    total = small[2] + small[3]
    vec_out[...] = total
    small_in[e] = total
    spot = small_in.at[e]
    plane_copies = [wire.send(spot, spot, (at.across(k), z)) for k in range(1, planes)]
    give(0)
    to_owner(1)
    own(2)
    to_owner(0)
    cross(1)
    cross(0)
    own(1)
    for copy in plane_copies:
        copy.wait_recv()
    total = small_in[0]
    for k in range(1, planes):
        total = total + small_in[k]
    norm_out[...] = total
    norm_rows = norm_out[0:2, :]
    mine = norm_out[0:2, tile(e, 128)]
    lanes = norm_shard.shape[1]
    value = mine[:, 0:lanes]
    for k in range(1, depth):
        value = jnp.where(z == k, mine[:, k * lanes : (k + 1) * lanes], value)
    norm_shard[...] = value
    lane = lax.broadcasted_iota(jnp.int32, (1, 128), 1)
    routed = jnp.sum(jnp.where(lane == e, norm_out[2:3, 0:128], 0.0), keepdims=True)
    gates = jnp.sum(scal[0:8, 0:1], keepdims=True) - 0.5 * (depth * planes * cap - routed)
    vec_rows = vec_out[3:6, :]
    squares = jnp.sum(norm_rows * norm_rows, axis=0, keepdims=True) / (planes * depth) + jnp.sum(
        vec_rows * vec_rows, axis=0, keepdims=True
    ) / depth
    local = scal[8:16, :]
    for m in (3, 2, 1):
        local = local + fold(square_lanes(shard_out[m]))
    lane_squares = squares[:, 0:128]
    for i in range(128, width, 128):
        lane_squares = lane_squares + squares[:, i : i + 128]
    head = lax.broadcasted_iota(jnp.int32, (8, 128), 0) == 0
    local = local + jnp.where(head, jnp.broadcast_to(lane_squares, (8, 128)), 0.0)
    own(0)
    square[0, e] = local + fold(square_lanes(shard_out[0]))
    spot = square.at[0, e]
    copies = [wire.send(spot, spot, (at.across(k), z)) for k in range(1, planes)]
    collect(0)
    home.finish()

    @pl.loop(0, width // 256)
    def _(j):
        cols = tile(j)
        block_out[:, cols] = (resid[:, cols] + part[0, :, cols].astype(jnp.float32)).astype(
            jnp.bfloat16
        )

    for copy in copies:
        copy.wait_recv()
    total = square[0, 0]
    for k in range(1, planes):
        total = total + square[0, k]
    square[1, z] = total
    spot = square.at[1, z]
    copies = [wire.send(spot, spot, at.mates[k]) for k in range(1, depth)]
    for copy in copies:
        copy.wait_recv()
    total = square[1, 0]
    for d in range(1, depth):
        total = total + square[1, d]
    norm = jnp.sqrt(jnp.sum(total, keepdims=True))
    which = lax.broadcasted_iota(jnp.int32, (8, 128), 0)
    stats = jnp.where(which == 0, routed / (count * depth), gates / routed)
    clip = clip_level / jnp.maximum(norm, clip_level)
    square_out[...] = jnp.where(which < 2, stats, jnp.where(which == 2, norm, clip))
    wire.drain()
    fetch.drain()


def attend_back(cap, shard, *args):
    tokens = args[6]
    count, width = tokens.shape
    depth = 4
    bf, full = jnp.bfloat16, jnp.float32
    column = depth * shard
    half = column // 2
    copies = 7 * depth + 96
    shapes = [
        ((count, width), bf),
        ((count, width), bf),
        ((4, shard, width), full),
        ((8, width), full),
        ((8, width), full),
        ((8, 128), full),
        ((2, width // 32), full),
    ]
    return pl.pallas_call(
        functools.partial(reduce_kernel, cap),
        out_shape=[jax.ShapeDtypeStruct(*one) for one in shapes],
        in_specs=[VMEM_SPEC] * 2
        + [ANY_SPEC] * 3
        + [VMEM_SPEC] * 4
        + [ANY_SPEC]
        + [VMEM_SPEC] * 3,
        out_specs=[VMEM_SPEC] * 7,
        scratch_shapes=[
            pltpu.VMEM((4, width, width), bf),
            pltpu.VMEM((3, count, width), bf),
            pltpu.VMEM((count, width), bf),
            pltpu.VMEM((depth, 8, cap, width), bf),
            pltpu.VMEM((count, width), full),
            pltpu.VMEM((count, width), bf),
            pltpu.VMEM((count, width), bf),
            pltpu.VMEM((3, count, width), bf),
            pltpu.VMEM((count, width), full),
            pltpu.VMEM((4, 2, 2, 2, column, width), bf),
            pltpu.VMEM((4, 2, 2, column, width), bf),
            pltpu.VMEM((4, 2, half, width), bf),
            pltpu.VMEM((4, 2, half, width), bf),
            pltpu.VMEM((4, half, width), bf),
            pltpu.VMEM((4, half, width), bf),
            pltpu.VMEM((4, depth, shard, width), bf),
            pltpu.VMEM((4, depth - 1, shard, width), bf),
            pltpu.VMEM((depth, 8, cap, width), bf),
            pltpu.VMEM((depth, count, width), bf),
            pltpu.VMEM((5, count, width), bf),
            pltpu.VMEM((8, cap, width), bf),
            pltpu.VMEM((4, 8, width), full),
            pltpu.VMEM((8, 8, width), full),
            pltpu.VMEM((2, 8, 8, 128), full),
            pltpu.SemaphoreType.DMA((copies,)),
            pltpu.SemaphoreType.DMA((copies,)),
            pltpu.SemaphoreType.DMA((16,)),
        ],
        compiler_params=pltpu.CompilerParams(
            collective_id=2, has_side_effects=True, vmem_limit_bytes=62 << 20
        ),
    )(*args)


def adam_quick(weight, first, second, grad, clip_factor, rate, decay):
    clipped = grad * clip_factor
    moment = beta_one * first + (1.0 - beta_one) * clipped
    square = beta_two * second + (1.0 - beta_two) * clipped * clipped
    root = jnp.sqrt(square * (1.0 / (1.0 - beta_two**STEP))) + adam_eps
    step = moment * (rate / (1.0 - beta_one**STEP)) / root
    return (weight * (1.0 - rate * decay) - step, moment, square)


def adam_kernel(*refs):
    ins, outs = refs[:23], refs[23:]
    facts, block_in, token_in = ins[20:23]
    clip = facts[3:4, 0:1]
    for k in range(3):
        weight, first, second, grad = ins[4 * k : 4 * k + 4]
        new, moment, square = outs[3 * k : 3 * k + 3]
        new[...], moment[...], square[...] = adam_quick(
            weight[...].astype(jnp.float32),
            first[...],
            second[...],
            grad[...].astype(jnp.float32),
            clip,
            rate_matrix,
            decay_rate,
        )

    @pl.when(pl.program_id(0) == 0)
    def _():
        weight, first, second, grad = ins[12:16]
        for k in range(3):
            got = adam_quick(
                weight[k], first[k], second[k], grad[3 + k : 4 + k, :], clip, rate_vector, 0.0
            )
            for out, value in zip(outs[9:12], got):
                out[k] = value
        weight, first, second, grad = ins[16:20]
        got = adam_quick(
            weight[...], first[...], second[...], grad[...], clip, rate_vector, 0.0
        )
        for out, value in zip(outs[12:15], got):
            out[...] = value
        outs[15][...] = block_in[...]
        outs[16][...] = token_in[...]
        outs[17][...] = facts[2:3, 0:1]
        outs[18][...] = jnp.concatenate([facts[0:1, 0:1], facts[1:2, 0:1]], axis=1)


def adam_all(up, down, attn, vector, norm, facts, block_out, token_grad):
    steps = 4
    full = jnp.float32

    def whole(shape):
        return pl.BlockSpec(shape, lambda i: (0,) * len(shape))

    def cut(v):
        return pl.BlockSpec((v.shape[0] // steps, v.shape[1]), lambda i: (i, 0))

    args, in_specs, out_specs, shapes = [], [], [], []
    for group in (up, down, attn):
        args += group
        in_specs += [cut(v) for v in group]
        out_specs += [cut(group[0])] * 3
        shapes += [jax.ShapeDtypeStruct(group[0].shape, full)] * 3
    for group in (vector, norm):
        args += group
        in_specs += [whole(v.shape) for v in group]
        out_specs += [whole(group[0].shape)] * 3
        shapes += [jax.ShapeDtypeStruct(group[0].shape, full)] * 3
    args += [facts]
    in_specs += [whole(facts.shape)]
    for v in (block_out, token_grad):
        args += [v]
        in_specs += [whole(v.shape)]
        out_specs += [whole(v.shape)]
        shapes += [jax.ShapeDtypeStruct(v.shape, v.dtype)]
    for shape in ((1, 1), (1, 2)):
        out_specs += [whole(shape)]
        shapes += [jax.ShapeDtypeStruct(shape, full)]
    return pl.pallas_call(
        adam_kernel,
        grid=(steps,),
        out_shape=shapes,
        in_specs=in_specs,
        out_specs=out_specs,
        compiler_params=pltpu.CompilerParams(vmem_limit_bytes=60 << 20),
    )(*args)


def shards(
    tokens,
    cotangent,
    routes,
    attn_weight,
    attn_first,
    attn_second,
    norm_param,
    norm_first,
    norm_second,
    up_weight,
    up_first,
    up_second,
    down_weight,
    down_first,
    down_second,
    expert_vector,
    vector_first,
    vector_second,
):
    experts_here = lax.axis_size(EX)
    hidden_size = lax.axis_size(HI)
    token_count = tokens.shape[0]
    features = tokens.shape[1]
    capacity = 2 * token_count // experts_here
    slot_rows = experts_here * capacity
    head_dim = features // HEADS
    scaling = head_dim ** (-0.5)
    attn_low = attn_weight.astype(jnp.bfloat16)
    norm_low = norm_param.astype(jnp.bfloat16)
    attn_full, norm_full = (
        lax.all_gather(attn_low, BOTH, axis=1, tiled=True),
        lax.all_gather(norm_low, BOTH, axis=1, tiled=True),
    )
    inputs = tokens.astype(jnp.float32)
    normed, norm_pull = jax.vjp(
        layer_norm, inputs, norm_full[0].astype(jnp.float32), norm_full[1].astype(jnp.float32)
    )
    normed_low = normed.astype(jnp.bfloat16)
    projected = jnp.einsum(
        "td,sde->ste", normed_low, attn_full[:3], preferred_element_type=jnp.float32
    ).astype(jnp.bfloat16)
    query = projected[0].reshape(token_count, HEADS, head_dim)
    keys_all = projected[1].reshape(token_count, HEADS, head_dim)
    values_all = projected[2].reshape(token_count, HEADS, head_dim)
    causal = jnp.arange(token_count)[:, None] >= jnp.arange(token_count)[None, :]

    def score_rows():
        raw = (
            jnp.einsum("qhe,khe->hqk", query, keys_all, preferred_element_type=jnp.float32)
            * scaling
        )
        return jnp.where(causal[None], raw, masked_fill)

    scores = score_rows()
    row_max = jnp.max(scores, axis=-1, keepdims=True)
    expo = jnp.exp(scores - row_max)
    row_total = jnp.sum(expo, axis=-1, keepdims=True)
    log_total = row_max + jnp.log(row_total)
    probs_low = (expo / row_total).astype(jnp.bfloat16)
    context = jnp.einsum("hqk,khe->qhe", probs_low, values_all, preferred_element_type=jnp.float32)
    context = context.reshape(token_count, features).astype(jnp.bfloat16)
    resid = inputs + jnp.dot(context, attn_full[3], preferred_element_type=jnp.float32)
    route = routes[:, 0]
    chosen = (route[:, None] == jnp.arange(experts_here, dtype=jnp.int32)[None, :]).astype(
        jnp.int32
    )
    ranked = jnp.sum((jnp.cumsum(chosen, axis=0) - 1) * chosen, axis=1)
    placed = route * capacity + ranked
    placing = (jnp.arange(slot_rows, dtype=jnp.int32)[:, None] == placed[None, :]).astype(
        jnp.bfloat16
    )
    outgoing = jnp.dot(
        placing, resid.astype(jnp.bfloat16), preferred_element_type=jnp.float32
    ).astype(jnp.bfloat16)
    occupied = jnp.sum(placing.astype(jnp.float32), axis=1).astype(jnp.bfloat16)
    arrived, arrived_mask = (
        lax.all_to_all(
            outgoing.reshape(experts_here, capacity, features),
            EX,
            split_axis=0,
            concat_axis=0,
            tiled=True,
        ),
        lax.all_to_all(
            occupied.reshape(experts_here, capacity),
            EX,
            split_axis=0,
            concat_axis=0,
            tiled=True,
        ),
    )
    gathered, gathered_mask = (
        lax.all_gather(arrived, HI, axis=0, tiled=True),
        lax.all_gather(arrived_mask, HI, axis=0, tiled=True),
    )
    rows_all = gathered.reshape(-1, features)
    mask_all = gathered_mask.reshape(-1).astype(jnp.float32)
    rows_float = rows_all.astype(jnp.float32)
    centroid = expert_vector[0, 0]
    gating = jax.nn.sigmoid(jnp.sum(rows_float * centroid, axis=-1))
    expert_normed, expert_pull = jax.vjp(
        layer_norm, rows_float, expert_vector[0, 1], expert_vector[0, 2]
    )
    expert_low = expert_normed.astype(jnp.bfloat16)
    before = jnp.dot(expert_low, up_weight[0], preferred_element_type=jnp.float32)
    after, gelu_pull = jax.vjp(gelu_exact, before)
    after_low = after.astype(jnp.bfloat16)
    branch_own = lax.psum_scatter(
        jnp.dot(after_low, down_weight[0], preferred_element_type=jnp.float32).astype(jnp.bfloat16),
        HI,
        scatter_dimension=0,
        tiled=True,
    ).astype(jnp.float32)
    own_start = lax.axis_index(HI) * slot_rows
    gating_own = lax.dynamic_slice_in_dim(gating, own_start, slot_rows, 0)
    delta = (gating_own[:, None] * branch_own).astype(jnp.bfloat16)
    returned = lax.all_to_all(
        delta.reshape(experts_here, capacity, features),
        EX,
        split_axis=0,
        concat_axis=0,
        tiled=True,
    )
    delta_tokens = jnp.einsum(
        "st,sd->td",
        placing,
        returned.reshape(slot_rows, features),
        preferred_element_type=jnp.float32,
    )
    block_out = (resid + delta_tokens).astype(jnp.bfloat16)
    routed_count = jnp.sum(mask_all)
    gate_total = jnp.sum(mask_all * gating)
    expert_stats = jnp.stack(
        [routed_count / (token_count * hidden_size), gate_total / routed_count]
    )[:, None]
    cot_slots = jnp.dot(placing, cotangent, preferred_element_type=jnp.float32).astype(jnp.bfloat16)
    cot_arrived = lax.all_to_all(
        cot_slots.reshape(experts_here, capacity, features),
        EX,
        split_axis=0,
        concat_axis=0,
        tiled=True,
    )
    cot_rows = lax.all_gather(cot_arrived, HI, axis=0, tiled=True).reshape(-1, features)
    d_branch = (gating[:, None] * cot_rows.astype(jnp.float32)).astype(jnp.bfloat16)
    grad_down = jnp.einsum("gf,gd->fd", after_low, d_branch, preferred_element_type=jnp.float32)
    d_after = jnp.einsum("gd,fd->gf", d_branch, down_weight[0], preferred_element_type=jnp.float32)
    d_before = gelu_pull(d_after)[0].astype(jnp.bfloat16)
    grad_up = jnp.einsum("gd,gf->df", expert_low, d_before, preferred_element_type=jnp.float32)
    d_expert_normed = jnp.einsum(
        "gf,df->gd", d_before, up_weight[0], preferred_element_type=jnp.float32
    )
    d_rows, d_expert_gain, d_expert_bias = expert_pull(d_expert_normed)
    d_rows_own = lax.psum_scatter(
        d_rows.astype(jnp.bfloat16), HI, scatter_dimension=0, tiled=True
    ).astype(jnp.float32)
    cot_own = lax.dynamic_slice_in_dim(cot_rows, own_start, slot_rows, 0).astype(jnp.float32)
    rows_own = lax.dynamic_slice_in_dim(rows_float, own_start, slot_rows, 0)
    d_gating = jnp.sum(cot_own * branch_own, axis=-1)
    d_logit = d_gating * gating_own * (1.0 - gating_own)
    d_centroid = jnp.sum(d_logit[:, None] * rows_own, axis=0)
    d_sent = (d_rows_own + d_logit[:, None] * centroid).astype(jnp.bfloat16)
    back_slots = lax.all_to_all(
        d_sent.reshape(experts_here, capacity, features),
        EX,
        split_axis=0,
        concat_axis=0,
        tiled=True,
    )
    d_resid = cotangent.astype(jnp.float32) + jnp.einsum(
        "st,sd->td",
        placing,
        back_slots.reshape(slot_rows, features),
        preferred_element_type=jnp.float32,
    )
    vector_grad = lax.psum(jnp.stack([d_centroid, d_expert_gain, d_expert_bias])[None], HI)
    d_project = d_resid.astype(jnp.bfloat16)
    grad_out_proj = jnp.einsum("td,te->de", context, d_project, preferred_element_type=jnp.float32)
    d_context = jnp.einsum(
        "te,de->td", d_project, attn_full[3], preferred_element_type=jnp.float32
    ).astype(jnp.bfloat16)
    d_context = d_context.reshape(token_count, HEADS, head_dim)
    attn_probs = jnp.exp(score_rows() - log_total)
    probs_again = attn_probs.astype(jnp.bfloat16)
    d_probs = jnp.einsum("qhe,khe->hqk", d_context, values_all, preferred_element_type=jnp.float32)
    d_values = jnp.einsum(
        "hqk,qhe->khe", probs_again, d_context, preferred_element_type=jnp.float32
    ).astype(jnp.bfloat16)
    d_scores = (
        attn_probs * (d_probs - jnp.sum(d_probs * attn_probs, axis=-1, keepdims=True))
    ).astype(jnp.bfloat16)
    d_query = (
        jnp.einsum("hqk,khe->qhe", d_scores, keys_all, preferred_element_type=jnp.float32) * scaling
    ).astype(jnp.bfloat16)
    d_keys = (
        jnp.einsum("hqk,qhe->khe", d_scores, query, preferred_element_type=jnp.float32) * scaling
    ).astype(jnp.bfloat16)
    d_projected = jnp.stack(
        [
            d_query.reshape(token_count, features),
            d_keys.reshape(token_count, features),
            d_values.reshape(token_count, features),
        ]
    )
    grad_qkv = jnp.einsum(
        "td,ste->sde", normed_low, d_projected, preferred_element_type=jnp.float32
    )
    d_normed = jnp.einsum(
        "ste,sde->td", d_projected, attn_full[:3], preferred_element_type=jnp.float32
    )
    d_inputs, d_norm_gain, d_norm_bias = norm_pull(d_normed)
    token_grad = (d_resid + d_inputs).astype(jnp.bfloat16)
    grad_attn = jnp.concatenate([grad_qkv, grad_out_proj[None]], axis=0)
    grad_norm_param = jnp.stack([d_norm_gain, d_norm_bias])
    attn_shard, norm_shard = (
        lax.psum_scatter(grad_attn, BOTH, scatter_dimension=1, tiled=True),
        lax.psum_scatter(grad_norm_param, BOTH, scatter_dimension=1, tiled=True),
    )
    local_square = (
        jnp.sum(attn_shard * attn_shard)
        + jnp.sum(norm_shard * norm_shard)
        + jnp.sum(grad_up * grad_up)
        + jnp.sum(grad_down * grad_down)
        + jnp.sum(vector_grad * vector_grad) / hidden_size
    )
    grad_norm = jnp.sqrt(lax.psum(local_square, BOTH))
    clip_factor = clip_level / jnp.maximum(grad_norm, clip_level)
    attn_new = adam_step(
        attn_weight, attn_first, attn_second, attn_shard, clip_factor, rate_matrix, decay_rate
    )
    norm_new = adam_step(
        norm_param, norm_first, norm_second, norm_shard, clip_factor, rate_vector, 0.0
    )
    up_new = adam_step(
        up_weight.astype(jnp.float32),
        up_first,
        up_second,
        grad_up[None],
        clip_factor,
        rate_matrix,
        decay_rate,
    )
    down_new = adam_step(
        down_weight.astype(jnp.float32),
        down_first,
        down_second,
        grad_down[None],
        clip_factor,
        rate_matrix,
        decay_rate,
    )
    vector_new = adam_step(
        expert_vector, vector_first, vector_second, vector_grad, clip_factor, rate_vector, 0.0
    )
    return (
        block_out,
        token_grad,
        grad_norm,
        attn_new[0],
        attn_new[1],
        attn_new[2],
        norm_new[0],
        norm_new[1],
        norm_new[2],
        up_new[0],
        up_new[1],
        up_new[2],
        down_new[0],
        down_new[1],
        down_new[2],
        vector_new[0],
        vector_new[1],
        vector_new[2],
        expert_stats,
    )


def fast_shards(
    tokens,
    cotangent,
    routes,
    attn_weight,
    attn_first,
    attn_second,
    norm_param,
    norm_first,
    norm_second,
    up_weight,
    up_first,
    up_second,
    down_weight,
    down_first,
    down_second,
    expert_vector,
    vector_first,
    vector_second,
):
    experts = lax.axis_size(EX)
    count, width = tokens.shape
    cap = 2 * count // experts
    shard = attn_weight.shape[1]
    w_full, qkv, normed, ctx, resid, sent, placed, gains, cot_raw, cot_zero = attend(
        cap, tokens, attn_weight, norm_param, routes.reshape(1, count), cotangent
    )
    rows = lambda v: v.reshape(3, 1, width)
    d_sum, grad_up, grad_down, delta, vec_part, scal = expert_layer(
        cap, sent, placed, cot_raw, cot_zero, up_weight[0], down_weight[0], rows(expert_vector)
    )
    block_out, token_grad, attn_shard, norm_grads, vec_grads, facts, norm_shard = attend_back(
        cap,
        shard,
        d_sum,
        cotangent,
        w_full,
        qkv,
        normed,
        ctx,
        tokens,
        gains,
        placed,
        delta,
        resid,
        vec_part,
        scal,
    )
    flat = lambda v: v.reshape(-1, v.shape[-1])
    new = adam_all(
        [flat(v) for v in (up_weight, up_first, up_second, grad_up)],
        [flat(v) for v in (down_weight, down_first, down_second, grad_down)],
        [flat(v) for v in (attn_weight, attn_first, attn_second, attn_shard)],
        [rows(v) for v in (expert_vector, vector_first, vector_second)] + [vec_grads],
        [norm_param, norm_first, norm_second, norm_shard],
        facts,
        block_out,
        token_grad,
    )
    up_new = [v.reshape(up_weight.shape) for v in new[0:3]]
    down_new = [v.reshape(down_weight.shape) for v in new[3:6]]
    attn_new = [v.reshape(attn_weight.shape) for v in new[6:9]]
    vector_new = [v.reshape(expert_vector.shape) for v in new[9:12]]
    norm_new = new[12:15]
    block_out, token_grad = new[15:17]
    grad_norm = new[17].reshape(())
    expert_stats = new[18].reshape(2, 1)
    return (
        block_out,
        token_grad,
        grad_norm,
        *attn_new,
        *norm_new,
        *up_new,
        *down_new,
        *vector_new,
        expert_stats,
    )


def solution(mesh):
    small = mesh.shape[EX] == 8 and mesh.shape[HI] == 4
    return jax.shard_map(
        fast_shards if small else shards,
        mesh=mesh,
        in_specs=(
            P(BOTH, None),
            P(BOTH, None),
            P(BOTH, None),
            P(None, BOTH, None),
            P(None, BOTH, None),
            P(None, BOTH, None),
            P(None, BOTH),
            P(None, BOTH),
            P(None, BOTH),
            P(EX, None, HI),
            P(EX, None, HI),
            P(EX, None, HI),
            P(EX, HI, None),
            P(EX, HI, None),
            P(EX, HI, None),
            P(EX, None, None),
            P(EX, None, None),
            P(EX, None, None),
        ),
        out_specs=(
            P(BOTH, None),
            P(BOTH, None),
            P(),
            P(None, BOTH, None),
            P(None, BOTH, None),
            P(None, BOTH, None),
            P(None, BOTH),
            P(None, BOTH),
            P(None, BOTH),
            P(EX, None, HI),
            P(EX, None, HI),
            P(EX, None, HI),
            P(EX, HI, None),
            P(EX, HI, None),
            P(EX, HI, None),
            P(EX, None, None),
            P(EX, None, None),
            P(EX, None, None),
            P(None, EX),
        ),
        check_vma=False,
    )
```
